32 devices in a mesh: fsdp: 2 (over core), ctx: 4 (over y, x), tp: 4 (over z).
Axes of the slice: x: 2, y: 2, z: 4, core: 2. Of those that a mesh axis runs over, the one named last changes fastest.
Arguments:
- tokens: bfloat16 [16, 680, 1024], P('fsdp', 'ctx'), may hold values from -6 to 6
- cotangent: bfloat16 [16, 680, 1024], P('fsdp', 'ctx'), may hold values from -6 to 6
- class_table: float32 [1000, 1024], replicated, may hold values from -6 to 6
- labels: int32 [16], P('fsdp'), may hold values from 0 to 999
- scale_ids: int32 [16, 680], P('fsdp', 'ctx'), may hold values from 0 to 9, as said below
- in_weight: float32 [1024, 13, 1024], P(('fsdp', 'ctx'), None, 'tp'), may hold values from -0.1875 to 0.1875
- in_first: float32 [1024, 13, 1024], P(('fsdp', 'ctx'), None, 'tp'), as said below
- in_second: float32 [1024, 13, 1024], P(('fsdp', 'ctx'), None, 'tp'), as said below
- out_weight: float32 [5, 1024, 1024], P(None, 'tp', ('fsdp', 'ctx')), as said below
- out_first: float32 [5, 1024, 1024], P(None, 'tp', ('fsdp', 'ctx')), as said below
- out_second: float32 [5, 1024, 1024], P(None, 'tp', ('fsdp', 'ctx')), as said below
- vectors: float32 [16, 1024], P(None, 'tp'), as said below
- vec_first: float32 [16, 1024], P(None, 'tp'), as said below
- vec_second: float32 [16, 1024], P(None, 'tp'), as said below
Outputs:
- mixed: bfloat16 [16, 680, 1024], P('fsdp', 'ctx')
- input_grad: float32 [16, 680, 1024], P('fsdp', 'ctx')
- condition_grad: float32 [16, 1024], P('fsdp')
- grad_norm: float32 [], replicated
- in_weight_new: float32 [1024, 13, 1024], P(('fsdp', 'ctx'), None, 'tp')
- in_first_new: float32 [1024, 13, 1024], P(('fsdp', 'ctx'), None, 'tp')
- in_second_new: float32 [1024, 13, 1024], P(('fsdp', 'ctx'), None, 'tp')
- in_copy: bfloat16 [1024, 13, 1024], P(('fsdp', 'ctx'), None, 'tp')
- out_weight_new: float32 [5, 1024, 1024], P(None, 'tp', ('fsdp', 'ctx'))
- out_first_new: float32 [5, 1024, 1024], P(None, 'tp', ('fsdp', 'ctx'))
- out_second_new: float32 [5, 1024, 1024], P(None, 'tp', ('fsdp', 'ctx'))
- out_copy: bfloat16 [5, 1024, 1024], P(None, 'tp', ('fsdp', 'ctx'))
- vec_new: float32 [16, 1024], P(None, 'tp')
- vec_first_new: float32 [16, 1024], P(None, 'tp')
- vec_second_new: float32 [16, 1024], P(None, 'tp')
- vec_copy: bfloat16 [16, 1024], P(None, 'tp')
- second_bias_grad: float32 [1024], P('tp')
The draws below stay inside these ranges and needn't reach their ends.
Inputs may be any that keep to these rules, and one draw needn't show every extreme that they name: `scale_ids`: in each sequence, scale s holds exactly k * k tokens, with k = 1, 2, 3, 4, 5, 6, 8, 10, 13, 16 for s = 0 to 9. `in_second`: positive. `out_second`: positive. `vec_second`: positive. `in_first`: of both signs. `out_first`: of both signs. `vec_first`: of both signs. `out_weight`: of both signs. `vectors`: of both signs.
All inputs are finite; a program needn't handle non-finite values.
Results may differ from the reference program's by a relative error of at most 0.02.
Values may be sent and summed in bfloat16 or wider, within the bound.
A program may use at most 192 MiB of HBM per device.

```python
import math
import jax
import jax.numpy as jnp
from jax import lax

D = 1024
HEADS = 16
HD = 64
FF = 4096
CLASSES = 1000
LEN = 680
STEP = 5
SEQ_DEV = 8
SEQS = 16
INROWS = 13
SHARD_ROWS = 128


SIDES = (1, 2, 3, 4, 5, 6, 8, 10, 13, 16)


def grad_unit():
    blocks_ff = FF // D
    return 1.0 / math.sqrt((10 + 2 * blocks_ff) * D * D + (12 + blocks_ff) * D)


def draw_scale_ids(key, part):
    key = jax.random.fold_in(key, 11)
    position = jnp.arange(LEN, dtype=jnp.int32)
    bounds = jnp.cumsum(jnp.array([side_length * side_length for side_length in SIDES], dtype=jnp.int32))
    ordered = jnp.sum((position[:, None] >= bounds[None, :]).astype(jnp.int32), axis=1)
    seq_keys = jax.random.split(key, SEQS)
    return jax.vmap(lambda one_key: jax.random.permutation(one_key, ordered))(seq_keys)


def draw_out_weight(key, part):
    key = jax.random.fold_in(key, 12)
    full_shape = (1 + FF // D, D, D)
    base = jax.random.normal(key, full_shape, jnp.float32)
    row_std = jnp.where(jnp.arange(full_shape[0])[:, None, None] == 0, 4.0 / math.sqrt(D), 1.5 / math.sqrt(FF))
    return base * row_std


def draw_vectors(key, part):
    key = jax.random.fold_in(key, 13)
    rows_total = 12 + FF // D
    noise_key, rough_key = jax.random.split(key)
    noise = jax.random.normal(noise_key, (rows_total, D), jnp.float32)
    rough = jnp.exp(jax.random.uniform(rough_key, (rows_total, D), jnp.float32, -0.35, 0.35))
    column = jnp.arange(D, dtype=jnp.float32)
    ramp = (column / D)[None, :]
    local_ramp = ((jnp.arange(D) % SHARD_ROWS).astype(jnp.float32) / SHARD_ROWS)[None, :]
    row_index = jnp.arange(rows_total)[:, None]
    gamma_rows = (0.6 + 0.8 * ramp) * rough
    scale_rows = 0.4 * ramp + 0.4 * local_ramp + 0.15 * noise
    gain_rows = (0.8 + 0.6 * ramp) * rough
    value_rows = (0.2 + 0.6 * ramp) * noise
    result = 0.3 * noise
    result = jnp.where((row_index == 0) | (row_index == 3), gamma_rows, result)
    result = jnp.where((row_index == 1) | (row_index == 4), scale_rows, result)
    result = jnp.where(row_index == 7, value_rows, result)
    result = jnp.where((row_index == 8) | (row_index == 9), gain_rows, result)
    result = jnp.where((row_index >= 10) & (row_index < 10 + FF // D), 0.5 * noise, result)
    return result


def first_moment(key, full_shape, amplitude):
    return jax.random.normal(key, full_shape, jnp.float32) * amplitude


def second_moment(key, full_shape, amplitude):
    factor = jnp.exp(jax.random.uniform(key, full_shape, jnp.float32, 0.0, math.log(4.0)))
    return factor * amplitude * amplitude


def draw_in_first(key, part):
    key = jax.random.fold_in(key, 21)
    full_shape = (D, 9 + FF // D, D)
    return first_moment(key, full_shape, grad_unit())


def draw_in_second(key, part):
    key = jax.random.fold_in(key, 22)
    full_shape = (D, 9 + FF // D, D)
    return second_moment(key, full_shape, grad_unit())


def draw_out_first(key, part):
    key = jax.random.fold_in(key, 23)
    full_shape = (1 + FF // D, D, D)
    return first_moment(key, full_shape, grad_unit())


def draw_out_second(key, part):
    key = jax.random.fold_in(key, 24)
    full_shape = (1 + FF // D, D, D)
    return second_moment(key, full_shape, grad_unit())


def draw_vec_first(key, part):
    key = jax.random.fold_in(key, 25)
    full_shape = (12 + FF // D, D)
    return first_moment(key, full_shape, 4.0 * grad_unit())


def draw_vec_second(key, part):
    key = jax.random.fold_in(key, 26)
    full_shape = (12 + FF // D, D)
    return second_moment(key, full_shape, 4.0 * grad_unit())


def touch_ends(drawn, key, least, largest):
    place = [jax.random.randint(jax.random.fold_in(key, axis), (), 0, length) for axis, length in enumerate(drawn.shape)]
    main_axis = drawn.shape.index(max(drawn.shape))
    next_to = place[:main_axis] + [(place[main_axis] + 1) % drawn.shape[main_axis]] + place[main_axis + 1:]
    return drawn.at[tuple(place)].set(least).at[tuple(next_to)].set(largest)


def block_scale(stream_key, dims, shards, smallest, top_value):
    level, own = 1.0, jax.random.fold_in(stream_key, 6)
    for axis_at, blocks in shards:
        steps = jnp.exp(jax.random.uniform(jax.random.fold_in(own, axis_at), (blocks,), jnp.float32, smallest / len(shards), top_value / len(shards)))
        level = level * jnp.repeat(steps, dims[axis_at] // blocks).reshape([-1 if axis == axis_at else 1 for axis in range(len(dims))])
    return level


def gaussian(stream_key, shape, width, reach, pieces=(), kind=jnp.bfloat16):
    drawn = width * jax.random.normal(stream_key, shape, jnp.float32)
    if pieces:
        drawn = drawn * block_scale(stream_key, shape, pieces, -0.22, 0.18)
    return jnp.clip(drawn, -reach, reach).astype(kind)


def setup_inputs(seed: int = 0) -> dict:
    arg_keys = jax.random.split(jax.random.key(seed), 15)
    return {
        "tokens": gaussian(arg_keys[0], (SEQS, LEN, D), 1.0, 6.0, ((0, 2), (1, 4))),
        "cotangent": gaussian(arg_keys[1], (SEQS, LEN, D), 1.0, 6.0, ((0, 2), (1, 4))),
        "class_table": gaussian(arg_keys[2], (CLASSES, D), 1.0, 6.0, (), jnp.float32),
        "labels": touch_ends(jax.random.randint(arg_keys[3], (SEQS,), 0, CLASSES), jax.random.fold_in(arg_keys[3], 1), 0, CLASSES - 1).astype(jnp.int32),
        "scale_ids": draw_scale_ids(jax.random.fold_in(arg_keys[14], 71), 0),
        "in_weight": gaussian(arg_keys[5], (D, INROWS, D), D ** -0.5, 0.1875, ((0, 8), (2, 4)), jnp.float32),
        "in_first": draw_in_first(jax.random.fold_in(arg_keys[14], 71), 0),
        "in_second": draw_in_second(jax.random.fold_in(arg_keys[14], 71), 0),
        "out_weight": draw_out_weight(jax.random.fold_in(arg_keys[14], 71), 0),
        "out_first": draw_out_first(jax.random.fold_in(arg_keys[14], 71), 0),
        "out_second": draw_out_second(jax.random.fold_in(arg_keys[14], 71), 0),
        "vectors": draw_vectors(jax.random.fold_in(arg_keys[14], 71), 0),
        "vec_first": draw_vec_first(jax.random.fold_in(arg_keys[14], 71), 0),
        "vec_second": draw_vec_second(jax.random.fold_in(arg_keys[14], 71), 0),
    }


@jax.custom_vjp
def low(v):
    return lax.optimization_barrier(v.astype(jnp.bfloat16)).astype(jnp.float32)

@jax.custom_vjp
def low_back(v):
    return v

def low_keep(v):
    return (low(v), None)

def low_pass(kept, grad):
    return (grad,)

def back_keep(v):
    return (v, None)

def back_low(kept, grad):
    return (low(grad),)
low.defvjp(low_keep, low_pass)
low_back.defvjp(back_keep, back_low)
PRECISE = lax.Precision.HIGHEST
NORM_EPS = 1e-06
CLIP_NORM = 1.0
BETA_ONE = 0.5
BETA_TWO = 0.5
RATE_MATRIX = 0.03
RATE_VECTOR = 0.3
WEIGHT_DECAY = 0.05
ADAM_EPS = 1e-08

def layer_norm(values):
    center = values - lax.optimization_barrier(jnp.mean(values, axis=-1, keepdims=True))
    spread = lax.optimization_barrier(jnp.mean(center * center, axis=-1, keepdims=True))
    return center * lax.rsqrt(spread + NORM_EPS)

def head_norm(values, gain):
    square_mean = lax.optimization_barrier(jnp.mean(values * values, axis=-1, keepdims=True))
    return values * lax.rsqrt(square_mean + NORM_EPS) * gain

def matmul(left, right):
    return jnp.matmul(left, right, precision=PRECISE)

def attend(inputs):
    queries, keys_all, values_all, seq_ids = inputs
    scores = jnp.einsum('qhd,khd->hqk', queries, keys_all, precision=PRECISE) * (1.0 / math.sqrt(HD))
    scores = low_back(scores)
    visible = seq_ids[None, None, :] <= seq_ids[None, :, None]
    scores = jnp.where(visible, scores, -1e+30)
    top_score = lax.optimization_barrier(jnp.max(scores, axis=-1, keepdims=True))
    weights = jnp.where(visible, jnp.exp(scores - top_score), 0.0)
    weights = low(weights / lax.optimization_barrier(jnp.sum(weights, axis=-1, keepdims=True)))
    mixed_heads = jnp.einsum('hqk,khd->qhd', weights, values_all, precision=PRECISE)
    return low_back(low(mixed_heads))

def forward(token_rows, conditions, in_master, out_master, vector_params, group_ids):
    blocks_ff = FF // D
    in_low = low(in_master)
    out_low = low(out_master)
    cond_act = low(jax.nn.silu(conditions))
    modulation = jnp.einsum('sd,drc->src', cond_act, in_low[:, 3 + blocks_ff:, :], precision=PRECISE) + vector_params[None, 0:6, :]
    gamma_attn = modulation[:, 0, None, :]
    scale_attn = modulation[:, 1, None, :]
    shift_attn = modulation[:, 2, None, :]
    gamma_ffn = modulation[:, 3, None, :]
    scale_ffn = modulation[:, 4, None, :]
    shift_ffn = modulation[:, 5, None, :]
    seq_count = token_rows.shape[0]
    hidden_in = low(layer_norm(token_rows) * (1.0 + scale_attn) + shift_attn)
    query_raw = low_back(matmul(hidden_in, in_low[:, 0, :]) + vector_params[6])
    key_raw = low_back(matmul(hidden_in, in_low[:, 1, :]))
    value_rows = low_back(low(matmul(hidden_in, in_low[:, 2, :]) + vector_params[7]))
    head_shape = (seq_count, LEN, HEADS, HD)
    query_hat = low(head_norm(query_raw.reshape(head_shape), vector_params[8].reshape(HEADS, HD)))
    key_hat = low(head_norm(key_raw.reshape(head_shape), vector_params[9].reshape(HEADS, HD)))
    attended = lax.map(jax.checkpoint(attend), (query_hat, key_hat, value_rows.reshape(head_shape), group_ids))
    attended = attended.reshape(seq_count, LEN, D)
    attn_out = low_back(matmul(attended, out_low[0]) + vector_params[10 + blocks_ff])
    middle = token_rows + gamma_attn * attn_out
    hidden_mid = low(layer_norm(middle) * (1.0 + scale_ffn) + shift_ffn)
    pre_act = low_back(matmul(hidden_mid, in_low[:, 3:3 + blocks_ff, :].reshape(D, FF)) + vector_params[10:10 + blocks_ff].reshape(FF))
    activated = low(jax.nn.gelu(pre_act, approximate=True))
    ffn_out = low_back(matmul(activated, out_low[1:].reshape(FF, D)) + vector_params[11 + blocks_ff])
    return middle + gamma_ffn * ffn_out

def adam_update(master, first, second, grad, factor, rate, decay):
    grad = grad * factor
    first = BETA_ONE * first + (1.0 - BETA_ONE) * grad
    second = BETA_TWO * second + (1.0 - BETA_TWO) * grad * grad
    fix_one = 1.0 - BETA_ONE ** STEP
    fix_two = 1.0 - BETA_TWO ** STEP
    stride = first / fix_one / (jnp.sqrt(second / fix_two) + ADAM_EPS)
    master = master - rate * (stride + decay * master)
    return (master, first, second, master.astype(jnp.bfloat16))

def reference(tokens, cotangent, class_table, labels, scale_ids, in_weight, in_first, in_second, out_weight, out_first, out_second, vectors, vec_first, vec_second):
    groups = SEQS // SEQ_DEV
    conditions = jnp.take(class_table, labels, axis=0)
    token_groups = tokens.astype(jnp.float32).reshape(groups, SEQ_DEV, LEN, D)
    cot_groups = cotangent.astype(jnp.float32).reshape(groups, SEQ_DEV, LEN, D)
    cond_groups = conditions.reshape(groups, SEQ_DEV, D)
    id_groups = scale_ids.reshape(groups, SEQ_DEV, LEN)

    def one_group(totals, inputs):
        token_grp, cot_grp, cond_grp, id_grp = inputs

        def apply_layer(token_rows, conds, in_master, out_master, vector_params):
            return forward(token_rows, conds, in_master, out_master, vector_params, id_grp)
        result, pull = jax.vjp(apply_layer, token_grp, cond_grp, in_weight, out_weight, vectors)
        grad_tokens, grad_cond, grad_in, grad_out, grad_vec = pull(cot_grp)
        totals = (totals[0] + grad_in, totals[1] + grad_out, totals[2] + grad_vec)
        return (totals, (result.astype(jnp.bfloat16), grad_tokens, grad_cond))
    zeros = (jnp.zeros_like(in_weight), jnp.zeros_like(out_weight), jnp.zeros_like(vectors))
    totals, outputs = lax.scan(one_group, zeros, (token_groups, cot_groups, cond_groups, id_groups))
    grad_in, grad_out, grad_vec = totals
    mixed = outputs[0].reshape(SEQS, LEN, D)
    input_grad = outputs[1].reshape(SEQS, LEN, D)
    condition_grad = outputs[2].reshape(SEQS, D)
    grad_norm = jnp.sqrt(jnp.sum(grad_in * grad_in) + jnp.sum(grad_out * grad_out) + jnp.sum(grad_vec * grad_vec))
    factor = CLIP_NORM / jnp.maximum(grad_norm, CLIP_NORM)
    in_new = adam_update(in_weight, in_first, in_second, grad_in, factor, RATE_MATRIX, WEIGHT_DECAY)
    out_new = adam_update(out_weight, out_first, out_second, grad_out, factor, RATE_MATRIX, WEIGHT_DECAY)
    vec_new = adam_update(vectors, vec_first, vec_second, grad_vec, factor, RATE_VECTOR, 0.0)
    second_bias_grad = factor * grad_vec[11 + FF // D]
    return (mixed, input_grad, condition_grad, grad_norm, in_new[0], in_new[1], in_new[2], in_new[3], out_new[0], out_new[1], out_new[2], out_new[3], vec_new[0], vec_new[1], vec_new[2], vec_new[3], second_bias_grad)
```

```python
import functools
import math

import jax
import jax.numpy as jnp
from jax import lax
from jax.experimental import pallas as pl
from jax.experimental.pallas import tpu as pltpu
from jax.sharding import PartitionSpec as P

HD = 64
STEP = 5
PRECISE = lax.Precision.HIGHEST
NORM_EPS = 1e-06
CLIP_NORM = 1.0
BETA_ONE = 0.5
BETA_TWO = 0.5
RATE_MATRIX = 0.03
RATE_VECTOR = 0.3
WEIGHT_DECAY = 0.05
ADAM_EPS = 1e-08

MESH = pl.DeviceIdType.MESH
F32 = jnp.float32
BF16 = jnp.bfloat16
LANES = 128
VMEM_BYTES = 60 * 2**20


def place():
    f = lax.axis_index("fsdp")
    c = lax.axis_index("ctx")
    z = lax.axis_index("tp")
    return f, c, z, lax.rem(f, 2), lax.rem(c, 2), c // 2


def partners(n_z):
    f, c, z, t, x, y = place()
    core = (f + 1 - 2 * t, c, z)
    xp = (f, 2 * y + (1 - x), z)
    yp = (f, 2 * (1 - y) + x, z)
    zs = [(f, c, lax.rem(z + d, n_z)) for d in range(1, n_z)]
    return core, xp, yp, zs


def enter(targets):
    barrier = pltpu.get_barrier_semaphore()
    for target in targets:
        pl.semaphore_signal(barrier, inc=1, device_id=target, device_id_type=MESH)
    pl.semaphore_wait(barrier, len(targets))


def lanes_at(index):
    return pl.ds(pl.multiple_of(index * LANES, LANES), LANES)


def gather_kernel(n_in, n_out, n_z, s_in, s_out, g_in, g_out, local_sem, send_sem, recv_sem):
    f, c, z, t, x, y = place()
    core, xp, yp, zs = partners(n_z)
    enter([core, xp, yp] + zs)
    order = [("i", 0), ("i", 1), ("i", 2), ("o", 0)]
    for r in range(n_out - 1):
        order += [("i", 3 + r), ("o", 1 + r)]
    zrows = pl.ds(pl.multiple_of(z * LANES, LANES), LANES)
    send = []

    def remote(p, slot, src, dst, target):
        copy = pltpu.make_async_remote_copy(
            src_ref=src, dst_ref=dst, send_sem=send_sem.at[p, slot], recv_sem=recv_sem.at[p, slot],
            device_id=target, device_id_type=MESH)
        copy.start()
        send.append(copy)
        return copy

    first, zcopies, one, two = {}, {}, {}, {}
    for p, (kind, m) in enumerate(order):
        if kind == "i":
            dst = g_in.at[m, t, c, :, lanes_at(z)]
            mine, other = s_in.at[m, t], s_in.at[m, 1 - t]
        else:
            dst = g_out.at[m, t, zrows, lanes_at(c)]
            mine = s_out.at[m, pl.ds(pl.multiple_of(t * LANES, LANES), LANES)]
            other = s_out.at[m, pl.ds(pl.multiple_of((1 - t) * LANES, LANES), LANES)]
        local = pltpu.make_async_copy(mine, dst, local_sem.at[p])
        local.start()
        first[p] = (local, remote(p, 0, other, dst, core))
    for p, (kind, m) in enumerate(order):
        first[p][0].wait()
        first[p][1].wait_recv()
        block = g_in.at[m, :, c, :, lanes_at(z)] if kind == "i" else g_out.at[m, :, zrows, lanes_at(c)]
        zcopies[p] = [remote(p, 1 + d, block, block, target) for d, target in enumerate(zs)]
    base = n_z

    def start_one(p):
        kind, m = order[p]
        for copy in zcopies[p]:
            copy.wait_recv()
        if kind == "i":
            block = g_in.at[m, :, c]
            one[p] = remote(p, base, block, block, xp)
        else:
            block = g_out.at[m, :, :, lanes_at(c)]
            one[p] = remote(p, base, block, block, yp)

    def start_two(p):
        kind, m = order[p]
        one[p].wait_recv()
        if kind == "i":
            block = g_in.at[m, :, pl.ds(2 * y, 2)]
            two[p] = [remote(p, base + 1, block, block, yp)]
        else:
            two[p] = []
            for k, at in enumerate((x, 2 + x)):
                block = g_out.at[m, :, :, lanes_at(at)]
                two[p].append(remote(p, base + 1 + k, block, block, xp))

    for p in range(len(order)):
        start_one(p)
        if p > 0:
            start_two(p - 1)
    start_two(len(order) - 1)
    for p in range(len(order)):
        for copy in two[p]:
            copy.wait_recv()
    for copy in send:
        copy.wait_send()


def gather_weights(s_in, s_out, n_z):
    n_in, n_out = s_in.shape[0], s_out.shape[0]
    pieces = n_in + n_out
    width = n_z * LANES
    return pl.pallas_call(
        functools.partial(gather_kernel, n_in, n_out, n_z),
        out_shape=(
            jax.ShapeDtypeStruct((n_in, 2, 4, LANES, width), BF16),
            jax.ShapeDtypeStruct((n_out, 2, width, 4 * LANES), BF16),
        ),
        in_specs=[pl.BlockSpec(memory_space=pl.ANY)] * 2,
        out_specs=[pl.BlockSpec(memory_space=pl.ANY)] * 2,
        scratch_shapes=[
            pltpu.SemaphoreType.DMA((pieces,)),
            pltpu.SemaphoreType.DMA((pieces, n_z + 3)),
            pltpu.SemaphoreType.DMA((pieces, n_z + 3)),
        ],
        compiler_params=pltpu.CompilerParams(collective_id=0, has_side_effects=True, vmem_limit_bytes=VMEM_BYTES),
    )(s_in, s_out)


def scatter_kernel(n_in, n_out, n_z, p_in, p_out, o_in, o_out,
                   a_in, a_out, b_in, b_out, z_in, z_out, f_in, f_out, send_sem, recv_sem):
    f, c, z, t, x, y = place()
    core, xp, yp, zs = partners(n_z)
    enter([core, xp, yp] + zs)
    order = []
    for r in range(n_out - 1):
        order += [("i", 3 + r), ("o", 1 + r)]
    order += [("o", 0), ("i", 2), ("i", 1), ("i", 0)]
    zrows = pl.ds(pl.multiple_of(z * LANES, LANES), LANES)
    send = []

    def remote(p, slot, src, dst, target):
        copy = pltpu.make_async_remote_copy(
            src_ref=src, dst_ref=dst, send_sem=send_sem.at[p, slot], recv_sem=recv_sem.at[p, slot],
            device_id=target, device_id_type=MESH)
        copy.start()
        send.append(copy)
        return copy

    one, two, three, four = {}, {}, {}, {}

    def start_one(p):
        kind, m = order[p]
        if kind == "i":
            one[p] = [remote(p, 0, p_in.at[m, :, pl.ds(2 * (1 - y), 2)], a_in.at[m], yp)]
        else:
            one[p] = [remote(p, k, p_out.at[m, :, :, lanes_at(2 * k + 1 - x)], a_out.at[m, :, k], xp) for k in (0, 1)]

    def start_two(p):
        kind, m = order[p]
        for copy in one[p]:
            copy.wait_recv()
        if kind == "i":
            rows = pl.ds(2 * y, 2)
            p_in[m, :, rows] = (p_in[m, :, rows].astype(F32) + a_in[m].astype(F32)).astype(BF16)
            two[p] = remote(p, 2, p_in.at[m, :, 2 * y + 1 - x], b_in.at[m], xp)
        else:
            for k in (0, 1):
                at = lanes_at(2 * k + x)
                p_out[m, :, :, at] = (p_out[m, :, :, at].astype(F32) + a_out[m, :, k].astype(F32)).astype(BF16)
            two[p] = remote(p, 2, p_out.at[m, :, :, lanes_at(2 * (1 - y) + x)], b_out.at[m], yp)

    def start_three(p):
        kind, m = order[p]
        two[p].wait_recv()
        three[p] = []
        if kind == "i":
            p_in[m, :, c] = (p_in[m, :, c].astype(F32) + b_in[m].astype(F32)).astype(BF16)
            for d in range(1, n_z):
                at = lanes_at(lax.rem(z + d, n_z))
                three[p].append(remote(p, 2 + d, p_in.at[m, :, c, :, at], z_in.at[m, d - 1], zs[d - 1]))
        else:
            at = lanes_at(c)
            p_out[m, :, :, at] = (p_out[m, :, :, at].astype(F32) + b_out[m].astype(F32)).astype(BF16)
            for d in range(1, n_z):
                zi = lax.rem(z + d, n_z)
                rows = pl.ds(pl.multiple_of(zi * LANES, LANES), LANES)
                three[p].append(remote(p, 2 + d, p_out.at[m, :, rows, at], z_out.at[m, d - 1], zs[d - 1]))

    def start_four(p):
        kind, m = order[p]
        for copy in three[p]:
            copy.wait_recv()
        if kind == "i":
            total = p_in[m, :, c, :, lanes_at(z)].astype(F32)
            for d in range(n_z - 1):
                total = total + z_in[m, d].astype(F32)
            f_in[m] = total
            o_in[m, t] = f_in[m, t]
            four[p] = remote(p, 2 + n_z, f_in.at[m, 1 - t], o_in.at[m, t], core)
        else:
            total = p_out[m, :, zrows, lanes_at(c)].astype(F32)
            for d in range(n_z - 1):
                total = total + z_out[m, d].astype(F32)
            f_out[m] = total
            o_out[m, t] = f_out[m, t]
            four[p] = remote(p, 2 + n_z, f_out.at[m, 1 - t], o_out.at[m, t], core)

    n = len(order)
    for p in range(n):
        start_one(p)
    for s in range(n + 2):
        if s < n:
            start_two(s)
        if 0 <= s - 1 < n:
            start_three(s - 1)
        if 0 <= s - 2 < n:
            start_four(s - 2)
    for p in range(n):
        four[p].wait_recv()
    for copy in send:
        copy.wait_send()


def scatter_gradients(p_in, p_out):
    n_in, n_out, n_z = p_in.shape[0], p_out.shape[0], p_in.shape[-1] // LANES
    pieces = n_in + n_out
    width = n_z * LANES
    vmem = pl.BlockSpec(memory_space=pltpu.VMEM)
    return pl.pallas_call(
        functools.partial(scatter_kernel, n_in, n_out, n_z),
        out_shape=(
            jax.ShapeDtypeStruct((n_in, 2, LANES, LANES), F32),
            jax.ShapeDtypeStruct((n_out, 2, LANES, LANES), F32),
        ),
        in_specs=[vmem] * 2,
        out_specs=[vmem] * 2,
        scratch_shapes=[
            pltpu.VMEM((n_in, 2, 2, LANES, width), BF16),
            pltpu.VMEM((n_out, 2, 2, width, LANES), BF16),
            pltpu.VMEM((n_in, 2, LANES, width), BF16),
            pltpu.VMEM((n_out, 2, width, LANES), BF16),
            pltpu.VMEM((n_in, n_z - 1, 2, LANES, LANES), BF16),
            pltpu.VMEM((n_out, n_z - 1, 2, LANES, LANES), BF16),
            pltpu.VMEM((n_in, 2, LANES, LANES), F32),
            pltpu.VMEM((n_out, 2, LANES, LANES), F32),
            pltpu.SemaphoreType.DMA((pieces, n_z + 3)),
            pltpu.SemaphoreType.DMA((pieces, n_z + 3)),
        ],
        compiler_params=pltpu.CompilerParams(collective_id=1, has_side_effects=True, vmem_limit_bytes=VMEM_BYTES),
    )(p_in, p_out)


def layer_norm(values):
    center = values - jnp.mean(values, axis=-1, keepdims=True)
    spread = jnp.mean(center * center, axis=-1, keepdims=True)
    return center * lax.rsqrt(spread + NORM_EPS)


def head_norm(values, gain):
    square_mean = jnp.mean(values * values, axis=-1, keepdims=True)
    return values * lax.rsqrt(square_mean + NORM_EPS) * gain


def gelu_tanh(values):
    return jax.nn.gelu(values, approximate=True)


def adam_update(master, first, second, grad, factor, rate, decay):
    grad = grad * factor
    first = BETA_ONE * first + (1.0 - BETA_ONE) * grad
    second = BETA_TWO * second + (1.0 - BETA_TWO) * grad * grad
    fix_one = 1.0 - BETA_ONE**STEP
    fix_two = 1.0 - BETA_TWO**STEP
    stride = first / fix_one / (jnp.sqrt(second / fix_two) + ADAM_EPS)
    master = master - rate * (stride + decay * master)
    return (master, first, second, master.astype(BF16))


def dot(a, b, dims):
    return lax.dot_general(a, b, (dims, ((), ())), preferred_element_type=F32)


NN = ((1,), (0,))
NT = ((1,), (1,))
TN = ((0,), (0,))


def per_device(n_f, n_c, n_z, tokens, cotangent, class_table, labels, scale_ids, in_weight, in_first, in_second,
               out_weight, out_first, out_second, vectors, vec_first, vec_second):
    n_hi = n_f // 2
    f, c, z, t, x, y = place()
    f_hi = f // 2
    seqs, piece, width = tokens.shape
    cols = in_weight.shape[2]
    n_ff = out_weight.shape[0] - 1
    ada = 3 + n_ff
    half = cols // 2
    pairs = [[2 * i, 2 * i + 1] for i in range(n_hi)]
    his = [[i + 2 * j for j in range(n_hi)] for i in range(2)]

    def into(a):
        if n_hi == 1:
            return a
        shape = a.shape[:-1]
        return jnp.swapaxes(a.reshape(shape + (n_hi, 2 * n_c, -1)), -3, -2).reshape(a.shape)

    def back(a):
        if n_hi == 1:
            return a
        shape = a.shape[:-1]
        return jnp.swapaxes(a.reshape(shape + (2 * n_c, n_hi, -1)), -3, -2).reshape(a.shape)

    def pair_sum(a):
        return lax.psum(a, "fsdp", axis_index_groups=pairs)

    in_low = in_weight.astype(BF16)
    out_low = out_weight.astype(BF16)
    if n_hi > 1:
        in_low = lax.all_gather(in_low, "fsdp", axis=0, tiled=True, axis_index_groups=his)
        out_low = lax.all_gather(out_low, "fsdp", axis=2, tiled=True, axis_index_groups=his)
    rows = in_low.shape[0]
    s_in = in_low[:, :ada].reshape(rows, ada, 2, half).transpose(1, 2, 0, 3)
    g_in, g_out = gather_weights(s_in, out_low, n_z)
    w_in = g_in.reshape(ada, width, n_z * half)
    w_out = g_out.transpose(0, 2, 1, 3).reshape(1 + n_ff, n_z * half, width)
    w_ada = in_low[:, ada:]

    def route(k):
        perm = []
        for fs in range(n_f):
            for cs in range(n_c):
                ys, xs = cs // 2, cs % 2
                dst_f = (fs // 2) * 2 + ys
                dst_c = ((xs + k) % 2) * 2 + fs % 2
                perm.append((fs * n_c + cs, dst_f * n_c + dst_c))
        return perm

    def to_chip(a):
        got = []
        for k in (0, 1):
            at = 2 * z + lax.rem(x + k, 2)
            got.append(lax.ppermute(lax.dynamic_index_in_dim(a, at, 0, keepdims=False), ("fsdp", "ctx"), route(k)))
        pair = jnp.where(y == 0, jnp.stack(got), jnp.stack(got[::-1]))
        mine = pair.reshape((2 * piece,) + a.shape[2:])
        return lax.all_gather(mine, "fsdp", axis=0, tiled=True, axis_index_groups=pairs)

    def from_chip(a):
        mine = lax.dynamic_slice_in_dim(a, t * 2 * piece, 2 * piece, 0).reshape((2, piece) + a.shape[1:])
        got = []
        for k in (0, 1):
            block = lax.dynamic_index_in_dim(mine, lax.rem(y + k, 2), 0, keepdims=False)
            got.append(lax.ppermute(block, ("fsdp", "ctx"), [(d, s) for s, d in route(k)]))
        pair = jnp.where(x == 0, jnp.stack(got), jnp.stack(got[::-1]))
        return lax.all_gather(pair, "tp", axis=0, tiled=True)

    token_rows = to_chip(into(tokens)).astype(F32)
    grad_output = to_chip(into(cotangent)).astype(F32)
    ids = to_chip(scale_ids)

    conditions = jnp.take(class_table, labels, axis=0)
    cond_act = jax.nn.silu(conditions).astype(BF16)
    act_all = lax.all_gather(cond_act, "fsdp", axis=0, tiled=False, axis_index_groups=pairs)
    act_chips = act_all.reshape(2, n_z, 2, width).transpose(2, 0, 1, 3).reshape(2 * 2 * n_z, width)
    act_rows = lax.dynamic_slice_in_dim(into(act_chips), (t * n_c + c) * rows, rows, 1)
    mod_part = jnp.einsum("sd,drc->src", act_rows, w_ada, preferred_element_type=F32)
    mod_z = lax.psum(mod_part, ("fsdp", "ctx"), axis_index_groups=None) if n_hi == 1 else lax.psum(
        lax.psum(mod_part, "fsdp", axis_index_groups=pairs), "ctx")
    mod_z = mod_z + vectors[None, 0:6, :]
    mod_z = lax.dynamic_slice_in_dim(mod_z, c * n_z, n_z, 0)
    mod = lax.all_to_all(mod_z, "tp", 0, 2, tiled=True)
    mod = into(mod.reshape(6, width))
    gamma_a, scale_a, shift_a, gamma_f, scale_f, shift_f = [mod[j][None] for j in range(6)]

    vec_all = lax.all_gather(vectors, "tp", axis=1, tiled=True)
    vec_t = lax.dynamic_index_in_dim(vec_all.reshape(-1, n_z, 2, half), t, 2, keepdims=False).reshape(-1, n_z * half)
    proj_bias = into(vec_all[10 + n_ff])
    ffn_bias = into(vec_all[11 + n_ff])

    normed_in = layer_norm(token_rows)
    hidden_in = (normed_in * (1.0 + scale_a) + shift_a).astype(BF16)
    query_raw = dot(hidden_in, w_in[0], NN) + vec_t[6]
    key_raw = dot(hidden_in, w_in[1], NN)
    value_low = (dot(hidden_in, w_in[2], NN) + vec_t[7]).astype(BF16)
    tokens_here = token_rows.shape[0]
    head_shape = (tokens_here, n_z * half // HD, HD)
    query_four, key_four = query_raw.reshape(head_shape), key_raw.reshape(head_shape)
    query_gain, key_gain = vec_t[8].reshape(head_shape[1:]), vec_t[9].reshape(head_shape[1:])
    query_hat = head_norm(query_four, query_gain).astype(BF16)
    key_hat = head_norm(key_four, key_gain).astype(BF16)
    value_four = value_low.reshape(head_shape)
    inverse_root = 1.0 / math.sqrt(HD)
    visible = ids[None, None, :] <= ids[None, :, None]
    scores = jnp.einsum("qhd,khd->hqk", query_hat, key_hat, preferred_element_type=F32) * inverse_root
    scores = jnp.where(visible, scores, -1e30)
    top = jnp.max(scores, axis=-1, keepdims=True)
    weights = jnp.where(visible, jnp.exp(scores - top), 0.0)
    weights = weights / jnp.sum(weights, axis=-1, keepdims=True)
    weights_low = weights.astype(BF16)
    attended = jnp.einsum("hqk,khd->qhd", weights_low, value_four, preferred_element_type=F32).astype(BF16)
    attended = attended.reshape(tokens_here, -1)
    attn_out = pair_sum(dot(attended, w_out[0], NN)) + proj_bias
    middle = token_rows + gamma_a * attn_out
    normed_mid = layer_norm(middle)
    hidden_mid = (normed_mid * (1.0 + scale_f) + shift_f).astype(BF16)
    w_one = [w_in[3 + r] for r in range(n_ff)]
    w_two = [w_out[1 + r] for r in range(n_ff)]
    pre_act = [dot(hidden_mid, w_one[r], NN) + vec_t[10 + r] for r in range(n_ff)]
    activated = [gelu_tanh(u).astype(BF16) for u in pre_act]
    ffn_out = pair_sum(sum(dot(activated[r], w_two[r], NN) for r in range(n_ff))) + ffn_bias
    mixed = from_chip((middle + gamma_f * ffn_out).astype(BF16))

    grad_ffn = (grad_output * gamma_f).astype(BF16)
    out_grads, in_grads, grad_pres = [], [], []
    grad_hmid = 0.0
    for r in range(n_ff):
        out_grads.append(dot(activated[r], grad_ffn, TN).astype(BF16))
        unused, pull = jax.vjp(gelu_tanh, pre_act[r])
        grad_pre = pull(dot(grad_ffn, w_two[r], NT))[0].astype(BF16)
        grad_pres.append(grad_pre)
        in_grads.append(dot(hidden_mid, grad_pre, TN).astype(BF16))
        grad_hmid = grad_hmid + dot(grad_pre, w_one[r], NT)
    grad_hmid = pair_sum(grad_hmid)
    unused, mid_pull = jax.vjp(layer_norm, middle)
    grad_middle = grad_output + mid_pull(grad_hmid * (1.0 + scale_f))[0]
    grad_attn = (grad_middle * gamma_a).astype(BF16)
    out_grads.insert(0, dot(attended, grad_attn, TN).astype(BF16))
    go = dot(grad_attn, w_out[0], NT).astype(BF16).reshape(head_shape)
    grad_weights = jnp.einsum("qhd,khd->hqk", go, value_four, preferred_element_type=F32)
    grad_value = jnp.einsum("hqk,qhd->khd", weights_low, go, preferred_element_type=F32).astype(BF16)
    grad_scores = weights * (grad_weights - jnp.sum(weights * grad_weights, axis=-1, keepdims=True))
    grad_scores = grad_scores.astype(BF16)
    grad_qhat = jnp.einsum("hqk,khd->qhd", grad_scores, key_hat, preferred_element_type=F32) * inverse_root
    grad_khat = jnp.einsum("hqk,qhd->khd", grad_scores, query_hat, preferred_element_type=F32) * inverse_root
    unused, query_pull = jax.vjp(head_norm, query_four, query_gain)
    grad_query, query_gain_grad = query_pull(grad_qhat)
    unused, key_pull = jax.vjp(head_norm, key_four, key_gain)
    grad_key, key_gain_grad = key_pull(grad_khat)
    grad_qkv = [a.reshape(tokens_here, -1).astype(BF16) for a in (grad_query, grad_key, grad_value)]
    in_grads = [dot(hidden_in, a, TN).astype(BF16) for a in grad_qkv] + in_grads
    grad_hin = pair_sum(sum(dot(grad_qkv[j], w_in[j], NT) for j in range(3)))
    unused, in_pull = jax.vjp(layer_norm, token_rows)
    grad_tokens = grad_middle + in_pull(grad_hin * (1.0 + scale_a))[0]
    input_grad = from_chip(grad_tokens.astype(BF16)).astype(F32)

    grad_mod = back(jnp.stack([
        jnp.sum(grad_middle * attn_out, axis=0),
        jnp.sum(grad_hin * normed_in, axis=0),
        jnp.sum(grad_hin, axis=0),
        jnp.sum(grad_output * ffn_out, axis=0),
        jnp.sum(grad_hmid * normed_mid, axis=0),
        jnp.sum(grad_hmid, axis=0),
    ]))
    mod_chips = lax.all_gather(grad_mod, ("ctx", "tp"), axis=0, tiled=False).reshape(-1, 6, width)
    mod_chips = lax.dynamic_slice_in_dim(mod_chips, z * cols, cols, 2)
    ada_grad = jnp.einsum("sd,src->drc", act_rows.astype(F32), mod_chips, precision=PRECISE)
    cond_part = jnp.einsum("src,drc->sd", mod_chips, w_ada.astype(F32), precision=PRECISE)
    cond_sum = lax.psum(cond_part, "tp")
    cond_sum = lax.all_gather(cond_sum, "ctx", axis=1, tiled=True)
    cond_sum = lax.all_gather(cond_sum, "fsdp", axis=1, tiled=True, axis_index_groups=pairs)
    cond_sum = back(cond_sum).reshape(2, 2, n_z, width).transpose(1, 2, 0, 3).reshape(2, 2 * n_z, width)
    cond_mine = lax.dynamic_index_in_dim(cond_sum, t, 0, keepdims=False)
    unused, silu_pull = jax.vjp(jax.nn.silu, conditions)
    condition_grad = silu_pull(cond_mine)[0]

    p_in = jnp.stack(in_grads).reshape(ada, 2, n_c, rows, n_z * half)
    p_out = jnp.stack(out_grads).reshape(1 + n_ff, n_z * half, 2, n_c * rows).transpose(0, 2, 1, 3)
    o_in, o_out = scatter_gradients(p_in, p_out)
    in_grad = jnp.concatenate([o_in.transpose(2, 0, 1, 3).reshape(rows, ada, cols), ada_grad], axis=1)
    out_grad = o_out.reshape(1 + n_ff, cols, rows)
    if n_hi > 1:
        in_grad = lax.psum_scatter(in_grad, "fsdp", scatter_dimension=0, tiled=True, axis_index_groups=his)
        out_grad = lax.psum_scatter(out_grad, "fsdp", scatter_dimension=2, tiled=True, axis_index_groups=his)

    def spread(a):
        wide = jnp.zeros((a.shape[0], n_z, 2, half), F32)
        return lax.dynamic_update_slice(wide, a.reshape(-1, n_z, 1, half), (0, 0, t, 0)).reshape(a.shape[0], width)

    def once(a):
        return jnp.where(t == 0, a, 0.0)

    def total(a):
        return jnp.sum(a, axis=0, dtype=F32)

    vec_part = jnp.concatenate([
        once(grad_mod),
        spread(jnp.stack([total(grad_qkv[0]), total(grad_qkv[2]), query_gain_grad.reshape(-1), key_gain_grad.reshape(-1)]
                         + [total(a) for a in grad_pres])),
        once(back(jnp.stack([total(grad_attn), total(grad_ffn)]))),
    ])
    vec_grad = lax.dynamic_slice_in_dim(lax.psum(vec_part, ("fsdp", "ctx", "tp")), z * cols, cols, 1)
    squares = jnp.sum(in_grad * in_grad) + jnp.sum(out_grad * out_grad)
    first_device = (f == 0) & (c == 0)
    squares = squares + jnp.where(first_device, jnp.sum(vec_grad * vec_grad), 0.0)
    grad_norm = jnp.sqrt(lax.psum(squares, ("fsdp", "ctx", "tp")))
    factor = CLIP_NORM / jnp.maximum(grad_norm, CLIP_NORM)
    in_new = adam_update(in_weight, in_first, in_second, in_grad, factor, RATE_MATRIX, WEIGHT_DECAY)
    out_new = adam_update(out_weight, out_first, out_second, out_grad, factor, RATE_MATRIX, WEIGHT_DECAY)
    vec_new = adam_update(vectors, vec_first, vec_second, vec_grad, factor, RATE_VECTOR, 0.0)
    return (back(mixed), back(input_grad), condition_grad, grad_norm, *in_new, *out_new, *vec_new,
            factor * vec_grad[11 + n_ff])


def solution(mesh):
    in_matrix = P(("fsdp", "ctx"), None, "tp")
    out_matrix = P(None, "tp", ("fsdp", "ctx"))
    vector = P(None, "tp")
    rows = P("fsdp", "ctx", None)
    return jax.shard_map(
        functools.partial(per_device, mesh.shape["fsdp"], mesh.shape["ctx"], mesh.shape["tp"]),
        mesh=mesh,
        in_specs=(rows, rows, P(), P("fsdp"), P("fsdp", "ctx"), in_matrix, in_matrix, in_matrix,
                  out_matrix, out_matrix, out_matrix, vector, vector, vector),
        out_specs=(rows, rows, P("fsdp", None), P(), in_matrix, in_matrix, in_matrix, in_matrix,
                   out_matrix, out_matrix, out_matrix, out_matrix, vector, vector, vector, vector, P("tp")),
        check_vma=False,
    )
```

```python
import functools
import math

import jax
import jax.numpy as jnp
from jax import lax
from jax.experimental import pallas as pl
from jax.experimental.pallas import tpu as pltpu
from jax.sharding import PartitionSpec as P

HD = 64
STEP = 5
PRECISE = lax.Precision.HIGHEST
NORM_EPS = 1e-06
CLIP_NORM = 1.0
BETA_ONE = 0.5
BETA_TWO = 0.5
RATE_MATRIX = 0.03
RATE_VECTOR = 0.3
WEIGHT_DECAY = 0.05
ADAM_EPS = 1e-08

MESH = pl.DeviceIdType.MESH
F32 = jnp.float32
BF16 = jnp.bfloat16
LANES = 128
VMEM_BYTES = 60 * 2**20


def place():
    f = lax.axis_index("fsdp")
    c = lax.axis_index("ctx")
    z = lax.axis_index("tp")
    return f, c, z, lax.rem(f, 2), lax.rem(c, 2), c // 2


def partners(n_z):
    f, c, z, t, x, y = place()
    core = (f + 1 - 2 * t, c, z)
    xp = (f, 2 * y + (1 - x), z)
    yp = (f, 2 * (1 - y) + x, z)
    zs = [(f, c, lax.rem(z + d, n_z)) for d in range(1, n_z)]
    return core, xp, yp, zs


def enter(targets):
    barrier = pltpu.get_barrier_semaphore()
    for target in targets:
        pl.semaphore_signal(barrier, inc=1, device_id=target, device_id_type=MESH)
    pl.semaphore_wait(barrier, len(targets))


def lanes_at(index):
    return pl.ds(pl.multiple_of(index * LANES, LANES), LANES)


def adam_update(master, first, second, grad, factor, rate, decay):
    grad = grad * factor
    first = BETA_ONE * first + (1.0 - BETA_ONE) * grad
    second = BETA_TWO * second + (1.0 - BETA_TWO) * grad * grad
    fix_one = 1.0 - BETA_ONE**STEP
    fix_two = 1.0 - BETA_TWO**STEP
    stride = first / fix_one / (jnp.sqrt(second / fix_two) + ADAM_EPS)
    master = master - rate * (stride + decay * master)
    return (master, first, second, master.astype(BF16))


def dot(a, b, dims):
    return lax.dot_general(a, b, (dims, ((), ())), preferred_element_type=F32)


NN = ((1,), (0,))
NT = ((1,), (1,))
TN = ((0,), (0,))


PIECE = 176
NEG = -1e30


def cat(parts, axis):
    return jnp.concatenate(parts, axis=axis)


def lane_of(shape):
    return lax.broadcasted_iota(jnp.int32, shape, len(shape) - 1)


def split_two(values):
    high = values.astype(BF16)
    return high, (values - high.astype(F32)).astype(BF16)


def split_three(values):
    high = values.astype(BF16)
    rest = values - high.astype(F32)
    middle = rest.astype(BF16)
    return high, middle, (rest - middle.astype(F32)).astype(BF16)


def head_mean(values):
    row = lax.broadcasted_iota(jnp.int32, (LANES, LANES), 0) // HD
    ones = jnp.where(row == lane_of((LANES, LANES)) // HD, 1.0 / HD, 0.0).astype(BF16)
    out = []
    for k in range(values.shape[1] // LANES):
        high, lower = split_two(values[:, k * LANES:(k + 1) * LANES])
        out.append(dot(high, ones, NN) + dot(lower, ones, NN))
    return cat(out, 1)


def gelu_both(u):
    k0, k1 = 0.7978845608028654, 0.044715
    square = u * u
    th = jnp.tanh(k0 * u * (1.0 + k1 * square))
    half = 0.5 * (1.0 + th)
    slope = half + 0.5 * u * (1.0 - th * th) * (k0 * (1.0 + 3.0 * k1 * square))
    return u * half, slope


def step_rows(body):
    for p in (0, 1):
        def one(i, carry, p=p):
            start = pl.multiple_of(i * 16, 16)
            body(pl.ds(start, 16), pl.ds(pl.multiple_of(p * PIECE + start, 16), 16), p)
            return carry
        lax.fori_loop(0, PIECE // 16, one, 0)


def normalize(values):
    center = values - jnp.mean(values, axis=-1, keepdims=True)
    scale = lax.rsqrt(jnp.mean(center * center, axis=-1, keepdims=True) + NORM_EPS)
    return center * scale, scale


def reorder(rows, n_hi, inverse=False):
    if n_hi == 1:
        return rows
    width = rows.shape[1]
    each = width // (8 * n_hi)
    out = []
    for k in range(width // LANES):
        at = k * LANES + lax.broadcasted_iota(jnp.int32, (width, LANES), 1)
        there = lax.broadcasted_iota(jnp.int32, (width, LANES), 0)
        if inverse:
            wanted = (at // each % 8) * (n_hi * each) + (at // (8 * each)) * each + at % each
        else:
            wanted = (at // each % n_hi) * (8 * each) + (at // (each * n_hi)) * each + at % each
        order = jnp.where(there == wanted, 1.0, 0.0).astype(BF16)
        out.append(sum(dot(part, order, NN) for part in split_three(rows)))
    return cat(out, 1)


class Wire:
    def __init__(self, send_sem, recv_sem):
        self.send_sem, self.recv_sem, self.sent = send_sem, recv_sem, []

    def make(self, at, src, dst, target, to=None):
        return pltpu.make_async_remote_copy(
            src_ref=src, dst_ref=dst, send_sem=self.send_sem.at[at], recv_sem=self.recv_sem.at[at if to is None else to],
            device_id=target, device_id_type=MESH)

    def start(self, at, src, dst, target, to=None):
        copy = self.make(at, src, dst, target, to)
        copy.start()
        self.sent.append(copy)
        return copy

    def finish(self):
        for copy in self.sent:
            copy.wait_send()


def forward_kernel(n_z, n_ff, n_hi, *refs):
    n_in, n_out = 3 + n_ff, 1 + n_ff
    (s_in, s_out, tok, cot, ids, act, wm, vec,
     x_wq, x_wo, x_h1, x_qr, x_kr, x_q8, x_kh, x_v, x_o, x_lse, x_ma, x_mb, x_tok, x_cot, x_attn, x_mid,
     x_fown, x_fsend, x_down, x_dsend, x_gin, x_gout, x_mod, x_gu, x_gf, x_vec,
     g_in, g_out, tokb, cotb, idb, actb, pm, rx, ry, rc, mz, vz, h1, gf, h2, qr, kr, q8, kh, vv, oo, lse, ma, mb,
     at_send, at_recv, attn, mid, facc, dacc, fsend, dsend, gin, gout, act_low, slope,
     local_sem, ag_send, ag_recv, m_send, m_recv, out_sem, tok_sem) = refs
    f, c, z, t, x, y = place()
    core, xp, yp, zs = partners(n_z)
    f_base = f - t

    barrier = pltpu.get_barrier_semaphore()
    for target in [core, xp, yp] + zs:
        pl.semaphore_signal(barrier, inc=1, device_id=target, device_id_type=MESH)
    loops = (y == t) & (x == t)
    for xs in (0, 1):
        @pl.when(jnp.logical_not(loops & (x == xs)))
        def _():
            pl.semaphore_signal(barrier, inc=1, device_id=(f_base + x, 2 * t + xs, z), device_id_type=MESH)
    pl.semaphore_wait(barrier, 4 + n_z - jnp.where(loops, 1, 0))

    ag = Wire(ag_send, ag_recv)
    misc = Wire(m_send, m_recv)

    shares = [(tok, tokb), (cot, cotb), (ids, None)]

    def send_share(j):
        src, dst = shares[j]
        for yd in (0, 1):
            own = loops & (y == yd)
            from_here = src.at[2 * z + yd]
            to_there = dst.at[x] if dst is not None else idb.at[2 * y + x]

            @pl.when(own)
            def _():
                pltpu.make_async_copy(from_here, to_there, tok_sem.at[1, j, x]).start()

            @pl.when(jnp.logical_not(own))
            def _():
                pltpu.make_async_remote_copy(
                    src_ref=from_here, dst_ref=to_there, send_sem=tok_sem.at[0, j, yd], recv_sem=tok_sem.at[1, j, x],
                    device_id=(f_base + y, 2 * yd + t, z), device_id_type=MESH).start()

    def got_share(j):
        dst = shares[j][1]
        for xs in (0, 1):
            ref = dst.at[xs] if dst is not None else idb.at[2 * t + xs]
            pltpu.make_async_copy(ref, ref, tok_sem.at[1, j, xs]).wait()

    act_copy = misc.start(0, act.at[:, lanes_at((1 - t) * 4 + c)], actb.at[1], core)
    vec_local = pltpu.make_async_copy(vec, vz.at[z], local_sem.at[n_in + n_out])
    vec_local.start()
    vec_copies = [misc.start(1 + d, vec, vz.at[z], target) for d, target in enumerate(zs)]

    order = [("i", 0), ("i", 1), ("i", 2), ("o", 0)]
    for r in range(n_ff):
        order += [("i", 3 + r), ("o", 1 + r)]
    zrows = pl.ds(pl.multiple_of(z * LANES, LANES), LANES)
    first, zcopies, one, two = {}, {}, {}, {}
    for p, (kind, m) in enumerate(order):
        if kind == "i":
            dst = g_in.at[m, t, c, :, lanes_at(z)]
            mine, other = s_in.at[m, t], s_in.at[m, 1 - t]
        else:
            dst = g_out.at[m, t, zrows, lanes_at(c)]
            mine = s_out.at[m, pl.ds(pl.multiple_of(t * LANES, LANES), LANES)]
            other = s_out.at[m, pl.ds(pl.multiple_of((1 - t) * LANES, LANES), LANES)]
        local = pltpu.make_async_copy(mine, dst, local_sem.at[p])
        local.start()
        first[p] = (local, ag.start((p, 0), other, dst, core))
    base = n_z

    def start_zero(p):
        if p >= len(order) or p in zcopies:
            return
        kind, m = order[p]
        first[p][0].wait()
        first[p][1].wait_recv()
        block = g_in.at[m, :, c, :, lanes_at(z)] if kind == "i" else g_out.at[m, :, zrows, lanes_at(c)]
        zcopies[p] = [ag.start((p, 1 + d), block, block, target) for d, target in enumerate(zs)]

    def x_first(p):
        return p % 2 == 0

    def start_one(p):
        kind, m = order[p]
        for copy in zcopies[p]:
            copy.wait_recv()
        block = g_in.at[m, :, c] if kind == "i" else g_out.at[m, :, :, lanes_at(c)]
        one[p] = ag.start((p, base), block, block, xp if x_first(p) else yp)

    def start_two(p):
        kind, m = order[p]
        one[p].wait_recv()
        held = (2 * y, 2 * y + 1) if x_first(p) else (x, 2 + x)
        two[p] = []
        if kind == "i" and x_first(p):
            block = g_in.at[m, :, pl.ds(2 * y, 2)]
            two[p].append(ag.start((p, base + 1), block, block, yp))
        else:
            for k, at in enumerate(held):
                block = g_in.at[m, :, at] if kind == "i" else g_out.at[m, :, :, lanes_at(at)]
                two[p].append(ag.start((p, base + 1 + k), block, block, yp if x_first(p) else xp))

    ticks = [(start_one, 0)]
    for p in range(1, len(order)):
        ticks += [(start_one, p), (start_two, p - 1)]
    ticks.append((start_two, len(order) - 1))

    def tick(n=1):
        for _ in range(n):
            if ticks:
                step, p = ticks.pop(0)
                if step is start_one:
                    for ahead in range(p + 3):
                        start_zero(ahead)
                step(p)

    def pump(n=1):
        tick(2 * n)

    def arrived(p):
        for copy in two[p]:
            copy.wait_recv()

    flushed = []

    def flush(src, dst):
        copy = pltpu.make_async_copy(src, dst, out_sem.at[len(flushed)])
        copy.start()
        flushed.append(copy)

    act_copy.wait_recv()
    own_at = lanes_at(t * 4 + c)
    mine = act[:, own_at]
    theirs = actb[1]
    for s in (0, 1):
        rows = jnp.where(t == s, mine, theirs)
        pm[s] = dot(rows.astype(BF16), wm[...], NN)
    x_copy = misc.start(1 + n_z, pm.at[1 - x], rx, xp)
    send_share(0)
    send_share(2)
    start_zero(0)
    start_zero(1)
    x_copy.wait_recv()
    pm[2] = pm[x] + rx[...]
    y_copy = misc.start(2 + n_z, pm.at[2], ry, yp)
    tick()
    y_copy.wait_recv()
    pm[3] = pm[2] + ry[...]
    c_copy = misc.start(3 + n_z, pm.at[3], rc, core)
    tick()
    c_copy.wait_recv()
    bias = cat([vec[j:j + 1, :] for j in range(6)], 1)
    mz[z] = pm[3] + rc[...] + bias
    mod_copies = [misc.start(4 + n_z + d, mz.at[z], mz.at[z], target) for d, target in enumerate(zs)]
    tick()
    for copy in mod_copies + vec_copies:
        copy.wait_recv()
    vec_local.wait()
    cols = vec.shape[1]
    seq_row = pl.ds(n_z * y + z, 1)
    x_mod[6:8, :] = jnp.zeros((2, n_z * cols), F32)
    for j in range(6):
        x_mod[j:j + 1, :] = cat([mz[zi, seq_row, j * cols:(j + 1) * cols] for zi in range(n_z)], 1)
    x_mod[...] = reorder(x_mod[...], n_hi)
    x_vec[...] = vz[...]
    tick()

    def wide(k):
        return cat([vz[zi, k:k + 1, :] for zi in range(n_z)], 1)

    def narrow(k):
        return cat([vz[zi, k:k + 1, lanes_at(t)] for zi in range(n_z)], 1)

    got_share(0)
    got_share(2)
    half = 2 * PIECE
    full = 2 * half
    mine_ids = idb.at[pl.ds(2 * t, 2)]
    id_copy = misc.start(3 + 2 * n_z, mine_ids, mine_ids, core)
    flush(tokb, x_tok)

    def first_norm(rows, at, p):
        normed, unused = normalize(tokb[p, rows, :].astype(F32))
        h1[t, at, :] = (normed * (1.0 + x_mod[1:2, :]) + x_mod[2:3, :]).astype(BF16)
    step_rows(first_norm)
    h1_copy = misc.start(4 + 2 * n_z, h1.at[t], h1.at[t], core)

    pump(2)
    id_copy.wait_recv()
    lanes = lane_of((full, LANES)) % HD
    scale = idb[...].reshape(full, LANES).astype(F32)
    feature = lanes.astype(F32)
    ma[...] = jnp.where((lanes < 16) & (feature > scale), 1.0, 0.0).astype(BF16)
    mb[...] = jnp.where((lanes < 16) & (feature == scale), NEG, 0.0).astype(BF16)
    flush(ma, x_ma)
    flush(mb, x_mb)
    pump(2)
    send_share(1)
    h1_copy.wait_recv()

    def whole(ref):
        return ref[...].reshape(full, ref.shape[-1])

    def w_in(m):
        return g_in[m].reshape(8 * LANES, n_z * LANES)

    arrived(0)
    qr[...] = dot(whole(h1), w_in(0), NN) + narrow(6)
    q8[...] = (qr[...] * lax.rsqrt(head_mean(qr[...] * qr[...]) + NORM_EPS) * narrow(8)).astype(BF16) * 0.125
    arrived(1)
    kr[...] = dot(whole(h1), w_in(1), NN)
    kh[...] = (kr[...] * lax.rsqrt(head_mean(kr[...] * kr[...]) + NORM_EPS) * narrow(9)).astype(BF16)
    flush(qr, x_qr)
    flush(kr, x_kr)
    flush(q8, x_q8)
    flush(kh, x_kh)
    pump(1)
    arrived(2)
    vv[...] = (dot(whole(h1), w_in(2), NN) + narrow(7)).astype(BF16)
    flush(vv, x_v)
    flush(h1, x_h1)
    flush(g_in.at[pl.ds(0, 3)], x_wq)
    got_share(1)
    flush(cotb, x_cot)

    def gate(rows, at, p):
        gf[t, at, :] = (cotb[p, rows, :].astype(F32) * x_mod[3:4, :]).astype(BF16)
    step_rows(gate)
    gf_copy = misc.start(5 + 2 * n_z, gf.at[t], gf.at[t], core)

    def attend(i, carry):
        at = lanes_at(i)
        q2, k2, v2 = q8[:, at], kh[:, at], vv[:, at]
        mine_a, mine_b = ma[...], mb[...]
        low = lane_of((full, LANES)) < HD
        outs, tops = [], []
        for h in (0, 1):
            here = low if h == 0 else jnp.logical_not(low)
            s = dot(jnp.where(here, q2, mine_a), jnp.where(here, k2, mine_b), NT)
            top = jnp.max(s, axis=1, keepdims=True)
            e = jnp.exp(s - top).astype(BF16)
            got = dot(e, jnp.where(here, v2, jnp.ones_like(v2)), NN)
            total = got[:, HD:HD + 1] if h == 0 else got[:, 0:1]
            outs.append(got / total)
            tops.append(top + jnp.log(total))
        oo[:, at] = jnp.where(low, outs[0], outs[1]).astype(BF16)
        lse[:, at] = jnp.where(low, tops[0], tops[1])
        return carry

    pairs = n_z * LANES // LANES
    for i in range(0, pairs, 2):
        lax.fori_loop(i, i + 2, attend, 0)
        pump(1)
    flush(oo, x_o)
    flush(lse, x_lse)

    arrived(3)
    flush(g_out.at[0], x_wo)
    width = 8 * LANES
    hw = width // 2
    for j in (0, 1):
        both = dot(oo[...], g_out[0, j], NN)
        attn[:, j * hw:(j + 1) * hw] = jnp.where(t == 0, both[:half], both[half:])
        at_send[:, j * hw:(j + 1) * hw] = jnp.where(t == 0, both[half:], both[:half]).astype(BF16)
    at_copy = misc.start(6 + 2 * n_z, at_send, at_recv, core)
    at_copy.wait_recv()
    proj_bias = reorder(wide(10 + n_ff), n_hi)


    def second_norm(rows, at, p):
        total = attn[at, :] + at_recv[at, :].astype(F32) + proj_bias
        attn[at, :] = total
        middle = tokb[p, rows, :].astype(F32) + x_mod[0:1, :] * total
        mid[at, :] = middle
        normed, unused = normalize(middle)
        h2[t, at, :] = (normed * (1.0 + x_mod[4:5, :]) + x_mod[5:6, :]).astype(BF16)
    step_rows(second_norm)
    h2_copy = misc.start(7 + 2 * n_z, h2.at[t], h2.at[t], core)
    flush(attn, x_attn)
    flush(mid, x_mid)
    gf_copy.wait_recv()
    pump(1)
    x_gf[...] = jnp.zeros_like(x_gf)
    x_gf[0:1, :] = jnp.sum(whole(gf).astype(F32), axis=0, keepdims=True)
    x_gu[...] = jnp.zeros_like(x_gu)
    h2_copy.wait_recv()

    for r in range(n_ff):
        arrived(4 + 2 * r)
        bias_row = narrow(10 + r)
        u = dot(whole(h2), w_in(3 + r), NN) + bias_row
        value, gradient = gelu_both(u)
        act_low[...] = value.astype(BF16)
        slope[...] = gradient
        pump(1)
        arrived(5 + 2 * r)
        for j in (0, 1):
            part = dot(act_low[...], g_out[1 + r, j], NN)
            cols_here = pl.ds(j * hw, hw)
            facc[:, cols_here] = part if r == 0 else facc[:, cols_here] + part
        for j in (0, 1):
            gout[r, j] = dot(act_low[...], gf[:, :, j * hw:(j + 1) * hw].reshape(full, hw), TN).astype(BF16)
        flush(gout.at[r], x_gout.at[r])
        back_act = (dot(gf[:, :, :hw].reshape(full, hw), g_out[1 + r, 0], NT)
                    + dot(gf[:, :, hw:].reshape(full, hw), g_out[1 + r, 1], NT))
        gu = (back_act * slope[...]).astype(BF16)
        act_low[...] = gu
        pump(1)
        x_gu[r:r + 1, :] = jnp.sum(gu.astype(F32), axis=0, keepdims=True)
        gin[r] = dot(whole(h2), act_low[...], TN).astype(BF16).reshape(gin.shape[1:])
        flush(gin.at[r], x_gin.at[r])
        part = dot(act_low[...], w_in(3 + r), NT)
        dacc[...] = part if r == 0 else dacc[...] + part

    mine_rows = pl.ds(pl.multiple_of(t * half, half), half)
    other_rows = pl.ds(pl.multiple_of((1 - t) * half, half), half)
    fsend[...] = facc[other_rows, :].astype(BF16)
    dsend[...] = dacc[other_rows, :].astype(BF16)
    flush(facc.at[mine_rows], x_fown)
    flush(fsend, x_fsend)
    flush(dacc.at[mine_rows], x_down)
    flush(dsend, x_dsend)
    for copy in flushed:
        copy.wait()
    for j, (src, dst) in enumerate(shares):
        for yd in (0, 1):
            @pl.when(jnp.logical_not(loops & (y == yd)))
            def _():
                ref = src.at[2 * z + yd]
                pltpu.make_async_remote_copy(
                    src_ref=ref, dst_ref=ref, send_sem=tok_sem.at[0, j, yd], recv_sem=tok_sem.at[1, j, x],
                    device_id=(f_base + y, 2 * yd + t, z), device_id_type=MESH).wait_send()
    ag.finish()
    misc.finish()


def forward(s_in, s_out, tok, cot, ids, act, wm, vec, n_z, n_hi):
    n_in, n_out = s_in.shape[0], s_out.shape[0]
    n_ff = n_out - 1
    pieces = n_in + n_out
    here, width = n_z * LANES, 8 * LANES
    half, full = 2 * PIECE, 4 * PIECE
    hw = width // 2
    S = jax.ShapeDtypeStruct
    wide_low, wide_full = S((half, width), BF16), S((half, width), F32)
    cols_low, cols_full = S((full, here), BF16), S((full, here), F32)
    mask = S((full, LANES), BF16)
    big = [
        S((3, 2, 4, LANES, here), BF16), S((2, here, hw), BF16), S((2, half, width), BF16), cols_full, cols_full,
        cols_low, cols_low, cols_low, cols_low, cols_full, mask, mask, S((2, PIECE, width), BF16),
        S((2, PIECE, width), BF16), wide_full, wide_full, wide_full, wide_low, wide_full, wide_low,
        S((n_ff, 2, 4, LANES, here), BF16), S((n_ff, 2, here, hw), BF16)]
    small = [S((8, width), F32), S((8, here), F32), S((8, width), F32), S((n_z,) + vec.shape, F32)]
    any_space, vmem = pl.BlockSpec(memory_space=pl.ANY), pl.BlockSpec(memory_space=pltpu.VMEM)
    mod_shape = (8, wm.shape[1])
    V = pltpu.VMEM
    dma = pltpu.SemaphoreType.DMA
    return pl.pallas_call(
        functools.partial(forward_kernel, n_z, n_ff, n_hi),
        out_shape=tuple(big + small),
        in_specs=[any_space] * 5 + [vmem] * 3,
        out_specs=tuple([any_space] * len(big) + [vmem] * len(small)),
        scratch_shapes=[
            V((n_in, 2, 4, LANES, here), BF16), V((n_out, 2, here, hw), BF16),
            V((2, PIECE, width), BF16), V((2, PIECE, width), BF16), V((4, PIECE, LANES), BF16),
            V((2, 8, LANES), F32), V((4,) + mod_shape, F32), V(mod_shape, F32), V(mod_shape, F32), V(mod_shape, F32),
            V((n_z,) + mod_shape, F32), V((n_z,) + vec.shape, F32),
            V((2, half, width), BF16), V((2, half, width), BF16), V((2, half, width), BF16),
            V((full, here), F32), V((full, here), F32), V((full, here), BF16), V((full, here), BF16), V((full, here), BF16),
            V((full, here), BF16), V((full, here), F32), V((full, LANES), BF16), V((full, LANES), BF16),
            V((half, width), BF16), V((half, width), BF16), V((half, width), F32), V((half, width), F32),
            V((full, width), F32), V((full, width), F32), V((half, width), BF16), V((half, width), BF16),
            V((n_ff, 2, 4, LANES, here), BF16), V((n_ff, 2, here, hw), BF16), V((full, here), BF16), V((full, here), F32),
            dma((pieces + 1,)), dma((pieces, n_z + 3)), dma((pieces, n_z + 3)), dma((8 + 2 * n_z,)), dma((8 + 2 * n_z,)),
            dma((len(big) + 2 * n_ff,)), dma((2, 3, 2)),
        ],
        compiler_params=pltpu.CompilerParams(collective_id=0, has_side_effects=True, vmem_limit_bytes=VMEM_BYTES),
    )(s_in, s_out, tok, cot, ids, act, wm, vec)

class Guarded:
    def __init__(self):
        self.sent = []

    def start(self, cond, copy):
        @pl.when(cond)
        def _():
            copy.start()
        self.sent.append((cond, copy))

    def finish(self):
        for cond, copy in self.sent:
            @pl.when(cond)
            def _(copy=copy):
                copy.wait_send()


def backward_kernel(n_z, n_ff, n_hi, *refs):
    n_in, n_out = 3 + n_ff, 1 + n_ff
    (x_wq, x_wo, x_h1, x_qr, x_kr, x_q8, x_kh, x_v, x_o, x_lse, x_ma, x_mb, x_tok, x_cot, x_attn, x_mid,
     x_fown, x_fsend, x_down, x_dsend, x_gin, x_gout, mod, gu_sum, gf_sum, vz,
     o_mixed, o_grad, o_in, o_out, o_dmod, o_vec,
     wq, wo, h1, qr, kr, q8, kh, vv, oo, lse, ma, mb, tokb, cotb, attn, mid, buf, f_recv, d_recv,
     dmid, ga, go, mixed, dsend, sums, vd, vdr, vs, vdz, zv, v_sum, v_get,
     p_full, q_full, p_half, q_half, a_in, a_out, b_in, b_out, z_in, z_out, f_in, f_out,
     load_sem, own_sem, rs_send, rs_recv, m_send, m_recv, t_send, t_recv, g_send, g_recv) = refs
    f, c, z, t, x, y = place()
    core, xp, yp, zs = partners(n_z)
    f_base = f - t
    last = n_z - 1
    half, full = 2 * PIECE, 4 * PIECE
    width = mod.shape[1]
    hw = width // 2

    barrier = pltpu.get_barrier_semaphore()
    for target in [core, xp, yp] + zs:
        pl.semaphore_signal(barrier, inc=1, device_id=target, device_id_type=MESH)
    loops = (y == t) & (x == t)
    for ys in (0, 1):
        @pl.when(jnp.logical_not(loops & (y == ys)))
        def _():
            pl.semaphore_signal(barrier, inc=1, device_id=(f_base + y, 2 * ys + t, z), device_id_type=MESH)

    loads = {}
    names = [("d", x_down, buf.at[1]), ("mid", x_mid, mid), ("cot", x_cot, cotb), ("attn", x_attn, attn),
             ("f", x_fown, buf.at[0]), ("wo", x_wo, wo), ("o", x_o, oo), ("q", x_q8, q8), ("k", x_kh, kh), ("v", x_v, vv),
             ("lse", x_lse, lse), ("ma", x_ma, ma), ("mb", x_mb, mb), ("qr", x_qr, qr), ("kr", x_kr, kr),
             ("h1", x_h1, h1), ("wq", x_wq, wq), ("tok", x_tok, tokb)]
    for i, (name, src, dst) in enumerate(names):
        loads[name] = pltpu.make_async_copy(src, dst, load_sem.at[i])
        loads[name].start()
    pl.semaphore_wait(barrier, 4 + n_z - jnp.where(loops, 1, 0))

    rs = Wire(rs_send, rs_recv)
    misc = Wire(m_send, m_recv)
    chain = Guarded()
    d_copy = misc.start(1, x_dsend, d_recv, core)
    f_copy = misc.start(0, x_fsend, f_recv, core)

    order = []
    for r in range(n_ff):
        order += [("i", 3 + r), ("o", 1 + r)]
    order += [("o", 0), ("i", 2), ("i", 1), ("i", 0)]
    pieces = len(order)
    one, two, four, own_half = {}, {}, {}, {}

    def y_first(p):
        return p % 2 == 0

    def parts(p, mine):
        if y_first(p):
            yy = y if mine else 1 - y
            return [2 * yy, 2 * yy + 1]
        xx = x if mine else 1 - x
        return [xx, 2 + xx]

    def source(p, at):
        kind, m = order[p]
        if kind == "i":
            return x_gin.at[m - 3, :, at] if m >= 3 else p_full.at[m, :, at]
        return x_gout.at[m - 1, :, :, lanes_at(at)] if m >= 1 else q_full.at[:, :, lanes_at(at)]

    def kept(p, k):
        kind, m = order[p]
        return p_half.at[m, k] if kind == "i" else q_half.at[m, k]

    def bufs(p, inner, outer):
        kind, m = order[p]
        return inner.at[m] if kind == "i" else outer.at[m]

    def step_one(p):
        one[p] = [rs.start((p, k), source(p, at), bufs(p, a_in, a_out).at[k], yp if y_first(p) else xp)
                  for k, at in enumerate(parts(p, False))]
        own_half[p] = []
        for k, at in enumerate(parts(p, True)):
            copy = pltpu.make_async_copy(source(p, at), kept(p, k), own_sem.at[p, k])
            copy.start()
            own_half[p].append(copy)

    def step_two(p):
        for copy in one[p]:
            copy.wait_recv()
        for copy in own_half[p]:
            copy.wait()
        for k in (0, 1):
            ref = kept(p, k)
            ref[...] = (ref[...].astype(F32) + bufs(p, a_in, a_out)[k].astype(F32)).astype(BF16)
        go_bit = (1 - x) if y_first(p) else (1 - y)
        two[p] = rs.start((p, 2), kept(p, go_bit), bufs(p, b_in, b_out), xp if y_first(p) else yp)

    def span(p, ref, lo, hi):
        if order[p][0] == "i":
            return ref.at[:, :, lo * LANES:hi * LANES]
        return ref.at[:, lo * LANES:hi * LANES, :]

    def right_copy(p, s):
        here = kept(p, x if y_first(p) else y)
        return pltpu.make_async_remote_copy(
            src_ref=span(p, here, s + 1, n_z), dst_ref=span(p, bufs(p, z_in, z_out), s + 2, n_z + 1),
            send_sem=rs_send.at[p, 3], recv_sem=rs_recv.at[p, 3], device_id=(f, c, z + 1), device_id_type=MESH)

    def left_copy(p, s):
        here = kept(p, x if y_first(p) else y)
        return pltpu.make_async_remote_copy(
            src_ref=span(p, here, 0, s), dst_ref=span(p, bufs(p, z_in, z_out), 0, s),
            send_sem=rs_send.at[p, 4], recv_sem=rs_recv.at[p, 4], device_id=(f, c, z - 1), device_id_type=MESH)

    def add_into(p, lo, hi, shift):
        here = kept(p, x if y_first(p) else y)
        a, b = span(p, here, lo, hi), span(p, bufs(p, z_in, z_out), lo + shift, hi + shift)
        a[...] = (a[...].astype(F32) + b[...].astype(F32)).astype(BF16)

    def step_z(p, s):
        if s == 0:
            two[p].wait_recv()
            here = kept(p, x if y_first(p) else y)
            here[...] = (here[...].astype(F32) + bufs(p, b_in, b_out)[...].astype(F32)).astype(BF16)

        @pl.when(z == s)
        def _():
            if s > 0:
                landed = span(p, bufs(p, z_in, z_out), s + 1, n_z + 1)
                pltpu.make_async_copy(landed, landed, rs_recv.at[p, 3]).wait()
            if s < last:
                if s > 0:
                    add_into(p, s + 1, n_z, 1)
                right_copy(p, s).start()

        @pl.when(z == last - s)
        def _():
            e = last - s
            if s > 0:
                landed = span(p, bufs(p, z_in, z_out), 0, e + 1)
                pltpu.make_async_copy(landed, landed, rs_recv.at[p, 4]).wait()
            if e > 0:
                if s > 0:
                    add_into(p, 0, e, 0)
                left_copy(p, e).start()

    def step_core(p):
        kind, m = order[p]
        here = kept(p, x if y_first(p) else y)
        total, result = (f_in, o_in) if kind == "i" else (f_out, o_out)
        for s in range(n_z):
            @pl.when(z == s)
            def _():
                value = span(p, here, s, s + 1)[...].astype(F32)
                if s > 0:
                    value = value + span(p, bufs(p, z_in, z_out), s + 1, s + 2)[...].astype(F32)
                if s < last:
                    value = value + span(p, bufs(p, z_in, z_out), s, s + 1)[...].astype(F32)
                total[m] = value
        result[m, t] = total[m, t]
        four[p] = rs.start((p, 5), total.at[m, 1 - t], result.at[m, t], core)

    def in_range(p):
        return 0 <= p < pieces

    ready = [2 * n_ff]
    started = [0]
    step = [0]

    def first_sends(upto):
        while started[0] < min(upto, ready[0], pieces):
            step_one(started[0])
            started[0] += 1

    def pump(n=1):
        for _ in range(n):
            k = step[0]
            first_sends(k + 3)
            if in_range(k) and k >= started[0]:
                return
            if in_range(k):
                step_two(k)
            for s in range(n_z):
                if in_range(k - 1 - s):
                    step_z(k - 1 - s, s)
            if in_range(k - n_z - 1):
                step_core(k - n_z - 1)
            step[0] += 1

    first_sends(3)

    def share_out(j, src, dst):
        for xs in (0, 1):
            own = loops & (x == xs)
            there = dst.at[2 * z + y]
            local = pltpu.make_async_copy(src.at[xs], there, t_recv.at[j, y])

            @pl.when(own)
            def _():
                local.start()
            chain.start(jnp.logical_not(own), pltpu.make_async_remote_copy(
                src_ref=src.at[xs], dst_ref=there, send_sem=t_send.at[j, xs], recv_sem=t_recv.at[j, y],
                device_id=(f_base + x, 2 * t + xs, z), device_id_type=MESH))

    def pass_along(j, dst, s):
        if s == 0:
            for ys in (0, 1):
                pltpu.make_async_copy(dst.at[2 * z + ys], dst.at[2 * z + ys], t_recv.at[j, ys]).wait()
        for side, (there, back_at) in enumerate(((z + 1, z - s), (z - 1, z + s))):
            valid = (back_at >= 0) & (back_at <= last)
            block = dst.at[pl.ds(2 * lax.clamp(0, back_at, last), 2)]
            if s > 0:
                @pl.when(valid)
                def _():
                    pltpu.make_async_copy(block, block, g_recv.at[j, side, s]).wait()
            if s < last:
                chain.start(valid & (there >= 0) & (there <= last), pltpu.make_async_remote_copy(
                    src_ref=block, dst_ref=block, send_sem=g_send.at[j, side, s], recv_sem=g_recv.at[j, side, s + 1],
                    device_id=(f, c, lax.clamp(0, there, last)), device_id_type=MESH))

    def wide(k):
        return cat([vz[zi, k:k + 1, :] for zi in range(n_z)], 1)

    def narrow(k):
        return cat([vz[zi, k:k + 1, lanes_at(t)] for zi in range(n_z)], 1)

    def tally(j, values):
        sums[j] = sums[j] + values[:8] + values[8:]

    sums[...] = jnp.zeros_like(sums)
    for name in ("d", "mid", "cot", "attn"):
        loads[name].wait()
    d_copy.wait_recv()

    def second_norm(rows, at, p):
        grad = buf[1, at, :] + d_recv[at, :].astype(F32)
        normed, scale = normalize(mid[at, :])
        tally(4, grad * normed)
        tally(5, grad)
        w = grad * (1.0 + mod[4:5, :])
        pulled = scale * (w - jnp.mean(w, axis=-1, keepdims=True) - normed * jnp.mean(w * normed, axis=-1, keepdims=True))
        total = cotb[p, rows, :].astype(F32) + pulled
        dmid[at, :] = total
        tally(0, total * attn[at, :])
        low = (total * mod[0:1, :]).astype(BF16)
        ga[t, at, :] = low
        tally(6, low.astype(F32))
    step_rows(second_norm)
    ga_copy = misc.start(2, ga.at[t], ga.at[t], core)

    ffn_bias = reorder(wide(11 + n_ff), n_hi)
    loads["f"].wait()
    f_copy.wait_recv()

    def mix(rows, at, p):
        out = buf[0, at, :] + f_recv[at, :].astype(F32) + ffn_bias
        tally(3, cotb[p, rows, :].astype(F32) * out)
        mixed[p, rows, :] = (mid[at, :] + mod[3:4, :] * out).astype(BF16)
    step_rows(mix)
    share_out(0, mixed, o_mixed)
    loads["wo"].wait()
    loads["o"].wait()
    ga_copy.wait_recv()
    pump(1)
    for j in (0, 1):
        ga_j = ga[:, :, j * hw:(j + 1) * hw].reshape(full, hw)
        part = dot(ga_j, wo[j], NT)
        if j == 0:
            first_part = part
        q_full[j] = dot(oo[...], ga_j, TN).astype(BF16)
    go[...] = (first_part + part).astype(BF16)
    ready[0] += 1
    for name in ("q", "k", "v", "lse", "ma", "mb", "qr", "kr"):
        loads[name].wait()
    pump(1)
    pass_along(0, o_mixed, 0)

    vs[...] = jnp.zeros_like(vs)

    def head_back(raw, grad, gain):
        scale = lax.rsqrt(head_mean(raw * raw) + NORM_EPS)
        normed = raw * scale
        gain_grad = jnp.sum(grad * normed, axis=0, keepdims=True)
        w = grad * gain
        return (scale * (w - normed * head_mean(w * normed))).astype(BF16), gain_grad

    def attend_back(i, carry):
        at = lanes_at(i)
        q2, k2, v2, g2, o2 = q8[:, at], kh[:, at], vv[:, at], go[:, at], oo[:, at]
        mine_a, mine_b = ma[...], mb[...]
        lanes = lane_of((full, LANES))
        low, l64 = lanes < HD, lanes % HD
        product = o2.astype(F32) * g2.astype(F32)
        dqs, dks, dvs = [], [], []
        one_like, zero_like = jnp.ones_like(v2), jnp.zeros_like(v2)
        for h in (0, 1):
            here = low if h == 0 else jnp.logical_not(low)
            l1, l2, l3 = split_three(lse[:, at][:, HD * h:HD * h + 1])
            qa = jnp.where(l64 == 40, -l1, jnp.where(l64 == 41, -l2, jnp.where(l64 == 42, -l3, mine_a)))
            ka = jnp.where((l64 >= 40) & (l64 < 43), one_like, mine_b)
            weight = jnp.exp(dot(jnp.where(here, k2, ka), jnp.where(here, q2, qa), NT))
            d1, d2, d3 = split_three(jnp.sum(jnp.where(here, product, 0.0), axis=1, keepdims=True))
            da = jnp.where(l64 == 0, -d1, jnp.where(l64 == 1, -d2, jnp.where(l64 == 2, -d3, zero_like)))
            va = jnp.where(l64 < 3, one_like, zero_like)
            ds = (weight * dot(jnp.where(here, v2, va), jnp.where(here, g2, da), NT)).astype(BF16)
            dvs.append(dot(weight.astype(BF16), g2, NN))
            dks.append(dot(ds, q2, NN))
            dqs.append(dot(ds, k2, TN))
        dq = jnp.where(low, dqs[0], dqs[1]) * 0.125
        dk = jnp.where(low, dks[0], dks[1])
        gq, q_gain = head_back(qr[:, at], dq, vs[8:9, at])
        gk, k_gain = head_back(kr[:, at], dk, vs[9:10, at])
        gv = jnp.where(low, dvs[0], dvs[1]).astype(BF16)
        q8[:, at] = gq
        kh[:, at] = gk
        vv[:, at] = gv
        vs[0:1, at] = jnp.sum(gq.astype(F32), axis=0, keepdims=True)
        vs[1:2, at] = jnp.sum(gv.astype(F32), axis=0, keepdims=True)
        vs[2:3, at] = q_gain
        vs[3:4, at] = k_gain
        return carry

    vs[8:9, :] = narrow(8)
    vs[9:10, :] = narrow(9)
    pairs = n_z
    for i in range(0, pairs, 2):
        lax.fori_loop(i, i + 2, attend_back, 0)
        pump(1)
    pass_along(0, o_mixed, 1)
    loads["h1"].wait()
    h1_all = h1[...].reshape(full, width)
    for m, ref in ((2, vv), (1, kh), (0, q8)):
        p_full[m] = dot(h1_all, ref[...], TN).astype(BF16).reshape(p_full.shape[1:])
        ready[0] += 1
    pump(1)

    loads["wq"].wait()
    part = dot(q8[...], wq[0].reshape(width, n_z * LANES), NT)
    part = part + dot(kh[...], wq[1].reshape(width, n_z * LANES), NT)
    part = part + dot(vv[...], wq[2].reshape(width, n_z * LANES), NT)
    buf[0] = jnp.where(t == 0, part[:half], part[half:])
    dsend[...] = jnp.where(t == 0, part[half:], part[:half]).astype(BF16)
    h_copy = misc.start(3, dsend, d_recv, core)
    loads["tok"].wait()
    h_copy.wait_recv()

    def first_norm(rows, at, p):
        grad = buf[0, at, :] + d_recv[at, :].astype(F32)
        normed, scale = normalize(tokb[p, rows, :].astype(F32))
        tally(1, grad * normed)
        tally(2, grad)
        w = grad * (1.0 + mod[1:2, :])
        pulled = scale * (w - jnp.mean(w, axis=-1, keepdims=True) - normed * jnp.mean(w * normed, axis=-1, keepdims=True))
        cotb[p, rows, :] = (dmid[at, :] + pulled).astype(BF16)
    step_rows(first_norm)
    share_out(1, cotb, o_grad)
    pump(1)
    pass_along(0, o_mixed, 2)

    for j in range(7):
        vd[j:j + 1, :] = jnp.sum(sums[j], axis=0, keepdims=True)
    vd[7:8, :] = gf_sum[0:1, :] * 0.5
    v_copy = misc.start(4, vd, vdr, core)
    vs[4:8, :] = gu_sum[0:4, :]
    v_copy.wait_recv()
    vd_all = reorder(vd[...] + vdr[...], n_hi, inverse=True)
    cols = width // n_z
    for zi in range(n_z):
        vdz[zi] = vd_all[:, zi * cols:(zi + 1) * cols]
    o_dmod[x, y, z] = vdz[z]
    zv[z] = vs[0:8, lanes_at(z)]
    z_copies = []
    for d, target in enumerate(zs):
        zi = lax.rem(z + 1 + d, n_z)
        z_copies.append(misc.start(5 + d, vdz.at[zi], o_dmod.at[x, y, z], target))
        z_copies.append(misc.start(4 + n_z + d, vs.at[pl.ds(0, 8), lanes_at(zi)], zv.at[z], target))
    pump(1)
    for copy in z_copies:
        copy.wait_recv()
    total = zv[0]
    for zi in range(1, n_z):
        total = total + zv[zi]
    v_sum[0] = total
    slot = 3 + 2 * n_z
    y_copies = [misc.start(slot, o_dmod.at[x, y], o_dmod.at[x, y], yp), misc.start(slot + 1, v_sum.at[0], v_get.at[0], yp)]
    pump(1)
    for copy in y_copies:
        copy.wait_recv()
    v_sum[1] = v_sum[0] + v_get[0]
    x_copies = [misc.start(slot + 2, o_dmod.at[x], o_dmod.at[x], xp), misc.start(slot + 3, v_sum.at[1], v_get.at[1], xp)]
    pump(1)
    for copy in x_copies:
        copy.wait_recv()
    o_vec[t] = v_sum[1] + v_get[1]
    c_copy = misc.start(slot + 4, o_vec.at[t], o_vec.at[t], core)

    passes = [(j, s) for j in (0, 1) for s in range(3 if j == 0 else 0, n_z)]
    while step[0] < pieces + n_z + 1:
        pump(1)
        if passes and step[0] >= pieces - 4:
            j, s = passes.pop(0)
            pass_along(j, o_mixed if j == 0 else o_grad, s)
    for j, s in passes:
        pass_along(j, o_mixed if j == 0 else o_grad, s)
    c_copy.wait_recv()
    for p in range(pieces):
        four[p].wait_recv()
    for p in range(pieces):
        for s in range(n_z):
            @pl.when(z == s)
            def _():
                if s < last:
                    right_copy(p, s).wait_send()
                if s > 0:
                    left_copy(p, s).wait_send()
    chain.finish()
    rs.finish()
    misc.finish()


def backward(operands, n_z, n_ff, n_hi):
    n_in, n_out = 3 + n_ff, 1 + n_ff
    here, width = n_z * LANES, 8 * LANES
    half, full = 2 * PIECE, 4 * PIECE
    hw, cols = width // 2, width // n_z
    S, V, dma = jax.ShapeDtypeStruct, pltpu.VMEM, pltpu.SemaphoreType.DMA
    any_space, vmem = pl.BlockSpec(memory_space=pl.ANY), pl.BlockSpec(memory_space=pltpu.VMEM)
    rows_out = S((2 * n_z, PIECE, width), BF16)
    pieces = n_in + n_out
    slots = 8 + 2 * n_z
    return pl.pallas_call(
        functools.partial(backward_kernel, n_z, n_ff, n_hi),
        out_shape=(rows_out, rows_out, S((n_in, 2, LANES, LANES), F32), S((n_out, 2, LANES, LANES), F32),
                   S((2, 2, n_z, 8, cols), F32), S((2, 8, LANES), F32)),
        in_specs=[any_space] * (len(operands) - 4) + [vmem] * 4,
        out_specs=(any_space, any_space, vmem, vmem, vmem, vmem),
        scratch_shapes=[
            V((3, 2, 4, LANES, here), BF16), V((2, here, hw), BF16), V((2, half, width), BF16),
            V((full, here), F32), V((full, here), F32), V((full, here), BF16), V((full, here), BF16),
            V((full, here), BF16), V((full, here), BF16), V((full, here), F32), V((full, LANES), BF16),
            V((full, LANES), BF16), V((2, PIECE, width), BF16), V((2, PIECE, width), BF16), V((half, width), F32),
            V((half, width), F32), V((2, half, width), F32), V((half, width), BF16), V((half, width), BF16),
            V((half, width), F32), V((2, half, width), BF16), V((full, here), BF16), V((2, PIECE, width), BF16),
            V((half, width), BF16), V((8, 8, width), F32), V((8, width), F32), V((8, width), F32), V((16, here), F32),
            V((n_z, 8, cols), F32), V((n_z, 8, LANES), F32), V((2, 8, LANES), F32), V((2, 8, LANES), F32),
            V((3, 2, 4, LANES, here), BF16), V((2, here, hw), BF16),
            V((n_in, 2, 2, LANES, here), BF16), V((n_out, 2, 2, here, LANES), BF16),
            V((n_in, 2, 2, LANES, here), BF16), V((n_out, 2, 2, here, LANES), BF16),
            V((n_in, 2, LANES, here), BF16), V((n_out, 2, here, LANES), BF16),
            V((n_in, 2, LANES, here + LANES), BF16), V((n_out, 2, here + LANES, LANES), BF16),
            V((n_in, 2, LANES, LANES), F32), V((n_out, 2, LANES, LANES), F32),
            dma((18,)), dma((pieces, 2)), dma((pieces, 6)), dma((pieces, 6)), dma((slots,)), dma((slots,)),
            dma((2, 2)), dma((2, 2)), dma((2, 2, n_z)), dma((2, 2, n_z)),
        ],
        compiler_params=pltpu.CompilerParams(collective_id=1, has_side_effects=True, vmem_limit_bytes=VMEM_BYTES),
    )(*operands)


def per_device(n_f, n_c, n_z, tokens, cotangent, class_table, labels, scale_ids, in_weight, in_first, in_second,
               out_weight, out_first, out_second, vectors, vec_first, vec_second):
    n_hi = n_f // 2
    f, c, z, t, x, y = place()
    seqs, piece, width = tokens.shape
    cols = in_weight.shape[2]
    n_ff = out_weight.shape[0] - 1
    ada = 3 + n_ff
    half = cols // 2
    pairs = [[2 * i, 2 * i + 1] for i in range(n_hi)]
    his = [[i + 2 * j for j in range(n_hi)] for i in range(2)]

    def into(a):
        if n_hi == 1:
            return a
        shape = a.shape[:-1]
        return jnp.swapaxes(a.reshape(shape + (n_hi, 2 * n_c, -1)), -3, -2).reshape(a.shape)

    def back(a):
        if n_hi == 1:
            return a
        shape = a.shape[:-1]
        return jnp.swapaxes(a.reshape(shape + (2 * n_c, n_hi, -1)), -3, -2).reshape(a.shape)

    in_low = in_weight.astype(BF16)
    out_low = out_weight.astype(BF16)
    if n_hi > 1:
        in_low = lax.all_gather(in_low, "fsdp", axis=0, tiled=True, axis_index_groups=his)
        out_low = lax.all_gather(out_low, "fsdp", axis=2, tiled=True, axis_index_groups=his)
    rows = in_low.shape[0]
    s_in = in_low[:, :ada].reshape(rows, ada, 2, half).transpose(1, 2, 0, 3)
    w_ada = in_low[:, ada:].reshape(rows, 6 * cols)
    pad = ((0, 0), (0, PIECE - piece), (0, 0))
    tok = jnp.pad(into(tokens), pad)
    cot = jnp.pad(into(cotangent), pad)
    ids = jnp.pad(scale_ids, pad[:2], constant_values=10).astype(BF16)
    ids = jnp.broadcast_to(ids[:, :, None], ids.shape + (LANES,))
    conditions = jnp.take(class_table, labels, axis=0)
    cond_act = jax.nn.silu(conditions).astype(BF16)
    act = into(cond_act).reshape(n_z, 2, width).transpose(1, 0, 2).reshape(2 * n_z, width).astype(F32)
    kept = forward(s_in, out_low, tok, cot, ids, act, w_ada, vectors, n_z, n_hi)
    mixed, input_grad, o_in, o_out, d_mod, d_vec = backward(kept, n_z, n_ff, n_hi)
    mixed = mixed[:, :piece]
    input_grad = input_grad[:, :piece].astype(F32)

    chips = 4 * n_z
    d_mod = d_mod.reshape(chips, 8, cols)
    act_all = lax.all_gather(act, "fsdp", axis=0, tiled=False, axis_index_groups=pairs).reshape(chips, width)
    act_rows = lax.dynamic_slice_in_dim(act_all, (t * n_c + c) * rows, rows, 1)
    ada_grad = jnp.einsum("sd,src->drc", act_rows, d_mod[:, :6], precision=PRECISE)
    cond_part = jnp.einsum("src,drc->sd", d_mod[:, :6], w_ada.reshape(rows, 6, cols).astype(F32), precision=PRECISE)
    cond_sum = lax.psum(cond_part, "tp")
    cond_sum = lax.all_gather(cond_sum, "ctx", axis=1, tiled=True)
    cond_sum = lax.all_gather(cond_sum, "fsdp", axis=1, tiled=True, axis_index_groups=pairs)
    cond_sum = back(cond_sum).reshape(2, 2, n_z, width).transpose(0, 2, 1, 3).reshape(2, 2 * n_z, width)
    cond_mine = lax.dynamic_index_in_dim(cond_sum, t, 0, keepdims=False)
    unused, silu_pull = jax.vjp(jax.nn.silu, conditions)
    condition_grad = silu_pull(cond_mine)[0]

    mod_sum = jnp.sum(d_mod, axis=0)
    vec_grad = jnp.concatenate([mod_sum[:6], d_vec.transpose(1, 0, 2).reshape(8, cols), mod_sum[6:]])
    in_grad = jnp.concatenate([o_in.transpose(2, 0, 1, 3).reshape(rows, ada, cols), ada_grad], axis=1)
    out_grad = o_out.reshape(1 + n_ff, cols, rows)
    if n_hi > 1:
        vec_grad = lax.psum(vec_grad, "fsdp", axis_index_groups=his)
        in_grad = lax.psum_scatter(in_grad, "fsdp", scatter_dimension=0, tiled=True, axis_index_groups=his)
        out_grad = lax.psum_scatter(out_grad, "fsdp", scatter_dimension=2, tiled=True, axis_index_groups=his)
    squares = jnp.sum(in_grad * in_grad) + jnp.sum(out_grad * out_grad)
    first_device = (f == 0) & (c == 0)
    squares = squares + jnp.where(first_device, jnp.sum(vec_grad * vec_grad), 0.0)
    grad_norm = jnp.sqrt(lax.psum(squares, ("fsdp", "ctx", "tp")))
    factor = CLIP_NORM / jnp.maximum(grad_norm, CLIP_NORM)
    in_new = adam_update(in_weight, in_first, in_second, in_grad, factor, RATE_MATRIX, WEIGHT_DECAY)
    out_new = adam_update(out_weight, out_first, out_second, out_grad, factor, RATE_MATRIX, WEIGHT_DECAY)
    vec_new = adam_update(vectors, vec_first, vec_second, vec_grad, factor, RATE_VECTOR, 0.0)
    return (back(mixed), back(input_grad), condition_grad, grad_norm, *in_new, *out_new, *vec_new,
            factor * vec_grad[11 + n_ff])


def solution(mesh):
    in_matrix = P(("fsdp", "ctx"), None, "tp")
    out_matrix = P(None, "tp", ("fsdp", "ctx"))
    vector = P(None, "tp")
    rows = P("fsdp", "ctx", None)
    return jax.shard_map(
        functools.partial(per_device, mesh.shape["fsdp"], mesh.shape["ctx"], mesh.shape["tp"]),
        mesh=mesh,
        in_specs=(rows, rows, P(), P("fsdp"), P("fsdp", "ctx"), in_matrix, in_matrix, in_matrix,
                  out_matrix, out_matrix, out_matrix, vector, vector, vector),
        out_specs=(rows, rows, P("fsdp", None), P(), in_matrix, in_matrix, in_matrix, in_matrix,
                   out_matrix, out_matrix, out_matrix, out_matrix, vector, vector, vector, vector, P("tp")),
        check_vma=False,
    )
```

```python
import functools
import math

import jax
import jax.numpy as jnp
from jax import lax
from jax.experimental import pallas as pl
from jax.experimental.pallas import tpu as pltpu
from jax.sharding import PartitionSpec as P

HD = 64
STEP = 5
PRECISE = lax.Precision.HIGHEST
NORM_EPS = 1e-06
CLIP_NORM = 1.0
BETA_ONE = 0.5
BETA_TWO = 0.5
RATE_MATRIX = 0.03
RATE_VECTOR = 0.3
WEIGHT_DECAY = 0.05
ADAM_EPS = 1e-08

MESH = pl.DeviceIdType.MESH
F32 = jnp.float32
BF16 = jnp.bfloat16
LANES = 128
VMEM_BYTES = 60 * 2**20


def place():
    f = lax.axis_index("fsdp")
    c = lax.axis_index("ctx")
    z = lax.axis_index("tp")
    return f, c, z, lax.rem(f, 2), lax.rem(c, 2), c // 2


def partners(n_z):
    f, c, z, t, x, y = place()
    core = (f + 1 - 2 * t, c, z)
    xp = (f, 2 * y + (1 - x), z)
    yp = (f, 2 * (1 - y) + x, z)
    zs = [(f, c, lax.rem(z + d, n_z)) for d in range(1, n_z)]
    return core, xp, yp, zs


def enter(targets):
    barrier = pltpu.get_barrier_semaphore()
    for target in targets:
        pl.semaphore_signal(barrier, inc=1, device_id=target, device_id_type=MESH)
    pl.semaphore_wait(barrier, len(targets))


def lanes_at(index):
    return pl.ds(pl.multiple_of(index * LANES, LANES), LANES)


def adam_update(master, first, second, grad, factor, rate, decay):
    grad = grad * factor
    first = BETA_ONE * first + (1.0 - BETA_ONE) * grad
    second = BETA_TWO * second + (1.0 - BETA_TWO) * grad * grad
    fix_one = 1.0 - BETA_ONE**STEP
    fix_two = 1.0 - BETA_TWO**STEP
    stride = first / fix_one / (jnp.sqrt(second / fix_two) + ADAM_EPS)
    master = master - rate * (stride + decay * master)
    return (master, first, second, master.astype(BF16))


def dot(a, b, dims):
    return lax.dot_general(a, b, (dims, ((), ())), preferred_element_type=F32)


NN = ((1,), (0,))
NT = ((1,), (1,))
TN = ((0,), (0,))


PIECE = 176
NEG = -1e30
PARTS = 4
PASSES = 3


def cat(parts, axis):
    return jnp.concatenate(parts, axis=axis)


def lane_of(shape):
    return lax.broadcasted_iota(jnp.int32, shape, len(shape) - 1)


def split_two(values):
    high = values.astype(BF16)
    return high, (values - high.astype(F32)).astype(BF16)


def split_three(values):
    high = values.astype(BF16)
    rest = values - high.astype(F32)
    middle = rest.astype(BF16)
    return high, middle, (rest - middle.astype(F32)).astype(BF16)


def head_mean(values):
    row = lax.broadcasted_iota(jnp.int32, (LANES, LANES), 0) // HD
    ones = jnp.where(row == lane_of((LANES, LANES)) // HD, 1.0 / HD, 0.0).astype(BF16)
    out = []
    for k in range(values.shape[1] // LANES):
        high, lower = split_two(values[:, k * LANES:(k + 1) * LANES])
        out.append(dot(high, ones, NN) + dot(lower, ones, NN))
    return cat(out, 1)


def gelu_both(u):
    k0, k1 = 0.7978845608028654, 0.044715
    square = u * u
    th = jnp.tanh(k0 * u * (1.0 + k1 * square))
    half = 0.5 * (1.0 + th)
    slope = half + 0.5 * u * (1.0 - th * th) * (k0 * (1.0 + 3.0 * k1 * square))
    return u * half, slope


def step_rows(piece, body):
    for p in (0, 1):
        def one(i, carry, p=p):
            start = pl.multiple_of(i * 16, 16)
            body(pl.ds(start, 16), pl.ds(pl.multiple_of(p * PIECE + start, 16), 16), p)
            return carry
        lax.fori_loop(0, piece // 16, one, 0)
        if piece % 16:
            start = piece // 16 * 16
            body(pl.ds(start, piece % 16), pl.ds(p * PIECE + start, piece % 16), p)


def clear_tail(ref, t):
    for p in (0, 1):
        ref[t, pl.ds(p * PIECE + PIECE - 16, 16), :] = jnp.zeros((16, ref.shape[2]), ref.dtype)


def normalize(values):
    center = values - jnp.mean(values, axis=-1, keepdims=True)
    scale = lax.rsqrt(jnp.mean(center * center, axis=-1, keepdims=True) + NORM_EPS)
    return center * scale, scale


def reorder(rows, n_hi, inverse=False):
    if n_hi == 1:
        return rows
    width = rows.shape[1]
    each = width // (8 * n_hi)
    out = []
    for k in range(width // LANES):
        at = k * LANES + lax.broadcasted_iota(jnp.int32, (width, LANES), 1)
        there = lax.broadcasted_iota(jnp.int32, (width, LANES), 0)
        if inverse:
            wanted = (at // each % 8) * (n_hi * each) + (at // (8 * each)) * each + at % each
        else:
            wanted = (at // each % n_hi) * (8 * each) + (at // (each * n_hi)) * each + at % each
        order = jnp.where(there == wanted, 1.0, 0.0).astype(BF16)
        out.append(sum(dot(part, order, NN) for part in split_three(rows)))
    return cat(out, 1)


class Wire:
    def __init__(self, send_sem, recv_sem):
        self.send_sem, self.recv_sem, self.sent = send_sem, recv_sem, []

    def make(self, at, src, dst, target, to=None):
        return pltpu.make_async_remote_copy(
            src_ref=src, dst_ref=dst, send_sem=self.send_sem.at[at], recv_sem=self.recv_sem.at[at if to is None else to],
            device_id=target, device_id_type=MESH)

    def start(self, at, src, dst, target, to=None):
        copy = self.make(at, src, dst, target, to)
        copy.start()
        self.sent.append(copy)
        return copy

    def finish(self):
        for copy in self.sent:
            copy.wait_send()


def forward_kernel(n_z, n_ff, n_hi, *refs):
    n_in, n_out = 3 + n_ff, 1 + n_ff
    (x_in, x_out, tok, cot, ids, act, vec,
     x_wq, x_wo, x_h1, x_qr, x_kr, x_q8, x_kh, x_v, x_o, x_lse, x_ma, x_mb, x_tok, x_cot, x_attn, x_mid,
     x_fown, x_fsend, x_down, x_dsend, x_gin, x_gout, x_mod, x_gu, x_gf, x_vec, x_act,
     g_in, g_out, tokb, cotb, idb, actb, pm, rx, ry, rc, mz, vz, h1, gf, h2, qr, kr, q8, kh, vv, oo, lse, ma, mb,
     at_send, at_recv, attn, mid, facc, dacc, fsend, dsend, gin, gout, act_low, slope,
     full_in, full_out, low_in, low_out, local_sem, ag_send, ag_recv, m_send, m_recv, out_sem, tok_sem, load_sem) = refs
    f, c, z, t, x, y = place()
    core, xp, yp, zs = partners(n_z)
    f_base = f - t

    piece = tok.shape[1]
    n_all = x_in.shape[0]
    order = [("i", 0), ("i", 1), ("i", 2), ("o", 0)]
    for r in range(n_ff):
        order += [("i", 3 + r), ("o", 1 + r)]
    loads = {}
    for kind, m in [("i", j) for j in range(n_in, n_all)] + order:
        src, dst, at = (x_in, full_in, m) if kind == "i" else (x_out, full_out, n_all + m)
        loads[kind, m] = pltpu.make_async_copy(src.at[m], dst.at[m], load_sem.at[at])
        loads[kind, m].start()
    for ref in (h1, gf, h2):
        clear_tail(ref, t)

    barrier = pltpu.get_barrier_semaphore()
    for target in [core, xp, yp] + zs:
        pl.semaphore_signal(barrier, inc=1, device_id=target, device_id_type=MESH)
    loops = (y == t) & (x == t)
    for xs in (0, 1):
        @pl.when(jnp.logical_not(loops & (x == xs)))
        def _():
            pl.semaphore_signal(barrier, inc=1, device_id=(f_base + x, 2 * t + xs, z), device_id_type=MESH)
    pl.semaphore_wait(barrier, 4 + n_z - jnp.where(loops, 1, 0))

    ag = Wire(ag_send, ag_recv)
    misc = Wire(m_send, m_recv)

    shares = [(tok, tokb), (cot, cotb), (ids, None)]

    def send_share(j):
        src, dst = shares[j]
        for yd in (0, 1):
            own = loops & (y == yd)
            from_here = src.at[yd]
            to_there = dst.at[x] if dst is not None else idb.at[2 * y + x]

            @pl.when(own)
            def _():
                pltpu.make_async_copy(from_here, to_there, tok_sem.at[1, j, x]).start()

            @pl.when(jnp.logical_not(own))
            def _():
                pltpu.make_async_remote_copy(
                    src_ref=from_here, dst_ref=to_there, send_sem=tok_sem.at[0, j, yd], recv_sem=tok_sem.at[1, j, x],
                    device_id=(f_base + y, 2 * yd + t, z), device_id_type=MESH).start()

    def got_share(j):
        dst = shares[j][1]
        for xs in (0, 1):
            ref = dst.at[xs] if dst is not None else idb.at[2 * t + xs]
            pltpu.make_async_copy(ref, ref, tok_sem.at[1, j, xs]).wait()

    act_copy = misc.start(0, act.at[:, lanes_at((1 - t) * 4 + c)], actb.at[1], core)
    vec_local = pltpu.make_async_copy(vec, vz.at[z], local_sem.at[n_in + n_out])
    vec_local.start()
    vec_copies = [misc.start(1 + d, vec, vz.at[z], target) for d, target in enumerate(zs)]

    zrows = pl.ds(pl.multiple_of(z * LANES, LANES), LANES)
    first, zcopies, one, two = {}, {}, {}, {}
    for p, (kind, m) in enumerate(order):
        loads[kind, m].wait()
        if kind == "i":
            dst = g_in.at[m, t, c, :, lanes_at(z)]
            for s in (0, 1):
                low_in[m, s] = full_in[m, :, s * LANES:(s + 1) * LANES].astype(BF16)
            mine, other = low_in.at[m, t], low_in.at[m, 1 - t]
        else:
            dst = g_out.at[m, t, zrows, lanes_at(c)]
            for s in (0, 1):
                low_out[m, s] = full_out[m, s * LANES:(s + 1) * LANES, :].astype(BF16)
            mine, other = low_out.at[m, t], low_out.at[m, 1 - t]
        local = pltpu.make_async_copy(mine, dst, local_sem.at[p])
        local.start()
        first[p] = (local, ag.start((p, 0), other, dst, core))
    base = n_z

    def start_zero(p):
        if p >= len(order) or p in zcopies:
            return
        kind, m = order[p]
        first[p][0].wait()
        first[p][1].wait_recv()
        block = g_in.at[m, :, c, :, lanes_at(z)] if kind == "i" else g_out.at[m, :, zrows, lanes_at(c)]
        zcopies[p] = [ag.start((p, 1 + d), block, block, target) for d, target in enumerate(zs)]

    def x_first(p):
        return p % 2 == 0

    def start_one(p):
        kind, m = order[p]
        for copy in zcopies[p]:
            copy.wait_recv()
        block = g_in.at[m, :, c] if kind == "i" else g_out.at[m, :, :, lanes_at(c)]
        one[p] = ag.start((p, base), block, block, xp if x_first(p) else yp)

    def start_two(p):
        kind, m = order[p]
        one[p].wait_recv()
        held = (2 * y, 2 * y + 1) if x_first(p) else (x, 2 + x)
        two[p] = []
        if kind == "i" and x_first(p):
            block = g_in.at[m, :, pl.ds(2 * y, 2)]
            two[p].append(ag.start((p, base + 1), block, block, yp))
        else:
            for k, at in enumerate(held):
                block = g_in.at[m, :, at] if kind == "i" else g_out.at[m, :, :, lanes_at(at)]
                two[p].append(ag.start((p, base + 1 + k), block, block, yp if x_first(p) else xp))

    ticks = [(start_one, 0)]
    for p in range(1, len(order)):
        ticks += [(start_one, p), (start_two, p - 1)]
    ticks.append((start_two, len(order) - 1))

    def tick(n=1):
        for _ in range(n):
            if ticks:
                step, p = ticks.pop(0)
                if step is start_one:
                    for ahead in range(p + 3):
                        start_zero(ahead)
                step(p)

    def pump(n=1):
        tick(2 * n)

    def arrived(p):
        for copy in two[p]:
            copy.wait_recv()

    flushed = []

    def flush(src, dst):
        copy = pltpu.make_async_copy(src, dst, out_sem.at[len(flushed)])
        copy.start()
        flushed.append(copy)

    act_copy.wait_recv()
    cols = vec.shape[1]
    for j in range(n_in, n_all):
        loads["i", j].wait()
    own_at = lanes_at(t * 4 + c)
    mine = act[:, own_at]
    theirs = actb[1]
    for s in (0, 1):
        rows = jnp.where(t == s, mine, theirs)
        x_act[2 * n_z * s:2 * n_z * (s + 1), :] = rows
        for j in range(n_all - n_in):
            pm[s, :, j * cols:(j + 1) * cols] = dot(rows.astype(BF16), full_in[n_in + j].astype(BF16), NN)
    x_copy = misc.start(1 + n_z, pm.at[1 - x], rx, xp)
    send_share(0)
    send_share(2)
    start_zero(0)
    start_zero(1)
    x_copy.wait_recv()
    pm[2] = pm[x] + rx[...]
    y_copy = misc.start(2 + n_z, pm.at[2], ry, yp)
    tick()
    y_copy.wait_recv()
    pm[3] = pm[2] + ry[...]
    c_copy = misc.start(3 + n_z, pm.at[3], rc, core)
    tick()
    c_copy.wait_recv()
    bias = cat([vec[j:j + 1, :] for j in range(6)], 1)
    mz[z] = pm[3] + rc[...] + bias
    mod_copies = [misc.start(4 + n_z + d, mz.at[z], mz.at[z], target) for d, target in enumerate(zs)]
    tick()
    for copy in mod_copies + vec_copies:
        copy.wait_recv()
    vec_local.wait()
    seq_row = pl.ds(n_z * y + z, 1)
    x_mod[6:8, :] = jnp.zeros((2, n_z * cols), F32)
    for j in range(6):
        x_mod[j:j + 1, :] = cat([mz[zi, seq_row, j * cols:(j + 1) * cols] for zi in range(n_z)], 1)
    x_mod[...] = reorder(x_mod[...], n_hi)
    x_vec[...] = vz[...]
    tick()

    def wide(k):
        return cat([vz[zi, k:k + 1, :] for zi in range(n_z)], 1)

    def narrow(k):
        return cat([vz[zi, k:k + 1, lanes_at(t)] for zi in range(n_z)], 1)

    got_share(0)
    got_share(2)
    half = 2 * PIECE
    full = 2 * half
    mine_ids = idb.at[pl.ds(2 * t, 2)]
    id_copy = misc.start(3 + 2 * n_z, mine_ids, mine_ids, core)
    flush(tokb, x_tok)

    def first_norm(rows, at, p):
        normed, unused = normalize(tokb[p, rows, :].astype(F32))
        h1[t, at, :] = (normed * (1.0 + x_mod[1:2, :]) + x_mod[2:3, :]).astype(BF16)
    step_rows(piece, first_norm)
    h1_copy = misc.start(4 + 2 * n_z, h1.at[t], h1.at[t], core)

    pump(2)
    id_copy.wait_recv()
    lanes = lane_of((full, LANES)) % HD
    scale = idb[...].reshape(full, LANES).astype(F32)
    feature = lanes.astype(F32)
    ma[...] = jnp.where((lanes < 16) & (feature > scale), 1.0, 0.0).astype(BF16)
    mb[...] = jnp.where((lanes < 16) & (feature == scale), NEG, 0.0).astype(BF16)
    flush(ma, x_ma)
    flush(mb, x_mb)
    pump(2)
    send_share(1)
    h1_copy.wait_recv()

    def whole(ref):
        return ref[...].reshape(full, ref.shape[-1])

    def w_in(m):
        return g_in[m].reshape(8 * LANES, n_z * LANES)

    arrived(0)
    qr[...] = dot(whole(h1), w_in(0), NN) + narrow(6)
    q8[...] = (qr[...] * lax.rsqrt(head_mean(qr[...] * qr[...]) + NORM_EPS) * narrow(8)).astype(BF16) * 0.125
    arrived(1)
    kr[...] = dot(whole(h1), w_in(1), NN)
    kh[...] = (kr[...] * lax.rsqrt(head_mean(kr[...] * kr[...]) + NORM_EPS) * narrow(9)).astype(BF16)
    flush(qr, x_qr)
    flush(kr, x_kr)
    flush(q8, x_q8)
    flush(kh, x_kh)
    pump(1)
    arrived(2)
    vv[...] = (dot(whole(h1), w_in(2), NN) + narrow(7)).astype(BF16)
    flush(vv, x_v)
    flush(h1, x_h1)
    flush(g_in.at[pl.ds(0, 3)], x_wq)
    got_share(1)
    flush(cotb, x_cot)

    def gate(rows, at, p):
        gf[t, at, :] = (cotb[p, rows, :].astype(F32) * x_mod[3:4, :]).astype(BF16)
    step_rows(piece, gate)
    gf_copy = misc.start(5 + 2 * n_z, gf.at[t], gf.at[t], core)

    def attend(i, carry):
        at = lanes_at(i)
        q2, k2, v2 = q8[:, at], kh[:, at], vv[:, at]
        mine_a, mine_b = ma[...], mb[...]
        low = lane_of((full, LANES)) < HD
        outs, tops = [], []
        for h in (0, 1):
            here = low if h == 0 else jnp.logical_not(low)
            s = dot(jnp.where(here, q2, mine_a), jnp.where(here, k2, mine_b), NT)
            top = jnp.max(s, axis=1, keepdims=True)
            e = jnp.exp(s - top).astype(BF16)
            got = dot(e, jnp.where(here, v2, jnp.ones_like(v2)), NN)
            total = got[:, HD:HD + 1] if h == 0 else got[:, 0:1]
            outs.append(got / total)
            tops.append(top + jnp.log(total))
        oo[:, at] = jnp.where(low, outs[0], outs[1]).astype(BF16)
        lse[:, at] = jnp.where(low, tops[0], tops[1])
        return carry

    pairs = n_z * LANES // LANES
    for i in range(0, pairs, 2):
        lax.fori_loop(i, i + 2, attend, 0)
        pump(1)
    flush(oo, x_o)
    flush(lse, x_lse)

    arrived(3)
    flush(g_out.at[0], x_wo)
    width = 8 * LANES
    hw = width // 2
    for j in (0, 1):
        both = dot(oo[...], g_out[0, j], NN)
        attn[:, j * hw:(j + 1) * hw] = jnp.where(t == 0, both[:half], both[half:])
        at_send[:, j * hw:(j + 1) * hw] = jnp.where(t == 0, both[half:], both[:half]).astype(BF16)
    at_copy = misc.start(6 + 2 * n_z, at_send, at_recv, core)
    at_copy.wait_recv()
    proj_bias = reorder(wide(10 + n_ff), n_hi)


    def second_norm(rows, at, p):
        total = attn[at, :] + at_recv[at, :].astype(F32) + proj_bias
        attn[at, :] = total
        middle = tokb[p, rows, :].astype(F32) + x_mod[0:1, :] * total
        mid[at, :] = middle
        normed, unused = normalize(middle)
        h2[t, at, :] = (normed * (1.0 + x_mod[4:5, :]) + x_mod[5:6, :]).astype(BF16)
    step_rows(piece, second_norm)
    h2_copy = misc.start(7 + 2 * n_z, h2.at[t], h2.at[t], core)
    flush(attn, x_attn)
    flush(mid, x_mid)
    gf_copy.wait_recv()
    pump(1)
    x_gf[...] = jnp.zeros_like(x_gf)
    x_gf[0:1, :] = jnp.sum(whole(gf).astype(F32), axis=0, keepdims=True)
    x_gu[...] = jnp.zeros_like(x_gu)
    h2_copy.wait_recv()

    for r in range(n_ff):
        arrived(4 + 2 * r)
        bias_row = narrow(10 + r)
        u = dot(whole(h2), w_in(3 + r), NN) + bias_row
        value, gradient = gelu_both(u)
        act_low[...] = value.astype(BF16)
        slope[...] = gradient
        pump(1)
        arrived(5 + 2 * r)
        for j in (0, 1):
            part = dot(act_low[...], g_out[1 + r, j], NN)
            cols_here = pl.ds(j * hw, hw)
            facc[:, cols_here] = part if r == 0 else facc[:, cols_here] + part
        for j in (0, 1):
            gout[r, j] = dot(act_low[...], gf[:, :, j * hw:(j + 1) * hw].reshape(full, hw), TN).astype(BF16)
        flush(gout.at[r], x_gout.at[r])
        back_act = (dot(gf[:, :, :hw].reshape(full, hw), g_out[1 + r, 0], NT)
                    + dot(gf[:, :, hw:].reshape(full, hw), g_out[1 + r, 1], NT))
        gu = (back_act * slope[...]).astype(BF16)
        act_low[...] = gu
        pump(1)
        x_gu[r:r + 1, :] = jnp.sum(gu.astype(F32), axis=0, keepdims=True)
        gin[r] = dot(whole(h2), act_low[...], TN).astype(BF16).reshape(gin.shape[1:])
        flush(gin.at[r], x_gin.at[r])
        part = dot(act_low[...], w_in(3 + r), NT)
        dacc[...] = part if r == 0 else dacc[...] + part

    mine_rows = pl.ds(pl.multiple_of(t * half, half), half)
    other_rows = pl.ds(pl.multiple_of((1 - t) * half, half), half)
    fsend[...] = facc[other_rows, :].astype(BF16)
    dsend[...] = dacc[other_rows, :].astype(BF16)
    flush(facc.at[mine_rows], x_fown)
    flush(fsend, x_fsend)
    flush(dacc.at[mine_rows], x_down)
    flush(dsend, x_dsend)
    for copy in flushed:
        copy.wait()
    for j, (src, dst) in enumerate(shares):
        for yd in (0, 1):
            @pl.when(jnp.logical_not(loops & (y == yd)))
            def _():
                ref = src.at[yd]
                pltpu.make_async_remote_copy(
                    src_ref=ref, dst_ref=ref, send_sem=tok_sem.at[0, j, yd], recv_sem=tok_sem.at[1, j, x],
                    device_id=(f_base + y, 2 * yd + t, z), device_id_type=MESH).wait_send()
    ag.finish()
    misc.finish()


def forward(x_in, x_out, tok, cot, ids, act, vec, n_z, n_hi):
    n_out = x_out.shape[0]
    n_ff = n_out - 1
    n_in = 3 + n_ff
    pieces = n_in + n_out
    here, width = n_z * LANES, 8 * LANES
    half, full = 2 * PIECE, 4 * PIECE
    piece = tok.shape[1]
    hw = width // 2
    S = jax.ShapeDtypeStruct
    wide_low, wide_full = S((half, width), BF16), S((half, width), F32)
    cols_low, cols_full = S((full, here), BF16), S((full, here), F32)
    mask = S((full, LANES), BF16)
    big = [
        S((3, 2, 4, LANES, here), BF16), S((2, here, hw), BF16), S((2, half, width), BF16), cols_full, cols_full,
        cols_low, cols_low, cols_low, cols_low, cols_full, mask, mask, S((2, piece, width), BF16),
        S((2, piece, width), BF16), wide_full, wide_full, wide_full, wide_low, wide_full, wide_low,
        S((n_ff, 2, 4, LANES, here), BF16), S((n_ff, 2, here, hw), BF16)]
    small = [S((8, width), F32), S((8, here), F32), S((8, width), F32), S((n_z,) + vec.shape, F32), S((4 * n_z, LANES), F32)]
    any_space, vmem = pl.BlockSpec(memory_space=pl.ANY), pl.BlockSpec(memory_space=pltpu.VMEM)
    mod_shape = (8, (x_in.shape[0] - n_in) * vec.shape[1])
    V = pltpu.VMEM
    dma = pltpu.SemaphoreType.DMA
    return pl.pallas_call(
        functools.partial(forward_kernel, n_z, n_ff, n_hi),
        out_shape=tuple(big + small),
        in_specs=[any_space] * 5 + [vmem] * 2,
        out_specs=tuple([any_space] * len(big) + [vmem] * len(small)),
        scratch_shapes=[
            V((n_in, 2, 4, LANES, here), BF16), V((n_out, 2, here, hw), BF16),
            V((2, piece, width), BF16), V((2, piece, width), BF16), V((4, PIECE, LANES), BF16),
            V((2, 8, LANES), F32), V((4,) + mod_shape, F32), V(mod_shape, F32), V(mod_shape, F32), V(mod_shape, F32),
            V((n_z,) + mod_shape, F32), V((n_z,) + vec.shape, F32),
            V((2, half, width), BF16), V((2, half, width), BF16), V((2, half, width), BF16),
            V((full, here), F32), V((full, here), F32), V((full, here), BF16), V((full, here), BF16), V((full, here), BF16),
            V((full, here), BF16), V((full, here), F32), V((full, LANES), BF16), V((full, LANES), BF16),
            V((half, width), BF16), V((half, width), BF16), V((half, width), F32), V((half, width), F32),
            V((full, width), F32), V((full, width), F32), V((half, width), BF16), V((half, width), BF16),
            V((n_ff, 2, 4, LANES, here), BF16), V((n_ff, 2, here, hw), BF16), V((full, here), BF16), V((full, here), F32),
            V(x_in.shape, F32), V(x_out.shape, F32), V((n_in, 2, LANES, LANES), BF16), V((n_out, 2, LANES, LANES), BF16),
            dma((pieces + 1,)), dma((pieces, n_z + 3)), dma((pieces, n_z + 3)), dma((8 + 2 * n_z,)), dma((8 + 2 * n_z,)),
            dma((len(big) + 2 * n_ff,)), dma((2, 3, 2)), dma((x_in.shape[0] + n_out,)),
        ],
        compiler_params=pltpu.CompilerParams(collective_id=0, has_side_effects=True, vmem_limit_bytes=VMEM_BYTES),
    )(x_in, x_out, tok, cot, ids, act, vec)

class Guarded:
    def __init__(self):
        self.sent = []

    def start(self, cond, copy):
        @pl.when(cond)
        def _():
            copy.start()
        self.sent.append((cond, copy))

    def finish(self):
        for cond, copy in self.sent:
            @pl.when(cond)
            def _(copy=copy):
                copy.wait_send()


def backward_kernel(n_z, n_ff, n_hi, *refs):
    n_in, n_out = 3 + n_ff, 1 + n_ff
    (x_wq, x_wo, x_h1, x_qr, x_kr, x_q8, x_kh, x_v, x_o, x_lse, x_ma, x_mb, x_tok, x_cot, x_attn, x_mid,
     x_fown, x_fsend, x_down, x_dsend, x_gin, x_gout, x_weight, mod, gu_sum, gf_sum, vz, act,
     o_mixed, o_grad, o_in, o_out, o_dmod, o_vec, o_ada, o_cond, o_norm,
     wq, wo, h1, qr, kr, q8, kh, vv, oo, lse, ma, mb, tokb, cotb, attn, mid, buf, f_recv, d_recv,
     dmid, ga, go, mixed, sums, vd, vdr, vs, vdz, zv, v_all, norm, norm_plane, norm_line, cond_z, cond_all,
     p_full, q_full, p_half, q_half, a_in, a_out, b_in, b_out, z_in, z_out, f_in, f_out,
     load_sem, own_sem, rs_send, rs_recv, m_send, m_recv, t_send, t_recv, g_send, g_recv) = refs
    f, c, z, t, x, y = place()
    core, xp, yp, zs = partners(n_z)
    f_base = f - t
    last = n_z - 1
    half, full = 2 * PIECE, 4 * PIECE
    width = mod.shape[1]
    hw = width // 2
    piece = x_tok.shape[1]
    clear_tail(ga, t)

    barrier = pltpu.get_barrier_semaphore()
    diagonal = (f, 3 - c, z)
    plane = [xp, yp, diagonal]
    other_line = [(f + 1 - 2 * t, c, target[2]) for target in zs]
    for target in [core] + plane + zs + other_line:
        pl.semaphore_signal(barrier, inc=1, device_id=target, device_id_type=MESH)
    loops = (y == t) & (x == t)
    for ys in (0, 1):
        @pl.when(jnp.logical_not(loops & (y == ys)))
        def _():
            pl.semaphore_signal(barrier, inc=1, device_id=(f_base + y, 2 * ys + t, z), device_id_type=MESH)

    loads = {}
    names = [("d", x_down, buf.at[1]), ("mid", x_mid, mid), ("cot", x_cot, cotb), ("attn", x_attn, attn),
             ("f", x_fown, buf.at[0]), ("wo", x_wo, wo), ("o", x_o, oo), ("q", x_q8, q8), ("k", x_kh, kh), ("v", x_v, vv),
             ("lse", x_lse, lse), ("ma", x_ma, ma), ("mb", x_mb, mb), ("qr", x_qr, qr), ("kr", x_kr, kr),
             ("h1", x_h1, h1), ("wq", x_wq, wq), ("tok", x_tok, tokb)]
    for i, (name, src, dst) in enumerate(names):
        loads[name] = pltpu.make_async_copy(src, dst, load_sem.at[i])
        loads[name].start()
    pl.semaphore_wait(barrier, 4 + 2 * n_z - jnp.where(loops, 1, 0))

    rs = Wire(rs_send, rs_recv)
    misc = Wire(m_send, m_recv)
    chain = Guarded()
    d_copy = misc.start(1, x_dsend, d_recv, core)
    f_copy = misc.start(0, x_fsend, f_recv, core)

    order = []
    for r in range(n_ff):
        order += [("i", 3 + r), ("o", 1 + r)]
    order += [("o", 0), ("i", 2), ("i", 1), ("i", 0)]
    pieces = len(order)
    one, two, four, own_half = {}, {}, {}, {}

    def y_first(p):
        return p % 2 == 0

    def parts(p, mine):
        if y_first(p):
            yy = y if mine else 1 - y
            return [2 * yy, 2 * yy + 1]
        xx = x if mine else 1 - x
        return [xx, 2 + xx]

    def source(p, at):
        kind, m = order[p]
        if kind == "i":
            return x_gin.at[m - 3, :, at] if m >= 3 else p_full.at[m, :, at]
        return x_gout.at[m - 1, :, :, lanes_at(at)] if m >= 1 else q_full.at[:, :, lanes_at(at)]

    def kept(p, k):
        kind, m = order[p]
        return p_half.at[m, k] if kind == "i" else q_half.at[m, k]

    def bufs(p, inner, outer):
        kind, m = order[p]
        return inner.at[m] if kind == "i" else outer.at[m]

    def step_one(p):
        one[p] = [rs.start((p, k), source(p, at), bufs(p, a_in, a_out).at[k], yp if y_first(p) else xp)
                  for k, at in enumerate(parts(p, False))]
        own_half[p] = []
        for k, at in enumerate(parts(p, True)):
            copy = pltpu.make_async_copy(source(p, at), kept(p, k), own_sem.at[p, k])
            copy.start()
            own_half[p].append(copy)

    def step_two(p):
        for copy in one[p]:
            copy.wait_recv()
        for copy in own_half[p]:
            copy.wait()
        for k in (0, 1):
            ref = kept(p, k)
            ref[...] = (ref[...].astype(F32) + bufs(p, a_in, a_out)[k].astype(F32)).astype(BF16)
        go_bit = (1 - x) if y_first(p) else (1 - y)
        two[p] = rs.start((p, 2), kept(p, go_bit), bufs(p, b_in, b_out), xp if y_first(p) else yp)

    def span(p, ref, lo, hi):
        if order[p][0] == "i":
            return ref.at[:, :, lo * LANES:hi * LANES]
        return ref.at[:, lo * LANES:hi * LANES, :]

    def right_copy(p, s):
        here = kept(p, x if y_first(p) else y)
        return pltpu.make_async_remote_copy(
            src_ref=span(p, here, s + 1, n_z), dst_ref=span(p, bufs(p, z_in, z_out), s + 2, n_z + 1),
            send_sem=rs_send.at[p, 3], recv_sem=rs_recv.at[p, 3], device_id=(f, c, z + 1), device_id_type=MESH)

    def left_copy(p, s):
        here = kept(p, x if y_first(p) else y)
        return pltpu.make_async_remote_copy(
            src_ref=span(p, here, 0, s), dst_ref=span(p, bufs(p, z_in, z_out), 0, s),
            send_sem=rs_send.at[p, 4], recv_sem=rs_recv.at[p, 4], device_id=(f, c, z - 1), device_id_type=MESH)

    def add_into(p, lo, hi, shift):
        here = kept(p, x if y_first(p) else y)
        a, b = span(p, here, lo, hi), span(p, bufs(p, z_in, z_out), lo + shift, hi + shift)
        a[...] = (a[...].astype(F32) + b[...].astype(F32)).astype(BF16)

    def step_z(p, s):
        if s == 0:
            two[p].wait_recv()
            here = kept(p, x if y_first(p) else y)
            here[...] = (here[...].astype(F32) + bufs(p, b_in, b_out)[...].astype(F32)).astype(BF16)

        @pl.when(z == s)
        def _():
            if s > 0:
                landed = span(p, bufs(p, z_in, z_out), s + 1, n_z + 1)
                pltpu.make_async_copy(landed, landed, rs_recv.at[p, 3]).wait()
            if s < last:
                if s > 0:
                    add_into(p, s + 1, n_z, 1)
                right_copy(p, s).start()

        @pl.when(z == last - s)
        def _():
            e = last - s
            if s > 0:
                landed = span(p, bufs(p, z_in, z_out), 0, e + 1)
                pltpu.make_async_copy(landed, landed, rs_recv.at[p, 4]).wait()
            if e > 0:
                if s > 0:
                    add_into(p, 0, e, 0)
                left_copy(p, e).start()

    norm[...] = jnp.zeros_like(norm)

    def add_squares(values):
        square = values * values
        parts = [square[8 * i:8 * i + 8] for i in range(square.shape[0] // 8)]
        while len(parts) > 1:
            parts = [a + b for a, b in zip(parts[::2], parts[1::2])]
        for k in range(square.shape[1] // LANES):
            norm[...] = norm[...] + parts[0][:, k * LANES:(k + 1) * LANES]

    def step_core(p):
        kind, m = order[p]
        here = kept(p, x if y_first(p) else y)
        total, result = (f_in, o_in) if kind == "i" else (f_out, o_out)
        for s in range(n_z):
            @pl.when(z == s)
            def _():
                value = span(p, here, s, s + 1)[...].astype(F32)
                if s > 0:
                    value = value + span(p, bufs(p, z_in, z_out), s + 1, s + 2)[...].astype(F32)
                if s < last:
                    value = value + span(p, bufs(p, z_in, z_out), s, s + 1)[...].astype(F32)
                total[m] = value
        result[m, t] = total[m, t]
        add_squares(total[m, 0])
        add_squares(total[m, 1])
        four[p] = rs.start((p, 5), total.at[m, 1 - t], result.at[m, t], core)

    def in_range(p):
        return 0 <= p < pieces

    ready = [2 * n_ff]
    started = [0]
    step = [0]

    def first_sends(upto):
        while started[0] < min(upto, ready[0], pieces):
            step_one(started[0])
            started[0] += 1

    passes, chores = [], []

    def pump(n=1):
        for _ in range(n):
            k = step[0]
            first_sends(k + 3)
            if in_range(k) and k >= started[0]:
                return
            if in_range(k):
                step_two(k)
            for unused in range(PASSES):
                if passes:
                    pass_along(*passes.pop(0))
            for s in range(n_z):
                if in_range(k - 1 - s):
                    step_z(k - 1 - s, s)
            if in_range(k - n_z - 1):
                step_core(k - n_z - 1)
            if chores:
                chore = chores.pop(0)
                if chore is not None:
                    chore()
            step[0] += 1

    first_sends(3)

    def share_out(j, src, dst):
        for xs in (0, 1):
            own = loops & (x == xs)
            there = dst.at[2 * z + y]
            local = pltpu.make_async_copy(src.at[xs], there, t_recv.at[j, y])

            @pl.when(own)
            def _():
                local.start()
            chain.start(jnp.logical_not(own), pltpu.make_async_remote_copy(
                src_ref=src.at[xs], dst_ref=there, send_sem=t_send.at[j, xs], recv_sem=t_recv.at[j, y],
                device_id=(f_base + x, 2 * t + xs, z), device_id_type=MESH))

    def pass_along(j, dst, s, part):
        lanes = pl.ds(part * (width // PARTS), width // PARTS)
        if s == 0 and part == 0:
            for ys in (0, 1):
                pltpu.make_async_copy(dst.at[2 * z + ys], dst.at[2 * z + ys], t_recv.at[j, ys]).wait()
        for side, (there, back_at) in enumerate(((z + 1, z - s), (z - 1, z + s))):
            valid = (back_at >= 0) & (back_at <= last)
            block = dst.at[pl.ds(2 * lax.clamp(0, back_at, last), 2), :, lanes]
            if s > 0:
                @pl.when(valid)
                def _():
                    pltpu.make_async_copy(block, block, g_recv.at[j, side, s, part]).wait()
            if s < last:
                chain.start(valid & (there >= 0) & (there <= last), pltpu.make_async_remote_copy(
                    src_ref=block, dst_ref=block, send_sem=g_send.at[j, side, s, part],
                    recv_sem=g_recv.at[j, side, s + 1, part],
                    device_id=(f, c, lax.clamp(0, there, last)), device_id_type=MESH))

    def pass_all(j, dst):
        passes.extend((j, dst, s, part) for s in range(n_z) for part in range(PARTS))

    def wide(k):
        return cat([vz[zi, k:k + 1, :] for zi in range(n_z)], 1)

    def narrow(k):
        return cat([vz[zi, k:k + 1, lanes_at(t)] for zi in range(n_z)], 1)

    def tally(j, values):
        if values.shape[0] == 16:
            sums[j] = sums[j] + values[:8] + values[8:]
        else:
            sums[j, 0:1] = sums[j, 0:1] + jnp.sum(values, axis=0, keepdims=True)

    sums[...] = jnp.zeros_like(sums)
    for name in ("d", "mid", "cot", "attn"):
        loads[name].wait()
    d_copy.wait_recv()

    def second_norm(rows, at, p):
        grad = buf[1, at, :] + d_recv[at, :].astype(F32)
        normed, scale = normalize(mid[at, :])
        tally(4, grad * normed)
        tally(5, grad)
        w = grad * (1.0 + mod[4:5, :])
        pulled = scale * (w - jnp.mean(w, axis=-1, keepdims=True) - normed * jnp.mean(w * normed, axis=-1, keepdims=True))
        total = cotb[p, rows, :].astype(F32) + pulled
        dmid[at, :] = total
        tally(0, total * attn[at, :])
        low = (total * mod[0:1, :]).astype(BF16)
        ga[t, at, :] = low
        tally(6, low.astype(F32))
    step_rows(piece, second_norm)
    ga_copy = misc.start(2, ga.at[t], ga.at[t], core)

    ffn_bias = reorder(wide(11 + n_ff), n_hi)
    loads["f"].wait()
    f_copy.wait_recv()

    def mix(rows, at, p):
        out = buf[0, at, :] + f_recv[at, :].astype(F32) + ffn_bias
        tally(3, cotb[p, rows, :].astype(F32) * out)
        mixed[p, rows, :] = (mid[at, :] + mod[3:4, :] * out).astype(BF16)
    step_rows(piece, mix)
    share_out(0, mixed, o_mixed)
    loads["wo"].wait()
    loads["o"].wait()
    ga_copy.wait_recv()
    pump(1)
    for j in (0, 1):
        ga_j = ga[:, :, j * hw:(j + 1) * hw].reshape(full, hw)
        part = dot(ga_j, wo[j], NT)
        if j == 0:
            first_part = part
        q_full[j] = dot(oo[...], ga_j, TN).astype(BF16)
    go[...] = (first_part + part).astype(BF16)
    ready[0] += 1
    for name in ("q", "k", "v", "lse", "ma", "mb", "qr", "kr"):
        loads[name].wait()
    pump(1)
    pass_all(0, o_mixed)

    vs[...] = jnp.zeros_like(vs)

    def head_back(raw, grad, gain):
        scale = lax.rsqrt(head_mean(raw * raw) + NORM_EPS)
        normed = raw * scale
        gain_grad = jnp.sum(grad * normed, axis=0, keepdims=True)
        w = grad * gain
        return (scale * (w - normed * head_mean(w * normed))).astype(BF16), gain_grad

    def attend_back(i, carry):
        at = lanes_at(i)
        q2, k2, v2, g2, o2 = q8[:, at], kh[:, at], vv[:, at], go[:, at], oo[:, at]
        mine_a, mine_b = ma[...], mb[...]
        lanes = lane_of((full, LANES))
        low, l64 = lanes < HD, lanes % HD
        product = o2.astype(F32) * g2.astype(F32)
        dqs, dks, dvs = [], [], []
        one_like, zero_like = jnp.ones_like(v2), jnp.zeros_like(v2)
        for h in (0, 1):
            here = low if h == 0 else jnp.logical_not(low)
            l1, l2, l3 = split_three(lse[:, at][:, HD * h:HD * h + 1])
            qa = jnp.where(l64 == 40, -l1, jnp.where(l64 == 41, -l2, jnp.where(l64 == 42, -l3, mine_a)))
            ka = jnp.where((l64 >= 40) & (l64 < 43), one_like, mine_b)
            weight = jnp.exp(dot(jnp.where(here, k2, ka), jnp.where(here, q2, qa), NT))
            d1, d2, d3 = split_three(jnp.sum(jnp.where(here, product, 0.0), axis=1, keepdims=True))
            da = jnp.where(l64 == 0, -d1, jnp.where(l64 == 1, -d2, jnp.where(l64 == 2, -d3, zero_like)))
            va = jnp.where(l64 < 3, one_like, zero_like)
            ds = (weight * dot(jnp.where(here, v2, va), jnp.where(here, g2, da), NT)).astype(BF16)
            dvs.append(dot(weight.astype(BF16), g2, NN))
            dks.append(dot(ds, q2, NN))
            dqs.append(dot(ds, k2, TN))
        dq = jnp.where(low, dqs[0], dqs[1]) * 0.125
        dk = jnp.where(low, dks[0], dks[1])
        gq, q_gain = head_back(qr[:, at], dq, vs[8:9, at])
        gk, k_gain = head_back(kr[:, at], dk, vs[9:10, at])
        gv = jnp.where(low, dvs[0], dvs[1]).astype(BF16)
        q8[:, at] = gq
        kh[:, at] = gk
        vv[:, at] = gv
        vs[0:1, at] = jnp.sum(gq.astype(F32), axis=0, keepdims=True)
        vs[1:2, at] = jnp.sum(gv.astype(F32), axis=0, keepdims=True)
        vs[2:3, at] = q_gain
        vs[3:4, at] = k_gain
        return carry

    vs[8:9, :] = narrow(8)
    vs[9:10, :] = narrow(9)
    pairs = n_z
    for i in range(0, pairs, 2):
        lax.fori_loop(i, i + 2, attend_back, 0)
        pump(1)
    loads["h1"].wait()
    h1_all = h1[...].reshape(full, width)
    for m, ref in ((2, vv), (1, kh), (0, q8)):
        p_full[m] = dot(h1_all, ref[...], TN).astype(BF16).reshape(p_full.shape[1:])
        ready[0] += 1
    pump(1)

    ada_refs, ada_loads = [], []
    for j in range(6):
        rows_at, cols_at = (j // 2) * LANES, (j % 2) * (n_z * LANES // 2)
        ada_refs.append(qr.at[rows_at:rows_at + LANES, cols_at:cols_at + n_z * LANES // 2])
        ada_loads.append(pltpu.make_async_copy(x_weight.at[3 + n_ff + j], ada_refs[j], load_sem.at[len(names) + j]))
        ada_loads[j].start()
    loads["wq"].wait()
    part = dot(q8[...], wq[0].reshape(width, n_z * LANES), NT)
    part = part + dot(kh[...], wq[1].reshape(width, n_z * LANES), NT)
    part = part + dot(vv[...], wq[2].reshape(width, n_z * LANES), NT)
    buf[0] = jnp.where(t == 0, part[:half], part[half:])
    f_recv[...] = jnp.where(t == 0, part[half:], part[:half]).astype(BF16)
    h_copy = misc.start(3, f_recv, d_recv, core)
    loads["tok"].wait()
    h_copy.wait_recv()

    def first_norm(rows, at, p):
        grad = buf[0, at, :] + d_recv[at, :].astype(F32)
        normed, scale = normalize(tokb[p, rows, :].astype(F32))
        tally(1, grad * normed)
        tally(2, grad)
        w = grad * (1.0 + mod[1:2, :])
        pulled = scale * (w - jnp.mean(w, axis=-1, keepdims=True) - normed * jnp.mean(w * normed, axis=-1, keepdims=True))
        cotb[p, rows, :] = (dmid[at, :] + pulled).astype(BF16)
    step_rows(piece, first_norm)
    share_out(1, cotb, o_grad)
    pass_all(1, o_grad)
    pump(1)

    for j in range(7):
        vd[j:j + 1, :] = jnp.sum(sums[j], axis=0, keepdims=True)
    vd[7:8, :] = gf_sum[0:1, :] * 0.5
    v_copy = misc.start(4, vd, vdr, core)
    vs[4:8, :] = gu_sum[0:4, :]
    cols = width // n_z
    n_ada = 6
    chips = 4 * n_z
    waits = {}

    def exact(a, b, dims):
        return lax.dot_general(a, b, (dims, ((), ())), precision=PRECISE, preferred_element_type=F32)

    def arrive(name):
        for copy in waits.pop(name):
            copy.wait_recv()

    def mods(j):
        return o_dmod[...].reshape(chips, 8, cols)[:, j, :]

    def along_line():
        v_copy.wait_recv()
        vd_all = reorder(vd[...] + vdr[...], n_hi, inverse=True)
        for zi in range(n_z):
            vdz[zi] = vd_all[:, zi * cols:(zi + 1) * cols]
        o_dmod[x, y, z] = vdz[z]
        zv[z] = vs[0:8, lanes_at(z)]
        waits["line"] = []
        for d, target in enumerate(zs):
            zi = lax.rem(z + 1 + d, n_z)
            waits["line"].append(misc.start(5 + d, vdz.at[zi], o_dmod.at[x, y, z], target))
            waits["line"].append(misc.start(4 + n_z + d, vs.at[pl.ds(0, 8), lanes_at(zi)], zv.at[z], target))

    slot = 3 + 2 * n_z

    def over_plane():
        arrive("line")
        total = zv[0]
        for zi in range(1, n_z):
            total = total + zv[zi]
        v_all[x, y] = total
        waits["plane"] = []
        for d, target in enumerate(plane):
            waits["plane"].append(misc.start(slot + d, o_dmod.at[x, y], o_dmod.at[x, y], target))
            waits["plane"].append(misc.start(slot + 3 + d, v_all.at[x, y], v_all.at[x, y], target))

    def products():
        arrive("plane")
        o_vec[t] = (v_all[0, 0] + v_all[0, 1]) + (v_all[1, 0] + v_all[1, 1])
        waits["vec"] = [misc.start(slot + 6, o_vec.at[t], o_vec.at[t], core)]
        for copy in ada_loads:
            copy.wait()
        total = 0.0
        for j, ref in enumerate(ada_refs):
            total = total + exact(mods(j), ref[...].astype(BF16).astype(F32), NT)
        cond_z[z] = total
        waits["cond line"] = [misc.start(slot + 7 + d, cond_z.at[z], cond_z.at[z], target) for d, target in enumerate(zs)]
        for j in range(n_ada):
            o_ada[j] = exact(act[...], mods(j), TN)
            if n_hi == 1:
                add_squares(o_ada[j])

    def cond_plane():
        arrive("cond line")
        total = cond_z[0]
        for zi in range(1, n_z):
            total = total + cond_z[zi]
        cond_all[t, c] = total
        at = slot + 6 + n_z
        waits["cond plane"] = [misc.start(at + d, cond_all.at[t, c], cond_all.at[t, c], target)
                               for d, target in enumerate(plane)]

    def cond_core():
        arrive("cond plane")
        waits["cond core"] = [misc.start(slot + 9 + n_z, cond_all.at[t], cond_all.at[t], core)]

    chores.extend([along_line, None, over_plane, None, products, None, cond_plane, None, cond_core])

    while step[0] < pieces + n_z + 1 or chores:
        pump(1)
    while passes:
        pass_along(*passes.pop(0))
    arrive("cond core")
    mine = pl.ds(pl.multiple_of(2 * n_z * t, 2 * n_z), 2 * n_z)
    o_cond[...] = cat([cond_all[ti, ck, mine, :] for ti in (0, 1) for ck in range(4)], 1)

    arrive("vec")
    if n_hi == 1:
        vec_squares = o_vec[0] * o_vec[0] + o_vec[1] * o_vec[1]
        first_row = lax.broadcasted_iota(jnp.int32, (8, LANES), 0) == 0
        for j in range(8):
            row = jnp.sum(mods(j), axis=0, keepdims=True)
            for k in range(cols // LANES):
                part = row[:, k * LANES:(k + 1) * LANES]
                vec_squares = vec_squares + jnp.where(first_row, part * part, 0.0)
        slot = slot + 10 + n_z
        norm_plane[c] = norm[...] + jnp.where((f == 0) & (c == 0), vec_squares, 0.0)
        copies = [misc.start(slot + d, norm_plane.at[c], norm_plane.at[c], target) for d, target in enumerate(plane)]
        for copy in copies:
            copy.wait_recv()
        norm_line[t, z] = (norm_plane[0] + norm_plane[1]) + (norm_plane[2] + norm_plane[3])
        copies = [misc.start(slot + 3 + d, norm_line.at[t, z], norm_line.at[t, z], target)
                  for d, target in enumerate([core] + zs + other_line)]
        for copy in copies:
            copy.wait_recv()
        total = norm_line[0, 0]
        for ti in (0, 1):
            for zi in range(n_z):
                if ti + zi > 0:
                    total = total + norm_line[ti, zi]
        total = jnp.sum(jnp.sum(total, axis=0, keepdims=True), axis=1, keepdims=True)
        o_norm[...] = jnp.broadcast_to(jnp.sqrt(total), o_norm.shape)
    else:
        o_norm[...] = jnp.zeros_like(o_norm)
    for p in range(pieces):
        four[p].wait_recv()
    for p in range(pieces):
        for s in range(n_z):
            @pl.when(z == s)
            def _():
                if s < last:
                    right_copy(p, s).wait_send()
                if s > 0:
                    left_copy(p, s).wait_send()
    chain.finish()
    rs.finish()
    misc.finish()


def backward(operands, n_z, n_ff, n_hi):
    n_in, n_out = 3 + n_ff, 1 + n_ff
    here, width = n_z * LANES, 8 * LANES
    half, full = 2 * PIECE, 4 * PIECE
    hw, cols = width // 2, width // n_z
    S, V, dma = jax.ShapeDtypeStruct, pltpu.VMEM, pltpu.SemaphoreType.DMA
    any_space, vmem = pl.BlockSpec(memory_space=pl.ANY), pl.BlockSpec(memory_space=pltpu.VMEM)
    piece = operands[12].shape[1]
    rows_out = S((2 * n_z, piece, width), BF16)
    pieces = n_in + n_out
    slots = 24 + 5 * n_z
    return pl.pallas_call(
        functools.partial(backward_kernel, n_z, n_ff, n_hi),
        out_shape=(rows_out, rows_out, S((n_in, 2, LANES, LANES), F32), S((n_out, 2, LANES, LANES), F32),
                   S((2, 2, n_z, 8, cols), F32), S((2, 8, LANES), F32), S((6, LANES, cols), F32), S((2 * n_z, width), F32),
                   S((8, LANES), F32)),
        in_specs=[any_space] * (len(operands) - 5) + [vmem] * 5,
        out_specs=tuple([any_space] * 2 + [vmem] * 7),
        scratch_shapes=[
            V((3, 2, 4, LANES, here), BF16), V((2, here, hw), BF16), V((2, half, width), BF16),
            V((full, here), F32), V((full, here), F32), V((full, here), BF16), V((full, here), BF16),
            V((full, here), BF16), V((full, here), BF16), V((full, here), F32), V((full, LANES), BF16),
            V((full, LANES), BF16), V((2, piece, width), BF16), V((2, piece, width), BF16), V((half, width), F32),
            V((half, width), F32), V((2, half, width), F32), V((half, width), BF16), V((half, width), BF16),
            V((half, width), F32), V((2, half, width), BF16), V((full, here), BF16), V((2, piece, width), BF16),
            V((8, 8, width), F32), V((8, width), F32), V((8, width), F32), V((16, here), F32),
            V((n_z, 8, cols), F32), V((n_z, 8, LANES), F32), V((2, 2, 8, LANES), F32),
            V((8, LANES), F32), V((4, 8, LANES), F32), V((2, n_z, 8, LANES), F32), V((n_z, 4 * n_z, LANES), F32), V((2, 4, 4 * n_z, LANES), F32),
            V((3, 2, 4, LANES, here), BF16), V((2, here, hw), BF16),
            V((n_in, 2, 2, LANES, here), BF16), V((n_out, 2, 2, here, LANES), BF16),
            V((n_in, 2, 2, LANES, here), BF16), V((n_out, 2, 2, here, LANES), BF16),
            V((n_in, 2, LANES, here), BF16), V((n_out, 2, here, LANES), BF16),
            V((n_in, 2, LANES, here + LANES), BF16), V((n_out, 2, here + LANES, LANES), BF16),
            V((n_in, 2, LANES, LANES), F32), V((n_out, 2, LANES, LANES), F32),
            dma((24,)), dma((pieces, 2)), dma((pieces, 6)), dma((pieces, 6)), dma((slots,)), dma((slots,)),
            dma((2, 2)), dma((2, 2)), dma((2, 2, n_z, PARTS)), dma((2, 2, n_z, PARTS)),
        ],
        compiler_params=pltpu.CompilerParams(collective_id=1, has_side_effects=True, vmem_limit_bytes=VMEM_BYTES),
    )(*operands)


def update_kernel(refs_per_kind, *refs):
    (norm, g_vec, w_vec, m_vec, v_vec, g_in, g_ada, g_out, w_in, m_in, v_in, w_out, m_out, v_out, mixed, grads,
     w_vec_new, m_vec_new, v_vec_new, c_vec_new, o_bias,
     w_in_new, m_in_new, v_in_new, c_in_new, w_out_new, m_out_new, v_out_new, c_out_new, o_mixed, o_grads,
     gi, ga, go, wi, mi, vi, ci, wo, mo, vo, co, low, wide, low_out, high, load_sem, store_sem) = refs
    n_seq = mixed.shape[0]
    loads, stores = {}, []

    def load(name, src, dst):
        loads[name] = pltpu.make_async_copy(src, dst, load_sem.at[len(loads)])
        loads[name].start()

    def store(src, dst):
        copy = pltpu.make_async_copy(src, dst, store_sem.at[len(stores)])
        copy.start()
        stores.append(copy)

    load("grads", grads, low.at[1])
    load("mixed", mixed, low.at[0])
    for name, src, dst in (("gi", g_in, gi), ("ga", g_ada, ga), ("wi", w_in, wi), ("mi", m_in, mi), ("vi", v_in, vi),
                           ("go", g_out, go), ("wo", w_out, wo), ("mo", m_out, mo), ("vo", v_out, vo)):
        load(name, src, dst)
    n_all, n_rows, cols = w_in.shape
    n_out = w_out.shape[0]
    factor = (CLIP_NORM / jnp.maximum(norm[0:1, 0:1], CLIP_NORM))
    factor_in = jnp.broadcast_to(factor, (1, cols))
    factor_out = jnp.broadcast_to(factor, (1, w_out.shape[2]))
    loads["grads"].wait()
    for i in range(n_seq):
        high[:, i, :] = low[1, i].astype(F32)
    store(high, o_grads)
    w_vec_new[...], m_vec_new[...], v_vec_new[...], c_vec_new[...] = adam_update(
        w_vec[...], m_vec[...], v_vec[...], g_vec[...], factor_in, RATE_VECTOR, 0.0)
    last = g_vec.shape[0]
    o_bias[...] = g_vec[last - 1:last] * factor_in
    for name in ("gi", "ga", "wi", "mi", "vi"):
        loads[name].wait()
    lead = n_all - ga.shape[0]

    def update(m, grad):
        wi[m], mi[m], vi[m], ci[m] = adam_update(wi[m], mi[m], vi[m], grad, factor_in, RATE_MATRIX, WEIGHT_DECAY)

    def lead_rows(m, carry):
        update(m, cat([gi[m, 0], gi[m, 1]], 1))
        return carry

    def ada_rows(m, carry):
        update(lead + m, ga[m])
        return carry

    for lo, hi, body, shift in ((0, lead, lead_rows, 0), (0, n_all - lead, ada_rows, lead)):
        lax.fori_loop(lo, hi, body, 0)
        at = pl.ds(shift, hi)
        for src, dst in ((wi, w_in_new), (mi, m_in_new), (vi, v_in_new), (ci, c_in_new)):
            store(src.at[at], dst.at[at])
    for name in ("go", "wo", "mo", "vo"):
        loads[name].wait()
    for m in range(n_out):
        grad = cat([go[m, 0], go[m, 1]], 0)
        wo[m], mo[m], vo[m], co[m] = adam_update(wo[m], mo[m], vo[m], grad, factor_out, RATE_MATRIX, WEIGHT_DECAY)
    for src, dst in ((wo, w_out_new), (mo, m_out_new), (vo, v_out_new), (co, c_out_new)):
        store(src, dst)
    loads["mixed"].wait()
    for i in range(n_seq):
        wide[:, i, :] = low[0, i].astype(F32)
    low_out[...] = wide[...].astype(BF16)
    store(low_out, o_mixed)
    for copy in stores:
        copy.wait()


def update(small, large, rows_low):
    S, V, dma = jax.ShapeDtypeStruct, pltpu.VMEM, pltpu.SemaphoreType.DMA
    any_space, vmem = pl.BlockSpec(memory_space=pl.ANY), pl.BlockSpec(memory_space=pltpu.VMEM)
    w_vec = small[2]
    g_in, g_ada, g_out, w_in, w_out = large[0], large[1], large[2], large[3], large[6]
    kinds = [S(a.shape, F32) for a in (w_vec, w_in, w_out)]
    news = [[k] * 3 + [S(k.shape, BF16)] for k in kinds]
    n_seq, piece, width = rows_low[0].shape
    turned = (piece, n_seq, width)
    return pl.pallas_call(
        functools.partial(update_kernel, 4),
        out_shape=tuple(news[0] + [S((1, w_vec.shape[1]), F32)] + news[1] + news[2] + [S(turned, BF16), S(turned, F32)]),
        in_specs=[vmem] * len(small) + [any_space] * (len(large) + 2),
        out_specs=tuple([vmem] * 5 + [any_space] * 10),
        scratch_shapes=[
            V(g_in.shape, F32), V(g_ada.shape, F32), V(g_out.shape, F32),
            V(w_in.shape, F32), V(w_in.shape, F32), V(w_in.shape, F32), V(w_in.shape, BF16),
            V(w_out.shape, F32), V(w_out.shape, F32), V(w_out.shape, F32), V(w_out.shape, BF16),
            V((2,) + rows_low[0].shape, BF16), V(turned, F32), V(turned, BF16), V(turned, F32), dma((11,)), dma((16,)),
        ],
        compiler_params=pltpu.CompilerParams(vmem_limit_bytes=VMEM_BYTES),
    )(*small, *large, *rows_low)


def per_device(n_f, n_c, n_z, tokens, cotangent, class_table, labels, scale_ids, in_weight, in_first, in_second,
               out_weight, out_first, out_second, vectors, vec_first, vec_second):
    n_hi = n_f // 2
    f, c, z, t, x, y = place()
    seqs, piece, width = tokens.shape
    cols = in_weight.shape[2]
    n_ff = out_weight.shape[0] - 1
    ada = 3 + n_ff
    half = cols // 2
    pairs = [[2 * i, 2 * i + 1] for i in range(n_hi)]
    his = [[i + 2 * j for j in range(n_hi)] for i in range(2)]

    def into(a):
        if n_hi == 1:
            return a
        shape = a.shape[:-1]
        return jnp.swapaxes(a.reshape(shape + (n_hi, 2 * n_c, -1)), -3, -2).reshape(a.shape)

    def back(a):
        if n_hi == 1:
            return a
        shape = a.shape[:-1]
        return jnp.swapaxes(a.reshape(shape + (2 * n_c, n_hi, -1)), -3, -2).reshape(a.shape)

    in_weight, in_first, in_second = [a.transpose(1, 0, 2) for a in (in_weight, in_first, in_second)]
    in_low, out_low = in_weight, out_weight
    if n_hi > 1:
        in_low = lax.all_gather(in_low.astype(BF16), "fsdp", axis=1, tiled=True, axis_index_groups=his).astype(F32)
        out_low = lax.all_gather(out_low.astype(BF16), "fsdp", axis=2, tiled=True, axis_index_groups=his).astype(F32)
    rows = in_low.shape[1]

    def two_seqs(a):
        return lax.dynamic_slice_in_dim(a, 2 * z, 2, 0)

    ids = jnp.pad(two_seqs(scale_ids), ((0, 0), (0, PIECE - piece)), constant_values=10).astype(BF16)
    ids = jnp.broadcast_to(ids[:, :, None], ids.shape + (LANES,))
    conditions = class_table.at[labels].get(mode="promise_in_bounds")
    cond_act = jax.nn.silu(conditions).astype(BF16)
    act = into(cond_act).reshape(n_z, 2, width).transpose(1, 0, 2).reshape(2 * n_z, width).astype(F32)
    *kept, vec_all, act_rows = forward(
        in_low, out_low, two_seqs(into(tokens)), two_seqs(into(cotangent)), ids, act, vectors, n_z, n_hi)
    big, small = kept[:-3], kept[-3:]
    mixed, grad_low, g_in, g_out, d_mod, g_vec, g_ada, cond_sum, norm = backward(
        big + [in_low] + small + [vec_all, act_rows], n_z, n_ff, n_hi)
    mod_sum = jnp.sum(d_mod.reshape(4 * n_z, 8, cols), axis=0)
    g_vec = jnp.concatenate([mod_sum[:6], g_vec.transpose(1, 0, 2).reshape(8, cols), mod_sum[6:]])
    if n_hi > 1:
        g_vec = lax.psum(g_vec, "fsdp", axis_index_groups=his)
        g_in = lax.psum_scatter(g_in, "fsdp", scatter_dimension=2, tiled=True, axis_index_groups=his)
        g_ada = lax.psum_scatter(g_ada, "fsdp", scatter_dimension=1, tiled=True, axis_index_groups=his)
        g_out = lax.psum_scatter(g_out, "fsdp", scatter_dimension=3, tiled=True, axis_index_groups=his)
        squares = jnp.sum(g_in * g_in) + jnp.sum(g_ada * g_ada) + jnp.sum(g_out * g_out)
        squares = squares + jnp.where((f == 0) & (c == 0), jnp.sum(g_vec * g_vec), 0.0)
        norm = jnp.broadcast_to(jnp.sqrt(lax.psum(squares, ("fsdp", "ctx", "tp"))), norm.shape)
    *news, mixed, input_grad = update(
        [norm, g_vec, vectors, vec_first, vec_second],
        [g_in, g_ada, g_out, in_weight, in_first, in_second, out_weight, out_first, out_second], [mixed, grad_low])
    bias_grad = news.pop(4)
    mixed = mixed.transpose(1, 0, 2)
    vec_new, in_new, out_new = news[:4], [a.transpose(1, 0, 2) for a in news[4:8]], news[8:]
    input_grad = input_grad.transpose(1, 0, 2)
    cond_sum = back(cond_sum).reshape(2, n_z, width).transpose(1, 0, 2).reshape(2 * n_z, width)
    unused, silu_pull = jax.vjp(jax.nn.silu, conditions)
    condition_grad = silu_pull(cond_sum)[0]
    return (back(mixed), back(input_grad), condition_grad, norm[0, 0], *in_new, *out_new, *vec_new, bias_grad[0])


def solution(mesh):
    in_matrix = P(("fsdp", "ctx"), None, "tp")
    out_matrix = P(None, "tp", ("fsdp", "ctx"))
    vector = P(None, "tp")
    rows = P("fsdp", "ctx", None)
    return jax.shard_map(
        functools.partial(per_device, mesh.shape["fsdp"], mesh.shape["ctx"], mesh.shape["tp"]),
        mesh=mesh,
        in_specs=(rows, rows, P(), P("fsdp"), P("fsdp", "ctx"), in_matrix, in_matrix, in_matrix,
                  out_matrix, out_matrix, out_matrix, vector, vector, vector),
        out_specs=(rows, rows, P("fsdp", None), P(), in_matrix, in_matrix, in_matrix, in_matrix,
                   out_matrix, out_matrix, out_matrix, out_matrix, vector, vector, vector, vector, P("tp")),
        check_vma=False,
    )
```

```python
import functools
import math

import jax
import jax.numpy as jnp
from jax import lax
from jax.experimental import pallas as pl
from jax.experimental.pallas import tpu as pltpu
from jax.sharding import PartitionSpec as P

HD = 64
STEP = 5
PRECISE = lax.Precision.HIGHEST
NORM_EPS = 1e-06
CLIP_NORM = 1.0
BETA_ONE = 0.5
BETA_TWO = 0.5
RATE_MATRIX = 0.03
RATE_VECTOR = 0.3
WEIGHT_DECAY = 0.05
ADAM_EPS = 1e-08

MESH = pl.DeviceIdType.MESH
F32 = jnp.float32
BF16 = jnp.bfloat16
LANES = 128
VMEM_BYTES = 60 * 2**20


def place():
    f = lax.axis_index("fsdp")
    c = lax.axis_index("ctx")
    z = lax.axis_index("tp")
    return f, c, z, lax.rem(f, 2), lax.rem(c, 2), c // 2


def partners(n_z):
    f, c, z, t, x, y = place()
    core = (f + 1 - 2 * t, c, z)
    xp = (f, 2 * y + (1 - x), z)
    yp = (f, 2 * (1 - y) + x, z)
    zs = [(f, c, lax.rem(z + d, n_z)) for d in range(1, n_z)]
    return core, xp, yp, zs


def enter(targets):
    barrier = pltpu.get_barrier_semaphore()
    for target in targets:
        pl.semaphore_signal(barrier, inc=1, device_id=target, device_id_type=MESH)
    pl.semaphore_wait(barrier, len(targets))


def lanes_at(index):
    return pl.ds(pl.multiple_of(index * LANES, LANES), LANES)


def adam_update(master, first, second, grad, factor, rate, decay):
    grad = grad * factor
    first = BETA_ONE * first + (1.0 - BETA_ONE) * grad
    second = BETA_TWO * second + (1.0 - BETA_TWO) * grad * grad
    fix_one = 1.0 - BETA_ONE**STEP
    fix_two = 1.0 - BETA_TWO**STEP
    stride = first / fix_one / (jnp.sqrt(second / fix_two) + ADAM_EPS)
    master = master - rate * (stride + decay * master)
    return (master, first, second, master.astype(BF16))


def dot(a, b, dims):
    return lax.dot_general(a, b, (dims, ((), ())), preferred_element_type=F32)


NN = ((1,), (0,))
NT = ((1,), (1,))
TN = ((0,), (0,))


PIECE = 176
NEG = -1e30
PLANE_FIRST = (10,)
EXTRA_EVERY = 2
PARTS = 4
PASSES = 3
PASS_PLAN = (3,)


def cat(parts, axis):
    return jnp.concatenate(parts, axis=axis)


def lane_of(shape):
    return lax.broadcasted_iota(jnp.int32, shape, len(shape) - 1)


def split_two(values):
    high = values.astype(BF16)
    return high, (values - high.astype(F32)).astype(BF16)


def split_three(values):
    high = values.astype(BF16)
    rest = values - high.astype(F32)
    middle = rest.astype(BF16)
    return high, middle, (rest - middle.astype(F32)).astype(BF16)


def head_mean(values):
    row = lax.broadcasted_iota(jnp.int32, (LANES, LANES), 0) // HD
    ones = jnp.where(row == lane_of((LANES, LANES)) // HD, 1.0 / HD, 0.0).astype(BF16)
    out = []
    for k in range(values.shape[1] // LANES):
        high, lower = split_two(values[:, k * LANES:(k + 1) * LANES])
        out.append(dot(high, ones, NN) + dot(lower, ones, NN))
    return cat(out, 1)


def gelu_both(u):
    k0, k1 = 0.7978845608028654, 0.044715
    square = u * u
    th = jnp.tanh(k0 * u * (1.0 + k1 * square))
    half = 0.5 * (1.0 + th)
    slope = half + 0.5 * u * (1.0 - th * th) * (k0 * (1.0 + 3.0 * k1 * square))
    return u * half, slope


def step_rows(piece, body):
    for p in (0, 1):
        def one(i, carry, p=p):
            start = pl.multiple_of(i * 16, 16)
            body(pl.ds(start, 16), pl.ds(pl.multiple_of(p * PIECE + start, 16), 16), p)
            return carry
        lax.fori_loop(0, piece // 16, one, 0)
        if piece % 16:
            start = piece // 16 * 16
            body(pl.ds(start, piece % 16), pl.ds(p * PIECE + start, piece % 16), p)


def clear_tail(ref, t):
    for p in (0, 1):
        ref[t, pl.ds(p * PIECE + PIECE - 16, 16), :] = jnp.zeros((16, ref.shape[2]), ref.dtype)


def normalize(values):
    center = values - jnp.mean(values, axis=-1, keepdims=True)
    scale = lax.rsqrt(jnp.mean(center * center, axis=-1, keepdims=True) + NORM_EPS)
    return center * scale, scale


def reorder(rows, n_hi, inverse=False):
    if n_hi == 1:
        return rows
    width = rows.shape[1]
    each = width // (8 * n_hi)
    out = []
    for k in range(width // LANES):
        at = k * LANES + lax.broadcasted_iota(jnp.int32, (width, LANES), 1)
        there = lax.broadcasted_iota(jnp.int32, (width, LANES), 0)
        if inverse:
            wanted = (at // each % 8) * (n_hi * each) + (at // (8 * each)) * each + at % each
        else:
            wanted = (at // each % n_hi) * (8 * each) + (at // (each * n_hi)) * each + at % each
        order = jnp.where(there == wanted, 1.0, 0.0).astype(BF16)
        out.append(sum(dot(part, order, NN) for part in split_three(rows)))
    return cat(out, 1)


class Wire:
    def __init__(self, send_sem, recv_sem):
        self.send_sem, self.recv_sem, self.sent = send_sem, recv_sem, []

    def make(self, at, src, dst, target, to=None):
        return pltpu.make_async_remote_copy(
            src_ref=src, dst_ref=dst, send_sem=self.send_sem.at[at], recv_sem=self.recv_sem.at[at if to is None else to],
            device_id=target, device_id_type=MESH)

    def start(self, at, src, dst, target, to=None):
        copy = self.make(at, src, dst, target, to)
        copy.start()
        self.sent.append(copy)
        return copy

    def finish(self):
        for copy in self.sent:
            copy.wait_send()


def forward_kernel(n_z, n_ff, n_hi, *refs):
    n_in, n_out = 3 + n_ff, 1 + n_ff
    (x_in, x_out, tok, cot, ids, act, vec,
     x_wq, x_wo, x_h1, x_qr, x_kr, x_q8, x_kh, x_v, x_o, x_lse, x_ma, x_mb, x_tok, x_cot, x_attn, x_mid,
     x_fown, x_fsend, x_down, x_dsend, x_gin, x_gout, x_mod, x_gu, x_gf, x_vec, x_act,
     g_in, g_out, tokb, cotb, idb, actb, pm, pr, ps, pf, vz, h1, gf, h2, qr, kr, q8, kh, vv, oo, lse, ma, mb,
     at_send, at_recv, attn, mid, facc, dacc, fsend, dsend, gin, gout, act_low, slope,
     full_in, full_out, low_in, low_out, local_sem, ag_send, ag_recv, m_send, m_recv, out_sem, tok_sem, load_sem) = refs
    f, c, z, t, x, y = place()
    core, xp, yp, zs = partners(n_z)
    f_base = f - t

    piece = tok.shape[1]
    n_all = x_in.shape[0]
    order = [("i", 0), ("i", 1), ("i", 2), ("o", 0)]
    for r in range(n_ff):
        order += [("i", 3 + r), ("o", 1 + r)]
    loads = {}
    for kind, m in [("i", j) for j in range(n_in, n_all)] + order:
        src, dst, at = (x_in, full_in, m) if kind == "i" else (x_out, full_out, n_all + m)
        loads[kind, m] = pltpu.make_async_copy(src.at[m], dst.at[m], load_sem.at[at])
        loads[kind, m].start()
    for ref in (h1, gf, h2):
        clear_tail(ref, t)

    barrier = pltpu.get_barrier_semaphore()
    plane = [xp, yp, (f, 3 - c, z)]
    other_line = [(f + 1 - 2 * t, c, target[2]) for target in zs]
    for target in [core] + plane + zs + other_line:
        pl.semaphore_signal(barrier, inc=1, device_id=target, device_id_type=MESH)
    loops = (y == t) & (x == t)
    for xs in (0, 1):
        @pl.when(jnp.logical_not(loops & (x == xs)))
        def _():
            pl.semaphore_signal(barrier, inc=1, device_id=(f_base + x, 2 * t + xs, z), device_id_type=MESH)
    pl.semaphore_wait(barrier, 4 + 2 * n_z - jnp.where(loops, 1, 0))

    ag = Wire(ag_send, ag_recv)
    misc = Wire(m_send, m_recv)

    shares = [(tok, tokb), (cot, cotb), (ids, None)]

    def send_share(j):
        src, dst = shares[j]
        for yd in (0, 1):
            own = loops & (y == yd)
            from_here = src.at[yd]
            to_there = dst.at[x] if dst is not None else idb.at[2 * y + x]

            @pl.when(own)
            def _():
                pltpu.make_async_copy(from_here, to_there, tok_sem.at[1, j, x]).start()

            @pl.when(jnp.logical_not(own))
            def _():
                pltpu.make_async_remote_copy(
                    src_ref=from_here, dst_ref=to_there, send_sem=tok_sem.at[0, j, yd], recv_sem=tok_sem.at[1, j, x],
                    device_id=(f_base + y, 2 * yd + t, z), device_id_type=MESH).start()

    def got_share(j):
        dst = shares[j][1]
        for xs in (0, 1):
            ref = dst.at[xs] if dst is not None else idb.at[2 * t + xs]
            pltpu.make_async_copy(ref, ref, tok_sem.at[1, j, xs]).wait()

    act_copy = misc.start(0, act.at[:, lanes_at((1 - t) * 4 + c)], actb.at[1], core)
    vec_local = pltpu.make_async_copy(vec, vz.at[z], local_sem.at[n_in + n_out])
    vec_local.start()
    vec_copies = [misc.start(1 + d, vec, vz.at[z], target) for d, target in enumerate(zs)]
    zrows = pl.ds(pl.multiple_of(z * LANES, LANES), LANES)
    first, zcopies, one, two = {}, {}, {}, {}

    def prepare(p):
        if p in first:
            return
        kind, m = order[p]
        loads[kind, m].wait()
        if kind == "i":
            dst = g_in.at[m, t, c, :, lanes_at(z)]
            for s in (0, 1):
                low_in[m, s] = full_in[m, :, s * LANES:(s + 1) * LANES].astype(BF16)
            mine, other = low_in.at[m, t], low_in.at[m, 1 - t]
        else:
            dst = g_out.at[m, t, zrows, lanes_at(c)]
            for s in (0, 1):
                low_out[m, s] = full_out[m, s * LANES:(s + 1) * LANES, :].astype(BF16)
            mine, other = low_out.at[m, t], low_out.at[m, 1 - t]
        local = pltpu.make_async_copy(mine, dst, local_sem.at[p])
        local.start()
        first[p] = (local, ag.start((p, 0), other, dst, core))

    base = n_z

    def start_zero(p):
        if p >= len(order) or p in zcopies or p in PLANE_FIRST:
            return
        kind, m = order[p]
        prepare(p)
        first[p][0].wait()
        first[p][1].wait_recv()
        block = g_in.at[m, :, c, :, lanes_at(z)] if kind == "i" else g_out.at[m, :, zrows, lanes_at(c)]
        zcopies[p] = [ag.start((p, 1 + d), block, block, target) for d, target in enumerate(zs)]

    line_first = [p for p in range(len(order)) if p not in PLANE_FIRST]

    def x_first(p):
        return line_first.index(p) % 2 == 0

    def start_one(p):
        kind, m = order[p]
        for copy in zcopies[p]:
            copy.wait_recv()
        block = g_in.at[m, :, c] if kind == "i" else g_out.at[m, :, :, lanes_at(c)]
        one[p] = ag.start((p, base), block, block, xp if x_first(p) else yp)

    def start_two(p):
        kind, m = order[p]
        one[p].wait_recv()
        held = (2 * y, 2 * y + 1) if x_first(p) else (x, 2 + x)
        two[p] = []
        if kind == "i" and x_first(p):
            block = g_in.at[m, :, pl.ds(2 * y, 2)]
            two[p].append(ag.start((p, base + 1), block, block, yp))
        else:
            for k, at in enumerate(held):
                block = g_in.at[m, :, at] if kind == "i" else g_out.at[m, :, :, lanes_at(at)]
                two[p].append(ag.start((p, base + 1 + k), block, block, yp if x_first(p) else xp))

    extras = []

    def start_plane(p):
        kind, m = order[p]
        prepare(p)
        first[p][0].wait()
        first[p][1].wait_recv()
        block = g_in.at[m, :, c, :, lanes_at(z)] if kind == "i" else g_out.at[m, :, zrows, lanes_at(c)]
        one[p] = [ag.start((p, base + k), block, block, target) for k, target in enumerate(plane)]
        two[p] = []

    def start_line(p, ck):
        kind, m = order[p]
        if ck == 0:
            for copy in one[p]:
                copy.wait_recv()
        block = g_in.at[m, :, ck, :, lanes_at(z)] if kind == "i" else g_out.at[m, :, zrows, lanes_at(ck)]
        for d, target in enumerate(zs):
            two[p].append(ag.start((p, base + 3 + 3 * ck + d), block, block, target))

    for p in PLANE_FIRST:
        extras.append((start_plane, (p,)))
    for p in PLANE_FIRST:
        extras += [(start_line, (p, ck)) for ck in range(4)]
    ticks = [(start_one, line_first[0])]
    for p, before in zip(line_first[1:], line_first[:-1]):
        ticks += [(start_one, p), (start_two, before)]
    ticks.append((start_two, line_first[-1]))
    ticked = [0]

    def tick(n=1):
        for _ in range(n):
            if ticks:
                step, p = ticks.pop(0)
                if step is start_one:
                    for ahead in range(p + 3):
                        start_zero(ahead)
                step(p)
            ticked[0] += 1
            if extras and ticked[0] >= 5 and ticked[0] % EXTRA_EVERY == 0:
                step, what = extras.pop(0)
                step(*what)

    def pump(n=1):
        tick(2 * n)

    def arrived(p):
        for copy in two[p]:
            copy.wait_recv()

    flushed = []

    def flush(src, dst):
        copy = pltpu.make_async_copy(src, dst, out_sem.at[len(flushed)])
        copy.start()
        flushed.append(copy)

    prepare(0)
    prepare(1)
    act_copy.wait_recv()
    cols = vec.shape[1]
    for j in range(n_in, n_all):
        loads["i", j].wait()
    own_at = lanes_at(t * 4 + c)
    mine = act[:, own_at]
    theirs = actb[1]
    pm[...] = jnp.zeros_like(pm)
    seqs = 2 * n_z
    for s in (0, 1):
        rows = jnp.where(t == s, mine, theirs)
        x_act[seqs * s:seqs * (s + 1), :] = rows
        for j in range(n_all - n_in):
            pm[seqs * s:seqs * (s + 1), j, :] = dot(rows.astype(BF16), full_in[n_in + j].astype(BF16), NN)

    def of_chip(xx, yy):
        return pm.at[pl.ds(seqs * xx + n_z * yy, n_z)]

    mod_copies = [misc.start(1 + n_z + k, of_chip(xx, yy), pr.at[k], target)
                  for k, (target, (xx, yy)) in enumerate(zip(plane, [(1 - x, y), (x, 1 - y), (1 - x, 1 - y)]))]
    send_share(0)
    send_share(2)
    start_zero(0)
    for copy in mod_copies:
        copy.wait_recv()
    ps[...] = (of_chip(x, y)[...] + pr[0]) + (pr[1] + pr[2])
    pf[t, z] = ps[z]
    mod_copies = [misc.start(4 + n_z + k, ps.at[target[2]], pf.at[t, z], target)
                  for k, target in enumerate([core] + zs + other_line)]
    start_zero(1)
    for p in range(2, len(order)):
        prepare(p)
    tick()
    for copy in mod_copies + vec_copies:
        copy.wait_recv()
    vec_local.wait()
    row = lax.broadcasted_iota(jnp.int32, (8, cols), 0)
    for zi in range(n_z):
        bias = jnp.where(row < 6, vz[zi, 0:8, :], 0.0)
        x_mod[:, zi * cols:(zi + 1) * cols] = pf[0, zi] + pf[1, zi] + bias
    x_mod[...] = reorder(x_mod[...], n_hi)
    x_vec[...] = vz[...]
    tick()

    def wide(k):
        return cat([vz[zi, k:k + 1, :] for zi in range(n_z)], 1)

    def narrow(k):
        return cat([vz[zi, k:k + 1, lanes_at(t)] for zi in range(n_z)], 1)

    got_share(0)
    got_share(2)
    half = 2 * PIECE
    full = 2 * half
    mine_ids = idb.at[pl.ds(2 * t, 2)]
    id_copy = misc.start(4 + 3 * n_z, mine_ids, mine_ids, core)
    flush(tokb, x_tok)

    def first_norm(rows, at, p):
        normed, unused = normalize(tokb[p, rows, :].astype(F32))
        h1[t, at, :] = (normed * (1.0 + x_mod[1:2, :]) + x_mod[2:3, :]).astype(BF16)
    step_rows(piece, first_norm)
    h1_copy = misc.start(5 + 3 * n_z, h1.at[t], h1.at[t], core)

    pump(2)
    id_copy.wait_recv()
    lanes = lane_of((full, LANES)) % HD
    scale = idb[...].reshape(full, LANES).astype(F32)
    feature = lanes.astype(F32)
    ma[...] = jnp.where((lanes < 16) & (feature > scale), 1.0, 0.0).astype(BF16)
    mb[...] = jnp.where((lanes < 16) & (feature == scale), NEG, 0.0).astype(BF16)
    flush(ma, x_ma)
    flush(mb, x_mb)
    pump(2)
    send_share(1)
    h1_copy.wait_recv()

    def whole(ref):
        return ref[...].reshape(full, ref.shape[-1])

    def w_in(m):
        return g_in[m].reshape(8 * LANES, n_z * LANES)

    arrived(0)
    qr[...] = dot(whole(h1), w_in(0), NN) + narrow(6)
    q8[...] = (qr[...] * lax.rsqrt(head_mean(qr[...] * qr[...]) + NORM_EPS) * narrow(8)).astype(BF16) * 0.125
    arrived(1)
    kr[...] = dot(whole(h1), w_in(1), NN)
    kh[...] = (kr[...] * lax.rsqrt(head_mean(kr[...] * kr[...]) + NORM_EPS) * narrow(9)).astype(BF16)
    flush(qr, x_qr)
    flush(kr, x_kr)
    flush(q8, x_q8)
    flush(kh, x_kh)
    pump(1)
    arrived(2)
    vv[...] = (dot(whole(h1), w_in(2), NN) + narrow(7)).astype(BF16)
    flush(vv, x_v)
    flush(h1, x_h1)
    flush(g_in.at[pl.ds(0, 3)], x_wq)
    got_share(1)
    flush(cotb, x_cot)

    def gate(rows, at, p):
        gf[t, at, :] = (cotb[p, rows, :].astype(F32) * x_mod[3:4, :]).astype(BF16)
    step_rows(piece, gate)
    gf_copy = misc.start(6 + 3 * n_z, gf.at[t], gf.at[t], core)

    def attend(i, carry):
        at = lanes_at(i)
        q2, k2, v2 = q8[:, at], kh[:, at], vv[:, at]
        mine_a, mine_b = ma[...], mb[...]
        low = lane_of((full, LANES)) < HD
        outs, tops = [], []
        for h in (0, 1):
            here = low if h == 0 else jnp.logical_not(low)
            s = dot(jnp.where(here, q2, mine_a), jnp.where(here, k2, mine_b), NT)
            top = jnp.max(s, axis=1, keepdims=True)
            e = jnp.exp(s - top).astype(BF16)
            got = dot(e, jnp.where(here, v2, jnp.ones_like(v2)), NN)
            total = got[:, HD:HD + 1] if h == 0 else got[:, 0:1]
            outs.append(got / total)
            tops.append(top + jnp.log(total))
        oo[:, at] = jnp.where(low, outs[0], outs[1]).astype(BF16)
        lse[:, at] = jnp.where(low, tops[0], tops[1])
        return carry

    pairs = n_z * LANES // LANES
    for i in range(0, pairs, 2):
        lax.fori_loop(i, i + 2, attend, 0)
        pump(1)
    flush(oo, x_o)
    flush(lse, x_lse)

    arrived(3)
    flush(g_out.at[0], x_wo)
    width = 8 * LANES
    hw = width // 2
    for j in (0, 1):
        both = dot(oo[...], g_out[0, j], NN)
        attn[:, j * hw:(j + 1) * hw] = jnp.where(t == 0, both[:half], both[half:])
        at_send[:, j * hw:(j + 1) * hw] = jnp.where(t == 0, both[half:], both[:half]).astype(BF16)
    at_copy = misc.start(7 + 3 * n_z, at_send, at_recv, core)
    at_copy.wait_recv()
    proj_bias = reorder(wide(10 + n_ff), n_hi)


    def second_norm(rows, at, p):
        total = attn[at, :] + at_recv[at, :].astype(F32) + proj_bias
        attn[at, :] = total
        middle = tokb[p, rows, :].astype(F32) + x_mod[0:1, :] * total
        mid[at, :] = middle
        normed, unused = normalize(middle)
        h2[t, at, :] = (normed * (1.0 + x_mod[4:5, :]) + x_mod[5:6, :]).astype(BF16)
    step_rows(piece, second_norm)
    h2_copy = misc.start(8 + 3 * n_z, h2.at[t], h2.at[t], core)
    flush(attn, x_attn)
    flush(mid, x_mid)
    gf_copy.wait_recv()
    pump(1)
    x_gf[...] = jnp.zeros_like(x_gf)
    x_gf[0:1, :] = jnp.sum(whole(gf).astype(F32), axis=0, keepdims=True)
    x_gu[...] = jnp.zeros_like(x_gu)
    h2_copy.wait_recv()

    for r in range(n_ff):
        arrived(4 + 2 * r)
        bias_row = narrow(10 + r)
        u = dot(whole(h2), w_in(3 + r), NN) + bias_row
        value, gradient = gelu_both(u)
        act_low[...] = value.astype(BF16)
        slope[...] = gradient
        pump(1)
        for j in (0, 1):
            gout[r, j] = dot(act_low[...], gf[:, :, j * hw:(j + 1) * hw].reshape(full, hw), TN).astype(BF16)
        flush(gout.at[r], x_gout.at[r])
        arrived(5 + 2 * r)
        for j in (0, 1):
            part = dot(act_low[...], g_out[1 + r, j], NN)
            cols_here = pl.ds(j * hw, hw)
            facc[:, cols_here] = part if r == 0 else facc[:, cols_here] + part
        back_act = (dot(gf[:, :, :hw].reshape(full, hw), g_out[1 + r, 0], NT)
                    + dot(gf[:, :, hw:].reshape(full, hw), g_out[1 + r, 1], NT))
        gu = (back_act * slope[...]).astype(BF16)
        act_low[...] = gu
        pump(1)
        x_gu[r:r + 1, :] = jnp.sum(gu.astype(F32), axis=0, keepdims=True)
        gin[r] = dot(whole(h2), act_low[...], TN).astype(BF16).reshape(gin.shape[1:])
        flush(gin.at[r], x_gin.at[r])
        part = dot(act_low[...], w_in(3 + r), NT)
        dacc[...] = part if r == 0 else dacc[...] + part

    mine_rows = pl.ds(pl.multiple_of(t * half, half), half)
    other_rows = pl.ds(pl.multiple_of((1 - t) * half, half), half)
    fsend[...] = facc[other_rows, :].astype(BF16)
    dsend[...] = dacc[other_rows, :].astype(BF16)
    flush(facc.at[mine_rows], x_fown)
    flush(fsend, x_fsend)
    flush(dacc.at[mine_rows], x_down)
    flush(dsend, x_dsend)
    for copy in flushed:
        copy.wait()
    for j, (src, dst) in enumerate(shares):
        for yd in (0, 1):
            @pl.when(jnp.logical_not(loops & (y == yd)))
            def _():
                ref = src.at[yd]
                pltpu.make_async_remote_copy(
                    src_ref=ref, dst_ref=ref, send_sem=tok_sem.at[0, j, yd], recv_sem=tok_sem.at[1, j, x],
                    device_id=(f_base + y, 2 * yd + t, z), device_id_type=MESH).wait_send()
    ag.finish()
    misc.finish()


def forward(x_in, x_out, tok, cot, ids, act, vec, n_z, n_hi):
    n_out = x_out.shape[0]
    n_ff = n_out - 1
    n_in = 3 + n_ff
    pieces = n_in + n_out
    here, width = n_z * LANES, 8 * LANES
    half, full = 2 * PIECE, 4 * PIECE
    piece = tok.shape[1]
    hw = width // 2
    S = jax.ShapeDtypeStruct
    wide_low, wide_full = S((half, width), BF16), S((half, width), F32)
    cols_low, cols_full = S((full, here), BF16), S((full, here), F32)
    mask = S((full, LANES), BF16)
    big = [
        S((3, 2, 4, LANES, here), BF16), S((2, here, hw), BF16), S((2, half, width), BF16), cols_full, cols_full,
        cols_low, cols_low, cols_low, cols_low, cols_full, mask, mask, S((2, piece, width), BF16),
        S((2, piece, width), BF16), wide_full, wide_full, wide_full, wide_low, wide_full, wide_low,
        S((n_ff, 2, 4, LANES, here), BF16), S((n_ff, 2, here, hw), BF16)]
    small = [S((8, width), F32), S((8, here), F32), S((8, width), F32), S((n_z,) + vec.shape, F32), S((4 * n_z, LANES), F32)]
    any_space, vmem = pl.BlockSpec(memory_space=pl.ANY), pl.BlockSpec(memory_space=pltpu.VMEM)
    mod_shape = (8, vec.shape[1])
    V = pltpu.VMEM
    dma = pltpu.SemaphoreType.DMA
    return pl.pallas_call(
        functools.partial(forward_kernel, n_z, n_ff, n_hi),
        out_shape=tuple(big + small),
        in_specs=[any_space] * 5 + [vmem] * 2,
        out_specs=tuple([any_space] * len(big) + [vmem] * len(small)),
        scratch_shapes=[
            V((n_in, 2, 4, LANES, here), BF16), V((n_out, 2, here, hw), BF16),
            V((2, piece, width), BF16), V((2, piece, width), BF16), V((4, PIECE, LANES), BF16),
            V((2, 2 * n_z, LANES), F32), V((4 * n_z,) + mod_shape, F32), V((3, n_z) + mod_shape, F32), V((n_z,) + mod_shape, F32),
            V((2, n_z) + mod_shape, F32), V((n_z,) + vec.shape, F32),
            V((2, half, width), BF16), V((2, half, width), BF16), V((2, half, width), BF16),
            V((full, here), F32), V((full, here), F32), V((full, here), BF16), V((full, here), BF16), V((full, here), BF16),
            V((full, here), BF16), V((full, here), F32), V((full, LANES), BF16), V((full, LANES), BF16),
            V((half, width), BF16), V((half, width), BF16), V((half, width), F32), V((half, width), F32),
            V((full, width), F32), V((full, width), F32), V((half, width), BF16), V((half, width), BF16),
            V((n_ff, 2, 4, LANES, here), BF16), V((n_ff, 2, here, hw), BF16), V((full, here), BF16), V((full, here), F32),
            V(x_in.shape, F32), V(x_out.shape, F32), V((n_in, 2, LANES, LANES), BF16), V((n_out, 2, LANES, LANES), BF16),
            dma((pieces + 1,)), dma((pieces, 4 * n_z + 3)), dma((pieces, 4 * n_z + 3)), dma((9 + 3 * n_z,)), dma((9 + 3 * n_z,)),
            dma((len(big) + 2 * n_ff,)), dma((2, 3, 2)), dma((x_in.shape[0] + n_out,)),
        ],
        compiler_params=pltpu.CompilerParams(collective_id=0, has_side_effects=True, vmem_limit_bytes=VMEM_BYTES),
    )(x_in, x_out, tok, cot, ids, act, vec)

class Guarded:
    def __init__(self):
        self.sent = []

    def start(self, cond, copy):
        @pl.when(cond)
        def _():
            copy.start()
        self.sent.append((cond, copy))

    def finish(self):
        for cond, copy in self.sent:
            @pl.when(cond)
            def _(copy=copy):
                copy.wait_send()


def backward_kernel(n_z, n_ff, n_hi, *refs):
    n_in, n_out = 3 + n_ff, 1 + n_ff
    (x_wq, x_wo, x_h1, x_qr, x_kr, x_q8, x_kh, x_v, x_o, x_lse, x_ma, x_mb, x_tok, x_cot, x_attn, x_mid,
     x_fown, x_fsend, x_down, x_dsend, x_gin, x_gout, x_weight, mod, gu_sum, gf_sum, vz, act,
     o_mixed, o_grad, o_in, o_out, o_dmod, o_vec, o_ada, o_cond, o_norm,
     wq, wo, h1, qr, kr, q8, kh, vv, oo, lse, ma, mb, tokb, cotb, attn, mid, buf, f_recv, d_recv,
     dmid, ga, go, mixed, sums, vd, vdr, vs, vdz, zv, v_all, norm, norm_plane, norm_line, cond_z, cond_all,
     p_full, q_full, p_half, q_half, a_in, a_out, b_in, b_out, z_in, z_out, f_in, f_out,
     load_sem, own_sem, rs_send, rs_recv, m_send, m_recv, t_send, t_recv, g_send, g_recv) = refs
    f, c, z, t, x, y = place()
    core, xp, yp, zs = partners(n_z)
    f_base = f - t
    last = n_z - 1
    half, full = 2 * PIECE, 4 * PIECE
    width = mod.shape[1]
    hw = width // 2
    piece = x_tok.shape[1]
    clear_tail(ga, t)

    barrier = pltpu.get_barrier_semaphore()
    diagonal = (f, 3 - c, z)
    plane = [xp, yp, diagonal]
    other_line = [(f + 1 - 2 * t, c, target[2]) for target in zs]
    for target in [core] + plane + zs + other_line:
        pl.semaphore_signal(barrier, inc=1, device_id=target, device_id_type=MESH)
    loops = (y == t) & (x == t)
    for ys in (0, 1):
        @pl.when(jnp.logical_not(loops & (y == ys)))
        def _():
            pl.semaphore_signal(barrier, inc=1, device_id=(f_base + y, 2 * ys + t, z), device_id_type=MESH)

    loads = {}
    names = [("f", x_fown, buf.at[0]), ("mid", x_mid, mid), ("cot", x_cot, cotb), ("d", x_down, buf.at[1]),
             ("attn", x_attn, attn), ("wo", x_wo, wo), ("o", x_o, oo), ("q", x_q8, q8), ("k", x_kh, kh), ("v", x_v, vv),
             ("lse", x_lse, lse), ("ma", x_ma, ma), ("mb", x_mb, mb), ("qr", x_qr, qr), ("kr", x_kr, kr),
             ("h1", x_h1, h1), ("wq", x_wq, wq), ("tok", x_tok, tokb)]
    for i, (name, src, dst) in enumerate(names):
        loads[name] = pltpu.make_async_copy(src, dst, load_sem.at[i])
        loads[name].start()
    pl.semaphore_wait(barrier, 4 + 2 * n_z - jnp.where(loops, 1, 0))

    rs = Wire(rs_send, rs_recv)
    misc = Wire(m_send, m_recv)
    chain = Guarded()
    f_copy = misc.start(0, x_fsend, f_recv, core)
    d_copy = misc.start(1, x_dsend, d_recv, core)

    order = []
    for r in range(n_ff):
        order += [("i", 3 + r), ("o", 1 + r)]
    order += [("o", 0), ("i", 2), ("i", 1), ("i", 0)]
    pieces = len(order)
    one, two, four, own_half = {}, {}, {}, {}

    def y_first(p):
        return p % 2 == 0

    def parts(p, mine):
        if y_first(p):
            yy = y if mine else 1 - y
            return [2 * yy, 2 * yy + 1]
        xx = x if mine else 1 - x
        return [xx, 2 + xx]

    def source(p, at):
        kind, m = order[p]
        if kind == "i":
            return x_gin.at[m - 3, :, at] if m >= 3 else p_full.at[m, :, at]
        return x_gout.at[m - 1, :, :, lanes_at(at)] if m >= 1 else q_full.at[:, :, lanes_at(at)]

    def kept(p, k):
        kind, m = order[p]
        return p_half.at[m, k] if kind == "i" else q_half.at[m, k]

    def bufs(p, inner, outer):
        kind, m = order[p]
        return inner.at[m] if kind == "i" else outer.at[m]

    def step_one(p):
        one[p] = [rs.start((p, k), source(p, at), bufs(p, a_in, a_out).at[k], yp if y_first(p) else xp)
                  for k, at in enumerate(parts(p, False))]
        own_half[p] = []
        for k, at in enumerate(parts(p, True)):
            copy = pltpu.make_async_copy(source(p, at), kept(p, k), own_sem.at[p, k])
            copy.start()
            own_half[p].append(copy)

    def step_two(p):
        for copy in one[p]:
            copy.wait_recv()
        for copy in own_half[p]:
            copy.wait()
        for k in (0, 1):
            ref = kept(p, k)
            ref[...] = (ref[...].astype(F32) + bufs(p, a_in, a_out)[k].astype(F32)).astype(BF16)
        go_bit = (1 - x) if y_first(p) else (1 - y)
        two[p] = rs.start((p, 2), kept(p, go_bit), bufs(p, b_in, b_out), xp if y_first(p) else yp)

    def span(p, ref, lo, hi):
        if order[p][0] == "i":
            return ref.at[:, :, lo * LANES:hi * LANES]
        return ref.at[:, lo * LANES:hi * LANES, :]

    def right_copy(p, s):
        here = kept(p, x if y_first(p) else y)
        return pltpu.make_async_remote_copy(
            src_ref=span(p, here, s + 1, n_z), dst_ref=span(p, bufs(p, z_in, z_out), s + 2, n_z + 1),
            send_sem=rs_send.at[p, 3], recv_sem=rs_recv.at[p, 3], device_id=(f, c, z + 1), device_id_type=MESH)

    def left_copy(p, s):
        here = kept(p, x if y_first(p) else y)
        return pltpu.make_async_remote_copy(
            src_ref=span(p, here, 0, s), dst_ref=span(p, bufs(p, z_in, z_out), 0, s),
            send_sem=rs_send.at[p, 4], recv_sem=rs_recv.at[p, 4], device_id=(f, c, z - 1), device_id_type=MESH)

    def add_into(p, lo, hi, shift):
        here = kept(p, x if y_first(p) else y)
        a, b = span(p, here, lo, hi), span(p, bufs(p, z_in, z_out), lo + shift, hi + shift)
        a[...] = (a[...].astype(F32) + b[...].astype(F32)).astype(BF16)

    def step_z(p, s):
        if s == 0:
            two[p].wait_recv()
            here = kept(p, x if y_first(p) else y)
            here[...] = (here[...].astype(F32) + bufs(p, b_in, b_out)[...].astype(F32)).astype(BF16)

        @pl.when(z == s)
        def _():
            if s > 0:
                landed = span(p, bufs(p, z_in, z_out), s + 1, n_z + 1)
                pltpu.make_async_copy(landed, landed, rs_recv.at[p, 3]).wait()
            if s < last:
                if s > 0:
                    add_into(p, s + 1, n_z, 1)
                right_copy(p, s).start()

        @pl.when(z == last - s)
        def _():
            e = last - s
            if s > 0:
                landed = span(p, bufs(p, z_in, z_out), 0, e + 1)
                pltpu.make_async_copy(landed, landed, rs_recv.at[p, 4]).wait()
            if e > 0:
                if s > 0:
                    add_into(p, 0, e, 0)
                left_copy(p, e).start()

    norm[...] = jnp.zeros_like(norm)

    def add_squares(values):
        square = values * values
        parts = [square[8 * i:8 * i + 8] for i in range(square.shape[0] // 8)]
        while len(parts) > 1:
            parts = [a + b for a, b in zip(parts[::2], parts[1::2])]
        for k in range(square.shape[1] // LANES):
            norm[...] = norm[...] + parts[0][:, k * LANES:(k + 1) * LANES]

    def step_core(p):
        kind, m = order[p]
        here = kept(p, x if y_first(p) else y)
        total, result = (f_in, o_in) if kind == "i" else (f_out, o_out)
        for s in range(n_z):
            @pl.when(z == s)
            def _():
                value = span(p, here, s, s + 1)[...].astype(F32)
                if s > 0:
                    value = value + span(p, bufs(p, z_in, z_out), s + 1, s + 2)[...].astype(F32)
                if s < last:
                    value = value + span(p, bufs(p, z_in, z_out), s, s + 1)[...].astype(F32)
                total[m] = value
        result[m, t] = total[m, t]
        add_squares(total[m, 0])
        add_squares(total[m, 1])
        four[p] = rs.start((p, 5), total.at[m, 1 - t], result.at[m, t], core)

    def in_range(p):
        return 0 <= p < pieces

    ready = [2 * n_ff]
    started = [0]
    step = [0]

    def first_sends(upto):
        while started[0] < min(upto, ready[0], pieces):
            step_one(started[0])
            started[0] += 1

    passes, chores = [], []

    def pump(n=1):
        for _ in range(n):
            k = step[0]
            first_sends(k + 3)
            if in_range(k) and k >= started[0]:
                return
            if in_range(k):
                step_two(k)
            for unused in range(PASSES if k < 0 else PASS_PLAN[min(k, len(PASS_PLAN) - 1)]):
                if passes:
                    pass_along(*passes.pop(0))
            for s in range(n_z):
                if in_range(k - 1 - 2 * s):
                    step_z(k - 1 - 2 * s, s)
            if in_range(k - 2 * n_z):
                step_core(k - 2 * n_z)
            if chores:
                chore = chores.pop(0)
                if chore is not None:
                    chore()
            step[0] += 1

    first_sends(2)

    def share_out(j, src, dst):
        for xs in (0, 1):
            own = loops & (x == xs)
            there = dst.at[2 * z + y]
            local = pltpu.make_async_copy(src.at[xs], there, t_recv.at[j, y])

            @pl.when(own)
            def _():
                local.start()
            chain.start(jnp.logical_not(own), pltpu.make_async_remote_copy(
                src_ref=src.at[xs], dst_ref=there, send_sem=t_send.at[j, xs], recv_sem=t_recv.at[j, y],
                device_id=(f_base + x, 2 * t + xs, z), device_id_type=MESH))

    def pass_along(j, dst, s, part):
        lanes = pl.ds(part * (width // PARTS), width // PARTS)
        if s == 0 and part == 0:
            for ys in (0, 1):
                pltpu.make_async_copy(dst.at[2 * z + ys], dst.at[2 * z + ys], t_recv.at[j, ys]).wait()
        for side, (there, back_at) in enumerate(((z + 1, z - s), (z - 1, z + s))):
            valid = (back_at >= 0) & (back_at <= last)
            block = dst.at[pl.ds(2 * lax.clamp(0, back_at, last), 2), :, lanes]
            if s > 0:
                @pl.when(valid)
                def _():
                    pltpu.make_async_copy(block, block, g_recv.at[j, side, s, part]).wait()
            if s < last:
                chain.start(valid & (there >= 0) & (there <= last), pltpu.make_async_remote_copy(
                    src_ref=block, dst_ref=block, send_sem=g_send.at[j, side, s, part],
                    recv_sem=g_recv.at[j, side, s + 1, part],
                    device_id=(f, c, lax.clamp(0, there, last)), device_id_type=MESH))

    def pass_all(j, dst):
        passes.extend((j, dst, s, part) for s in range(n_z) for part in range(PARTS))

    def wide(k):
        return cat([vz[zi, k:k + 1, :] for zi in range(n_z)], 1)

    def narrow(k):
        return cat([vz[zi, k:k + 1, lanes_at(t)] for zi in range(n_z)], 1)

    def tally(j, values):
        if values.shape[0] == 16:
            sums[j] = sums[j] + values[:8] + values[8:]
        else:
            sums[j, 0:1] = sums[j, 0:1] + jnp.sum(values, axis=0, keepdims=True)

    sums[...] = jnp.zeros_like(sums)
    ffn_bias = reorder(wide(11 + n_ff), n_hi)
    for name in ("f", "mid", "cot"):
        loads[name].wait()
    f_copy.wait_recv()

    def mix(rows, at, p):
        out = buf[0, at, :] + f_recv[at, :].astype(F32) + ffn_bias
        tally(3, cotb[p, rows, :].astype(F32) * out)
        mixed[p, rows, :] = (mid[at, :] + mod[3:4, :] * out).astype(BF16)
    step_rows(piece, mix)
    share_out(0, mixed, o_mixed)
    first_sends(3)

    for name in ("d", "attn"):
        loads[name].wait()
    d_copy.wait_recv()

    def second_norm(rows, at, p):
        grad = buf[1, at, :] + d_recv[at, :].astype(F32)
        normed, scale = normalize(mid[at, :])
        tally(4, grad * normed)
        tally(5, grad)
        w = grad * (1.0 + mod[4:5, :])
        pulled = scale * (w - jnp.mean(w, axis=-1, keepdims=True) - normed * jnp.mean(w * normed, axis=-1, keepdims=True))
        total = cotb[p, rows, :].astype(F32) + pulled
        dmid[at, :] = total
        tally(0, total * attn[at, :])
        low = (total * mod[0:1, :]).astype(BF16)
        ga[t, at, :] = low
        tally(6, low.astype(F32))
    step_rows(piece, second_norm)
    ga_copy = misc.start(2, ga.at[t], ga.at[t], core)

    loads["wo"].wait()
    loads["o"].wait()
    ga_copy.wait_recv()
    for j in (0, 1):
        ga_j = ga[:, :, j * hw:(j + 1) * hw].reshape(full, hw)
        part = dot(ga_j, wo[j], NT)
        if j == 0:
            first_part = part
        q_full[j] = dot(oo[...], ga_j, TN).astype(BF16)
    go[...] = (first_part + part).astype(BF16)
    ready[0] += 1
    for name in ("q", "k", "v", "lse", "ma", "mb", "qr", "kr"):
        loads[name].wait()
    pass_all(0, o_mixed)

    vs[...] = jnp.zeros_like(vs)

    def head_back(raw, grad, gain):
        scale = lax.rsqrt(head_mean(raw * raw) + NORM_EPS)
        normed = raw * scale
        gain_grad = jnp.sum(grad * normed, axis=0, keepdims=True)
        w = grad * gain
        return (scale * (w - normed * head_mean(w * normed))).astype(BF16), gain_grad

    def attend_back(i, carry):
        at = lanes_at(i)
        q2, k2, v2, g2, o2 = q8[:, at], kh[:, at], vv[:, at], go[:, at], oo[:, at]
        mine_a, mine_b = ma[...], mb[...]
        lanes = lane_of((full, LANES))
        low, l64 = lanes < HD, lanes % HD
        product = o2.astype(F32) * g2.astype(F32)
        dqs, dks, dvs = [], [], []
        one_like, zero_like = jnp.ones_like(v2), jnp.zeros_like(v2)
        for h in (0, 1):
            here = low if h == 0 else jnp.logical_not(low)
            l1, l2, l3 = split_three(lse[:, at][:, HD * h:HD * h + 1])
            qa = jnp.where(l64 == 40, -l1, jnp.where(l64 == 41, -l2, jnp.where(l64 == 42, -l3, mine_a)))
            ka = jnp.where((l64 >= 40) & (l64 < 43), one_like, mine_b)
            weight = jnp.exp(dot(jnp.where(here, k2, ka), jnp.where(here, q2, qa), NT))
            d1, d2, d3 = split_three(jnp.sum(jnp.where(here, product, 0.0), axis=1, keepdims=True))
            da = jnp.where(l64 == 0, -d1, jnp.where(l64 == 1, -d2, jnp.where(l64 == 2, -d3, zero_like)))
            va = jnp.where(l64 < 3, one_like, zero_like)
            ds = (weight * dot(jnp.where(here, v2, va), jnp.where(here, g2, da), NT)).astype(BF16)
            dvs.append(dot(weight.astype(BF16), g2, NN))
            dks.append(dot(ds, q2, NN))
            dqs.append(dot(ds, k2, TN))
        dq = jnp.where(low, dqs[0], dqs[1]) * 0.125
        dk = jnp.where(low, dks[0], dks[1])
        gq, q_gain = head_back(qr[:, at], dq, vs[8:9, at])
        gk, k_gain = head_back(kr[:, at], dk, vs[9:10, at])
        gv = jnp.where(low, dvs[0], dvs[1]).astype(BF16)
        q8[:, at] = gq
        kh[:, at] = gk
        vv[:, at] = gv
        vs[0:1, at] = jnp.sum(gq.astype(F32), axis=0, keepdims=True)
        vs[1:2, at] = jnp.sum(gv.astype(F32), axis=0, keepdims=True)
        vs[2:3, at] = q_gain
        vs[3:4, at] = k_gain
        return carry

    vs[8:9, :] = narrow(8)
    vs[9:10, :] = narrow(9)
    pairs = n_z
    for i in range(0, pairs, 2):
        lax.fori_loop(i, i + 2, attend_back, 0)
        pump(1)
    ada_refs, ada_loads = [], []
    for j in range(6):
        rows_at, cols_at = (j // 2) * LANES, (j % 2) * (n_z * LANES // 2)
        ada_refs.append(qr.at[rows_at:rows_at + LANES, cols_at:cols_at + n_z * LANES // 2])
        ada_loads.append(pltpu.make_async_copy(x_weight.at[3 + n_ff + j], ada_refs[j], load_sem.at[len(names) + j]))
        ada_loads[j].start()
    loads["wq"].wait()
    part = dot(q8[...], wq[0].reshape(width, n_z * LANES), NT)
    part = part + dot(kh[...], wq[1].reshape(width, n_z * LANES), NT)
    part = part + dot(vv[...], wq[2].reshape(width, n_z * LANES), NT)
    buf[0] = jnp.where(t == 0, part[:half], part[half:])
    f_recv[...] = jnp.where(t == 0, part[half:], part[:half]).astype(BF16)
    h_copy = misc.start(3, f_recv, d_recv, core)
    loads["tok"].wait()
    pump(1)
    h_copy.wait_recv()

    def first_norm(rows, at, p):
        grad = buf[0, at, :] + d_recv[at, :].astype(F32)
        normed, scale = normalize(tokb[p, rows, :].astype(F32))
        tally(1, grad * normed)
        tally(2, grad)
        w = grad * (1.0 + mod[1:2, :])
        pulled = scale * (w - jnp.mean(w, axis=-1, keepdims=True) - normed * jnp.mean(w * normed, axis=-1, keepdims=True))
        cotb[p, rows, :] = (dmid[at, :] + pulled).astype(BF16)
    step_rows(piece, first_norm)
    share_out(1, cotb, o_grad)
    pass_all(1, o_grad)
    loads["h1"].wait()
    h1_all = h1[...].reshape(full, width)
    for m, ref in ((2, vv), (1, kh), (0, q8)):
        p_full[m] = dot(h1_all, ref[...], TN).astype(BF16).reshape(p_full.shape[1:])
        ready[0] += 1
    pump(1)


    for j in range(7):
        vd[j:j + 1, :] = jnp.sum(sums[j], axis=0, keepdims=True)
    vd[7:8, :] = gf_sum[0:1, :] * 0.5
    v_copy = misc.start(4, vd, vdr, core)
    vs[4:8, :] = gu_sum[0:4, :]
    cols = width // n_z
    n_ada = 6
    chips = 4 * n_z
    waits = {}

    def exact(a, b, dims):
        return lax.dot_general(a, b, (dims, ((), ())), precision=PRECISE, preferred_element_type=F32)

    def arrive(name):
        for copy in waits.pop(name):
            copy.wait_recv()

    def mods(j):
        return o_dmod[...].reshape(chips, 8, cols)[:, j, :]

    def along_line():
        v_copy.wait_recv()
        vd_all = reorder(vd[...] + vdr[...], n_hi, inverse=True)
        for zi in range(n_z):
            vdz[zi] = vd_all[:, zi * cols:(zi + 1) * cols]
        o_dmod[x, y, z] = vdz[z]
        zv[z] = vs[0:8, lanes_at(z)]
        waits["line"] = []
        for d, target in enumerate(zs):
            zi = lax.rem(z + 1 + d, n_z)
            waits["line"].append(misc.start(5 + d, vdz.at[zi], o_dmod.at[x, y, z], target))
            waits["line"].append(misc.start(4 + n_z + d, vs.at[pl.ds(0, 8), lanes_at(zi)], zv.at[z], target))

    slot = 3 + 2 * n_z

    def over_plane():
        arrive("line")
        total = zv[0]
        for zi in range(1, n_z):
            total = total + zv[zi]
        v_all[x, y] = total
        waits["plane"] = []
        for d, target in enumerate(plane):
            waits["plane"].append(misc.start(slot + d, o_dmod.at[x, y], o_dmod.at[x, y], target))
            waits["plane"].append(misc.start(slot + 3 + d, v_all.at[x, y], v_all.at[x, y], target))

    def products():
        arrive("plane")
        o_vec[t] = (v_all[0, 0] + v_all[0, 1]) + (v_all[1, 0] + v_all[1, 1])
        waits["vec"] = [misc.start(slot + 6, o_vec.at[t], o_vec.at[t], core)]
        for copy in ada_loads:
            copy.wait()
        total = 0.0
        for j, ref in enumerate(ada_refs):
            total = total + exact(mods(j), ref[...].astype(BF16).astype(F32), NT)
        cond_z[z] = total
        waits["cond line"] = [misc.start(slot + 7 + d, cond_z.at[z], cond_z.at[z], target) for d, target in enumerate(zs)]
        for j in range(n_ada):
            o_ada[j] = exact(act[...], mods(j), TN)
            if n_hi == 1:
                add_squares(o_ada[j])

    def cond_plane():
        arrive("cond line")
        total = cond_z[0]
        for zi in range(1, n_z):
            total = total + cond_z[zi]
        cond_all[t, c] = total
        at = slot + 6 + n_z
        waits["cond plane"] = [misc.start(at + d, cond_all.at[t, c], cond_all.at[t, c], target)
                               for d, target in enumerate(plane)]

    def cond_core():
        arrive("cond plane")
        waits["cond core"] = [misc.start(slot + 9 + n_z, cond_all.at[t], cond_all.at[t], core)]

    chores.extend([along_line, None, over_plane, None, products, None, cond_plane, None, cond_core])

    while step[0] < pieces + 2 * n_z or chores:
        pump(1)
    while passes:
        pass_along(*passes.pop(0))
    arrive("cond core")
    mine = pl.ds(pl.multiple_of(2 * n_z * t, 2 * n_z), 2 * n_z)
    o_cond[...] = cat([cond_all[ti, ck, mine, :] for ti in (0, 1) for ck in range(4)], 1)

    arrive("vec")
    if n_hi == 1:
        vec_squares = o_vec[0] * o_vec[0] + o_vec[1] * o_vec[1]
        first_row = lax.broadcasted_iota(jnp.int32, (8, LANES), 0) == 0
        for j in range(8):
            row = jnp.sum(mods(j), axis=0, keepdims=True)
            for k in range(cols // LANES):
                part = row[:, k * LANES:(k + 1) * LANES]
                vec_squares = vec_squares + jnp.where(first_row, part * part, 0.0)
        slot = slot + 10 + n_z
        norm_plane[c] = norm[...] + jnp.where((f == 0) & (c == 0), vec_squares, 0.0)
        copies = [misc.start(slot + d, norm_plane.at[c], norm_plane.at[c], target) for d, target in enumerate(plane)]
        for copy in copies:
            copy.wait_recv()
        norm_line[t, z] = (norm_plane[0] + norm_plane[1]) + (norm_plane[2] + norm_plane[3])
        copies = [misc.start(slot + 3 + d, norm_line.at[t, z], norm_line.at[t, z], target)
                  for d, target in enumerate([core] + zs + other_line)]
        for copy in copies:
            copy.wait_recv()
        total = norm_line[0, 0]
        for ti in (0, 1):
            for zi in range(n_z):
                if ti + zi > 0:
                    total = total + norm_line[ti, zi]
        total = jnp.sum(jnp.sum(total, axis=0, keepdims=True), axis=1, keepdims=True)
        o_norm[...] = jnp.broadcast_to(jnp.sqrt(total), o_norm.shape)
    else:
        o_norm[...] = jnp.zeros_like(o_norm)
    for p in range(pieces):
        four[p].wait_recv()
    for p in range(pieces):
        for s in range(n_z):
            @pl.when(z == s)
            def _():
                if s < last:
                    right_copy(p, s).wait_send()
                if s > 0:
                    left_copy(p, s).wait_send()
    chain.finish()
    rs.finish()
    misc.finish()


def backward(operands, n_z, n_ff, n_hi):
    n_in, n_out = 3 + n_ff, 1 + n_ff
    here, width = n_z * LANES, 8 * LANES
    half, full = 2 * PIECE, 4 * PIECE
    hw, cols = width // 2, width // n_z
    S, V, dma = jax.ShapeDtypeStruct, pltpu.VMEM, pltpu.SemaphoreType.DMA
    any_space, vmem = pl.BlockSpec(memory_space=pl.ANY), pl.BlockSpec(memory_space=pltpu.VMEM)
    piece = operands[12].shape[1]
    rows_out = S((2 * n_z, piece, width), BF16)
    pieces = n_in + n_out
    slots = 24 + 5 * n_z
    return pl.pallas_call(
        functools.partial(backward_kernel, n_z, n_ff, n_hi),
        out_shape=(rows_out, rows_out, S((n_in, 2, LANES, LANES), F32), S((n_out, 2, LANES, LANES), F32),
                   S((2, 2, n_z, 8, cols), F32), S((2, 8, LANES), F32), S((6, LANES, cols), F32), S((2 * n_z, width), F32),
                   S((8, LANES), F32)),
        in_specs=[any_space] * (len(operands) - 5) + [vmem] * 5,
        out_specs=tuple([any_space] * 2 + [vmem] * 7),
        scratch_shapes=[
            V((3, 2, 4, LANES, here), BF16), V((2, here, hw), BF16), V((2, half, width), BF16),
            V((full, here), F32), V((full, here), F32), V((full, here), BF16), V((full, here), BF16),
            V((full, here), BF16), V((full, here), BF16), V((full, here), F32), V((full, LANES), BF16),
            V((full, LANES), BF16), V((2, piece, width), BF16), V((2, piece, width), BF16), V((half, width), F32),
            V((half, width), F32), V((2, half, width), F32), V((half, width), BF16), V((half, width), BF16),
            V((half, width), F32), V((2, half, width), BF16), V((full, here), BF16), V((2, piece, width), BF16),
            V((8, 8, width), F32), V((8, width), F32), V((8, width), F32), V((16, here), F32),
            V((n_z, 8, cols), F32), V((n_z, 8, LANES), F32), V((2, 2, 8, LANES), F32),
            V((8, LANES), F32), V((4, 8, LANES), F32), V((2, n_z, 8, LANES), F32), V((n_z, 4 * n_z, LANES), F32), V((2, 4, 4 * n_z, LANES), F32),
            V((3, 2, 4, LANES, here), BF16), V((2, here, hw), BF16),
            V((n_in, 2, 2, LANES, here), BF16), V((n_out, 2, 2, here, LANES), BF16),
            V((n_in, 2, 2, LANES, here), BF16), V((n_out, 2, 2, here, LANES), BF16),
            V((n_in, 2, LANES, here), BF16), V((n_out, 2, here, LANES), BF16),
            V((n_in, 2, LANES, here + LANES), BF16), V((n_out, 2, here + LANES, LANES), BF16),
            V((n_in, 2, LANES, LANES), F32), V((n_out, 2, LANES, LANES), F32),
            dma((24,)), dma((pieces, 2)), dma((pieces, 6)), dma((pieces, 6)), dma((slots,)), dma((slots,)),
            dma((2, 2)), dma((2, 2)), dma((2, 2, n_z, PARTS)), dma((2, 2, n_z, PARTS)),
        ],
        compiler_params=pltpu.CompilerParams(collective_id=1, has_side_effects=True, vmem_limit_bytes=VMEM_BYTES),
    )(*operands)


def update_kernel(refs_per_kind, *refs):
    (norm, g_vec, w_vec, m_vec, v_vec, g_in, g_ada, g_out, w_in, m_in, v_in, w_out, m_out, v_out, mixed, grads,
     w_vec_new, m_vec_new, v_vec_new, c_vec_new, o_bias,
     w_in_new, m_in_new, v_in_new, c_in_new, w_out_new, m_out_new, v_out_new, c_out_new, o_mixed, o_grads,
     gi, ga, go, wi, mi, vi, ci, wo, mo, vo, co, low, wide, low_out, high, load_sem, store_sem) = refs
    n_seq = mixed.shape[0]
    loads, stores = {}, []

    def load(name, src, dst):
        loads[name] = pltpu.make_async_copy(src, dst, load_sem.at[len(loads)])
        loads[name].start()

    def store(src, dst):
        copy = pltpu.make_async_copy(src, dst, store_sem.at[len(stores)])
        copy.start()
        stores.append(copy)

    load("grads", grads, low.at[1])
    load("mixed", mixed, low.at[0])
    for name, src, dst in (("gi", g_in, gi), ("ga", g_ada, ga), ("wi", w_in, wi), ("mi", m_in, mi), ("vi", v_in, vi),
                           ("go", g_out, go), ("wo", w_out, wo), ("mo", m_out, mo), ("vo", v_out, vo)):
        load(name, src, dst)
    n_all, n_rows, cols = w_in.shape
    n_out = w_out.shape[0]
    factor = (CLIP_NORM / jnp.maximum(norm[0:1, 0:1], CLIP_NORM))
    factor_in = jnp.broadcast_to(factor, (1, cols))
    factor_out = jnp.broadcast_to(factor, (1, w_out.shape[2]))
    loads["grads"].wait()
    for i in range(n_seq):
        high[:, i, :] = low[1, i].astype(F32)
    store(high, o_grads)
    w_vec_new[...], m_vec_new[...], v_vec_new[...], c_vec_new[...] = adam_update(
        w_vec[...], m_vec[...], v_vec[...], g_vec[...], factor_in, RATE_VECTOR, 0.0)
    last = g_vec.shape[0]
    o_bias[...] = g_vec[last - 1:last] * factor_in
    for name in ("gi", "ga", "wi", "mi", "vi"):
        loads[name].wait()
    lead = n_all - ga.shape[0]

    def update(m, grad):
        wi[m], mi[m], vi[m], ci[m] = adam_update(wi[m], mi[m], vi[m], grad, factor_in, RATE_MATRIX, WEIGHT_DECAY)

    def lead_rows(m, carry):
        update(m, cat([gi[m, 0], gi[m, 1]], 1))
        return carry

    def ada_rows(m, carry):
        update(lead + m, ga[m])
        return carry

    for lo, hi, body, shift in ((0, lead, lead_rows, 0), (0, n_all - lead, ada_rows, lead)):
        lax.fori_loop(lo, hi, body, 0)
        at = pl.ds(shift, hi)
        for src, dst in ((wi, w_in_new), (mi, m_in_new), (vi, v_in_new), (ci, c_in_new)):
            store(src.at[at], dst.at[at])
    for name in ("go", "wo", "mo", "vo"):
        loads[name].wait()
    for m in range(n_out):
        grad = cat([go[m, 0], go[m, 1]], 0)
        wo[m], mo[m], vo[m], co[m] = adam_update(wo[m], mo[m], vo[m], grad, factor_out, RATE_MATRIX, WEIGHT_DECAY)
    for src, dst in ((wo, w_out_new), (mo, m_out_new), (vo, v_out_new), (co, c_out_new)):
        store(src, dst)
    loads["mixed"].wait()
    for i in range(n_seq):
        wide[:, i, :] = low[0, i].astype(F32)
    low_out[...] = wide[...].astype(BF16)
    store(low_out, o_mixed)
    for copy in stores:
        copy.wait()


def update(small, large, rows_low):
    S, V, dma = jax.ShapeDtypeStruct, pltpu.VMEM, pltpu.SemaphoreType.DMA
    any_space, vmem = pl.BlockSpec(memory_space=pl.ANY), pl.BlockSpec(memory_space=pltpu.VMEM)
    w_vec = small[2]
    g_in, g_ada, g_out, w_in, w_out = large[0], large[1], large[2], large[3], large[6]
    kinds = [S(a.shape, F32) for a in (w_vec, w_in, w_out)]
    news = [[k] * 3 + [S(k.shape, BF16)] for k in kinds]
    n_seq, piece, width = rows_low[0].shape
    turned = (piece, n_seq, width)
    return pl.pallas_call(
        functools.partial(update_kernel, 4),
        out_shape=tuple(news[0] + [S((1, w_vec.shape[1]), F32)] + news[1] + news[2] + [S(turned, BF16), S(turned, F32)]),
        in_specs=[vmem] * len(small) + [any_space] * (len(large) + 2),
        out_specs=tuple([vmem] * 5 + [any_space] * 10),
        scratch_shapes=[
            V(g_in.shape, F32), V(g_ada.shape, F32), V(g_out.shape, F32),
            V(w_in.shape, F32), V(w_in.shape, F32), V(w_in.shape, F32), V(w_in.shape, BF16),
            V(w_out.shape, F32), V(w_out.shape, F32), V(w_out.shape, F32), V(w_out.shape, BF16),
            V((2,) + rows_low[0].shape, BF16), V(turned, F32), V(turned, BF16), V(turned, F32), dma((11,)), dma((16,)),
        ],
        compiler_params=pltpu.CompilerParams(vmem_limit_bytes=VMEM_BYTES),
    )(*small, *large, *rows_low)


def per_device(n_f, n_c, n_z, tokens, cotangent, class_table, labels, scale_ids, in_weight, in_first, in_second,
               out_weight, out_first, out_second, vectors, vec_first, vec_second):
    n_hi = n_f // 2
    f, c, z, t, x, y = place()
    seqs, piece, width = tokens.shape
    cols = in_weight.shape[2]
    n_ff = out_weight.shape[0] - 1
    ada = 3 + n_ff
    half = cols // 2
    pairs = [[2 * i, 2 * i + 1] for i in range(n_hi)]
    his = [[i + 2 * j for j in range(n_hi)] for i in range(2)]

    def into(a):
        if n_hi == 1:
            return a
        shape = a.shape[:-1]
        return jnp.swapaxes(a.reshape(shape + (n_hi, 2 * n_c, -1)), -3, -2).reshape(a.shape)

    def back(a):
        if n_hi == 1:
            return a
        shape = a.shape[:-1]
        return jnp.swapaxes(a.reshape(shape + (2 * n_c, n_hi, -1)), -3, -2).reshape(a.shape)

    in_weight, in_first, in_second = [a.transpose(1, 0, 2) for a in (in_weight, in_first, in_second)]
    in_low, out_low = in_weight, out_weight
    if n_hi > 1:
        in_low = lax.all_gather(in_low.astype(BF16), "fsdp", axis=1, tiled=True, axis_index_groups=his).astype(F32)
        out_low = lax.all_gather(out_low.astype(BF16), "fsdp", axis=2, tiled=True, axis_index_groups=his).astype(F32)
    rows = in_low.shape[1]

    def two_seqs(a):
        return lax.dynamic_slice_in_dim(a, 2 * z, 2, 0)

    ids = jnp.pad(two_seqs(scale_ids), ((0, 0), (0, PIECE - piece)), constant_values=10).astype(BF16)
    ids = jnp.broadcast_to(ids[:, :, None], ids.shape + (LANES,))
    conditions = class_table.at[labels].get(mode="promise_in_bounds")
    cond_act = jax.nn.silu(conditions).astype(BF16)
    act = into(cond_act).reshape(n_z, 2, width).transpose(1, 0, 2).reshape(2 * n_z, width).astype(F32)
    *kept, vec_all, act_rows = forward(
        in_low, out_low, two_seqs(into(tokens)), two_seqs(into(cotangent)), ids, act, vectors, n_z, n_hi)
    big, small = kept[:-3], kept[-3:]
    mixed, grad_low, g_in, g_out, d_mod, g_vec, g_ada, cond_sum, norm = backward(
        big + [in_low] + small + [vec_all, act_rows], n_z, n_ff, n_hi)
    mod_sum = jnp.sum(d_mod.reshape(4 * n_z, 8, cols), axis=0)
    g_vec = jnp.concatenate([mod_sum[:6], g_vec.transpose(1, 0, 2).reshape(8, cols), mod_sum[6:]])
    if n_hi > 1:
        g_vec = lax.psum(g_vec, "fsdp", axis_index_groups=his)
        g_in = lax.psum_scatter(g_in, "fsdp", scatter_dimension=2, tiled=True, axis_index_groups=his)
        g_ada = lax.psum_scatter(g_ada, "fsdp", scatter_dimension=1, tiled=True, axis_index_groups=his)
        g_out = lax.psum_scatter(g_out, "fsdp", scatter_dimension=3, tiled=True, axis_index_groups=his)
        squares = jnp.sum(g_in * g_in) + jnp.sum(g_ada * g_ada) + jnp.sum(g_out * g_out)
        squares = squares + jnp.where((f == 0) & (c == 0), jnp.sum(g_vec * g_vec), 0.0)
        norm = jnp.broadcast_to(jnp.sqrt(lax.psum(squares, ("fsdp", "ctx", "tp"))), norm.shape)
    *news, mixed, input_grad = update(
        [norm, g_vec, vectors, vec_first, vec_second],
        [g_in, g_ada, g_out, in_weight, in_first, in_second, out_weight, out_first, out_second], [mixed, grad_low])
    bias_grad = news.pop(4)
    mixed = mixed.transpose(1, 0, 2)
    vec_new, in_new, out_new = news[:4], [a.transpose(1, 0, 2) for a in news[4:8]], news[8:]
    input_grad = input_grad.transpose(1, 0, 2)
    cond_sum = back(cond_sum).reshape(2, n_z, width).transpose(1, 0, 2).reshape(2 * n_z, width)
    unused, silu_pull = jax.vjp(jax.nn.silu, conditions)
    condition_grad = silu_pull(cond_sum)[0]
    return (back(mixed), back(input_grad), condition_grad, norm[0, 0], *in_new, *out_new, *vec_new, bias_grad[0])


def solution(mesh):
    in_matrix = P(("fsdp", "ctx"), None, "tp")
    out_matrix = P(None, "tp", ("fsdp", "ctx"))
    vector = P(None, "tp")
    rows = P("fsdp", "ctx", None)
    return jax.shard_map(
        functools.partial(per_device, mesh.shape["fsdp"], mesh.shape["ctx"], mesh.shape["tp"]),
        mesh=mesh,
        in_specs=(rows, rows, P(), P("fsdp"), P("fsdp", "ctx"), in_matrix, in_matrix, in_matrix,
                  out_matrix, out_matrix, out_matrix, vector, vector, vector),
        out_specs=(rows, rows, P("fsdp", None), P(), in_matrix, in_matrix, in_matrix, in_matrix,
                   out_matrix, out_matrix, out_matrix, out_matrix, vector, vector, vector, vector, P("tp")),
        check_vma=False,
    )
```

```python
import functools
import math

import jax
import jax.numpy as jnp
from jax import lax
from jax.experimental import pallas as pl
from jax.experimental.pallas import tpu as pltpu
from jax.sharding import PartitionSpec as P

HD = 64
STEP = 5
PRECISE = lax.Precision.HIGHEST
NORM_EPS = 1e-06
CLIP_NORM = 1.0
BETA_ONE = 0.5
BETA_TWO = 0.5
RATE_MATRIX = 0.03
RATE_VECTOR = 0.3
WEIGHT_DECAY = 0.05
ADAM_EPS = 1e-08

MESH = pl.DeviceIdType.MESH
F32 = jnp.float32
BF16 = jnp.bfloat16
LANES = 128
VMEM_BYTES = 60 * 2**20


def place():
    f = lax.axis_index("fsdp")
    c = lax.axis_index("ctx")
    z = lax.axis_index("tp")
    return f, c, z, lax.rem(f, 2), lax.rem(c, 2), c // 2


def partners(n_z):
    f, c, z, t, x, y = place()
    core = (f + 1 - 2 * t, c, z)
    xp = (f, 2 * y + (1 - x), z)
    yp = (f, 2 * (1 - y) + x, z)
    zs = [(f, c, lax.rem(z + d, n_z)) for d in range(1, n_z)]
    return core, xp, yp, zs


def enter(targets):
    barrier = pltpu.get_barrier_semaphore()
    for target in targets:
        pl.semaphore_signal(barrier, inc=1, device_id=target, device_id_type=MESH)
    pl.semaphore_wait(barrier, len(targets))


def lanes_at(index):
    return pl.ds(pl.multiple_of(index * LANES, LANES), LANES)


def adam_update(master, first, second, grad, factor, rate, decay):
    grad = grad * factor
    first = BETA_ONE * first + (1.0 - BETA_ONE) * grad
    second = BETA_TWO * second + (1.0 - BETA_TWO) * grad * grad
    fix_one = 1.0 - BETA_ONE**STEP
    fix_two = 1.0 - BETA_TWO**STEP
    stride = first / fix_one / (jnp.sqrt(second / fix_two) + ADAM_EPS)
    master = master - rate * (stride + decay * master)
    return (master, first, second, master.astype(BF16))


def dot(a, b, dims):
    return lax.dot_general(a, b, (dims, ((), ())), preferred_element_type=F32)


NN = ((1,), (0,))
NT = ((1,), (1,))
TN = ((0,), (0,))


PIECE = 176
NEG = -1e30
PLANE_FIRST = (10, 11)
EXTRA_EVERY = 2
EXTRA_FROM = 2
AHEAD = 2
TICKS = (2, 2, 2, 2, 1, 0, 2, 1, 2, 1, 1, 0, 0, 3, 0, 1, 0, 1, 2, 2, 2, 1)
PARTS = 4
PASSES = 3
LOOK = 3
UNROLL = 2


def cat(parts, axis):
    return jnp.concatenate(parts, axis=axis)


def lane_of(shape):
    return lax.broadcasted_iota(jnp.int32, shape, len(shape) - 1)


def split_two(values):
    high = values.astype(BF16)
    return high, (values - high.astype(F32)).astype(BF16)


def split_three(values):
    high = values.astype(BF16)
    rest = values - high.astype(F32)
    middle = rest.astype(BF16)
    return high, middle, (rest - middle.astype(F32)).astype(BF16)


def head_mean(values):
    row = lax.broadcasted_iota(jnp.int32, (LANES, LANES), 0) // HD
    ones = jnp.where(row == lane_of((LANES, LANES)) // HD, 1.0 / HD, 0.0).astype(BF16)
    out = []
    for k in range(values.shape[1] // LANES):
        high, lower = split_two(values[:, k * LANES:(k + 1) * LANES])
        out.append(dot(high, ones, NN) + dot(lower, ones, NN))
    return cat(out, 1)


def gelu_both(u):
    k0, k1 = 0.7978845608028654, 0.044715
    square = u * u
    th = jnp.tanh(k0 * u * (1.0 + k1 * square))
    half = 0.5 * (1.0 + th)
    slope = half + 0.5 * u * (1.0 - th * th) * (k0 * (1.0 + 3.0 * k1 * square))
    return u * half, slope


def step_rows(piece, body):
    for p in (0, 1):
        def one(i, carry, p=p):
            start = pl.multiple_of(i * 16, 16)
            body(pl.ds(start, 16), pl.ds(pl.multiple_of(p * PIECE + start, 16), 16), p)
            return carry
        lax.fori_loop(0, piece // 16, one, 0, unroll=UNROLL)
        if piece % 16:
            start = piece // 16 * 16
            body(pl.ds(start, piece % 16), pl.ds(p * PIECE + start, piece % 16), p)


def clear_tail(ref, t):
    for p in (0, 1):
        ref[t, pl.ds(p * PIECE + PIECE - 16, 16), :] = jnp.zeros((16, ref.shape[2]), ref.dtype)


def normalize(values):
    center = values - jnp.mean(values, axis=-1, keepdims=True)
    scale = lax.rsqrt(jnp.mean(center * center, axis=-1, keepdims=True) + NORM_EPS)
    return center * scale, scale


def reorder(rows, n_hi, inverse=False):
    if n_hi == 1:
        return rows
    width = rows.shape[1]
    each = width // (8 * n_hi)
    out = []
    for k in range(width // LANES):
        at = k * LANES + lax.broadcasted_iota(jnp.int32, (width, LANES), 1)
        there = lax.broadcasted_iota(jnp.int32, (width, LANES), 0)
        if inverse:
            wanted = (at // each % 8) * (n_hi * each) + (at // (8 * each)) * each + at % each
        else:
            wanted = (at // each % n_hi) * (8 * each) + (at // (each * n_hi)) * each + at % each
        order = jnp.where(there == wanted, 1.0, 0.0).astype(BF16)
        out.append(sum(dot(part, order, NN) for part in split_three(rows)))
    return cat(out, 1)


class Wire:
    def __init__(self, send_sem, recv_sem):
        self.send_sem, self.recv_sem, self.sent = send_sem, recv_sem, []

    def make(self, at, src, dst, target, to=None):
        return pltpu.make_async_remote_copy(
            src_ref=src, dst_ref=dst, send_sem=self.send_sem.at[at], recv_sem=self.recv_sem.at[at if to is None else to],
            device_id=target, device_id_type=MESH)

    def start(self, at, src, dst, target, to=None):
        copy = self.make(at, src, dst, target, to)
        copy.start()
        self.sent.append(copy)
        return copy

    def finish(self):
        for copy in self.sent:
            copy.wait_send()


def forward_kernel(n_z, n_ff, n_hi, *refs):
    n_in, n_out = 3 + n_ff, 1 + n_ff
    (x_in, x_out, tok, cot, ids, act, vec,
     x_wq, x_wo, x_h1, x_qr, x_kr, x_q8, x_kh, x_v, x_o, x_lse, x_ma, x_mb, x_tok, x_cot, x_attn, x_mid,
     x_fown, x_fsend, x_down, x_dsend, x_gin, x_gout, x_mod, x_gu, x_gf, x_vec, x_act,
     g_in, g_out, tokb, cotb, idb, actb, pm, pr, ps, pf, vz, h1, gf, h2, qr, kr, q8, kh, vv, oo, lse, ma, mb,
     at_send, at_recv, attn, mid, facc, dacc, fsend, dsend, gin, gout, act_low, slope,
     full_in, full_out, low_in, low_out, local_sem, ag_send, ag_recv, m_send, m_recv, out_sem, tok_sem, load_sem) = refs
    f, c, z, t, x, y = place()
    core, xp, yp, zs = partners(n_z)
    f_base = f - t

    piece = tok.shape[1]
    n_all = x_in.shape[0]
    order = [("i", 0), ("i", 1), ("i", 2), ("o", 0)]
    for r in range(n_ff):
        order += [("i", 3 + r), ("o", 1 + r)]
    loads = {}
    for kind, m in [("i", j) for j in range(n_in, n_all)] + order:
        src, dst, at = (x_in, full_in, m) if kind == "i" else (x_out, full_out, n_all + m)
        loads[kind, m] = pltpu.make_async_copy(src.at[m], dst.at[m], load_sem.at[at])
        loads[kind, m].start()
    for ref in (h1, gf, h2):
        clear_tail(ref, t)

    barrier = pltpu.get_barrier_semaphore()
    plane = [xp, yp, (f, 3 - c, z)]
    other_line = [(f + 1 - 2 * t, c, target[2]) for target in zs]
    for target in [core] + plane + zs + other_line:
        pl.semaphore_signal(barrier, inc=1, device_id=target, device_id_type=MESH)
    loops = (y == t) & (x == t)
    for xs in (0, 1):
        @pl.when(jnp.logical_not(loops & (x == xs)))
        def _():
            pl.semaphore_signal(barrier, inc=1, device_id=(f_base + x, 2 * t + xs, z), device_id_type=MESH)
    pl.semaphore_wait(barrier, 4 + 2 * n_z - jnp.where(loops, 1, 0))

    ag = Wire(ag_send, ag_recv)
    misc = Wire(m_send, m_recv)

    shares = [(tok, tokb), (cot, cotb), (ids, None)]

    def send_share(j):
        src, dst = shares[j]
        for yd in (0, 1):
            own = loops & (y == yd)
            from_here = src.at[yd]
            to_there = dst.at[x] if dst is not None else idb.at[2 * y + x]

            @pl.when(own)
            def _():
                pltpu.make_async_copy(from_here, to_there, tok_sem.at[1, j, x]).start()

            @pl.when(jnp.logical_not(own))
            def _():
                pltpu.make_async_remote_copy(
                    src_ref=from_here, dst_ref=to_there, send_sem=tok_sem.at[0, j, yd], recv_sem=tok_sem.at[1, j, x],
                    device_id=(f_base + y, 2 * yd + t, z), device_id_type=MESH).start()

    def got_share(j):
        dst = shares[j][1]
        for xs in (0, 1):
            ref = dst.at[xs] if dst is not None else idb.at[2 * t + xs]
            pltpu.make_async_copy(ref, ref, tok_sem.at[1, j, xs]).wait()

    act_copy = misc.start(0, act.at[:, lanes_at((1 - t) * 4 + c)], actb.at[1], core)
    vec_local = pltpu.make_async_copy(vec, vz.at[z], local_sem.at[n_in + n_out])
    vec_local.start()
    vec_copies = [misc.start(1 + d, vec, vz.at[z], target) for d, target in enumerate(zs)]
    zrows = pl.ds(pl.multiple_of(z * LANES, LANES), LANES)
    first, zcopies, one, two = {}, {}, {}, {}

    def prepare(p):
        if p in first:
            return
        kind, m = order[p]
        loads[kind, m].wait()
        if kind == "i":
            dst = g_in.at[m, t, c, :, lanes_at(z)]
            for s in (0, 1):
                low_in[m, s] = full_in[m, :, s * LANES:(s + 1) * LANES].astype(BF16)
            mine, other = low_in.at[m, t], low_in.at[m, 1 - t]
        else:
            dst = g_out.at[m, t, zrows, lanes_at(c)]
            for s in (0, 1):
                low_out[m, s] = full_out[m, s * LANES:(s + 1) * LANES, :].astype(BF16)
            mine, other = low_out.at[m, t], low_out.at[m, 1 - t]
        local = pltpu.make_async_copy(mine, dst, local_sem.at[p])
        local.start()
        first[p] = (local, ag.start((p, 0), other, dst, core))

    base = n_z

    def start_zero(p):
        if p >= len(order) or p in zcopies or p in PLANE_FIRST:
            return
        kind, m = order[p]
        prepare(p)
        first[p][0].wait()
        first[p][1].wait_recv()
        block = g_in.at[m, :, c, :, lanes_at(z)] if kind == "i" else g_out.at[m, :, zrows, lanes_at(c)]
        zcopies[p] = [ag.start((p, 1 + d), block, block, target) for d, target in enumerate(zs)]

    line_first = [p for p in range(len(order)) if p not in PLANE_FIRST]

    def x_first(p):
        return line_first.index(p) % 2 == 0

    def start_one(p):
        kind, m = order[p]
        for copy in zcopies[p]:
            copy.wait_recv()
        block = g_in.at[m, :, c] if kind == "i" else g_out.at[m, :, :, lanes_at(c)]
        one[p] = ag.start((p, base), block, block, xp if x_first(p) else yp)

    def start_two(p):
        kind, m = order[p]
        one[p].wait_recv()
        held = (2 * y, 2 * y + 1) if x_first(p) else (x, 2 + x)
        two[p] = []
        if kind == "i" and x_first(p):
            block = g_in.at[m, :, pl.ds(2 * y, 2)]
            two[p].append(ag.start((p, base + 1), block, block, yp))
        else:
            for k, at in enumerate(held):
                block = g_in.at[m, :, at] if kind == "i" else g_out.at[m, :, :, lanes_at(at)]
                two[p].append(ag.start((p, base + 1 + k), block, block, yp if x_first(p) else xp))

    extras = []

    def start_plane(p):
        kind, m = order[p]
        prepare(p)
        first[p][0].wait()
        first[p][1].wait_recv()
        block = g_in.at[m, :, c, :, lanes_at(z)] if kind == "i" else g_out.at[m, :, zrows, lanes_at(c)]
        one[p] = [ag.start((p, base + k), block, block, target) for k, target in enumerate(plane)]
        two[p] = []

    def start_line(p, ck):
        kind, m = order[p]
        if ck == 0:
            for copy in one[p]:
                copy.wait_recv()
        block = g_in.at[m, :, ck, :, lanes_at(z)] if kind == "i" else g_out.at[m, :, zrows, lanes_at(ck)]
        for d, target in enumerate(zs):
            two[p].append(ag.start((p, base + 3 + 3 * ck + d), block, block, target))

    for p in PLANE_FIRST:
        extras.append((start_plane, (p,)))
    for p in PLANE_FIRST:
        extras += [(start_line, (p, ck)) for ck in range(4)]
    ticks = [(start_one, line_first[0])]
    for p, before in zip(line_first[1:], line_first[:-1]):
        ticks += [(start_one, p), (start_two, before)]
    ticks.append((start_two, line_first[-1]))
    ticked = [0]

    def tick(n=1):
        for _ in range(n):
            if ticks:
                step, p = ticks.pop(0)
                if step is start_one:
                    for ahead in range(p + AHEAD):
                        start_zero(ahead)
                step(p)
            ticked[0] += 1
            if extras and ticked[0] >= EXTRA_FROM and ticked[0] % EXTRA_EVERY == 0:
                step, what = extras.pop(0)
                step(*what)

    def arrived(p):
        while p not in two or (p in PLANE_FIRST and any(what[0] == p for unused, what in extras)):
            tick()
        for copy in two[p]:
            copy.wait_recv()

    flushed = []

    def flush(src, dst):
        copy = pltpu.make_async_copy(src, dst, out_sem.at[len(flushed)])
        copy.start()
        flushed.append(copy)

    prepare(0)
    prepare(1)
    act_copy.wait_recv()
    cols = vec.shape[1]
    for j in range(n_in, n_all):
        loads["i", j].wait()
    own_at = lanes_at(t * 4 + c)
    mine = act[:, own_at]
    theirs = actb[1]
    pm[...] = jnp.zeros_like(pm)
    seqs = 2 * n_z
    for s in (0, 1):
        rows = jnp.where(t == s, mine, theirs)
        x_act[seqs * s:seqs * (s + 1), :] = rows
        for j in range(n_all - n_in):
            pm[seqs * s:seqs * (s + 1), j, :] = dot(rows.astype(BF16), full_in[n_in + j].astype(BF16), NN)

    def of_chip(xx, yy):
        return pm.at[pl.ds(seqs * xx + n_z * yy, n_z)]

    mod_copies = [misc.start(1 + n_z + k, of_chip(xx, yy), pr.at[k], target)
                  for k, (target, (xx, yy)) in enumerate(zip(plane, [(1 - x, y), (x, 1 - y), (1 - x, 1 - y)]))]
    send_share(0)
    send_share(2)
    start_zero(0)
    for copy in mod_copies:
        copy.wait_recv()
    ps[...] = (of_chip(x, y)[...] + pr[0]) + (pr[1] + pr[2])
    pf[t, z] = ps[z]
    mod_copies = [misc.start(4 + n_z + k, ps.at[target[2]], pf.at[t, z], target)
                  for k, target in enumerate([core] + zs + other_line)]
    start_zero(1)
    for p in range(2, len(order)):
        prepare(p)
    tick()
    for copy in mod_copies + vec_copies:
        copy.wait_recv()
    vec_local.wait()
    row = lax.broadcasted_iota(jnp.int32, (8, cols), 0)
    for zi in range(n_z):
        bias = jnp.where(row < 6, vz[zi, 0:8, :], 0.0)
        x_mod[:, zi * cols:(zi + 1) * cols] = pf[0, zi] + pf[1, zi] + bias
    x_mod[...] = reorder(x_mod[...], n_hi)
    x_vec[...] = vz[...]
    tick()

    def wide(k):
        return cat([vz[zi, k:k + 1, :] for zi in range(n_z)], 1)

    def narrow(k):
        return cat([vz[zi, k:k + 1, lanes_at(t)] for zi in range(n_z)], 1)

    got_share(0)
    got_share(2)
    half = 2 * PIECE
    full = 2 * half
    mine_ids = idb.at[pl.ds(2 * t, 2)]
    id_copy = misc.start(4 + 3 * n_z, mine_ids, mine_ids, core)
    flush(tokb, x_tok)

    def first_norm(rows, at, p):
        normed, unused = normalize(tokb[p, rows, :].astype(F32))
        h1[t, at, :] = (normed * (1.0 + x_mod[1:2, :]) + x_mod[2:3, :]).astype(BF16)
    step_rows(piece, first_norm)
    h1_copy = misc.start(5 + 3 * n_z, h1.at[t], h1.at[t], core)

    tick(TICKS[0])
    id_copy.wait_recv()
    lanes = lane_of((full, LANES)) % HD
    scale = idb[...].reshape(full, LANES).astype(F32)
    feature = lanes.astype(F32)
    ma[...] = jnp.where((lanes < 16) & (feature > scale), 1.0, 0.0).astype(BF16)
    mb[...] = jnp.where((lanes < 16) & (feature == scale), NEG, 0.0).astype(BF16)
    flush(ma, x_ma)
    flush(mb, x_mb)
    tick(TICKS[1])
    h1_copy.wait_recv()

    def whole(ref):
        return ref[...].reshape(full, ref.shape[-1])

    def w_in(m):
        return g_in[m].reshape(8 * LANES, n_z * LANES)

    arrived(0)
    qr[...] = dot(whole(h1), w_in(0), NN) + narrow(6)
    q8[...] = (qr[...] * lax.rsqrt(head_mean(qr[...] * qr[...]) + NORM_EPS) * narrow(8)).astype(BF16) * 0.125
    tick(TICKS[2])
    arrived(1)
    kr[...] = dot(whole(h1), w_in(1), NN)
    kh[...] = (kr[...] * lax.rsqrt(head_mean(kr[...] * kr[...]) + NORM_EPS) * narrow(9)).astype(BF16)
    flush(qr, x_qr)
    flush(kr, x_kr)
    flush(q8, x_q8)
    flush(kh, x_kh)
    tick(TICKS[3])
    send_share(1)
    arrived(2)
    vv[...] = (dot(whole(h1), w_in(2), NN) + narrow(7)).astype(BF16)
    flush(vv, x_v)
    flush(h1, x_h1)
    flush(g_in.at[pl.ds(0, 3)], x_wq)
    def attend(i, carry):
        at = lanes_at(i)
        q2, k2, v2 = q8[:, at], kh[:, at], vv[:, at]
        mine_a, mine_b = ma[...], mb[...]
        low = lane_of((full, LANES)) < HD
        outs, tops = [], []
        for h in (0, 1):
            here = low if h == 0 else jnp.logical_not(low)
            s = dot(jnp.where(here, q2, mine_a), jnp.where(here, k2, mine_b), NT)
            top = jnp.max(s, axis=1, keepdims=True)
            e = jnp.exp(s - top).astype(BF16)
            got = dot(e, jnp.where(here, v2, jnp.ones_like(v2)), NN)
            total = got[:, HD:HD + 1] if h == 0 else got[:, 0:1]
            outs.append(got / total)
            tops.append(top + jnp.log(total))
        oo[:, at] = jnp.where(low, outs[0], outs[1]).astype(BF16)
        lse[:, at] = jnp.where(low, tops[0], tops[1])
        return carry

    pairs = n_z * LANES // LANES
    done = 0
    for i in range(pairs):
        tick(TICKS[4 + i])
        if i + 1 == pairs or TICKS[5 + i]:
            lax.fori_loop(done, i + 1, attend, 0)
            done = i + 1
    flush(oo, x_o)
    flush(lse, x_lse)

    arrived(3)
    flush(g_out.at[0], x_wo)
    width = 8 * LANES
    hw = width // 2
    for j in (0, 1):
        both = dot(oo[...], g_out[0, j], NN)
        attn[:, j * hw:(j + 1) * hw] = jnp.where(t == 0, both[:half], both[half:])
        at_send[:, j * hw:(j + 1) * hw] = jnp.where(t == 0, both[half:], both[:half]).astype(BF16)
    at_copy = misc.start(7 + 3 * n_z, at_send, at_recv, core)
    tick(TICKS[8])
    at_copy.wait_recv()
    proj_bias = reorder(wide(10 + n_ff), n_hi)


    def second_norm(rows, at, p):
        total = attn[at, :] + at_recv[at, :].astype(F32) + proj_bias
        attn[at, :] = total
        middle = tokb[p, rows, :].astype(F32) + x_mod[0:1, :] * total
        mid[at, :] = middle
        normed, unused = normalize(middle)
        h2[t, at, :] = (normed * (1.0 + x_mod[4:5, :]) + x_mod[5:6, :]).astype(BF16)
    step_rows(piece, second_norm)
    h2_copy = misc.start(8 + 3 * n_z, h2.at[t], h2.at[t], core)
    flush(attn, x_attn)
    flush(mid, x_mid)
    got_share(1)
    flush(cotb, x_cot)

    def gate(rows, at, p):
        gf[t, at, :] = (cotb[p, rows, :].astype(F32) * x_mod[3:4, :]).astype(BF16)
    step_rows(piece, gate)
    gf_copy = misc.start(6 + 3 * n_z, gf.at[t], gf.at[t], core)

    tick(TICKS[9])
    h2_copy.wait_recv()
    gf_copy.wait_recv()
    x_gf[...] = jnp.zeros_like(x_gf)
    x_gf[0:1, :] = jnp.sum(whole(gf).astype(F32), axis=0, keepdims=True)
    x_gu[...] = jnp.zeros_like(x_gu)

    for r in range(n_ff):
        arrived(4 + 2 * r)
        bias_row = narrow(10 + r)
        u = dot(whole(h2), w_in(3 + r), NN) + bias_row
        value, gradient = gelu_both(u)
        act_low[...] = value.astype(BF16)
        slope[...] = gradient
        tick(TICKS[10 + 3 * r])
        for j in (0, 1):
            gout[r, j] = dot(act_low[...], gf[:, :, j * hw:(j + 1) * hw].reshape(full, hw), TN).astype(BF16)
        flush(gout.at[r], x_gout.at[r])
        arrived(5 + 2 * r)
        for j in (0, 1):
            part = dot(act_low[...], g_out[1 + r, j], NN)
            cols_here = pl.ds(j * hw, hw)
            facc[:, cols_here] = part if r == 0 else facc[:, cols_here] + part
        back_act = (dot(gf[:, :, :hw].reshape(full, hw), g_out[1 + r, 0], NT)
                    + dot(gf[:, :, hw:].reshape(full, hw), g_out[1 + r, 1], NT))
        gu = (back_act * slope[...]).astype(BF16)
        act_low[...] = gu
        tick(TICKS[11 + 3 * r])
        x_gu[r:r + 1, :] = jnp.sum(gu.astype(F32), axis=0, keepdims=True)
        gin[r] = dot(whole(h2), act_low[...], TN).astype(BF16).reshape(gin.shape[1:])
        flush(gin.at[r], x_gin.at[r])
        tick(TICKS[12 + 3 * r])
        part = dot(act_low[...], w_in(3 + r), NT)
        dacc[...] = part if r == 0 else dacc[...] + part

    assert not ticks and not extras
    mine_rows = pl.ds(pl.multiple_of(t * half, half), half)
    other_rows = pl.ds(pl.multiple_of((1 - t) * half, half), half)
    fsend[...] = facc[other_rows, :].astype(BF16)
    dsend[...] = dacc[other_rows, :].astype(BF16)
    flush(facc.at[mine_rows], x_fown)
    flush(fsend, x_fsend)
    flush(dacc.at[mine_rows], x_down)
    flush(dsend, x_dsend)
    for copy in flushed:
        copy.wait()
    for j, (src, dst) in enumerate(shares):
        for yd in (0, 1):
            @pl.when(jnp.logical_not(loops & (y == yd)))
            def _():
                ref = src.at[yd]
                pltpu.make_async_remote_copy(
                    src_ref=ref, dst_ref=ref, send_sem=tok_sem.at[0, j, yd], recv_sem=tok_sem.at[1, j, x],
                    device_id=(f_base + y, 2 * yd + t, z), device_id_type=MESH).wait_send()
    ag.finish()
    misc.finish()


def forward(x_in, x_out, tok, cot, ids, act, vec, n_z, n_hi):
    n_out = x_out.shape[0]
    n_ff = n_out - 1
    n_in = 3 + n_ff
    pieces = n_in + n_out
    here, width = n_z * LANES, 8 * LANES
    half, full = 2 * PIECE, 4 * PIECE
    piece = tok.shape[1]
    hw = width // 2
    S = jax.ShapeDtypeStruct
    wide_low, wide_full = S((half, width), BF16), S((half, width), F32)
    cols_low, cols_full = S((full, here), BF16), S((full, here), F32)
    mask = S((full, LANES), BF16)
    big = [
        S((3, 2, 4, LANES, here), BF16), S((2, here, hw), BF16), S((2, half, width), BF16), cols_full, cols_full,
        cols_low, cols_low, cols_low, cols_low, cols_full, mask, mask, S((2, piece, width), BF16),
        S((2, piece, width), BF16), wide_full, wide_full, wide_full, wide_low, wide_full, wide_low,
        S((n_ff, 2, 4, LANES, here), BF16), S((n_ff, 2, here, hw), BF16)]
    small = [S((8, width), F32), S((8, here), F32), S((8, width), F32), S((n_z,) + vec.shape, F32), S((4 * n_z, LANES), F32)]
    any_space, vmem = pl.BlockSpec(memory_space=pl.ANY), pl.BlockSpec(memory_space=pltpu.VMEM)
    mod_shape = (8, vec.shape[1])
    V = pltpu.VMEM
    dma = pltpu.SemaphoreType.DMA
    return pl.pallas_call(
        functools.partial(forward_kernel, n_z, n_ff, n_hi),
        out_shape=tuple(big + small),
        in_specs=[any_space] * 5 + [vmem] * 2,
        out_specs=tuple([any_space] * len(big) + [vmem] * len(small)),
        scratch_shapes=[
            V((n_in, 2, 4, LANES, here), BF16), V((n_out, 2, here, hw), BF16),
            V((2, piece, width), BF16), V((2, piece, width), BF16), V((4, PIECE, LANES), BF16),
            V((2, 2 * n_z, LANES), F32), V((4 * n_z,) + mod_shape, F32), V((3, n_z) + mod_shape, F32), V((n_z,) + mod_shape, F32),
            V((2, n_z) + mod_shape, F32), V((n_z,) + vec.shape, F32),
            V((2, half, width), BF16), V((2, half, width), BF16), V((2, half, width), BF16),
            V((full, here), F32), V((full, here), F32), V((full, here), BF16), V((full, here), BF16), V((full, here), BF16),
            V((full, here), BF16), V((full, here), F32), V((full, LANES), BF16), V((full, LANES), BF16),
            V((half, width), BF16), V((half, width), BF16), V((half, width), F32), V((half, width), F32),
            V((full, width), F32), V((full, width), F32), V((half, width), BF16), V((half, width), BF16),
            V((n_ff, 2, 4, LANES, here), BF16), V((n_ff, 2, here, hw), BF16), V((full, here), BF16), V((full, here), F32),
            V(x_in.shape, F32), V(x_out.shape, F32), V((n_in, 2, LANES, LANES), BF16), V((n_out, 2, LANES, LANES), BF16),
            dma((pieces + 1,)), dma((pieces, 4 * n_z + 3)), dma((pieces, 4 * n_z + 3)), dma((9 + 3 * n_z,)), dma((9 + 3 * n_z,)),
            dma((len(big) + 2 * n_ff,)), dma((2, 3, 2)), dma((x_in.shape[0] + n_out,)),
        ],
        compiler_params=pltpu.CompilerParams(collective_id=0, has_side_effects=True, vmem_limit_bytes=VMEM_BYTES),
    )(x_in, x_out, tok, cot, ids, act, vec)

class Guarded:
    def __init__(self):
        self.sent = []

    def start(self, cond, copy):
        @pl.when(cond)
        def _():
            copy.start()
        self.sent.append((cond, copy))

    def finish(self):
        for cond, copy in self.sent:
            @pl.when(cond)
            def _(copy=copy):
                copy.wait_send()


def backward_kernel(n_z, n_ff, n_hi, *refs):
    n_in, n_out = 3 + n_ff, 1 + n_ff
    (x_wq, x_wo, x_h1, x_qr, x_kr, x_q8, x_kh, x_v, x_o, x_lse, x_ma, x_mb, x_tok, x_cot, x_attn, x_mid,
     x_fown, x_fsend, x_down, x_dsend, x_gin, x_gout, x_weight, mod, gu_sum, gf_sum, vz, act,
     o_mixed, o_grad, o_in, o_out, o_vec, o_ada, o_cond, o_norm,
     wq, wo, h1, qr, kr, q8, kh, vv, oo, lse, ma, mb, tokb, cotb, attn, mid, buf, f_recv, d_recv,
     dmid, ga, go, mixed, sums, vd, vdr, vs, vdz, zv, v_all, d_mod, v_half, norm, norm_plane, norm_line, cond_z, cond_all,
     p_full, q_full, p_half, q_half, a_in, a_out, b_in, b_out, z_in, z_out, f_in, f_out,
     load_sem, own_sem, rs_send, rs_recv, m_send, m_recv, t_send, t_recv, g_send, g_recv) = refs
    f, c, z, t, x, y = place()
    core, xp, yp, zs = partners(n_z)
    f_base = f - t
    last = n_z - 1
    half, full = 2 * PIECE, 4 * PIECE
    width = mod.shape[1]
    hw = width // 2
    piece = x_tok.shape[1]
    clear_tail(ga, t)

    barrier = pltpu.get_barrier_semaphore()
    diagonal = (f, 3 - c, z)
    plane = [xp, yp, diagonal]
    other_line = [(f + 1 - 2 * t, c, target[2]) for target in zs]
    for target in [core] + plane + zs + other_line:
        pl.semaphore_signal(barrier, inc=1, device_id=target, device_id_type=MESH)
    loops = (y == t) & (x == t)
    for ys in (0, 1):
        @pl.when(jnp.logical_not(loops & (y == ys)))
        def _():
            pl.semaphore_signal(barrier, inc=1, device_id=(f_base + y, 2 * ys + t, z), device_id_type=MESH)

    loads = {}
    names = [("f", x_fown, buf.at[0]), ("mid", x_mid, mid), ("cot", x_cot, cotb), ("d", x_down, buf.at[1]),
             ("attn", x_attn, attn), ("wo", x_wo, wo), ("o", x_o, oo), ("q", x_q8, q8), ("k", x_kh, kh), ("v", x_v, vv),
             ("lse", x_lse, lse), ("ma", x_ma, ma), ("mb", x_mb, mb), ("qr", x_qr, qr), ("kr", x_kr, kr),
             ("h1", x_h1, h1), ("wq", x_wq, wq), ("tok", x_tok, tokb)]
    for i, (name, src, dst) in enumerate(names):
        loads[name] = pltpu.make_async_copy(src, dst, load_sem.at[i])
        loads[name].start()
    pl.semaphore_wait(barrier, 4 + 2 * n_z - jnp.where(loops, 1, 0))

    rs = Wire(rs_send, rs_recv)
    misc = Wire(m_send, m_recv)
    chain = Guarded()
    f_copy = misc.start(0, x_fsend, f_recv, core)
    d_copy = misc.start(1, x_dsend, d_recv, core)

    order = []
    for r in range(n_ff):
        order += [("i", 3 + r), ("o", 1 + r)]
    order += [("o", 0), ("i", 2), ("i", 1), ("i", 0)]
    pieces = len(order)
    one, two, four, own_half = {}, {}, {}, {}

    def y_first(p):
        return p % 2 == 0

    def parts(p, mine):
        if y_first(p):
            yy = y if mine else 1 - y
            return [2 * yy, 2 * yy + 1]
        xx = x if mine else 1 - x
        return [xx, 2 + xx]

    def source(p, at):
        kind, m = order[p]
        if kind == "i":
            return x_gin.at[m - 3, :, at] if m >= 3 else p_full.at[m, :, at]
        return x_gout.at[m - 1, :, :, lanes_at(at)] if m >= 1 else q_full.at[:, :, lanes_at(at)]

    def kept(p, k):
        kind, m = order[p]
        return p_half.at[m, k] if kind == "i" else q_half.at[m, k]

    def bufs(p, inner, outer):
        kind, m = order[p]
        return inner.at[m] if kind == "i" else outer.at[m]

    def step_one(p):
        one[p] = [rs.start((p, k), source(p, at), bufs(p, a_in, a_out).at[k], yp if y_first(p) else xp)
                  for k, at in enumerate(parts(p, False))]
        own_half[p] = []
        for k, at in enumerate(parts(p, True)):
            copy = pltpu.make_async_copy(source(p, at), kept(p, k), own_sem.at[p, k])
            copy.start()
            own_half[p].append(copy)

    def step_two(p):
        for copy in one[p]:
            copy.wait_recv()
        for copy in own_half[p]:
            copy.wait()
        for k in (0, 1):
            ref = kept(p, k)
            ref[...] = (ref[...].astype(F32) + bufs(p, a_in, a_out)[k].astype(F32)).astype(BF16)
        go_bit = (1 - x) if y_first(p) else (1 - y)
        two[p] = rs.start((p, 2), kept(p, go_bit), bufs(p, b_in, b_out), xp if y_first(p) else yp)

    def span(p, ref, lo, hi):
        if order[p][0] == "i":
            return ref.at[:, :, lo * LANES:hi * LANES]
        return ref.at[:, lo * LANES:hi * LANES, :]

    def right_copy(p, s):
        here = kept(p, x if y_first(p) else y)
        return pltpu.make_async_remote_copy(
            src_ref=span(p, here, s + 1, n_z), dst_ref=span(p, bufs(p, z_in, z_out), s + 2, n_z + 1),
            send_sem=rs_send.at[p, 3], recv_sem=rs_recv.at[p, 3], device_id=(f, c, z + 1), device_id_type=MESH)

    def left_copy(p, s):
        here = kept(p, x if y_first(p) else y)
        return pltpu.make_async_remote_copy(
            src_ref=span(p, here, 0, s), dst_ref=span(p, bufs(p, z_in, z_out), 0, s),
            send_sem=rs_send.at[p, 4], recv_sem=rs_recv.at[p, 4], device_id=(f, c, z - 1), device_id_type=MESH)

    def add_into(p, lo, hi, shift):
        here = kept(p, x if y_first(p) else y)
        a, b = span(p, here, lo, hi), span(p, bufs(p, z_in, z_out), lo + shift, hi + shift)
        a[...] = (a[...].astype(F32) + b[...].astype(F32)).astype(BF16)

    def step_z(p, s):
        if s == 0:
            two[p].wait_recv()
            here = kept(p, x if y_first(p) else y)
            here[...] = (here[...].astype(F32) + bufs(p, b_in, b_out)[...].astype(F32)).astype(BF16)

        @pl.when(z == s)
        def _():
            if s > 0:
                landed = span(p, bufs(p, z_in, z_out), s + 1, n_z + 1)
                pltpu.make_async_copy(landed, landed, rs_recv.at[p, 3]).wait()
            if s < last:
                if s > 0:
                    add_into(p, s + 1, n_z, 1)
                right_copy(p, s).start()

        @pl.when(z == last - s)
        def _():
            e = last - s
            if s > 0:
                landed = span(p, bufs(p, z_in, z_out), 0, e + 1)
                pltpu.make_async_copy(landed, landed, rs_recv.at[p, 4]).wait()
            if e > 0:
                if s > 0:
                    add_into(p, 0, e, 0)
                left_copy(p, e).start()

    norm[...] = jnp.zeros_like(norm)

    def add_squares(values):
        square = values * values
        parts = [square[8 * i:8 * i + 8] for i in range(square.shape[0] // 8)]
        while len(parts) > 1:
            parts = [a + b for a, b in zip(parts[::2], parts[1::2])]
        for k in range(square.shape[1] // LANES):
            norm[...] = norm[...] + parts[0][:, k * LANES:(k + 1) * LANES]

    def step_core(p):
        kind, m = order[p]
        here = kept(p, x if y_first(p) else y)
        total, result = (f_in, o_in) if kind == "i" else (f_out, o_out)
        for s in range(n_z):
            @pl.when(z == s)
            def _():
                value = span(p, here, s, s + 1)[...].astype(F32)
                if s > 0:
                    value = value + span(p, bufs(p, z_in, z_out), s + 1, s + 2)[...].astype(F32)
                if s < last:
                    value = value + span(p, bufs(p, z_in, z_out), s, s + 1)[...].astype(F32)
                total[m] = value
        result[m, t] = total[m, t]
        add_squares(total[m, 0])
        add_squares(total[m, 1])
        four[p] = rs.start((p, 5), total.at[m, 1 - t], result.at[m, t], core)

    def in_range(p):
        return 0 <= p < pieces

    ready = [2 * n_ff]
    started = [0]
    step = [0]

    def first_sends(upto):
        while started[0] < min(upto, ready[0], pieces):
            step_one(started[0])
            started[0] += 1

    passes, chores = [], []

    def pump(n=1):
        for _ in range(n):
            k = step[0]
            first_sends(k + LOOK)
            if in_range(k) and k >= started[0]:
                return
            if in_range(k):
                step_two(k)
            for unused in range(PASSES):
                if passes:
                    pass_along(*passes.pop(0))
            for s in range(n_z):
                if in_range(k - 1 - 2 * s):
                    step_z(k - 1 - 2 * s, s)
            if in_range(k - 2 * n_z):
                step_core(k - 2 * n_z)
            if chores:
                chore = chores.pop(0)
                if chore is not None:
                    chore()
            step[0] += 1

    first_sends(2)

    def share_out(j, src, dst):
        for xs in (0, 1):
            own = loops & (x == xs)
            there = dst.at[2 * z + y]
            local = pltpu.make_async_copy(src.at[xs], there, t_recv.at[j, y])

            @pl.when(own)
            def _():
                local.start()
            chain.start(jnp.logical_not(own), pltpu.make_async_remote_copy(
                src_ref=src.at[xs], dst_ref=there, send_sem=t_send.at[j, xs], recv_sem=t_recv.at[j, y],
                device_id=(f_base + x, 2 * t + xs, z), device_id_type=MESH))

    def pass_along(j, dst, s, part):
        lanes = pl.ds(part * (width // PARTS), width // PARTS)
        if s == 0 and part == 0:
            for ys in (0, 1):
                pltpu.make_async_copy(dst.at[2 * z + ys], dst.at[2 * z + ys], t_recv.at[j, ys]).wait()
        for side, (there, back_at) in enumerate(((z + 1, z - s), (z - 1, z + s))):
            valid = (back_at >= 0) & (back_at <= last)
            block = dst.at[pl.ds(2 * lax.clamp(0, back_at, last), 2), :, lanes]
            if s > 0:
                @pl.when(valid)
                def _():
                    pltpu.make_async_copy(block, block, g_recv.at[j, side, s, part]).wait()
            if s < last:
                chain.start(valid & (there >= 0) & (there <= last), pltpu.make_async_remote_copy(
                    src_ref=block, dst_ref=block, send_sem=g_send.at[j, side, s, part],
                    recv_sem=g_recv.at[j, side, s + 1, part],
                    device_id=(f, c, lax.clamp(0, there, last)), device_id_type=MESH))

    def pass_all(j, dst):
        passes.extend((j, dst, s, part) for s in range(n_z) for part in range(PARTS))

    def wide(k):
        return cat([vz[zi, k:k + 1, :] for zi in range(n_z)], 1)

    def narrow(k):
        return cat([vz[zi, k:k + 1, lanes_at(t)] for zi in range(n_z)], 1)

    def tally(j, values):
        if values.shape[0] == 16:
            sums[j] = sums[j] + values[:8] + values[8:]
        else:
            sums[j, 0:1] = sums[j, 0:1] + jnp.sum(values, axis=0, keepdims=True)

    sums[...] = jnp.zeros_like(sums)

    ffn_bias = reorder(wide(11 + n_ff), n_hi)
    for name in ("f", "mid", "cot"):
        loads[name].wait()
    f_copy.wait_recv()

    def mix(rows, at, p):
        out = buf[0, at, :] + f_recv[at, :].astype(F32) + ffn_bias
        tally(3, cotb[p, rows, :].astype(F32) * out)
        mixed[p, rows, :] = (mid[at, :] + mod[3:4, :] * out).astype(BF16)
    step_rows(piece, mix)
    share_out(0, mixed, o_mixed)

    first_sends(LOOK)
    for name in ("d", "attn"):
        loads[name].wait()
    d_copy.wait_recv()

    def second_norm(rows, at, p):
        grad = buf[1, at, :] + d_recv[at, :].astype(F32)
        normed, scale = normalize(mid[at, :])
        tally(4, grad * normed)
        tally(5, grad)
        w = grad * (1.0 + mod[4:5, :])
        pulled = scale * (w - jnp.mean(w, axis=-1, keepdims=True) - normed * jnp.mean(w * normed, axis=-1, keepdims=True))
        total = cotb[p, rows, :].astype(F32) + pulled
        dmid[at, :] = total
        tally(0, total * attn[at, :])
        low = (total * mod[0:1, :]).astype(BF16)
        ga[t, at, :] = low
        tally(6, low.astype(F32))
    step_rows(piece, second_norm)
    ga_copy = misc.start(2, ga.at[t], ga.at[t], core)


    loads["wo"].wait()
    loads["o"].wait()
    ga_copy.wait_recv()
    pump(1)
    for j in (0, 1):
        ga_j = ga[:, :, j * hw:(j + 1) * hw].reshape(full, hw)
        part = dot(ga_j, wo[j], NT)
        if j == 0:
            first_part = part
    go[...] = (first_part + part).astype(BF16)
    for name in ("q", "k", "v", "lse", "ma", "mb", "qr", "kr"):
        loads[name].wait()
    pass_all(0, o_mixed)

    vs[...] = jnp.zeros_like(vs)

    def head_back(raw, grad, gain):
        scale = lax.rsqrt(head_mean(raw * raw) + NORM_EPS)
        normed = raw * scale
        gain_grad = jnp.sum(grad * normed, axis=0, keepdims=True)
        w = grad * gain
        return (scale * (w - normed * head_mean(w * normed))).astype(BF16), gain_grad

    def attend_back(i, carry):
        at = lanes_at(i)
        q2, k2, v2, g2, o2 = q8[:, at], kh[:, at], vv[:, at], go[:, at], oo[:, at]
        mine_a, mine_b = ma[...], mb[...]
        lanes = lane_of((full, LANES))
        low, l64 = lanes < HD, lanes % HD
        product = o2.astype(F32) * g2.astype(F32)
        dqs, dks, dvs = [], [], []
        one_like, zero_like = jnp.ones_like(v2), jnp.zeros_like(v2)
        for h in (0, 1):
            here = low if h == 0 else jnp.logical_not(low)
            l1, l2, l3 = split_three(lse[:, at][:, HD * h:HD * h + 1])
            qa = jnp.where(l64 == 40, -l1, jnp.where(l64 == 41, -l2, jnp.where(l64 == 42, -l3, mine_a)))
            ka = jnp.where((l64 >= 40) & (l64 < 43), one_like, mine_b)
            weight = jnp.exp(dot(jnp.where(here, k2, ka), jnp.where(here, q2, qa), NT))
            d1, d2, d3 = split_three(jnp.sum(jnp.where(here, product, 0.0), axis=1, keepdims=True))
            da = jnp.where(l64 == 0, -d1, jnp.where(l64 == 1, -d2, jnp.where(l64 == 2, -d3, zero_like)))
            va = jnp.where(l64 < 3, one_like, zero_like)
            ds = (weight * dot(jnp.where(here, v2, va), jnp.where(here, g2, da), NT)).astype(BF16)
            dvs.append(dot(weight.astype(BF16), g2, NN))
            dks.append(dot(ds, q2, NN))
            dqs.append(dot(ds, k2, TN))
        dq = jnp.where(low, dqs[0], dqs[1]) * 0.125
        dk = jnp.where(low, dks[0], dks[1])
        gq, q_gain = head_back(qr[:, at], dq, vs[8:9, at])
        gk, k_gain = head_back(kr[:, at], dk, vs[9:10, at])
        gv = jnp.where(low, dvs[0], dvs[1]).astype(BF16)
        q8[:, at] = gq
        kh[:, at] = gk
        vv[:, at] = gv
        vs[0:1, at] = jnp.sum(gq.astype(F32), axis=0, keepdims=True)
        vs[1:2, at] = jnp.sum(gv.astype(F32), axis=0, keepdims=True)
        vs[2:3, at] = q_gain
        vs[3:4, at] = k_gain
        return carry

    vs[8:9, :] = narrow(8)
    vs[9:10, :] = narrow(9)
    pairs = n_z
    for i in range(0, pairs, 2):
        lax.fori_loop(i, i + 2, attend_back, 0)
        pump(1)
    ada_refs, ada_loads = [], []
    for j in range(6):
        rows_at, cols_at = (j // 2) * LANES, (j % 2) * (n_z * LANES // 2)
        ada_refs.append(qr.at[rows_at:rows_at + LANES, cols_at:cols_at + n_z * LANES // 2])
        ada_loads.append(pltpu.make_async_copy(x_weight.at[3 + n_ff + j], ada_refs[j], load_sem.at[len(names) + j]))
        ada_loads[j].start()
    loads["wq"].wait()
    part = dot(q8[...], wq[0].reshape(width, n_z * LANES), NT)
    part = part + dot(kh[...], wq[1].reshape(width, n_z * LANES), NT)
    part = part + dot(vv[...], wq[2].reshape(width, n_z * LANES), NT)
    buf[0] = jnp.where(t == 0, part[:half], part[half:])
    f_recv[...] = jnp.where(t == 0, part[half:], part[:half]).astype(BF16)
    h_copy = misc.start(3, f_recv, d_recv, core)
    for j in (0, 1):
        ga_j = ga[:, :, j * hw:(j + 1) * hw].reshape(full, hw)
        q_full[j] = dot(oo[...], ga_j, TN).astype(BF16)
    ready[0] += 1
    loads["h1"].wait()
    h1_all = h1[...].reshape(full, width)
    for m, ref in ((2, vv), (1, kh), (0, q8)):
        p_full[m] = dot(h1_all, ref[...], TN).astype(BF16).reshape(p_full.shape[1:])
        ready[0] += 1
    loads["tok"].wait()
    pump(1)
    h_copy.wait_recv()

    def first_norm(rows, at, p):
        grad = buf[0, at, :] + d_recv[at, :].astype(F32)
        normed, scale = normalize(tokb[p, rows, :].astype(F32))
        tally(1, grad * normed)
        tally(2, grad)
        w = grad * (1.0 + mod[1:2, :])
        pulled = scale * (w - jnp.mean(w, axis=-1, keepdims=True) - normed * jnp.mean(w * normed, axis=-1, keepdims=True))
        cotb[p, rows, :] = (dmid[at, :] + pulled).astype(BF16)
    step_rows(piece, first_norm)
    share_out(1, cotb, o_grad)
    pass_all(1, o_grad)
    pump(1)

    for j in range(7):
        vd[j:j + 1, :] = jnp.sum(sums[j], axis=0, keepdims=True)
    vd[7:8, :] = gf_sum[0:1, :] * 0.5
    v_copy = misc.start(4, vd, vdr, core)
    vs[4:8, :] = gu_sum[0:4, :]
    cols = width // n_z
    n_ada = 6
    chips = 4 * n_z
    waits = {}

    def exact(a, b, dims):
        return lax.dot_general(a, b, (dims, ((), ())), precision=PRECISE, preferred_element_type=F32)

    def arrive(name):
        for copy in waits.pop(name):
            copy.wait_recv()

    def mods(j):
        return d_mod[...].reshape(chips, 8, cols)[:, j, :]

    def along_line():
        v_copy.wait_recv()
        vd_all = reorder(vd[...] + vdr[...], n_hi, inverse=True)
        for zi in range(n_z):
            vdz[zi] = vd_all[:, zi * cols:(zi + 1) * cols]
        d_mod[x, y, z] = vdz[z]
        zv[z] = vs[0:8, lanes_at(z)]
        waits["line"] = []
        for d, target in enumerate(zs):
            zi = lax.rem(z + 1 + d, n_z)
            waits["line"].append(misc.start(5 + d, vdz.at[zi], d_mod.at[x, y, z], target))
            waits["line"].append(misc.start(4 + n_z + d, vs.at[pl.ds(0, 8), lanes_at(zi)], zv.at[z], target))

    slot = 3 + 2 * n_z

    def over_plane():
        arrive("line")
        total = zv[0]
        for zi in range(1, n_z):
            total = total + zv[zi]
        v_all[x, y] = total
        waits["plane"] = []
        for d, target in enumerate(plane):
            waits["plane"].append(misc.start(slot + d, d_mod.at[x, y], d_mod.at[x, y], target))
            waits["plane"].append(misc.start(slot + 3 + d, v_all.at[x, y], v_all.at[x, y], target))

    def products():
        arrive("plane")
        v_half[t] = (v_all[0, 0] + v_all[0, 1]) + (v_all[1, 0] + v_all[1, 1])
        waits["vec"] = [misc.start(slot + 6, v_half.at[t], v_half.at[t], core)]
        for copy in ada_loads:
            copy.wait()
        total = 0.0
        for j, ref in enumerate(ada_refs):
            total = total + exact(mods(j), ref[...].astype(BF16).astype(F32), NT)
        cond_z[z] = total
        waits["cond line"] = [misc.start(slot + 7 + d, cond_z.at[z], cond_z.at[z], target) for d, target in enumerate(zs)]
        for j in range(n_ada):
            o_ada[j] = exact(act[...], mods(j), TN)
            if n_hi == 1:
                add_squares(o_ada[j])

    def cond_plane():
        arrive("cond line")
        total = cond_z[0]
        for zi in range(1, n_z):
            total = total + cond_z[zi]
        cond_all[t, c] = total
        at = slot + 6 + n_z
        waits["cond plane"] = [misc.start(at + d, cond_all.at[t, c], cond_all.at[t, c], target)
                               for d, target in enumerate(plane)]

    def cond_core():
        arrive("cond plane")
        waits["cond core"] = [misc.start(slot + 9 + n_z, cond_all.at[t], cond_all.at[t], core)]

    chores.extend([along_line, None, over_plane, None, products, None, cond_plane, None, cond_core])

    while step[0] < pieces + 2 * n_z or chores:
        pump(1)
    while passes:
        pass_along(*passes.pop(0))
    arrive("cond core")
    mine = pl.ds(pl.multiple_of(2 * n_z * t, 2 * n_z), 2 * n_z)
    o_cond[...] = cat([cond_all[ti, ck, mine, :] for ti in (0, 1) for ck in range(4)], 1)

    arrive("vec")
    mod_sum = jnp.sum(d_mod[...].reshape(chips, 8, cols), axis=0)
    o_vec[...] = cat([mod_sum[:n_ada], cat([v_half[0], v_half[1]], 1), mod_sum[n_ada:]], 0)
    if n_hi == 1:
        square = o_vec[...] * o_vec[...]
        square = square[:8] + square[8:]
        vec_squares = sum(square[:, k * LANES:(k + 1) * LANES] for k in range(cols // LANES))
        slot = slot + 10 + n_z
        norm_plane[c] = norm[...] + jnp.where((f == 0) & (c == 0), vec_squares, 0.0)
        copies = [misc.start(slot + d, norm_plane.at[c], norm_plane.at[c], target) for d, target in enumerate(plane)]
        for copy in copies:
            copy.wait_recv()
        norm_line[t, z] = (norm_plane[0] + norm_plane[1]) + (norm_plane[2] + norm_plane[3])
        copies = [misc.start(slot + 3 + d, norm_line.at[t, z], norm_line.at[t, z], target)
                  for d, target in enumerate([core] + zs + other_line)]
        for copy in copies:
            copy.wait_recv()
        total = norm_line[0, 0]
        for ti in (0, 1):
            for zi in range(n_z):
                if ti + zi > 0:
                    total = total + norm_line[ti, zi]
        total = jnp.sum(jnp.sum(total, axis=0, keepdims=True), axis=1, keepdims=True)
        o_norm[...] = jnp.broadcast_to(jnp.sqrt(total), o_norm.shape)
    else:
        o_norm[...] = jnp.zeros_like(o_norm)
    for p in range(pieces):
        four[p].wait_recv()
    for p in range(pieces):
        for s in range(n_z):
            @pl.when(z == s)
            def _():
                if s < last:
                    right_copy(p, s).wait_send()
                if s > 0:
                    left_copy(p, s).wait_send()
    chain.finish()
    rs.finish()
    misc.finish()


def backward(operands, n_z, n_ff, n_hi):
    n_in, n_out = 3 + n_ff, 1 + n_ff
    here, width = n_z * LANES, 8 * LANES
    half, full = 2 * PIECE, 4 * PIECE
    hw, cols = width // 2, width // n_z
    S, V, dma = jax.ShapeDtypeStruct, pltpu.VMEM, pltpu.SemaphoreType.DMA
    any_space, vmem = pl.BlockSpec(memory_space=pl.ANY), pl.BlockSpec(memory_space=pltpu.VMEM)
    piece = operands[12].shape[1]
    rows_out = S((2 * n_z, piece, width), BF16)
    pieces = n_in + n_out
    slots = 24 + 5 * n_z
    return pl.pallas_call(
        functools.partial(backward_kernel, n_z, n_ff, n_hi),
        out_shape=(rows_out, rows_out, S((n_in, 2, LANES, LANES), F32), S((n_out, 2, LANES, LANES), F32),
                   S((16, cols), F32), S((6, LANES, cols), F32), S((2 * n_z, width), F32),
                   S((8, LANES), F32)),
        in_specs=[any_space] * (len(operands) - 5) + [vmem] * 5,
        out_specs=tuple([any_space] * 2 + [vmem] * 6),
        scratch_shapes=[
            V((3, 2, 4, LANES, here), BF16), V((2, here, hw), BF16), V((2, half, width), BF16),
            V((full, here), F32), V((full, here), F32), V((full, here), BF16), V((full, here), BF16),
            V((full, here), BF16), V((full, here), BF16), V((full, here), F32), V((full, LANES), BF16),
            V((full, LANES), BF16), V((2, piece, width), BF16), V((2, piece, width), BF16), V((half, width), F32),
            V((half, width), F32), V((2, half, width), F32), V((half, width), BF16), V((half, width), BF16),
            V((half, width), F32), V((2, half, width), BF16), V((full, here), BF16), V((2, piece, width), BF16),
            V((8, 8, width), F32), V((8, width), F32), V((8, width), F32), V((16, here), F32),
            V((n_z, 8, cols), F32), V((n_z, 8, LANES), F32), V((2, 2, 8, LANES), F32),
            V((2, 2, n_z, 8, cols), F32), V((2, 8, LANES), F32), V((8, LANES), F32), V((4, 8, LANES), F32), V((2, n_z, 8, LANES), F32), V((n_z, 4 * n_z, LANES), F32), V((2, 4, 4 * n_z, LANES), F32),
            V((3, 2, 4, LANES, here), BF16), V((2, here, hw), BF16),
            V((n_in, 2, 2, LANES, here), BF16), V((n_out, 2, 2, here, LANES), BF16),
            V((n_in, 2, 2, LANES, here), BF16), V((n_out, 2, 2, here, LANES), BF16),
            V((n_in, 2, LANES, here), BF16), V((n_out, 2, here, LANES), BF16),
            V((n_in, 2, LANES, here + LANES), BF16), V((n_out, 2, here + LANES, LANES), BF16),
            V((n_in, 2, LANES, LANES), F32), V((n_out, 2, LANES, LANES), F32),
            dma((24,)), dma((pieces, 2)), dma((pieces, 6)), dma((pieces, 6)), dma((slots,)), dma((slots,)),
            dma((2, 2)), dma((2, 2)), dma((2, 2, n_z, PARTS)), dma((2, 2, n_z, PARTS)),
        ],
        compiler_params=pltpu.CompilerParams(collective_id=1, has_side_effects=True, vmem_limit_bytes=VMEM_BYTES),
    )(*operands)


def update_kernel(n_z, n_hi, *refs):
    (norm, cond_sum, cond, g_vec, w_vec, m_vec, v_vec, g_in, g_ada, g_out, w_in, m_in, v_in, w_out, m_out, v_out, mixed, grads,
     w_vec_new, m_vec_new, v_vec_new, c_vec_new, o_bias, o_cond, o_norm,
     w_in_new, m_in_new, v_in_new, c_in_new, w_out_new, m_out_new, v_out_new, c_out_new, o_mixed, o_grads,
     gi, ga, go, wi, mi, vi, ci, wo, mo, vo, co, low, wide, low_out, high, load_sem, store_sem) = refs
    n_seq = mixed.shape[0]
    loads, stores = {}, []

    def load(name, src, dst):
        loads[name] = pltpu.make_async_copy(src, dst, load_sem.at[len(loads)])
        loads[name].start()

    def store(src, dst):
        copy = pltpu.make_async_copy(src, dst, store_sem.at[len(stores)])
        copy.start()
        stores.append(copy)

    load("grads", grads, low.at[1])
    load("mixed", mixed, low.at[0])
    for name, src, dst in (("gi", g_in, gi), ("ga", g_ada, ga), ("wi", w_in, wi), ("mi", m_in, mi), ("vi", v_in, vi),
                           ("go", g_out, go), ("wo", w_out, wo), ("mo", m_out, mo), ("vo", v_out, vo)):
        load(name, src, dst)
    n_all, n_rows, cols = w_in.shape
    n_out = w_out.shape[0]
    factor = (CLIP_NORM / jnp.maximum(norm[0:1, 0:1], CLIP_NORM))
    factor_in = jnp.broadcast_to(factor, (1, cols))
    factor_out = jnp.broadcast_to(factor, (1, w_out.shape[2]))
    o_norm[...] = norm[0:1, 0:1]
    back = reorder(cond_sum[...], n_hi, inverse=True)
    rows = [back[n_z * yy + zi:n_z * yy + zi + 1] for zi in range(n_z) for yy in (0, 1)]
    gate = 1.0 / (1.0 + jnp.exp(-cond[...]))
    o_cond[...] = cat(rows, 0) * (gate * (1.0 + cond[...] * (1.0 - gate)))
    loads["grads"].wait()
    for i in range(n_seq):
        high[:, i, :] = low[1, i].astype(F32)
    store(high, o_grads)
    w_vec_new[...], m_vec_new[...], v_vec_new[...], c_vec_new[...] = adam_update(
        w_vec[...], m_vec[...], v_vec[...], g_vec[...], factor_in, RATE_VECTOR, 0.0)
    last = g_vec.shape[0]
    o_bias[...] = g_vec[last - 1:last] * factor_in
    for name in ("gi", "ga", "wi", "mi", "vi"):
        loads[name].wait()
    lead = n_all - ga.shape[0]

    def update(m, grad):
        wi[m], mi[m], vi[m], ci[m] = adam_update(wi[m], mi[m], vi[m], grad, factor_in, RATE_MATRIX, WEIGHT_DECAY)

    def lead_rows(m, carry):
        update(m, cat([gi[m, 0], gi[m, 1]], 1))
        return carry

    def ada_rows(m, carry):
        update(lead + m, ga[m])
        return carry

    for lo, hi, body, shift in ((0, lead, lead_rows, 0), (0, n_all - lead, ada_rows, lead)):
        lax.fori_loop(lo, hi, body, 0)
        at = pl.ds(shift, hi)
        for src, dst in ((wi, w_in_new), (mi, m_in_new), (vi, v_in_new), (ci, c_in_new)):
            store(src.at[at], dst.at[at])
    for name in ("go", "wo", "mo", "vo"):
        loads[name].wait()
    for m in range(n_out):
        grad = cat([go[m, 0], go[m, 1]], 0)
        wo[m], mo[m], vo[m], co[m] = adam_update(wo[m], mo[m], vo[m], grad, factor_out, RATE_MATRIX, WEIGHT_DECAY)
    for src, dst in ((wo, w_out_new), (mo, m_out_new), (vo, v_out_new), (co, c_out_new)):
        store(src, dst)
    loads["mixed"].wait()
    for i in range(n_seq):
        wide[:, i, :] = low[0, i].astype(F32)
    low_out[...] = wide[...].astype(BF16)
    store(low_out, o_mixed)
    for copy in stores:
        copy.wait()


def update(small, large, rows_low, n_z, n_hi):
    S, V, dma = jax.ShapeDtypeStruct, pltpu.VMEM, pltpu.SemaphoreType.DMA
    any_space, vmem = pl.BlockSpec(memory_space=pl.ANY), pl.BlockSpec(memory_space=pltpu.VMEM)
    w_vec = small[4]
    g_in, g_ada, g_out, w_in, w_out = large[0], large[1], large[2], large[3], large[6]
    kinds = [S(a.shape, F32) for a in (w_vec, w_in, w_out)]
    news = [[k] * 3 + [S(k.shape, BF16)] for k in kinds]
    n_seq, piece, width = rows_low[0].shape
    turned = (piece, n_seq, width)
    return pl.pallas_call(
        functools.partial(update_kernel, n_z, n_hi),
        out_shape=tuple(news[0] + [S((1, w_vec.shape[1]), F32), S(small[2].shape, F32), S((1, 1), F32)] + news[1] + news[2] + [S(turned, BF16), S(turned, F32)]),
        in_specs=[vmem] * len(small) + [any_space] * (len(large) + 2),
        out_specs=tuple([vmem] * 7 + [any_space] * 10),
        scratch_shapes=[
            V(g_in.shape, F32), V(g_ada.shape, F32), V(g_out.shape, F32),
            V(w_in.shape, F32), V(w_in.shape, F32), V(w_in.shape, F32), V(w_in.shape, BF16),
            V(w_out.shape, F32), V(w_out.shape, F32), V(w_out.shape, F32), V(w_out.shape, BF16),
            V((2,) + rows_low[0].shape, BF16), V(turned, F32), V(turned, BF16), V(turned, F32), dma((11,)), dma((16,)),
        ],
        compiler_params=pltpu.CompilerParams(vmem_limit_bytes=VMEM_BYTES),
    )(*small, *large, *rows_low)


def per_device(n_f, n_c, n_z, tokens, cotangent, class_table, labels, scale_ids, in_weight, in_first, in_second,
               out_weight, out_first, out_second, vectors, vec_first, vec_second):
    n_hi = n_f // 2
    f, c, z, t, x, y = place()
    seqs, piece, width = tokens.shape
    cols = in_weight.shape[2]
    n_ff = out_weight.shape[0] - 1
    ada = 3 + n_ff
    half = cols // 2
    pairs = [[2 * i, 2 * i + 1] for i in range(n_hi)]
    his = [[i + 2 * j for j in range(n_hi)] for i in range(2)]

    def into(a):
        if n_hi == 1:
            return a
        shape = a.shape[:-1]
        return jnp.swapaxes(a.reshape(shape + (n_hi, 2 * n_c, -1)), -3, -2).reshape(a.shape)

    def back(a):
        if n_hi == 1:
            return a
        shape = a.shape[:-1]
        return jnp.swapaxes(a.reshape(shape + (2 * n_c, n_hi, -1)), -3, -2).reshape(a.shape)

    in_weight, in_first, in_second = [a.transpose(1, 0, 2) for a in (in_weight, in_first, in_second)]
    in_low, out_low = in_weight, out_weight
    if n_hi > 1:
        in_low = lax.all_gather(in_low.astype(BF16), "fsdp", axis=1, tiled=True, axis_index_groups=his).astype(F32)
        out_low = lax.all_gather(out_low.astype(BF16), "fsdp", axis=2, tiled=True, axis_index_groups=his).astype(F32)
    rows = in_low.shape[1]

    def two_seqs(a):
        return lax.dynamic_slice_in_dim(a, 2 * z, 2, 0)

    ids = jnp.pad(two_seqs(scale_ids), ((0, 0), (0, PIECE - piece)), constant_values=10).astype(BF16)
    ids = jnp.broadcast_to(ids[:, :, None], ids.shape + (LANES,))
    conditions = class_table.at[labels].get(mode="promise_in_bounds", wrap_negative_indices=False)
    cond_act = jax.nn.silu(conditions).astype(BF16)
    act = into(cond_act).reshape(n_z, 2, width).transpose(1, 0, 2).reshape(2 * n_z, width).astype(F32)
    *kept, vec_all, act_rows = forward(
        in_low, out_low, two_seqs(into(tokens)), two_seqs(into(cotangent)), ids, act, vectors, n_z, n_hi)
    big, small = kept[:-3], kept[-3:]
    mixed, grad_low, g_in, g_out, g_vec, g_ada, cond_sum, norm = backward(
        big + [in_low] + small + [vec_all, act_rows], n_z, n_ff, n_hi)
    if n_hi > 1:
        g_vec = lax.psum(g_vec, "fsdp", axis_index_groups=his)
        g_in = lax.psum_scatter(g_in, "fsdp", scatter_dimension=2, tiled=True, axis_index_groups=his)
        g_ada = lax.psum_scatter(g_ada, "fsdp", scatter_dimension=1, tiled=True, axis_index_groups=his)
        g_out = lax.psum_scatter(g_out, "fsdp", scatter_dimension=3, tiled=True, axis_index_groups=his)
        squares = jnp.sum(g_in * g_in) + jnp.sum(g_ada * g_ada) + jnp.sum(g_out * g_out)
        squares = squares + jnp.where((f == 0) & (c == 0), jnp.sum(g_vec * g_vec), 0.0)
        norm = jnp.broadcast_to(jnp.sqrt(lax.psum(squares, ("fsdp", "ctx", "tp"))), norm.shape)
    *news, mixed, input_grad = update(
        [norm, cond_sum, conditions, g_vec, vectors, vec_first, vec_second],
        [g_in, g_ada, g_out, in_weight, in_first, in_second, out_weight, out_first, out_second], [mixed, grad_low],
        n_z, n_hi)
    bias_grad, condition_grad, norm = news[4:7]
    del news[4:7]
    mixed = mixed.transpose(1, 0, 2)
    vec_new, in_new, out_new = news[:4], [a.transpose(1, 0, 2) for a in news[4:8]], news[8:]
    input_grad = input_grad.transpose(1, 0, 2)
    return (back(mixed), back(input_grad), condition_grad, norm.reshape(()), *in_new, *out_new, *vec_new, bias_grad[0])


def solution(mesh):
    in_matrix = P(("fsdp", "ctx"), None, "tp")
    out_matrix = P(None, "tp", ("fsdp", "ctx"))
    vector = P(None, "tp")
    rows = P("fsdp", "ctx", None)
    return jax.shard_map(
        functools.partial(per_device, mesh.shape["fsdp"], mesh.shape["ctx"], mesh.shape["tp"]),
        mesh=mesh,
        in_specs=(rows, rows, P(), P("fsdp"), P("fsdp", "ctx"), in_matrix, in_matrix, in_matrix,
                  out_matrix, out_matrix, out_matrix, vector, vector, vector),
        out_specs=(rows, rows, P("fsdp", None), P(), in_matrix, in_matrix, in_matrix, in_matrix,
                   out_matrix, out_matrix, out_matrix, out_matrix, vector, vector, vector, vector, P("tp")),
        check_vma=False,
    )
```

```python
import functools
import math

import jax
import jax.numpy as jnp
from jax import lax
from jax.experimental import pallas as pl
from jax.experimental.pallas import tpu as pltpu
from jax.sharding import PartitionSpec as P

HD = 64
STEP = 5
PRECISE = lax.Precision.HIGHEST
NORM_EPS = 1e-06
CLIP_NORM = 1.0
BETA_ONE = 0.5
BETA_TWO = 0.5
RATE_MATRIX = 0.03
RATE_VECTOR = 0.3
WEIGHT_DECAY = 0.05
ADAM_EPS = 1e-08

MESH = pl.DeviceIdType.MESH
F32 = jnp.float32
BF16 = jnp.bfloat16
LANES = 128
VMEM_BYTES = 60 * 2**20


def place():
    f = lax.axis_index("fsdp")
    c = lax.axis_index("ctx")
    z = lax.axis_index("tp")
    return f, c, z, lax.rem(f, 2), lax.rem(c, 2), c // 2


def partners(n_z):
    f, c, z, t, x, y = place()
    core = (f + 1 - 2 * t, c, z)
    xp = (f, 2 * y + (1 - x), z)
    yp = (f, 2 * (1 - y) + x, z)
    zs = [(f, c, lax.rem(z + d, n_z)) for d in range(1, n_z)]
    return core, xp, yp, zs


def enter(targets):
    barrier = pltpu.get_barrier_semaphore()
    for target in targets:
        pl.semaphore_signal(barrier, inc=1, device_id=target, device_id_type=MESH)
    pl.semaphore_wait(barrier, len(targets))


def lanes_at(index):
    return pl.ds(pl.multiple_of(index * LANES, LANES), LANES)


def adam_update(master, first, second, grad, factor, rate, decay):
    grad = grad * factor
    first = BETA_ONE * first + (1.0 - BETA_ONE) * grad
    second = BETA_TWO * second + (1.0 - BETA_TWO) * grad * grad
    fix_one = 1.0 - BETA_ONE**STEP
    fix_two = 1.0 - BETA_TWO**STEP
    stride = first / fix_one / (jnp.sqrt(second / fix_two) + ADAM_EPS)
    master = master - rate * (stride + decay * master)
    return (master, first, second, master.astype(BF16))


def dot(a, b, dims):
    return lax.dot_general(a, b, (dims, ((), ())), preferred_element_type=F32)


NN = ((1,), (0,))
NT = ((1,), (1,))
TN = ((0,), (0,))


PIECE = 176
NEG = -1e30
PLANE_FIRST = (10, 11)
EXTRA_EVERY = 2
EXTRA_FROM = 2
AHEAD = 2
TICKS = (2, 2, 2, 2, 1, 0, 2, 1, 2, 1, 1, 0, 0, 3, 0, 1, 0, 1, 2, 2, 2, 1)
PARTS = 4
PASSES = 3
LOOK = 3
UNROLL = 2


def cat(parts, axis):
    return jnp.concatenate(parts, axis=axis)


def lane_of(shape):
    return lax.broadcasted_iota(jnp.int32, shape, len(shape) - 1)


def split_two(values):
    high = values.astype(BF16)
    return high, (values - high.astype(F32)).astype(BF16)


def split_three(values):
    high = values.astype(BF16)
    rest = values - high.astype(F32)
    middle = rest.astype(BF16)
    return high, middle, (rest - middle.astype(F32)).astype(BF16)


def head_mean(values):
    row = lax.broadcasted_iota(jnp.int32, (LANES, LANES), 0) // HD
    ones = jnp.where(row == lane_of((LANES, LANES)) // HD, 1.0 / HD, 0.0).astype(BF16)
    out = []
    for k in range(values.shape[1] // LANES):
        high, lower = split_two(values[:, k * LANES:(k + 1) * LANES])
        out.append(dot(high, ones, NN) + dot(lower, ones, NN))
    return cat(out, 1)


def gelu_both(u):
    k0, k1 = 0.7978845608028654, 0.044715
    square = u * u
    th = jnp.tanh(k0 * u * (1.0 + k1 * square))
    half = 0.5 * (1.0 + th)
    slope = half + 0.5 * u * (1.0 - th * th) * (k0 * (1.0 + 3.0 * k1 * square))
    return u * half, slope


def step_rows(piece, body):
    for p in (0, 1):
        def one(i, carry, p=p):
            start = pl.multiple_of(i * 16, 16)
            body(pl.ds(start, 16), pl.ds(pl.multiple_of(p * PIECE + start, 16), 16), p)
            return carry
        lax.fori_loop(0, piece // 16, one, 0, unroll=UNROLL)
        if piece % 16:
            start = piece // 16 * 16
            body(pl.ds(start, piece % 16), pl.ds(p * PIECE + start, piece % 16), p)


def clear_tail(ref, t):
    for p in (0, 1):
        ref[t, pl.ds(p * PIECE + PIECE - 16, 16), :] = jnp.zeros((16, ref.shape[2]), ref.dtype)


def normalize(values):
    center = values - jnp.mean(values, axis=-1, keepdims=True)
    scale = lax.rsqrt(jnp.mean(center * center, axis=-1, keepdims=True) + NORM_EPS)
    return center * scale, scale


def reorder(rows, n_hi, inverse=False):
    if n_hi == 1:
        return rows
    width = rows.shape[1]
    each = width // (8 * n_hi)
    out = []
    for k in range(width // LANES):
        at = k * LANES + lax.broadcasted_iota(jnp.int32, (width, LANES), 1)
        there = lax.broadcasted_iota(jnp.int32, (width, LANES), 0)
        if inverse:
            wanted = (at // each % 8) * (n_hi * each) + (at // (8 * each)) * each + at % each
        else:
            wanted = (at // each % n_hi) * (8 * each) + (at // (each * n_hi)) * each + at % each
        order = jnp.where(there == wanted, 1.0, 0.0).astype(BF16)
        out.append(sum(dot(part, order, NN) for part in split_three(rows)))
    return cat(out, 1)


class Wire:
    def __init__(self, send_sem, recv_sem):
        self.send_sem, self.recv_sem, self.sent = send_sem, recv_sem, []

    def make(self, at, src, dst, target, to=None):
        return pltpu.make_async_remote_copy(
            src_ref=src, dst_ref=dst, send_sem=self.send_sem.at[at], recv_sem=self.recv_sem.at[at if to is None else to],
            device_id=target, device_id_type=MESH)

    def start(self, at, src, dst, target, to=None):
        copy = self.make(at, src, dst, target, to)
        copy.start()
        self.sent.append(copy)
        return copy

    def finish(self):
        for copy in self.sent:
            copy.wait_send()


def forward_kernel(n_z, n_ff, n_hi, *refs):
    n_in, n_out = 3 + n_ff, 1 + n_ff
    (x_in, x_out, raw_tok, raw_cot, ids, act, vec,
     x_wq, x_wo, x_h1, x_qr, x_kr, x_q8, x_kh, x_v, x_o, x_lse, x_ma, x_mb, x_tok, x_cot, x_attn, x_mid,
     x_fown, x_fsend, x_down, x_dsend, x_gin, x_gout, x_mod, x_gu, x_gf, x_vec, x_act,
     g_in, g_out, tokb, cotb, idb, actb, pm, pr, ps, pf, vz, h1, gf, h2, qr, kr, q8, kh, vv, oo, lse, ma, mb,
     at_send, at_recv, attn, mid, facc, dacc, fsend, dsend, gin, gout, act_low, slope,
     full_in, full_out, low_in, low_out, local_sem, ag_send, ag_recv, m_send, m_recv, out_sem, tok_sem, load_sem,
     raw, widened, tok, cot, raw_sem) = refs
    f, c, z, t, x, y = place()
    core, xp, yp, zs = partners(n_z)
    f_base = f - t

    piece = raw_tok.shape[0]
    pick_loads = [pltpu.make_async_copy(raw_tok, raw, raw_sem.at[0]), pltpu.make_async_copy(raw_cot, raw, raw_sem.at[1])]
    pick_loads[0].start()

    def pick(load, dst):
        load.wait()

        def rows(at, count):
            widened[pl.ds(0, count)] = raw[at].astype(F32)
            for k in (0, 1):
                dst[k, at, :] = widened[pl.ds(0, count), 2 * z + k, :].astype(BF16)

        def one(i, carry):
            rows(pl.ds(pl.multiple_of(i * 16, 16), 16), 16)
            return carry
        lax.fori_loop(0, piece // 16, one, 0)
        if piece % 16:
            rows(pl.ds(piece // 16 * 16, piece % 16), piece % 16)

    n_all = x_in.shape[0]
    order = [("i", 0), ("i", 1), ("i", 2), ("o", 0)]
    for r in range(n_ff):
        order += [("i", 3 + r), ("o", 1 + r)]
    loads = {}
    for kind, m in [("i", j) for j in range(n_in, n_all)] + order:
        src, dst, at = (x_in, full_in, m) if kind == "i" else (x_out, full_out, n_all + m)
        loads[kind, m] = pltpu.make_async_copy(src.at[m], dst.at[m], load_sem.at[at])
        loads[kind, m].start()
    for ref in (h1, gf, h2):
        clear_tail(ref, t)

    barrier = pltpu.get_barrier_semaphore()
    plane = [xp, yp, (f, 3 - c, z)]
    other_line = [(f + 1 - 2 * t, c, target[2]) for target in zs]
    for target in [core] + plane + zs + other_line:
        pl.semaphore_signal(barrier, inc=1, device_id=target, device_id_type=MESH)
    loops = (y == t) & (x == t)
    for xs in (0, 1):
        @pl.when(jnp.logical_not(loops & (x == xs)))
        def _():
            pl.semaphore_signal(barrier, inc=1, device_id=(f_base + x, 2 * t + xs, z), device_id_type=MESH)
    pl.semaphore_wait(barrier, 4 + 2 * n_z - jnp.where(loops, 1, 0))

    ag = Wire(ag_send, ag_recv)
    misc = Wire(m_send, m_recv)

    shares = [(tok, tokb), (cot, cotb), (ids, None)]

    def send_share(j):
        src, dst = shares[j]
        for yd in (0, 1):
            own = loops & (y == yd)
            from_here = src.at[yd]
            to_there = dst.at[x] if dst is not None else idb.at[2 * y + x]

            @pl.when(own)
            def _():
                pltpu.make_async_copy(from_here, to_there, tok_sem.at[1, j, x]).start()

            @pl.when(jnp.logical_not(own))
            def _():
                pltpu.make_async_remote_copy(
                    src_ref=from_here, dst_ref=to_there, send_sem=tok_sem.at[0, j, yd], recv_sem=tok_sem.at[1, j, x],
                    device_id=(f_base + y, 2 * yd + t, z), device_id_type=MESH).start()

    def got_share(j):
        dst = shares[j][1]
        for xs in (0, 1):
            ref = dst.at[xs] if dst is not None else idb.at[2 * t + xs]
            pltpu.make_async_copy(ref, ref, tok_sem.at[1, j, xs]).wait()

    act_copy = misc.start(0, act.at[:, lanes_at((1 - t) * 4 + c)], actb.at[1], core)
    vec_local = pltpu.make_async_copy(vec, vz.at[z], local_sem.at[n_in + n_out])
    vec_local.start()
    vec_copies = [misc.start(1 + d, vec, vz.at[z], target) for d, target in enumerate(zs)]
    zrows = pl.ds(pl.multiple_of(z * LANES, LANES), LANES)
    first, zcopies, one, two = {}, {}, {}, {}

    def prepare(p):
        if p in first:
            return
        kind, m = order[p]
        loads[kind, m].wait()
        if kind == "i":
            dst = g_in.at[m, t, c, :, lanes_at(z)]
            for s in (0, 1):
                low_in[m, s] = full_in[m, :, s * LANES:(s + 1) * LANES].astype(BF16)
            mine, other = low_in.at[m, t], low_in.at[m, 1 - t]
        else:
            dst = g_out.at[m, t, zrows, lanes_at(c)]
            for s in (0, 1):
                low_out[m, s] = full_out[m, s * LANES:(s + 1) * LANES, :].astype(BF16)
            mine, other = low_out.at[m, t], low_out.at[m, 1 - t]
        local = pltpu.make_async_copy(mine, dst, local_sem.at[p])
        local.start()
        first[p] = (local, ag.start((p, 0), other, dst, core))

    base = n_z

    def start_zero(p):
        if p >= len(order) or p in zcopies or p in PLANE_FIRST:
            return
        kind, m = order[p]
        prepare(p)
        first[p][0].wait()
        first[p][1].wait_recv()
        block = g_in.at[m, :, c, :, lanes_at(z)] if kind == "i" else g_out.at[m, :, zrows, lanes_at(c)]
        zcopies[p] = [ag.start((p, 1 + d), block, block, target) for d, target in enumerate(zs)]

    line_first = [p for p in range(len(order)) if p not in PLANE_FIRST]

    def x_first(p):
        return line_first.index(p) % 2 == 0

    def start_one(p):
        kind, m = order[p]
        for copy in zcopies[p]:
            copy.wait_recv()
        block = g_in.at[m, :, c] if kind == "i" else g_out.at[m, :, :, lanes_at(c)]
        one[p] = ag.start((p, base), block, block, xp if x_first(p) else yp)

    def start_two(p):
        kind, m = order[p]
        one[p].wait_recv()
        held = (2 * y, 2 * y + 1) if x_first(p) else (x, 2 + x)
        two[p] = []
        if kind == "i" and x_first(p):
            block = g_in.at[m, :, pl.ds(2 * y, 2)]
            two[p].append(ag.start((p, base + 1), block, block, yp))
        else:
            for k, at in enumerate(held):
                block = g_in.at[m, :, at] if kind == "i" else g_out.at[m, :, :, lanes_at(at)]
                two[p].append(ag.start((p, base + 1 + k), block, block, yp if x_first(p) else xp))

    extras = []

    def start_plane(p):
        kind, m = order[p]
        prepare(p)
        first[p][0].wait()
        first[p][1].wait_recv()
        block = g_in.at[m, :, c, :, lanes_at(z)] if kind == "i" else g_out.at[m, :, zrows, lanes_at(c)]
        one[p] = [ag.start((p, base + k), block, block, target) for k, target in enumerate(plane)]
        two[p] = []

    def start_line(p, ck):
        kind, m = order[p]
        if ck == 0:
            for copy in one[p]:
                copy.wait_recv()
        block = g_in.at[m, :, ck, :, lanes_at(z)] if kind == "i" else g_out.at[m, :, zrows, lanes_at(ck)]
        for d, target in enumerate(zs):
            two[p].append(ag.start((p, base + 3 + 3 * ck + d), block, block, target))

    for p in PLANE_FIRST:
        extras.append((start_plane, (p,)))
    for p in PLANE_FIRST:
        extras += [(start_line, (p, ck)) for ck in range(4)]
    ticks = [(start_one, line_first[0])]
    for p, before in zip(line_first[1:], line_first[:-1]):
        ticks += [(start_one, p), (start_two, before)]
    ticks.append((start_two, line_first[-1]))
    ticked = [0]

    def tick(n=1):
        for _ in range(n):
            if ticks:
                step, p = ticks.pop(0)
                if step is start_one:
                    for ahead in range(p + AHEAD):
                        start_zero(ahead)
                step(p)
            ticked[0] += 1
            if extras and ticked[0] >= EXTRA_FROM and ticked[0] % EXTRA_EVERY == 0:
                step, what = extras.pop(0)
                step(*what)

    def arrived(p):
        while p not in two or (p in PLANE_FIRST and any(what[0] == p for unused, what in extras)):
            tick()
        for copy in two[p]:
            copy.wait_recv()

    flushed = []

    def flush(src, dst):
        copy = pltpu.make_async_copy(src, dst, out_sem.at[len(flushed)])
        copy.start()
        flushed.append(copy)

    prepare(0)
    prepare(1)
    pick(pick_loads[0], tok)
    pick_loads[1].start()
    act_copy.wait_recv()
    cols = vec.shape[1]
    for j in range(n_in, n_all):
        loads["i", j].wait()
    own_at = lanes_at(t * 4 + c)
    mine = act[:, own_at]
    theirs = actb[1]
    pm[...] = jnp.zeros_like(pm)
    seqs = 2 * n_z
    for s in (0, 1):
        rows = jnp.where(t == s, mine, theirs)
        x_act[seqs * s:seqs * (s + 1), :] = rows
        for j in range(n_all - n_in):
            pm[seqs * s:seqs * (s + 1), j, :] = dot(rows.astype(BF16), full_in[n_in + j].astype(BF16), NN)

    def of_chip(xx, yy):
        return pm.at[pl.ds(seqs * xx + n_z * yy, n_z)]

    mod_copies = [misc.start(1 + n_z + k, of_chip(xx, yy), pr.at[k], target)
                  for k, (target, (xx, yy)) in enumerate(zip(plane, [(1 - x, y), (x, 1 - y), (1 - x, 1 - y)]))]
    send_share(0)
    send_share(2)
    start_zero(0)
    for copy in mod_copies:
        copy.wait_recv()
    ps[...] = (of_chip(x, y)[...] + pr[0]) + (pr[1] + pr[2])
    pf[t, z] = ps[z]
    mod_copies = [misc.start(4 + n_z + k, ps.at[target[2]], pf.at[t, z], target)
                  for k, target in enumerate([core] + zs + other_line)]
    start_zero(1)
    for p in range(2, len(order)):
        prepare(p)
    tick()
    for copy in mod_copies + vec_copies:
        copy.wait_recv()
    vec_local.wait()
    row = lax.broadcasted_iota(jnp.int32, (8, cols), 0)
    for zi in range(n_z):
        bias = jnp.where(row < 6, vz[zi, 0:8, :], 0.0)
        x_mod[:, zi * cols:(zi + 1) * cols] = pf[0, zi] + pf[1, zi] + bias
    x_mod[...] = reorder(x_mod[...], n_hi)
    x_vec[...] = vz[...]
    tick()

    def wide(k):
        return cat([vz[zi, k:k + 1, :] for zi in range(n_z)], 1)

    def narrow(k):
        return cat([vz[zi, k:k + 1, lanes_at(t)] for zi in range(n_z)], 1)

    got_share(0)
    got_share(2)
    half = 2 * PIECE
    full = 2 * half
    mine_ids = idb.at[pl.ds(2 * t, 2)]
    id_copy = misc.start(4 + 3 * n_z, mine_ids, mine_ids, core)
    flush(tokb, x_tok)

    def first_norm(rows, at, p):
        normed, unused = normalize(tokb[p, rows, :].astype(F32))
        h1[t, at, :] = (normed * (1.0 + x_mod[1:2, :]) + x_mod[2:3, :]).astype(BF16)
    step_rows(piece, first_norm)
    h1_copy = misc.start(5 + 3 * n_z, h1.at[t], h1.at[t], core)

    tick(TICKS[0])
    id_copy.wait_recv()
    lanes = lane_of((full, LANES)) % HD
    scale = idb[...].reshape(full, LANES).astype(F32)
    feature = lanes.astype(F32)
    ma[...] = jnp.where((lanes < 16) & (feature > scale), 1.0, 0.0).astype(BF16)
    mb[...] = jnp.where((lanes < 16) & (feature == scale), NEG, 0.0).astype(BF16)
    flush(ma, x_ma)
    flush(mb, x_mb)
    tick(TICKS[1])
    h1_copy.wait_recv()

    def whole(ref):
        return ref[...].reshape(full, ref.shape[-1])

    def w_in(m):
        return g_in[m].reshape(8 * LANES, n_z * LANES)

    arrived(0)
    qr[...] = dot(whole(h1), w_in(0), NN) + narrow(6)
    q8[...] = (qr[...] * lax.rsqrt(head_mean(qr[...] * qr[...]) + NORM_EPS) * narrow(8)).astype(BF16) * 0.125
    tick(TICKS[2])
    arrived(1)
    kr[...] = dot(whole(h1), w_in(1), NN)
    kh[...] = (kr[...] * lax.rsqrt(head_mean(kr[...] * kr[...]) + NORM_EPS) * narrow(9)).astype(BF16)
    flush(qr, x_qr)
    flush(kr, x_kr)
    flush(q8, x_q8)
    flush(kh, x_kh)
    tick(TICKS[3])
    pick(pick_loads[1], cot)
    send_share(1)
    arrived(2)
    vv[...] = (dot(whole(h1), w_in(2), NN) + narrow(7)).astype(BF16)
    flush(vv, x_v)
    flush(h1, x_h1)
    flush(g_in.at[pl.ds(0, 3)], x_wq)
    def attend(i, carry):
        at = lanes_at(i)
        q2, k2, v2 = q8[:, at], kh[:, at], vv[:, at]
        mine_a, mine_b = ma[...], mb[...]
        low = lane_of((full, LANES)) < HD
        outs, tops = [], []
        for h in (0, 1):
            here = low if h == 0 else jnp.logical_not(low)
            s = dot(jnp.where(here, q2, mine_a), jnp.where(here, k2, mine_b), NT)
            top = jnp.max(s, axis=1, keepdims=True)
            e = jnp.exp(s - top).astype(BF16)
            got = dot(e, jnp.where(here, v2, jnp.ones_like(v2)), NN)
            total = got[:, HD:HD + 1] if h == 0 else got[:, 0:1]
            outs.append(got / total)
            tops.append(top + jnp.log(total))
        oo[:, at] = jnp.where(low, outs[0], outs[1]).astype(BF16)
        lse[:, at] = jnp.where(low, tops[0], tops[1])
        return carry

    pairs = n_z * LANES // LANES
    done = 0
    for i in range(pairs):
        tick(TICKS[4 + i])
        if i + 1 == pairs or TICKS[5 + i]:
            lax.fori_loop(done, i + 1, attend, 0)
            done = i + 1
    flush(oo, x_o)
    flush(lse, x_lse)

    arrived(3)
    flush(g_out.at[0], x_wo)
    width = 8 * LANES
    hw = width // 2
    for j in (0, 1):
        both = dot(oo[...], g_out[0, j], NN)
        attn[:, j * hw:(j + 1) * hw] = jnp.where(t == 0, both[:half], both[half:])
        at_send[:, j * hw:(j + 1) * hw] = jnp.where(t == 0, both[half:], both[:half]).astype(BF16)
    at_copy = misc.start(7 + 3 * n_z, at_send, at_recv, core)
    tick(TICKS[8])
    at_copy.wait_recv()
    proj_bias = reorder(wide(10 + n_ff), n_hi)


    def second_norm(rows, at, p):
        total = attn[at, :] + at_recv[at, :].astype(F32) + proj_bias
        attn[at, :] = total
        middle = tokb[p, rows, :].astype(F32) + x_mod[0:1, :] * total
        mid[at, :] = middle
        normed, unused = normalize(middle)
        h2[t, at, :] = (normed * (1.0 + x_mod[4:5, :]) + x_mod[5:6, :]).astype(BF16)
    step_rows(piece, second_norm)
    h2_copy = misc.start(8 + 3 * n_z, h2.at[t], h2.at[t], core)
    flush(attn, x_attn)
    flush(mid, x_mid)
    got_share(1)
    flush(cotb, x_cot)

    def gate(rows, at, p):
        gf[t, at, :] = (cotb[p, rows, :].astype(F32) * x_mod[3:4, :]).astype(BF16)
    step_rows(piece, gate)
    gf_copy = misc.start(6 + 3 * n_z, gf.at[t], gf.at[t], core)

    tick(TICKS[9])
    h2_copy.wait_recv()
    gf_copy.wait_recv()
    x_gf[...] = jnp.zeros_like(x_gf)
    x_gf[0:1, :] = jnp.sum(whole(gf).astype(F32), axis=0, keepdims=True)
    x_gu[...] = jnp.zeros_like(x_gu)

    mine_rows = pl.ds(pl.multiple_of(t * half, half), half)
    other_rows = pl.ds(pl.multiple_of((1 - t) * half, half), half)
    for r in range(n_ff):
        arrived(4 + 2 * r)
        bias_row = narrow(10 + r)
        u = dot(whole(h2), w_in(3 + r), NN) + bias_row
        value, gradient = gelu_both(u)
        act_low[...] = value.astype(BF16)
        slope[...] = gradient
        tick(TICKS[10 + 3 * r])
        for j in (0, 1):
            gout[r, j] = dot(act_low[...], gf[:, :, j * hw:(j + 1) * hw].reshape(full, hw), TN).astype(BF16)
        flush(gout.at[r], x_gout.at[r])
        arrived(5 + 2 * r)
        for j in (0, 1):
            part = dot(act_low[...], g_out[1 + r, j], NN)
            cols_here = pl.ds(j * hw, hw)
            facc[:, cols_here] = part if r == 0 else facc[:, cols_here] + part
        if r == n_ff - 1:
            fsend[...] = facc[other_rows, :].astype(BF16)
            flush(facc.at[mine_rows], x_fown)
            flush(fsend, x_fsend)
        back_act = (dot(gf[:, :, :hw].reshape(full, hw), g_out[1 + r, 0], NT)
                    + dot(gf[:, :, hw:].reshape(full, hw), g_out[1 + r, 1], NT))
        gu = (back_act * slope[...]).astype(BF16)
        act_low[...] = gu
        tick(TICKS[11 + 3 * r])
        x_gu[r:r + 1, :] = jnp.sum(gu.astype(F32), axis=0, keepdims=True)
        gin[r] = dot(whole(h2), act_low[...], TN).astype(BF16).reshape(gin.shape[1:])
        flush(gin.at[r], x_gin.at[r])
        tick(TICKS[12 + 3 * r])
        part = dot(act_low[...], w_in(3 + r), NT)
        dacc[...] = part if r == 0 else dacc[...] + part

    assert not ticks and not extras
    dsend[...] = dacc[other_rows, :].astype(BF16)
    flush(dacc.at[mine_rows], x_down)
    flush(dsend, x_dsend)
    for copy in flushed:
        copy.wait()
    for j, (src, dst) in enumerate(shares):
        for yd in (0, 1):
            @pl.when(jnp.logical_not(loops & (y == yd)))
            def _():
                ref = src.at[yd]
                pltpu.make_async_remote_copy(
                    src_ref=ref, dst_ref=ref, send_sem=tok_sem.at[0, j, yd], recv_sem=tok_sem.at[1, j, x],
                    device_id=(f_base + y, 2 * yd + t, z), device_id_type=MESH).wait_send()
    ag.finish()
    misc.finish()


def forward(x_in, x_out, tok, cot, ids, act, vec, n_z, n_hi):
    n_out = x_out.shape[0]
    n_ff = n_out - 1
    n_in = 3 + n_ff
    pieces = n_in + n_out
    here, width = n_z * LANES, 8 * LANES
    half, full = 2 * PIECE, 4 * PIECE
    piece, n_seq = tok.shape[:2]
    hw = width // 2
    S = jax.ShapeDtypeStruct
    wide_low, wide_full = S((half, width), BF16), S((half, width), F32)
    cols_low, cols_full = S((full, here), BF16), S((full, here), F32)
    mask = S((full, LANES), BF16)
    big = [
        S((3, 2, 4, LANES, here), BF16), S((2, here, hw), BF16), S((2, half, width), BF16), cols_full, cols_full,
        cols_low, cols_low, cols_low, cols_low, cols_full, mask, mask, S((2, piece, width), BF16),
        S((2, piece, width), BF16), wide_full, wide_full, wide_full, wide_low, wide_full, wide_low,
        S((n_ff, 2, 4, LANES, here), BF16), S((n_ff, 2, here, hw), BF16)]
    small = [S((8, width), F32), S((8, here), F32), S((8, width), F32), S((n_z,) + vec.shape, F32), S((4 * n_z, LANES), F32)]
    any_space, vmem = pl.BlockSpec(memory_space=pl.ANY), pl.BlockSpec(memory_space=pltpu.VMEM)
    mod_shape = (8, vec.shape[1])
    V = pltpu.VMEM
    dma = pltpu.SemaphoreType.DMA
    return pl.pallas_call(
        functools.partial(forward_kernel, n_z, n_ff, n_hi),
        out_shape=tuple(big + small),
        in_specs=[any_space] * 5 + [vmem] * 2,
        out_specs=tuple([any_space] * len(big) + [vmem] * len(small)),
        scratch_shapes=[
            V((n_in, 2, 4, LANES, here), BF16), V((n_out, 2, here, hw), BF16),
            V((2, piece, width), BF16), V((2, piece, width), BF16), V((4, PIECE, LANES), BF16),
            V((2, 2 * n_z, LANES), F32), V((4 * n_z,) + mod_shape, F32), V((3, n_z) + mod_shape, F32), V((n_z,) + mod_shape, F32),
            V((2, n_z) + mod_shape, F32), V((n_z,) + vec.shape, F32),
            V((2, half, width), BF16), V((2, half, width), BF16), V((2, half, width), BF16),
            V((full, here), F32), V((full, here), F32), V((full, here), BF16), V((full, here), BF16), V((full, here), BF16),
            V((full, here), BF16), V((full, here), F32), V((full, LANES), BF16), V((full, LANES), BF16),
            V((half, width), BF16), V((half, width), BF16), V((half, width), F32), V((half, width), F32),
            V((full, width), F32), V((full, width), F32), V((half, width), BF16), V((half, width), BF16),
            V((n_ff, 2, 4, LANES, here), BF16), V((n_ff, 2, here, hw), BF16), V((full, here), BF16), V((full, here), F32),
            V(x_in.shape, F32), V(x_out.shape, F32), V((n_in, 2, LANES, LANES), BF16), V((n_out, 2, LANES, LANES), BF16),
            dma((pieces + 1,)), dma((pieces, 4 * n_z + 3)), dma((pieces, 4 * n_z + 3)), dma((9 + 3 * n_z,)), dma((9 + 3 * n_z,)),
            dma((len(big) + 2 * n_ff,)), dma((2, 3, 2)), dma((x_in.shape[0] + n_out,)),
            V((piece, n_seq, width), BF16), V((16, n_seq, width), F32), V((2, piece, width), BF16), V((2, piece, width), BF16),
            dma((2,)),
        ],
        compiler_params=pltpu.CompilerParams(collective_id=0, has_side_effects=True, vmem_limit_bytes=VMEM_BYTES),
    )(x_in, x_out, tok, cot, ids, act, vec)

class Guarded:
    def __init__(self):
        self.sent = []

    def start(self, cond, copy):
        @pl.when(cond)
        def _():
            copy.start()
        self.sent.append((cond, copy))

    def finish(self):
        for cond, copy in self.sent:
            @pl.when(cond)
            def _(copy=copy):
                copy.wait_send()


def backward_kernel(n_z, n_ff, n_hi, *refs):
    n_in, n_out = 3 + n_ff, 1 + n_ff
    (x_wq, x_wo, x_h1, x_qr, x_kr, x_q8, x_kh, x_v, x_o, x_lse, x_ma, x_mb, x_tok, x_cot, x_attn, x_mid,
     x_fown, x_fsend, x_down, x_dsend, x_gin, x_gout, x_weight, mod, gu_sum, gf_sum, vz, act,
     o_mixed, o_grad, o_in, o_out, o_vec, o_ada, o_cond, o_norm,
     wq, wo, h1, qr, kr, q8, kh, vv, oo, lse, ma, mb, tokb, cotb, attn, mid, buf, f_recv, d_recv,
     dmid, ga, go, mixed, sums, vd, vdr, vs, vdz, zv, v_all, d_mod, v_half, norm, norm_plane, norm_line, cond_z, cond_all,
     p_full, q_full, p_half, q_half, a_in, a_out, b_in, b_out, z_in, z_out, f_in, f_out,
     load_sem, own_sem, rs_send, rs_recv, m_send, m_recv, t_send, t_recv, g_send, g_recv) = refs
    f, c, z, t, x, y = place()
    core, xp, yp, zs = partners(n_z)
    f_base = f - t
    last = n_z - 1
    half, full = 2 * PIECE, 4 * PIECE
    width = mod.shape[1]
    hw = width // 2
    piece = x_tok.shape[1]
    clear_tail(ga, t)

    barrier = pltpu.get_barrier_semaphore()
    diagonal = (f, 3 - c, z)
    plane = [xp, yp, diagonal]
    other_line = [(f + 1 - 2 * t, c, target[2]) for target in zs]
    for target in [core] + plane + zs + other_line:
        pl.semaphore_signal(barrier, inc=1, device_id=target, device_id_type=MESH)
    loops = (y == t) & (x == t)
    for ys in (0, 1):
        @pl.when(jnp.logical_not(loops & (y == ys)))
        def _():
            pl.semaphore_signal(barrier, inc=1, device_id=(f_base + y, 2 * ys + t, z), device_id_type=MESH)

    loads = {}
    names = [("f", x_fown, buf.at[0]), ("mid", x_mid, mid), ("cot", x_cot, cotb), ("d", x_down, buf.at[1]),
             ("attn", x_attn, attn), ("wo", x_wo, wo), ("o", x_o, oo), ("q", x_q8, q8), ("k", x_kh, kh), ("v", x_v, vv),
             ("lse", x_lse, lse), ("ma", x_ma, ma), ("mb", x_mb, mb), ("qr", x_qr, qr), ("kr", x_kr, kr),
             ("h1", x_h1, h1), ("wq", x_wq, wq), ("tok", x_tok, tokb)]
    for i, (name, src, dst) in enumerate(names):
        loads[name] = pltpu.make_async_copy(src, dst, load_sem.at[i])
        loads[name].start()
    pl.semaphore_wait(barrier, 4 + 2 * n_z - jnp.where(loops, 1, 0))

    rs = Wire(rs_send, rs_recv)
    misc = Wire(m_send, m_recv)
    chain = Guarded()
    f_copy = misc.start(0, x_fsend, f_recv, core)
    d_copy = misc.start(1, x_dsend, d_recv, core)

    order = []
    for r in range(n_ff):
        order += [("i", 3 + r), ("o", 1 + r)]
    order += [("o", 0), ("i", 2), ("i", 1), ("i", 0)]
    pieces = len(order)
    one, two, four, own_half = {}, {}, {}, {}

    def y_first(p):
        return p % 2 == 0

    def parts(p, mine):
        if y_first(p):
            yy = y if mine else 1 - y
            return [2 * yy, 2 * yy + 1]
        xx = x if mine else 1 - x
        return [xx, 2 + xx]

    def source(p, at):
        kind, m = order[p]
        if kind == "i":
            return x_gin.at[m - 3, :, at] if m >= 3 else p_full.at[m, :, at]
        return x_gout.at[m - 1, :, :, lanes_at(at)] if m >= 1 else q_full.at[:, :, lanes_at(at)]

    def kept(p, k):
        kind, m = order[p]
        return p_half.at[m, k] if kind == "i" else q_half.at[m, k]

    def bufs(p, inner, outer):
        kind, m = order[p]
        return inner.at[m] if kind == "i" else outer.at[m]

    def step_one(p):
        one[p] = [rs.start((p, k), source(p, at), bufs(p, a_in, a_out).at[k], yp if y_first(p) else xp)
                  for k, at in enumerate(parts(p, False))]
        own_half[p] = []
        for k, at in enumerate(parts(p, True)):
            copy = pltpu.make_async_copy(source(p, at), kept(p, k), own_sem.at[p, k])
            copy.start()
            own_half[p].append(copy)

    def step_two(p):
        for copy in one[p]:
            copy.wait_recv()
        for copy in own_half[p]:
            copy.wait()
        for k in (0, 1):
            ref = kept(p, k)
            ref[...] = (ref[...].astype(F32) + bufs(p, a_in, a_out)[k].astype(F32)).astype(BF16)
        go_bit = (1 - x) if y_first(p) else (1 - y)
        two[p] = rs.start((p, 2), kept(p, go_bit), bufs(p, b_in, b_out), xp if y_first(p) else yp)

    def span(p, ref, lo, hi):
        if order[p][0] == "i":
            return ref.at[:, :, lo * LANES:hi * LANES]
        return ref.at[:, lo * LANES:hi * LANES, :]

    def right_copy(p, s):
        here = kept(p, x if y_first(p) else y)
        return pltpu.make_async_remote_copy(
            src_ref=span(p, here, s + 1, n_z), dst_ref=span(p, bufs(p, z_in, z_out), s + 2, n_z + 1),
            send_sem=rs_send.at[p, 3], recv_sem=rs_recv.at[p, 3], device_id=(f, c, z + 1), device_id_type=MESH)

    def left_copy(p, s):
        here = kept(p, x if y_first(p) else y)
        return pltpu.make_async_remote_copy(
            src_ref=span(p, here, 0, s), dst_ref=span(p, bufs(p, z_in, z_out), 0, s),
            send_sem=rs_send.at[p, 4], recv_sem=rs_recv.at[p, 4], device_id=(f, c, z - 1), device_id_type=MESH)

    def add_into(p, lo, hi, shift):
        here = kept(p, x if y_first(p) else y)
        a, b = span(p, here, lo, hi), span(p, bufs(p, z_in, z_out), lo + shift, hi + shift)
        a[...] = (a[...].astype(F32) + b[...].astype(F32)).astype(BF16)

    def step_z(p, s):
        if s == 0:
            two[p].wait_recv()
            here = kept(p, x if y_first(p) else y)
            here[...] = (here[...].astype(F32) + bufs(p, b_in, b_out)[...].astype(F32)).astype(BF16)

        @pl.when(z == s)
        def _():
            if s > 0:
                landed = span(p, bufs(p, z_in, z_out), s + 1, n_z + 1)
                pltpu.make_async_copy(landed, landed, rs_recv.at[p, 3]).wait()
            if s < last:
                if s > 0:
                    add_into(p, s + 1, n_z, 1)
                right_copy(p, s).start()

        @pl.when(z == last - s)
        def _():
            e = last - s
            if s > 0:
                landed = span(p, bufs(p, z_in, z_out), 0, e + 1)
                pltpu.make_async_copy(landed, landed, rs_recv.at[p, 4]).wait()
            if e > 0:
                if s > 0:
                    add_into(p, 0, e, 0)
                left_copy(p, e).start()

    norm[...] = jnp.zeros_like(norm)

    def add_squares(values):
        square = values * values
        parts = [square[8 * i:8 * i + 8] for i in range(square.shape[0] // 8)]
        while len(parts) > 1:
            parts = [a + b for a, b in zip(parts[::2], parts[1::2])]
        for k in range(square.shape[1] // LANES):
            norm[...] = norm[...] + parts[0][:, k * LANES:(k + 1) * LANES]

    def step_core(p):
        kind, m = order[p]
        here = kept(p, x if y_first(p) else y)
        total, result = (f_in, o_in) if kind == "i" else (f_out, o_out)
        for s in range(n_z):
            @pl.when(z == s)
            def _():
                value = span(p, here, s, s + 1)[...].astype(F32)
                if s > 0:
                    value = value + span(p, bufs(p, z_in, z_out), s + 1, s + 2)[...].astype(F32)
                if s < last:
                    value = value + span(p, bufs(p, z_in, z_out), s, s + 1)[...].astype(F32)
                total[m] = value
        result[m, t] = total[m, t]
        add_squares(total[m, 0])
        add_squares(total[m, 1])
        four[p] = rs.start((p, 5), total.at[m, 1 - t], result.at[m, t], core)

    def in_range(p):
        return 0 <= p < pieces

    ready = [2 * n_ff]
    started = [0]
    step = [0]

    def first_sends(upto):
        while started[0] < min(upto, ready[0], pieces):
            step_one(started[0])
            started[0] += 1

    passes, chores = [], []

    def pump(n=1):
        for _ in range(n):
            k = step[0]
            first_sends(k + LOOK)
            if in_range(k) and k >= started[0]:
                return
            if in_range(k):
                step_two(k)
            for unused in range(PASSES):
                if passes:
                    pass_along(*passes.pop(0))
            for s in range(n_z):
                if in_range(k - 1 - 2 * s):
                    step_z(k - 1 - 2 * s, s)
            if in_range(k - 2 * n_z):
                step_core(k - 2 * n_z)
            if chores:
                chore = chores.pop(0)
                if chore is not None:
                    chore()
            step[0] += 1

    first_sends(2)

    def share_out(j, src, dst):
        for xs in (0, 1):
            own = loops & (x == xs)
            there = dst.at[2 * z + y]
            local = pltpu.make_async_copy(src.at[xs], there, t_recv.at[j, y])

            @pl.when(own)
            def _():
                local.start()
            chain.start(jnp.logical_not(own), pltpu.make_async_remote_copy(
                src_ref=src.at[xs], dst_ref=there, send_sem=t_send.at[j, xs], recv_sem=t_recv.at[j, y],
                device_id=(f_base + x, 2 * t + xs, z), device_id_type=MESH))

    def pass_along(j, dst, s, part):
        lanes = pl.ds(part * (width // PARTS), width // PARTS)
        if s == 0 and part == 0:
            for ys in (0, 1):
                pltpu.make_async_copy(dst.at[2 * z + ys], dst.at[2 * z + ys], t_recv.at[j, ys]).wait()
        for side, (there, back_at) in enumerate(((z + 1, z - s), (z - 1, z + s))):
            valid = (back_at >= 0) & (back_at <= last)
            block = dst.at[pl.ds(2 * lax.clamp(0, back_at, last), 2), :, lanes]
            if s > 0:
                @pl.when(valid)
                def _():
                    pltpu.make_async_copy(block, block, g_recv.at[j, side, s, part]).wait()
            if s < last:
                chain.start(valid & (there >= 0) & (there <= last), pltpu.make_async_remote_copy(
                    src_ref=block, dst_ref=block, send_sem=g_send.at[j, side, s, part],
                    recv_sem=g_recv.at[j, side, s + 1, part],
                    device_id=(f, c, lax.clamp(0, there, last)), device_id_type=MESH))

    def pass_all(j, dst):
        passes.extend((j, dst, s, part) for s in range(n_z) for part in range(PARTS))

    def wide(k):
        return cat([vz[zi, k:k + 1, :] for zi in range(n_z)], 1)

    def narrow(k):
        return cat([vz[zi, k:k + 1, lanes_at(t)] for zi in range(n_z)], 1)

    def tally(j, values):
        if values.shape[0] == 16:
            sums[j] = sums[j] + values[:8] + values[8:]
        else:
            sums[j, 0:1] = sums[j, 0:1] + jnp.sum(values, axis=0, keepdims=True)

    sums[...] = jnp.zeros_like(sums)

    ffn_bias = reorder(wide(11 + n_ff), n_hi)
    for name in ("f", "mid", "cot"):
        loads[name].wait()
    f_copy.wait_recv()

    def mix(rows, at, p):
        out = buf[0, at, :] + f_recv[at, :].astype(F32) + ffn_bias
        tally(3, cotb[p, rows, :].astype(F32) * out)
        mixed[p, rows, :] = (mid[at, :] + mod[3:4, :] * out).astype(BF16)
    step_rows(piece, mix)
    share_out(0, mixed, o_mixed)

    first_sends(LOOK)
    for name in ("d", "attn"):
        loads[name].wait()
    d_copy.wait_recv()

    def second_norm(rows, at, p):
        grad = buf[1, at, :] + d_recv[at, :].astype(F32)
        normed, scale = normalize(mid[at, :])
        tally(4, grad * normed)
        tally(5, grad)
        w = grad * (1.0 + mod[4:5, :])
        pulled = scale * (w - jnp.mean(w, axis=-1, keepdims=True) - normed * jnp.mean(w * normed, axis=-1, keepdims=True))
        total = cotb[p, rows, :].astype(F32) + pulled
        dmid[at, :] = total
        tally(0, total * attn[at, :])
        low = (total * mod[0:1, :]).astype(BF16)
        ga[t, at, :] = low
        tally(6, low.astype(F32))
    step_rows(piece, second_norm)
    ga_copy = misc.start(2, ga.at[t], ga.at[t], core)


    loads["wo"].wait()
    loads["o"].wait()
    ga_copy.wait_recv()
    pump(1)
    for j in (0, 1):
        ga_j = ga[:, :, j * hw:(j + 1) * hw].reshape(full, hw)
        part = dot(ga_j, wo[j], NT)
        if j == 0:
            first_part = part
    go[...] = (first_part + part).astype(BF16)
    for name in ("q", "k", "v", "lse", "ma", "mb", "qr", "kr"):
        loads[name].wait()
    pass_all(0, o_mixed)

    vs[...] = jnp.zeros_like(vs)

    def head_back(raw, grad, gain):
        scale = lax.rsqrt(head_mean(raw * raw) + NORM_EPS)
        normed = raw * scale
        gain_grad = jnp.sum(grad * normed, axis=0, keepdims=True)
        w = grad * gain
        return (scale * (w - normed * head_mean(w * normed))).astype(BF16), gain_grad

    def attend_back(i, carry):
        at = lanes_at(i)
        q2, k2, v2, g2, o2 = q8[:, at], kh[:, at], vv[:, at], go[:, at], oo[:, at]
        mine_a, mine_b = ma[...], mb[...]
        lanes = lane_of((full, LANES))
        low, l64 = lanes < HD, lanes % HD
        product = o2.astype(F32) * g2.astype(F32)
        dqs, dks, dvs = [], [], []
        one_like, zero_like = jnp.ones_like(v2), jnp.zeros_like(v2)
        for h in (0, 1):
            here = low if h == 0 else jnp.logical_not(low)
            l1, l2, l3 = split_three(lse[:, at][:, HD * h:HD * h + 1])
            qa = jnp.where(l64 == 40, -l1, jnp.where(l64 == 41, -l2, jnp.where(l64 == 42, -l3, mine_a)))
            ka = jnp.where((l64 >= 40) & (l64 < 43), one_like, mine_b)
            weight = jnp.exp(dot(jnp.where(here, k2, ka), jnp.where(here, q2, qa), NT))
            d1, d2, d3 = split_three(jnp.sum(jnp.where(here, product, 0.0), axis=1, keepdims=True))
            da = jnp.where(l64 == 0, -d1, jnp.where(l64 == 1, -d2, jnp.where(l64 == 2, -d3, zero_like)))
            va = jnp.where(l64 < 3, one_like, zero_like)
            ds = (weight * dot(jnp.where(here, v2, va), jnp.where(here, g2, da), NT)).astype(BF16)
            dvs.append(dot(weight.astype(BF16), g2, NN))
            dks.append(dot(ds, q2, NN))
            dqs.append(dot(ds, k2, TN))
        dq = jnp.where(low, dqs[0], dqs[1]) * 0.125
        dk = jnp.where(low, dks[0], dks[1])
        gq, q_gain = head_back(qr[:, at], dq, vs[8:9, at])
        gk, k_gain = head_back(kr[:, at], dk, vs[9:10, at])
        gv = jnp.where(low, dvs[0], dvs[1]).astype(BF16)
        q8[:, at] = gq
        kh[:, at] = gk
        vv[:, at] = gv
        vs[0:1, at] = jnp.sum(gq.astype(F32), axis=0, keepdims=True)
        vs[1:2, at] = jnp.sum(gv.astype(F32), axis=0, keepdims=True)
        vs[2:3, at] = q_gain
        vs[3:4, at] = k_gain
        return carry

    vs[8:9, :] = narrow(8)
    vs[9:10, :] = narrow(9)
    pairs = n_z
    for i in range(0, pairs, 2):
        lax.fori_loop(i, i + 2, attend_back, 0)
        pump(1)
    ada_refs, ada_loads = [], []
    for j in range(6):
        rows_at, cols_at = (j // 2) * LANES, (j % 2) * (n_z * LANES // 2)
        ada_refs.append(qr.at[rows_at:rows_at + LANES, cols_at:cols_at + n_z * LANES // 2])
        ada_loads.append(pltpu.make_async_copy(x_weight.at[3 + n_ff + j], ada_refs[j], load_sem.at[len(names) + j]))
        ada_loads[j].start()
    loads["wq"].wait()
    part = dot(q8[...], wq[0].reshape(width, n_z * LANES), NT)
    part = part + dot(kh[...], wq[1].reshape(width, n_z * LANES), NT)
    part = part + dot(vv[...], wq[2].reshape(width, n_z * LANES), NT)
    buf[0] = jnp.where(t == 0, part[:half], part[half:])
    f_recv[...] = jnp.where(t == 0, part[half:], part[:half]).astype(BF16)
    h_copy = misc.start(3, f_recv, d_recv, core)
    for j in (0, 1):
        ga_j = ga[:, :, j * hw:(j + 1) * hw].reshape(full, hw)
        q_full[j] = dot(oo[...], ga_j, TN).astype(BF16)
    ready[0] += 1
    loads["h1"].wait()
    h1_all = h1[...].reshape(full, width)
    for m, ref in ((2, vv), (1, kh), (0, q8)):
        p_full[m] = dot(h1_all, ref[...], TN).astype(BF16).reshape(p_full.shape[1:])
        ready[0] += 1
    loads["tok"].wait()
    pump(1)
    h_copy.wait_recv()

    def first_norm(rows, at, p):
        grad = buf[0, at, :] + d_recv[at, :].astype(F32)
        normed, scale = normalize(tokb[p, rows, :].astype(F32))
        tally(1, grad * normed)
        tally(2, grad)
        w = grad * (1.0 + mod[1:2, :])
        pulled = scale * (w - jnp.mean(w, axis=-1, keepdims=True) - normed * jnp.mean(w * normed, axis=-1, keepdims=True))
        cotb[p, rows, :] = (dmid[at, :] + pulled).astype(BF16)
    step_rows(piece, first_norm)
    share_out(1, cotb, o_grad)
    pass_all(1, o_grad)
    pump(1)

    for j in range(7):
        vd[j:j + 1, :] = jnp.sum(sums[j], axis=0, keepdims=True)
    vd[7:8, :] = gf_sum[0:1, :] * 0.5
    v_copy = misc.start(4, vd, vdr, core)
    vs[4:8, :] = gu_sum[0:4, :]
    cols = width // n_z
    n_ada = 6
    chips = 4 * n_z
    waits = {}

    def exact(a, b, dims):
        return lax.dot_general(a, b, (dims, ((), ())), precision=PRECISE, preferred_element_type=F32)

    def arrive(name):
        for copy in waits.pop(name):
            copy.wait_recv()

    def mods(j):
        return d_mod[...].reshape(chips, 8, cols)[:, j, :]

    def along_line():
        v_copy.wait_recv()
        vd_all = reorder(vd[...] + vdr[...], n_hi, inverse=True)
        for zi in range(n_z):
            vdz[zi] = vd_all[:, zi * cols:(zi + 1) * cols]
        d_mod[x, y, z] = vdz[z]
        zv[z] = vs[0:8, lanes_at(z)]
        waits["line"] = []
        for d, target in enumerate(zs):
            zi = lax.rem(z + 1 + d, n_z)
            waits["line"].append(misc.start(5 + d, vdz.at[zi], d_mod.at[x, y, z], target))
            waits["line"].append(misc.start(4 + n_z + d, vs.at[pl.ds(0, 8), lanes_at(zi)], zv.at[z], target))

    slot = 3 + 2 * n_z

    def over_plane():
        arrive("line")
        total = zv[0]
        for zi in range(1, n_z):
            total = total + zv[zi]
        v_all[x, y] = total
        waits["plane"] = []
        for d, target in enumerate(plane):
            waits["plane"].append(misc.start(slot + d, d_mod.at[x, y], d_mod.at[x, y], target))
            waits["plane"].append(misc.start(slot + 3 + d, v_all.at[x, y], v_all.at[x, y], target))

    def products():
        arrive("plane")
        v_half[t] = (v_all[0, 0] + v_all[0, 1]) + (v_all[1, 0] + v_all[1, 1])
        waits["vec"] = [misc.start(slot + 6, v_half.at[t], v_half.at[t], core)]
        for copy in ada_loads:
            copy.wait()
        total = 0.0
        for j, ref in enumerate(ada_refs):
            total = total + exact(mods(j), ref[...].astype(BF16).astype(F32), NT)
        cond_z[z] = total
        waits["cond line"] = [misc.start(slot + 7 + d, cond_z.at[z], cond_z.at[z], target) for d, target in enumerate(zs)]
        for j in range(n_ada):
            o_ada[j] = exact(act[...], mods(j), TN)
            if n_hi == 1:
                add_squares(o_ada[j])

    def cond_plane():
        arrive("cond line")
        total = cond_z[0]
        for zi in range(1, n_z):
            total = total + cond_z[zi]
        cond_all[t, c] = total
        at = slot + 6 + n_z
        waits["cond plane"] = [misc.start(at + d, cond_all.at[t, c], cond_all.at[t, c], target)
                               for d, target in enumerate(plane)]

    def cond_core():
        arrive("cond plane")
        waits["cond core"] = [misc.start(slot + 9 + n_z, cond_all.at[t], cond_all.at[t], core)]

    chores.extend([along_line, None, over_plane, None, products, None, cond_plane, None, cond_core])

    while step[0] < pieces + 2 * n_z or chores:
        pump(1)
    while passes:
        pass_along(*passes.pop(0))
    arrive("cond core")
    mine = pl.ds(pl.multiple_of(2 * n_z * t, 2 * n_z), 2 * n_z)
    o_cond[...] = cat([cond_all[ti, ck, mine, :] for ti in (0, 1) for ck in range(4)], 1)

    arrive("vec")
    mod_sum = jnp.sum(d_mod[...].reshape(chips, 8, cols), axis=0)
    o_vec[...] = cat([mod_sum[:n_ada], cat([v_half[0], v_half[1]], 1), mod_sum[n_ada:]], 0)
    if n_hi == 1:
        square = o_vec[...] * o_vec[...]
        square = square[:8] + square[8:]
        vec_squares = sum(square[:, k * LANES:(k + 1) * LANES] for k in range(cols // LANES))
        slot = slot + 10 + n_z
        norm_plane[c] = norm[...] + jnp.where((f == 0) & (c == 0), vec_squares, 0.0)
        copies = [misc.start(slot + d, norm_plane.at[c], norm_plane.at[c], target) for d, target in enumerate(plane)]
        for copy in copies:
            copy.wait_recv()
        norm_line[t, z] = (norm_plane[0] + norm_plane[1]) + (norm_plane[2] + norm_plane[3])
        copies = [misc.start(slot + 3 + d, norm_line.at[t, z], norm_line.at[t, z], target)
                  for d, target in enumerate([core] + zs + other_line)]
        for copy in copies:
            copy.wait_recv()
        total = norm_line[0, 0]
        for ti in (0, 1):
            for zi in range(n_z):
                if ti + zi > 0:
                    total = total + norm_line[ti, zi]
        total = jnp.sum(jnp.sum(total, axis=0, keepdims=True), axis=1, keepdims=True)
        o_norm[...] = jnp.broadcast_to(jnp.sqrt(total), o_norm.shape)
    else:
        o_norm[...] = jnp.zeros_like(o_norm)
    for p in range(pieces):
        four[p].wait_recv()
    for p in range(pieces):
        for s in range(n_z):
            @pl.when(z == s)
            def _():
                if s < last:
                    right_copy(p, s).wait_send()
                if s > 0:
                    left_copy(p, s).wait_send()
    chain.finish()
    rs.finish()
    misc.finish()


def backward(operands, n_z, n_ff, n_hi):
    n_in, n_out = 3 + n_ff, 1 + n_ff
    here, width = n_z * LANES, 8 * LANES
    half, full = 2 * PIECE, 4 * PIECE
    hw, cols = width // 2, width // n_z
    S, V, dma = jax.ShapeDtypeStruct, pltpu.VMEM, pltpu.SemaphoreType.DMA
    any_space, vmem = pl.BlockSpec(memory_space=pl.ANY), pl.BlockSpec(memory_space=pltpu.VMEM)
    piece = operands[12].shape[1]
    rows_out = S((2 * n_z, piece, width), BF16)
    pieces = n_in + n_out
    slots = 24 + 5 * n_z
    return pl.pallas_call(
        functools.partial(backward_kernel, n_z, n_ff, n_hi),
        out_shape=(rows_out, rows_out, S((n_in, 2, LANES, LANES), F32), S((n_out, 2, LANES, LANES), F32),
                   S((16, cols), F32), S((6, LANES, cols), F32), S((2 * n_z, width), F32),
                   S((8, LANES), F32)),
        in_specs=[any_space] * (len(operands) - 5) + [vmem] * 5,
        out_specs=tuple([any_space] * 2 + [vmem] * 6),
        scratch_shapes=[
            V((3, 2, 4, LANES, here), BF16), V((2, here, hw), BF16), V((2, half, width), BF16),
            V((full, here), F32), V((full, here), F32), V((full, here), BF16), V((full, here), BF16),
            V((full, here), BF16), V((full, here), BF16), V((full, here), F32), V((full, LANES), BF16),
            V((full, LANES), BF16), V((2, piece, width), BF16), V((2, piece, width), BF16), V((half, width), F32),
            V((half, width), F32), V((2, half, width), F32), V((half, width), BF16), V((half, width), BF16),
            V((half, width), F32), V((2, half, width), BF16), V((full, here), BF16), V((2, piece, width), BF16),
            V((8, 8, width), F32), V((8, width), F32), V((8, width), F32), V((16, here), F32),
            V((n_z, 8, cols), F32), V((n_z, 8, LANES), F32), V((2, 2, 8, LANES), F32),
            V((2, 2, n_z, 8, cols), F32), V((2, 8, LANES), F32), V((8, LANES), F32), V((4, 8, LANES), F32), V((2, n_z, 8, LANES), F32), V((n_z, 4 * n_z, LANES), F32), V((2, 4, 4 * n_z, LANES), F32),
            V((3, 2, 4, LANES, here), BF16), V((2, here, hw), BF16),
            V((n_in, 2, 2, LANES, here), BF16), V((n_out, 2, 2, here, LANES), BF16),
            V((n_in, 2, 2, LANES, here), BF16), V((n_out, 2, 2, here, LANES), BF16),
            V((n_in, 2, LANES, here), BF16), V((n_out, 2, here, LANES), BF16),
            V((n_in, 2, LANES, here + LANES), BF16), V((n_out, 2, here + LANES, LANES), BF16),
            V((n_in, 2, LANES, LANES), F32), V((n_out, 2, LANES, LANES), F32),
            dma((24,)), dma((pieces, 2)), dma((pieces, 6)), dma((pieces, 6)), dma((slots,)), dma((slots,)),
            dma((2, 2)), dma((2, 2)), dma((2, 2, n_z, PARTS)), dma((2, 2, n_z, PARTS)),
        ],
        compiler_params=pltpu.CompilerParams(collective_id=1, has_side_effects=True, vmem_limit_bytes=VMEM_BYTES),
    )(*operands)


def update_kernel(n_z, n_hi, *refs):
    (norm, cond_sum, cond, g_vec, w_vec, m_vec, v_vec, g_in, g_ada, g_out, w_in, m_in, v_in, w_out, m_out, v_out, mixed, grads,
     w_vec_new, m_vec_new, v_vec_new, c_vec_new, o_bias, o_cond, o_norm,
     w_in_new, m_in_new, v_in_new, c_in_new, w_out_new, m_out_new, v_out_new, c_out_new, o_mixed, o_grads,
     gi, ga, go, wi, mi, vi, ci, wo, mo, vo, co, low, wide, low_out, high, load_sem, store_sem) = refs
    n_seq, piece = mixed.shape[:2]
    loads, stores = {}, []

    def load(name, src, dst):
        loads[name] = pltpu.make_async_copy(src, dst, load_sem.at[len(loads)])
        loads[name].start()

    def store(src, dst):
        copy = pltpu.make_async_copy(src, dst, store_sem.at[len(stores)])
        copy.start()
        stores.append(copy)

    load("grads", grads, low.at[1])
    load("mixed", mixed, low.at[0])
    for name, src, dst in (("gi", g_in, gi), ("ga", g_ada, ga), ("wi", w_in, wi), ("mi", m_in, mi), ("vi", v_in, vi),
                           ("go", g_out, go), ("wo", w_out, wo), ("mo", m_out, mo), ("vo", v_out, vo)):
        load(name, src, dst)
    n_all, n_rows, cols = w_in.shape
    n_out = w_out.shape[0]
    factor = (CLIP_NORM / jnp.maximum(norm[0:1, 0:1], CLIP_NORM))
    factor_in = jnp.broadcast_to(factor, (1, cols))
    factor_out = jnp.broadcast_to(factor, (1, w_out.shape[2]))
    o_norm[...] = norm[0:1, 0:1]
    back = reorder(cond_sum[...], n_hi, inverse=True)
    rows = [back[n_z * yy + zi:n_z * yy + zi + 1] for zi in range(n_z) for yy in (0, 1)]
    gate = 1.0 / (1.0 + jnp.exp(-cond[...]))
    o_cond[...] = cat(rows, 0) * (gate * (1.0 + cond[...] * (1.0 - gate)))
    loads["grads"].wait()
    for i in range(n_seq):
        high[0:piece, i, :] = low[1, i].astype(F32)
    store(high.at[pl.ds(0, piece)], o_grads)
    w_vec_new[...], m_vec_new[...], v_vec_new[...], c_vec_new[...] = adam_update(
        w_vec[...], m_vec[...], v_vec[...], g_vec[...], factor_in, RATE_VECTOR, 0.0)
    last = g_vec.shape[0]
    o_bias[...] = g_vec[last - 1:last] * factor_in
    for name in ("gi", "ga", "wi", "mi", "vi"):
        loads[name].wait()
    lead = n_all - ga.shape[0]

    def update(m, grad):
        wi[m], mi[m], vi[m], ci[m] = adam_update(wi[m], mi[m], vi[m], grad, factor_in, RATE_MATRIX, WEIGHT_DECAY)

    def lead_rows(m, carry):
        update(m, cat([gi[m, 0], gi[m, 1]], 1))
        return carry

    def ada_rows(m, carry):
        update(lead + m, ga[m])
        return carry

    for lo, hi, body, shift in ((0, lead, lead_rows, 0), (0, n_all - lead, ada_rows, lead)):
        lax.fori_loop(lo, hi, body, 0)
        at = pl.ds(shift, hi)
        for src, dst in ((wi, w_in_new), (mi, m_in_new), (vi, v_in_new), (ci, c_in_new)):
            store(src.at[at], dst.at[at])
    for name in ("go", "wo", "mo", "vo"):
        loads[name].wait()
    for m in range(n_out):
        grad = cat([go[m, 0], go[m, 1]], 0)
        wo[m], mo[m], vo[m], co[m] = adam_update(wo[m], mo[m], vo[m], grad, factor_out, RATE_MATRIX, WEIGHT_DECAY)
    for src, dst in ((wo, w_out_new), (mo, m_out_new), (vo, v_out_new), (co, c_out_new)):
        store(src, dst)
    loads["mixed"].wait()
    for i in range(n_seq):
        wide[0:piece, i, :] = low[0, i].astype(F32)
    low_out[...] = wide[0:piece].astype(BF16)
    store(low_out, o_mixed)
    for copy in stores:
        copy.wait()


def update(small, large, rows_low, n_z, n_hi):
    S, V, dma = jax.ShapeDtypeStruct, pltpu.VMEM, pltpu.SemaphoreType.DMA
    any_space, vmem = pl.BlockSpec(memory_space=pl.ANY), pl.BlockSpec(memory_space=pltpu.VMEM)
    w_vec = small[4]
    g_in, g_ada, g_out, w_in, w_out = large[0], large[1], large[2], large[3], large[6]
    kinds = [S(a.shape, F32) for a in (w_vec, w_in, w_out)]
    news = [[k] * 3 + [S(k.shape, BF16)] for k in kinds]
    n_seq, piece, width = rows_low[0].shape
    turned = (piece, n_seq, width)
    whole = (PIECE, n_seq, width)
    return pl.pallas_call(
        functools.partial(update_kernel, n_z, n_hi),
        out_shape=tuple(news[0] + [S((1, w_vec.shape[1]), F32), S(small[2].shape, F32), S((1, 1), F32)] + news[1] + news[2] + [S(turned, BF16), S(turned, F32)]),
        in_specs=[vmem] * len(small) + [any_space] * (len(large) + 2),
        out_specs=tuple([vmem] * 7 + [any_space] * 10),
        scratch_shapes=[
            V(g_in.shape, F32), V(g_ada.shape, F32), V(g_out.shape, F32),
            V(w_in.shape, F32), V(w_in.shape, F32), V(w_in.shape, F32), V(w_in.shape, BF16),
            V(w_out.shape, F32), V(w_out.shape, F32), V(w_out.shape, F32), V(w_out.shape, BF16),
            V((2,) + rows_low[0].shape, BF16), V(whole, F32), V(turned, BF16), V(whole, F32), dma((11,)), dma((16,)),
        ],
        compiler_params=pltpu.CompilerParams(vmem_limit_bytes=VMEM_BYTES),
    )(*small, *large, *rows_low)


def condition_kernel(n_z, n_hi, labels, ids, table, act, cond, columns, sem):
    z = lax.axis_index("tp")
    n_seq, piece = ids.shape
    copies = [pltpu.make_async_copy(table.at[pl.ds(labels[i], 1)], cond.at[pl.ds(i, 1)], sem.at[i]) for i in range(n_seq)]
    for copy in copies:
        copy.start()
    low_ids = ids[...].astype(F32).astype(BF16)
    row = lax.broadcasted_iota(jnp.int32, (n_seq, LANES), 0)
    columns[...] = jnp.full(columns.shape, 10.0, BF16)
    for k in (0, 1):
        pick = jnp.where(row == 2 * z + k, 1.0, 0.0).astype(BF16)
        columns[k, 0:piece, :] = dot(low_ids, pick, TN).astype(BF16)
    for copy in copies:
        copy.wait()
    value = cond[...]
    value = (value / (1.0 + jnp.exp(-value))).astype(BF16).astype(F32)
    act[...] = reorder(cat([value[2 * zi + yi:2 * zi + yi + 1] for yi in (0, 1) for zi in range(n_z)], 0), n_hi)


def condition(labels, ids, table, n_z, n_hi):
    S, vmem = jax.ShapeDtypeStruct, pl.BlockSpec(memory_space=pltpu.VMEM)
    rows = S((labels.shape[0], table.shape[1]), F32)
    return pl.pallas_call(
        functools.partial(condition_kernel, n_z, n_hi),
        out_shape=(rows, rows, S((2, PIECE, LANES), BF16)),
        in_specs=[pl.BlockSpec(memory_space=pltpu.SMEM), vmem, pl.BlockSpec(memory_space=pl.ANY)],
        out_specs=(vmem, vmem, vmem),
        scratch_shapes=[pltpu.SemaphoreType.DMA((labels.shape[0],))],
        compiler_params=pltpu.CompilerParams(vmem_limit_bytes=VMEM_BYTES),
    )(labels, ids, table)


def per_device(n_f, n_c, n_z, tokens, cotangent, class_table, labels, scale_ids, in_weight, in_first, in_second,
               out_weight, out_first, out_second, vectors, vec_first, vec_second):
    n_hi = n_f // 2
    f, c, z, t, x, y = place()
    seqs, piece, width = tokens.shape
    cols = in_weight.shape[2]
    n_ff = out_weight.shape[0] - 1
    ada = 3 + n_ff
    half = cols // 2
    pairs = [[2 * i, 2 * i + 1] for i in range(n_hi)]
    his = [[i + 2 * j for j in range(n_hi)] for i in range(2)]

    def into(a):
        if n_hi == 1:
            return a
        shape = a.shape[:-1]
        return jnp.swapaxes(a.reshape(shape + (n_hi, 2 * n_c, -1)), -3, -2).reshape(a.shape)

    def back(a):
        if n_hi == 1:
            return a
        shape = a.shape[:-1]
        return jnp.swapaxes(a.reshape(shape + (2 * n_c, n_hi, -1)), -3, -2).reshape(a.shape)

    in_weight, in_first, in_second = [a.transpose(1, 0, 2) for a in (in_weight, in_first, in_second)]
    in_low, out_low = in_weight, out_weight
    if n_hi > 1:
        in_low = lax.all_gather(in_low.astype(BF16), "fsdp", axis=1, tiled=True, axis_index_groups=his).astype(F32)
        out_low = lax.all_gather(out_low.astype(BF16), "fsdp", axis=2, tiled=True, axis_index_groups=his).astype(F32)
    rows = in_low.shape[1]

    act, conditions, ids = condition(labels, scale_ids, class_table, n_z, n_hi)
    *kept, vec_all, act_rows = forward(
        in_low, out_low, into(tokens).transpose(1, 0, 2), into(cotangent).transpose(1, 0, 2), ids, act, vectors, n_z, n_hi)
    big, small = kept[:-3], kept[-3:]
    mixed, grad_low, g_in, g_out, g_vec, g_ada, cond_sum, norm = backward(
        big + [in_low] + small + [vec_all, act_rows], n_z, n_ff, n_hi)
    if n_hi > 1:
        g_vec = lax.psum(g_vec, "fsdp", axis_index_groups=his)
        g_in = lax.psum_scatter(g_in, "fsdp", scatter_dimension=2, tiled=True, axis_index_groups=his)
        g_ada = lax.psum_scatter(g_ada, "fsdp", scatter_dimension=1, tiled=True, axis_index_groups=his)
        g_out = lax.psum_scatter(g_out, "fsdp", scatter_dimension=3, tiled=True, axis_index_groups=his)
        squares = jnp.sum(g_in * g_in) + jnp.sum(g_ada * g_ada) + jnp.sum(g_out * g_out)
        squares = squares + jnp.where((f == 0) & (c == 0), jnp.sum(g_vec * g_vec), 0.0)
        norm = jnp.broadcast_to(jnp.sqrt(lax.psum(squares, ("fsdp", "ctx", "tp"))), norm.shape)
    *news, mixed, input_grad = update(
        [norm, cond_sum, conditions, g_vec, vectors, vec_first, vec_second],
        [g_in, g_ada, g_out, in_weight, in_first, in_second, out_weight, out_first, out_second], [mixed, grad_low],
        n_z, n_hi)
    bias_grad, condition_grad, norm = news[4:7]
    del news[4:7]
    mixed = mixed.transpose(1, 0, 2)
    vec_new, in_new, out_new = news[:4], [a.transpose(1, 0, 2) for a in news[4:8]], news[8:]
    input_grad = input_grad.transpose(1, 0, 2)
    return (back(mixed), back(input_grad), condition_grad, norm.reshape(()), *in_new, *out_new, *vec_new, bias_grad[0])


def solution(mesh):
    in_matrix = P(("fsdp", "ctx"), None, "tp")
    out_matrix = P(None, "tp", ("fsdp", "ctx"))
    vector = P(None, "tp")
    rows = P("fsdp", "ctx", None)
    return jax.shard_map(
        functools.partial(per_device, mesh.shape["fsdp"], mesh.shape["ctx"], mesh.shape["tp"]),
        mesh=mesh,
        in_specs=(rows, rows, P(), P("fsdp"), P("fsdp", "ctx"), in_matrix, in_matrix, in_matrix,
                  out_matrix, out_matrix, out_matrix, vector, vector, vector),
        out_specs=(rows, rows, P("fsdp", None), P(), in_matrix, in_matrix, in_matrix, in_matrix,
                   out_matrix, out_matrix, out_matrix, out_matrix, vector, vector, vector, vector, P("tp")),
        check_vma=False,
    )
```

```python
import functools
import math

import jax
import jax.numpy as jnp
from jax import lax
from jax.experimental import pallas as pl
from jax.experimental.pallas import tpu as pltpu
from jax.sharding import PartitionSpec as P

HD = 64
STEP = 5
PRECISE = lax.Precision.HIGHEST
NORM_EPS = 1e-06
CLIP_NORM = 1.0
BETA_ONE = 0.5
BETA_TWO = 0.5
RATE_MATRIX = 0.03
RATE_VECTOR = 0.3
WEIGHT_DECAY = 0.05
ADAM_EPS = 1e-08

MESH = pl.DeviceIdType.MESH
F32 = jnp.float32
BF16 = jnp.bfloat16
LANES = 128
VMEM_BYTES = 60 * 2**20


def place():
    f = lax.axis_index("fsdp")
    c = lax.axis_index("ctx")
    z = lax.axis_index("tp")
    return f, c, z, lax.rem(f, 2), lax.rem(c, 2), c // 2


def partners(n_z):
    f, c, z, t, x, y = place()
    core = (f + 1 - 2 * t, c, z)
    xp = (f, 2 * y + (1 - x), z)
    yp = (f, 2 * (1 - y) + x, z)
    zs = [(f, c, lax.rem(z + d, n_z)) for d in range(1, n_z)]
    return core, xp, yp, zs


def enter(targets):
    barrier = pltpu.get_barrier_semaphore()
    for target in targets:
        pl.semaphore_signal(barrier, inc=1, device_id=target, device_id_type=MESH)
    pl.semaphore_wait(barrier, len(targets))


def lanes_at(index):
    return pl.ds(pl.multiple_of(index * LANES, LANES), LANES)


def adam_update(master, first, second, grad, factor, rate, decay):
    grad = grad * factor
    first = BETA_ONE * first + (1.0 - BETA_ONE) * grad
    second = BETA_TWO * second + (1.0 - BETA_TWO) * grad * grad
    fix_one = 1.0 - BETA_ONE**STEP
    fix_two = 1.0 - BETA_TWO**STEP
    stride = first / fix_one / (jnp.sqrt(second / fix_two) + ADAM_EPS)
    master = master - rate * (stride + decay * master)
    return (master, first, second, master.astype(BF16))


def dot(a, b, dims):
    return lax.dot_general(a, b, (dims, ((), ())), preferred_element_type=F32)


NN = ((1,), (0,))
NT = ((1,), (1,))
TN = ((0,), (0,))


PIECE = 176
NEG = -1e30
PLANE_FIRST = (10, 11)
EXTRA_EVERY = 2
EXTRA_FROM = 2
AHEAD = 2
TICKS = (2, 2, 2, 2, 1, 1, 1, 1, 2, 1, 1, 0, 0, 3, 0, 1, 0, 1, 2, 2, 2, 1)
PARTS = 4
PASSES = 3
LOOK = 3
UNROLL = 2


def cat(parts, axis):
    return jnp.concatenate(parts, axis=axis)


def lane_of(shape):
    return lax.broadcasted_iota(jnp.int32, shape, len(shape) - 1)


def split_two(values):
    high = values.astype(BF16)
    return high, (values - high.astype(F32)).astype(BF16)


def split_three(values):
    high = values.astype(BF16)
    rest = values - high.astype(F32)
    middle = rest.astype(BF16)
    return high, middle, (rest - middle.astype(F32)).astype(BF16)


def head_mean(values):
    row = lax.broadcasted_iota(jnp.int32, (LANES, LANES), 0) // HD
    ones = jnp.where(row == lane_of((LANES, LANES)) // HD, 1.0 / HD, 0.0).astype(BF16)
    out = []
    for k in range(values.shape[1] // LANES):
        high, lower = split_two(values[:, k * LANES:(k + 1) * LANES])
        out.append(dot(high, ones, NN) + dot(lower, ones, NN))
    return cat(out, 1)


def gelu_both(u):
    k0, k1 = 0.7978845608028654, 0.044715
    square = u * u
    th = jnp.tanh(k0 * u * (1.0 + k1 * square))
    half = 0.5 * (1.0 + th)
    slope = half + 0.5 * u * (1.0 - th * th) * (k0 * (1.0 + 3.0 * k1 * square))
    return u * half, slope


def step_rows(piece, body):
    for p in (0, 1):
        def one(i, carry, p=p):
            start = pl.multiple_of(i * 16, 16)
            body(pl.ds(start, 16), pl.ds(pl.multiple_of(p * PIECE + start, 16), 16), p)
            return carry
        lax.fori_loop(0, piece // 16, one, 0, unroll=UNROLL)
        if piece % 16:
            start = piece // 16 * 16
            body(pl.ds(start, piece % 16), pl.ds(p * PIECE + start, piece % 16), p)


def clear_tail(ref, t):
    for p in (0, 1):
        ref[t, pl.ds(p * PIECE + PIECE - 16, 16), :] = jnp.zeros((16, ref.shape[2]), ref.dtype)


def normalize(values):
    center = values - jnp.mean(values, axis=-1, keepdims=True)
    scale = lax.rsqrt(jnp.mean(center * center, axis=-1, keepdims=True) + NORM_EPS)
    return center * scale, scale


def reorder(rows, n_hi, inverse=False):
    if n_hi == 1:
        return rows
    width = rows.shape[1]
    each = width // (8 * n_hi)
    out = []
    for k in range(width // LANES):
        at = k * LANES + lax.broadcasted_iota(jnp.int32, (width, LANES), 1)
        there = lax.broadcasted_iota(jnp.int32, (width, LANES), 0)
        if inverse:
            wanted = (at // each % 8) * (n_hi * each) + (at // (8 * each)) * each + at % each
        else:
            wanted = (at // each % n_hi) * (8 * each) + (at // (each * n_hi)) * each + at % each
        order = jnp.where(there == wanted, 1.0, 0.0).astype(BF16)
        out.append(sum(dot(part, order, NN) for part in split_three(rows)))
    return cat(out, 1)


class Wire:
    def __init__(self, send_sem, recv_sem):
        self.send_sem, self.recv_sem, self.sent = send_sem, recv_sem, []

    def make(self, at, src, dst, target, to=None):
        return pltpu.make_async_remote_copy(
            src_ref=src, dst_ref=dst, send_sem=self.send_sem.at[at], recv_sem=self.recv_sem.at[at if to is None else to],
            device_id=target, device_id_type=MESH)

    def start(self, at, src, dst, target, to=None):
        copy = self.make(at, src, dst, target, to)
        copy.start()
        self.sent.append(copy)
        return copy

    def finish(self):
        for copy in self.sent:
            copy.wait_send()


def forward_kernel(n_z, n_ff, n_hi, *refs):
    n_in, n_out = 3 + n_ff, 1 + n_ff
    (x_in, x_out, raw_tok, raw_cot, ids, act, vec,
     x_wq, x_wo, x_h1, x_qr, x_kr, x_q8, x_kh, x_v, x_o, x_lse, x_ma, x_mb, x_tok, x_cot, x_attn, x_mid,
     x_fown, x_fsend, x_down, x_dsend, x_gin, x_gout, x_mod, x_gu, x_gf, x_vec, x_act,
     g_in, g_out, tokb, cotb, idb, actb, pm, pr, ps, pf, vz, h1, gf, h2, qr, kr, q8, kh, vv, oo, lse, ma, mb,
     at_send, at_recv, attn, mid, facc, dacc, fsend, dsend, gin, gout, act_low, slope,
     full_in, full_out, low_in, low_out, local_sem, ag_send, ag_recv, m_send, m_recv, out_sem, tok_sem, load_sem,
     raw, widened, tok, cot, raw_sem) = refs
    f, c, z, t, x, y = place()
    core, xp, yp, zs = partners(n_z)
    f_base = f - t

    piece = raw_tok.shape[0]
    pick_loads = [pltpu.make_async_copy(raw_tok, raw, raw_sem.at[0]), pltpu.make_async_copy(raw_cot, raw, raw_sem.at[1])]
    pick_loads[0].start()

    def pick(load, dst):
        load.wait()

        def rows(at, count):
            widened[pl.ds(0, count)] = raw[at].astype(F32)
            for k in (0, 1):
                dst[k, at, :] = widened[pl.ds(0, count), 2 * z + k, :].astype(BF16)

        def one(i, carry):
            rows(pl.ds(pl.multiple_of(i * 16, 16), 16), 16)
            return carry
        lax.fori_loop(0, piece // 16, one, 0)
        if piece % 16:
            rows(pl.ds(piece // 16 * 16, piece % 16), piece % 16)

    n_all = x_in.shape[0]
    order = [("i", 0), ("i", 1), ("i", 2), ("o", 0)]
    for r in range(n_ff):
        order += [("i", 3 + r), ("o", 1 + r)]
    loads = {}
    for kind, m in [("i", j) for j in range(n_in, n_all)] + order:
        src, dst, at = (x_in, full_in, m) if kind == "i" else (x_out, full_out, n_all + m)
        loads[kind, m] = pltpu.make_async_copy(src.at[m], dst.at[m], load_sem.at[at])
        loads[kind, m].start()
    for ref in (h1, gf, h2):
        clear_tail(ref, t)

    barrier = pltpu.get_barrier_semaphore()
    plane = [xp, yp, (f, 3 - c, z)]
    other_line = [(f + 1 - 2 * t, c, target[2]) for target in zs]
    for target in [core] + plane + zs + other_line:
        pl.semaphore_signal(barrier, inc=1, device_id=target, device_id_type=MESH)
    loops = (y == t) & (x == t)
    for xs in (0, 1):
        @pl.when(jnp.logical_not(loops & (x == xs)))
        def _():
            pl.semaphore_signal(barrier, inc=1, device_id=(f_base + x, 2 * t + xs, z), device_id_type=MESH)
    pl.semaphore_wait(barrier, 4 + 2 * n_z - jnp.where(loops, 1, 0))

    ag = Wire(ag_send, ag_recv)
    misc = Wire(m_send, m_recv)

    shares = [(tok, tokb), (cot, cotb), (ids, None)]

    def send_share(j):
        src, dst = shares[j]
        for yd in (0, 1):
            own = loops & (y == yd)
            from_here = src.at[yd]
            to_there = dst.at[x] if dst is not None else idb.at[2 * y + x]

            @pl.when(own)
            def _():
                pltpu.make_async_copy(from_here, to_there, tok_sem.at[1, j, x]).start()

            @pl.when(jnp.logical_not(own))
            def _():
                pltpu.make_async_remote_copy(
                    src_ref=from_here, dst_ref=to_there, send_sem=tok_sem.at[0, j, yd], recv_sem=tok_sem.at[1, j, x],
                    device_id=(f_base + y, 2 * yd + t, z), device_id_type=MESH).start()

    def got_share(j):
        dst = shares[j][1]
        for xs in (0, 1):
            ref = dst.at[xs] if dst is not None else idb.at[2 * t + xs]
            pltpu.make_async_copy(ref, ref, tok_sem.at[1, j, xs]).wait()

    act_copy = misc.start(0, act.at[:, lanes_at((1 - t) * 4 + c)], actb.at[1], core)
    vec_local = pltpu.make_async_copy(vec, vz.at[z], local_sem.at[n_in + n_out])
    vec_local.start()
    vec_copies = [misc.start(1 + d, vec, vz.at[z], target) for d, target in enumerate(zs)]
    zrows = pl.ds(pl.multiple_of(z * LANES, LANES), LANES)
    first, zcopies, one, two = {}, {}, {}, {}

    def prepare(p):
        if p in first:
            return
        kind, m = order[p]
        loads[kind, m].wait()
        if kind == "i":
            dst = g_in.at[m, t, c, :, lanes_at(z)]
            for s in (0, 1):
                low_in[m, s] = full_in[m, :, s * LANES:(s + 1) * LANES].astype(BF16)
            mine, other = low_in.at[m, t], low_in.at[m, 1 - t]
        else:
            dst = g_out.at[m, t, zrows, lanes_at(c)]
            for s in (0, 1):
                low_out[m, s] = full_out[m, s * LANES:(s + 1) * LANES, :].astype(BF16)
            mine, other = low_out.at[m, t], low_out.at[m, 1 - t]
        local = pltpu.make_async_copy(mine, dst, local_sem.at[p])
        local.start()
        first[p] = (local, ag.start((p, 0), other, dst, core))

    base = n_z

    def start_zero(p):
        if p >= len(order) or p in zcopies or p in PLANE_FIRST:
            return
        kind, m = order[p]
        prepare(p)
        first[p][0].wait()
        first[p][1].wait_recv()
        block = g_in.at[m, :, c, :, lanes_at(z)] if kind == "i" else g_out.at[m, :, zrows, lanes_at(c)]
        zcopies[p] = [ag.start((p, 1 + d), block, block, target) for d, target in enumerate(zs)]

    line_first = [p for p in range(len(order)) if p not in PLANE_FIRST]

    def x_first(p):
        return line_first.index(p) % 2 == 0

    def start_one(p):
        kind, m = order[p]
        for copy in zcopies[p]:
            copy.wait_recv()
        block = g_in.at[m, :, c] if kind == "i" else g_out.at[m, :, :, lanes_at(c)]
        one[p] = ag.start((p, base), block, block, xp if x_first(p) else yp)

    def start_two(p):
        kind, m = order[p]
        one[p].wait_recv()
        held = (2 * y, 2 * y + 1) if x_first(p) else (x, 2 + x)
        two[p] = []
        if kind == "i" and x_first(p):
            block = g_in.at[m, :, pl.ds(2 * y, 2)]
            two[p].append(ag.start((p, base + 1), block, block, yp))
        else:
            for k, at in enumerate(held):
                block = g_in.at[m, :, at] if kind == "i" else g_out.at[m, :, :, lanes_at(at)]
                two[p].append(ag.start((p, base + 1 + k), block, block, yp if x_first(p) else xp))

    extras = []

    def start_plane(p):
        kind, m = order[p]
        prepare(p)
        first[p][0].wait()
        first[p][1].wait_recv()
        block = g_in.at[m, :, c, :, lanes_at(z)] if kind == "i" else g_out.at[m, :, zrows, lanes_at(c)]
        one[p] = [ag.start((p, base + k), block, block, target) for k, target in enumerate(plane)]
        two[p] = []

    def start_line(p, ck):
        kind, m = order[p]
        if ck == 0:
            for copy in one[p]:
                copy.wait_recv()
        block = g_in.at[m, :, ck, :, lanes_at(z)] if kind == "i" else g_out.at[m, :, zrows, lanes_at(ck)]
        for d, target in enumerate(zs):
            two[p].append(ag.start((p, base + 3 + 3 * ck + d), block, block, target))

    for p in PLANE_FIRST:
        extras.append((start_plane, (p,)))
    for p in PLANE_FIRST:
        extras += [(start_line, (p, ck)) for ck in range(4)]
    ticks = [(start_one, line_first[0])]
    for p, before in zip(line_first[1:], line_first[:-1]):
        ticks += [(start_one, p), (start_two, before)]
    ticks.append((start_two, line_first[-1]))
    ticked = [0]

    def tick(n=1):
        for _ in range(n):
            if ticks:
                step, p = ticks.pop(0)
                if step is start_one:
                    for ahead in range(p + AHEAD):
                        start_zero(ahead)
                step(p)
            ticked[0] += 1
            if extras and ticked[0] >= EXTRA_FROM and ticked[0] % EXTRA_EVERY == 0:
                step, what = extras.pop(0)
                step(*what)

    def arrived(p):
        while p not in two or (p in PLANE_FIRST and any(what[0] == p for unused, what in extras)):
            tick()
        for copy in two[p]:
            copy.wait_recv()

    flushed = []

    def flush(src, dst):
        copy = pltpu.make_async_copy(src, dst, out_sem.at[len(flushed)])
        copy.start()
        flushed.append(copy)

    prepare(0)
    prepare(1)
    pick(pick_loads[0], tok)
    pick_loads[1].start()
    act_copy.wait_recv()
    cols = vec.shape[1]
    for j in range(n_in, n_all):
        loads["i", j].wait()
    own_at = lanes_at(t * 4 + c)
    mine = act[:, own_at]
    theirs = actb[1]
    pm[...] = jnp.zeros_like(pm)
    seqs = 2 * n_z
    for s in (0, 1):
        rows = jnp.where(t == s, mine, theirs)
        x_act[seqs * s:seqs * (s + 1), :] = rows
        for j in range(n_all - n_in):
            pm[seqs * s:seqs * (s + 1), j, :] = dot(rows.astype(BF16), full_in[n_in + j].astype(BF16), NN)

    def of_chip(xx, yy):
        return pm.at[pl.ds(seqs * xx + n_z * yy, n_z)]

    mod_copies = [misc.start(1 + n_z + k, of_chip(xx, yy), pr.at[k], target)
                  for k, (target, (xx, yy)) in enumerate(zip(plane, [(1 - x, y), (x, 1 - y), (1 - x, 1 - y)]))]
    send_share(0)
    send_share(2)
    start_zero(0)
    for copy in mod_copies:
        copy.wait_recv()
    ps[...] = (of_chip(x, y)[...] + pr[0]) + (pr[1] + pr[2])
    pf[t, z] = ps[z]
    mod_copies = [misc.start(4 + n_z + k, ps.at[target[2]], pf.at[t, z], target)
                  for k, target in enumerate([core] + zs + other_line)]
    start_zero(1)
    for p in range(2, len(order)):
        prepare(p)
    tick()
    for copy in mod_copies + vec_copies:
        copy.wait_recv()
    vec_local.wait()
    row = lax.broadcasted_iota(jnp.int32, (8, cols), 0)
    for zi in range(n_z):
        bias = jnp.where(row < 6, vz[zi, 0:8, :], 0.0)
        x_mod[:, zi * cols:(zi + 1) * cols] = pf[0, zi] + pf[1, zi] + bias
    x_mod[...] = reorder(x_mod[...], n_hi)
    x_vec[...] = vz[...]
    tick()

    def wide(k):
        return cat([vz[zi, k:k + 1, :] for zi in range(n_z)], 1)

    def narrow(k):
        return cat([vz[zi, k:k + 1, lanes_at(t)] for zi in range(n_z)], 1)

    got_share(0)
    got_share(2)
    half = 2 * PIECE
    full = 2 * half
    mine_ids = idb.at[pl.ds(2 * t, 2)]
    id_copy = misc.start(4 + 3 * n_z, mine_ids, mine_ids, core)
    flush(tokb, x_tok)

    def first_norm(rows, at, p):
        normed, unused = normalize(tokb[p, rows, :].astype(F32))
        h1[t, at, :] = (normed * (1.0 + x_mod[1:2, :]) + x_mod[2:3, :]).astype(BF16)
    step_rows(piece, first_norm)
    h1_copy = misc.start(5 + 3 * n_z, h1.at[t], h1.at[t], core)

    tick(TICKS[0])
    id_copy.wait_recv()
    lanes = lane_of((full, LANES)) % HD
    scale = idb[...].reshape(full, LANES).astype(F32)
    feature = lanes.astype(F32)
    ma[...] = jnp.where((lanes < 16) & (feature > scale), 1.0, 0.0).astype(BF16)
    mb[...] = jnp.where((lanes < 16) & (feature == scale), NEG, 0.0).astype(BF16)
    flush(ma, x_ma)
    flush(mb, x_mb)
    tick(TICKS[1])
    h1_copy.wait_recv()

    def whole(ref):
        return ref[...].reshape(full, ref.shape[-1])

    def w_in(m):
        return g_in[m].reshape(8 * LANES, n_z * LANES)

    arrived(0)
    qr[...] = dot(whole(h1), w_in(0), NN) + narrow(6)
    q8[...] = (qr[...] * lax.rsqrt(head_mean(qr[...] * qr[...]) + NORM_EPS) * narrow(8)).astype(BF16) * 0.125
    tick(TICKS[2])
    arrived(1)
    kr[...] = dot(whole(h1), w_in(1), NN)
    kh[...] = (kr[...] * lax.rsqrt(head_mean(kr[...] * kr[...]) + NORM_EPS) * narrow(9)).astype(BF16)
    flush(qr, x_qr)
    flush(kr, x_kr)
    flush(q8, x_q8)
    flush(kh, x_kh)
    tick(TICKS[3])
    pick(pick_loads[1], cot)
    send_share(1)
    arrived(2)
    vv[...] = (dot(whole(h1), w_in(2), NN) + narrow(7)).astype(BF16)
    flush(vv, x_v)
    flush(h1, x_h1)
    flush(g_in.at[pl.ds(0, 3)], x_wq)
    def attend(i, carry):
        at = lanes_at(i)
        q2, k2, v2 = q8[:, at], kh[:, at], vv[:, at]
        mine_a, mine_b = ma[...], mb[...]
        low = lane_of((full, LANES)) < HD
        outs, tops = [], []
        for h in (0, 1):
            here = low if h == 0 else jnp.logical_not(low)
            s = dot(jnp.where(here, q2, mine_a), jnp.where(here, k2, mine_b), NT)
            top = jnp.max(s, axis=1, keepdims=True)
            e = jnp.exp(s - top).astype(BF16)
            got = dot(e, jnp.where(here, v2, jnp.ones_like(v2)), NN)
            total = got[:, HD:HD + 1] if h == 0 else got[:, 0:1]
            outs.append(got / total)
            tops.append(top + jnp.log(total))
        oo[:, at] = jnp.where(low, outs[0], outs[1]).astype(BF16)
        lse[:, at] = jnp.where(low, tops[0], tops[1])
        return carry

    pairs = n_z * LANES // LANES
    done = 0
    for i in range(pairs):
        tick(TICKS[4 + i])
        if i + 1 == pairs or TICKS[5 + i]:
            lax.fori_loop(done, i + 1, attend, 0)
            done = i + 1
    flush(oo, x_o)
    flush(lse, x_lse)

    arrived(3)
    flush(g_out.at[0], x_wo)
    width = 8 * LANES
    hw = width // 2
    for j in (0, 1):
        both = dot(oo[...], g_out[0, j], NN)
        attn[:, j * hw:(j + 1) * hw] = jnp.where(t == 0, both[:half], both[half:])
        at_send[:, j * hw:(j + 1) * hw] = jnp.where(t == 0, both[half:], both[:half]).astype(BF16)
    at_copy = misc.start(7 + 3 * n_z, at_send, at_recv, core)
    tick(TICKS[8])
    at_copy.wait_recv()
    proj_bias = reorder(wide(10 + n_ff), n_hi)


    def second_norm(rows, at, p):
        total = attn[at, :] + at_recv[at, :].astype(F32) + proj_bias
        attn[at, :] = total
        middle = tokb[p, rows, :].astype(F32) + x_mod[0:1, :] * total
        mid[at, :] = middle
        normed, unused = normalize(middle)
        h2[t, at, :] = (normed * (1.0 + x_mod[4:5, :]) + x_mod[5:6, :]).astype(BF16)
    step_rows(piece, second_norm)
    h2_copy = misc.start(8 + 3 * n_z, h2.at[t], h2.at[t], core)
    flush(attn, x_attn)
    flush(mid, x_mid)
    got_share(1)
    flush(cotb, x_cot)

    def gate(rows, at, p):
        gf[t, at, :] = (cotb[p, rows, :].astype(F32) * x_mod[3:4, :]).astype(BF16)
    step_rows(piece, gate)
    gf_copy = misc.start(6 + 3 * n_z, gf.at[t], gf.at[t], core)

    tick(TICKS[9])
    h2_copy.wait_recv()
    gf_copy.wait_recv()
    x_gf[...] = jnp.zeros_like(x_gf)
    x_gf[0:1, :] = jnp.sum(whole(gf).astype(F32), axis=0, keepdims=True)
    x_gu[...] = jnp.zeros_like(x_gu)

    mine_rows = pl.ds(pl.multiple_of(t * half, half), half)
    other_rows = pl.ds(pl.multiple_of((1 - t) * half, half), half)
    for r in range(n_ff):
        arrived(4 + 2 * r)
        bias_row = narrow(10 + r)
        u = dot(whole(h2), w_in(3 + r), NN) + bias_row
        value, gradient = gelu_both(u)
        act_low[...] = value.astype(BF16)
        slope[...] = gradient
        tick(TICKS[10 + 3 * r])
        for j in (0, 1):
            gout[r, j] = dot(act_low[...], gf[:, :, j * hw:(j + 1) * hw].reshape(full, hw), TN).astype(BF16)
        flush(gout.at[r], x_gout.at[r])
        arrived(5 + 2 * r)
        for j in (0, 1):
            part = dot(act_low[...], g_out[1 + r, j], NN)
            cols_here = pl.ds(j * hw, hw)
            facc[:, cols_here] = part if r == 0 else facc[:, cols_here] + part
        if r == n_ff - 1:
            fsend[...] = facc[other_rows, :].astype(BF16)
            flush(facc.at[mine_rows], x_fown)
            flush(fsend, x_fsend)
        back_act = (dot(gf[:, :, :hw].reshape(full, hw), g_out[1 + r, 0], NT)
                    + dot(gf[:, :, hw:].reshape(full, hw), g_out[1 + r, 1], NT))
        gu = (back_act * slope[...]).astype(BF16)
        act_low[...] = gu
        tick(TICKS[11 + 3 * r])
        x_gu[r:r + 1, :] = jnp.sum(gu.astype(F32), axis=0, keepdims=True)
        gin[r] = dot(whole(h2), act_low[...], TN).astype(BF16).reshape(gin.shape[1:])
        flush(gin.at[r], x_gin.at[r])
        tick(TICKS[12 + 3 * r])
        part = dot(act_low[...], w_in(3 + r), NT)
        dacc[...] = part if r == 0 else dacc[...] + part

    assert not ticks and not extras
    dsend[...] = dacc[other_rows, :].astype(BF16)
    flush(dacc.at[mine_rows], x_down)
    flush(dsend, x_dsend)
    for copy in flushed:
        copy.wait()
    for j, (src, dst) in enumerate(shares):
        for yd in (0, 1):
            @pl.when(jnp.logical_not(loops & (y == yd)))
            def _():
                ref = src.at[yd]
                pltpu.make_async_remote_copy(
                    src_ref=ref, dst_ref=ref, send_sem=tok_sem.at[0, j, yd], recv_sem=tok_sem.at[1, j, x],
                    device_id=(f_base + y, 2 * yd + t, z), device_id_type=MESH).wait_send()
    ag.finish()
    misc.finish()


def forward(x_in, x_out, tok, cot, ids, act, vec, n_z, n_hi):
    n_out = x_out.shape[0]
    n_ff = n_out - 1
    n_in = 3 + n_ff
    pieces = n_in + n_out
    here, width = n_z * LANES, 8 * LANES
    half, full = 2 * PIECE, 4 * PIECE
    piece, n_seq = tok.shape[:2]
    hw = width // 2
    S = jax.ShapeDtypeStruct
    wide_low, wide_full = S((half, width), BF16), S((half, width), F32)
    cols_low, cols_full = S((full, here), BF16), S((full, here), F32)
    mask = S((full, LANES), BF16)
    big = [
        S((3, 2, 4, LANES, here), BF16), S((2, here, hw), BF16), S((2, half, width), BF16), cols_full, cols_full,
        cols_low, cols_low, cols_low, cols_low, cols_full, mask, mask, S((2, piece, width), BF16),
        S((2, piece, width), BF16), wide_full, wide_full, wide_full, wide_low, wide_full, wide_low,
        S((n_ff, 2, 4, LANES, here), BF16), S((n_ff, 2, here, hw), BF16)]
    small = [S((8, width), F32), S((8, here), F32), S((8, width), F32), S((n_z,) + vec.shape, F32), S((4 * n_z, LANES), F32)]
    any_space, vmem = pl.BlockSpec(memory_space=pl.ANY), pl.BlockSpec(memory_space=pltpu.VMEM)
    mod_shape = (8, vec.shape[1])
    V = pltpu.VMEM
    dma = pltpu.SemaphoreType.DMA
    return pl.pallas_call(
        functools.partial(forward_kernel, n_z, n_ff, n_hi),
        out_shape=tuple(big + small),
        in_specs=[any_space] * 5 + [vmem] * 2,
        out_specs=tuple([any_space] * len(big) + [vmem] * len(small)),
        scratch_shapes=[
            V((n_in, 2, 4, LANES, here), BF16), V((n_out, 2, here, hw), BF16),
            V((2, piece, width), BF16), V((2, piece, width), BF16), V((4, PIECE, LANES), BF16),
            V((2, 2 * n_z, LANES), F32), V((4 * n_z,) + mod_shape, F32), V((3, n_z) + mod_shape, F32), V((n_z,) + mod_shape, F32),
            V((2, n_z) + mod_shape, F32), V((n_z,) + vec.shape, F32),
            V((2, half, width), BF16), V((2, half, width), BF16), V((2, half, width), BF16),
            V((full, here), F32), V((full, here), F32), V((full, here), BF16), V((full, here), BF16), V((full, here), BF16),
            V((full, here), BF16), V((full, here), F32), V((full, LANES), BF16), V((full, LANES), BF16),
            V((half, width), BF16), V((half, width), BF16), V((half, width), F32), V((half, width), F32),
            V((full, width), F32), V((full, width), F32), V((half, width), BF16), V((half, width), BF16),
            V((n_ff, 2, 4, LANES, here), BF16), V((n_ff, 2, here, hw), BF16), V((full, here), BF16), V((full, here), F32),
            V(x_in.shape, F32), V(x_out.shape, F32), V((n_in, 2, LANES, LANES), BF16), V((n_out, 2, LANES, LANES), BF16),
            dma((pieces + 1,)), dma((pieces, 4 * n_z + 3)), dma((pieces, 4 * n_z + 3)), dma((9 + 3 * n_z,)), dma((9 + 3 * n_z,)),
            dma((len(big) + 2 * n_ff,)), dma((2, 3, 2)), dma((x_in.shape[0] + n_out,)),
            V((piece, n_seq, width), BF16), V((16, n_seq, width), F32), V((2, piece, width), BF16), V((2, piece, width), BF16),
            dma((2,)),
        ],
        compiler_params=pltpu.CompilerParams(collective_id=0, has_side_effects=True, vmem_limit_bytes=VMEM_BYTES),
    )(x_in, x_out, tok, cot, ids, act, vec)

class Guarded:
    def __init__(self):
        self.sent = []

    def start(self, cond, copy):
        @pl.when(cond)
        def _():
            copy.start()
        self.sent.append((cond, copy))

    def finish(self):
        for cond, copy in self.sent:
            @pl.when(cond)
            def _(copy=copy):
                copy.wait_send()


def backward_kernel(n_z, n_ff, n_hi, *refs):
    n_in, n_out = 3 + n_ff, 1 + n_ff
    (x_wq, x_wo, x_h1, x_qr, x_kr, x_q8, x_kh, x_v, x_o, x_lse, x_ma, x_mb, x_tok, x_cot, x_attn, x_mid,
     x_fown, x_fsend, x_down, x_dsend, x_gin, x_gout, x_weight, mod, gu_sum, gf_sum, vz, act,
     o_mixed, o_grad, o_in, o_out, o_vec, o_ada, o_cond, o_norm,
     wq, wo, h1, qr, kr, q8, kh, vv, oo, lse, ma, mb, tokb, cotb, attn, mid, buf, f_recv, d_recv,
     dmid, ga, go, mixed, sums, vd, vdr, vs, vdz, zv, v_all, d_mod, v_half, norm, norm_plane, norm_line, cond_z, cond_all,
     p_full, q_full, p_half, q_half, a_in, a_out, b_in, b_out, z_in, z_out, f_in, f_out,
     load_sem, own_sem, rs_send, rs_recv, m_send, m_recv, t_send, t_recv, g_send, g_recv) = refs
    f, c, z, t, x, y = place()
    core, xp, yp, zs = partners(n_z)
    f_base = f - t
    last = n_z - 1
    half, full = 2 * PIECE, 4 * PIECE
    width = mod.shape[1]
    hw = width // 2
    piece = x_tok.shape[1]
    clear_tail(ga, t)

    barrier = pltpu.get_barrier_semaphore()
    diagonal = (f, 3 - c, z)
    plane = [xp, yp, diagonal]
    other_line = [(f + 1 - 2 * t, c, target[2]) for target in zs]
    for target in [core] + plane + zs + other_line:
        pl.semaphore_signal(barrier, inc=1, device_id=target, device_id_type=MESH)
    loops = (y == t) & (x == t)
    for ys in (0, 1):
        @pl.when(jnp.logical_not(loops & (y == ys)))
        def _():
            pl.semaphore_signal(barrier, inc=1, device_id=(f_base + y, 2 * ys + t, z), device_id_type=MESH)

    loads = {}
    names = [("f", x_fown, buf.at[0]), ("mid", x_mid, mid), ("cot", x_cot, cotb), ("d", x_down, buf.at[1]),
             ("attn", x_attn, attn), ("wo", x_wo, wo), ("o", x_o, oo), ("q", x_q8, q8), ("k", x_kh, kh), ("v", x_v, vv),
             ("lse", x_lse, lse), ("ma", x_ma, ma), ("mb", x_mb, mb), ("qr", x_qr, qr), ("kr", x_kr, kr),
             ("h1", x_h1, h1), ("wq", x_wq, wq), ("tok", x_tok, tokb)]
    for i, (name, src, dst) in enumerate(names):
        loads[name] = pltpu.make_async_copy(src, dst, load_sem.at[i])
        loads[name].start()
    pl.semaphore_wait(barrier, 4 + 2 * n_z - jnp.where(loops, 1, 0))

    rs = Wire(rs_send, rs_recv)
    misc = Wire(m_send, m_recv)
    chain = Guarded()
    f_copy = misc.start(0, x_fsend, f_recv, core)
    d_copy = misc.start(1, x_dsend, d_recv, core)

    order = []
    for r in range(n_ff):
        order += [("i", 3 + r), ("o", 1 + r)]
    order += [("o", 0), ("i", 2), ("i", 1), ("i", 0)]
    pieces = len(order)
    one, two, four, own_half = {}, {}, {}, {}

    def y_first(p):
        return p % 2 == 0

    def parts(p, mine):
        if y_first(p):
            yy = y if mine else 1 - y
            return [2 * yy, 2 * yy + 1]
        xx = x if mine else 1 - x
        return [xx, 2 + xx]

    def source(p, at):
        kind, m = order[p]
        if kind == "i":
            return x_gin.at[m - 3, :, at] if m >= 3 else p_full.at[m, :, at]
        return x_gout.at[m - 1, :, :, lanes_at(at)] if m >= 1 else q_full.at[:, :, lanes_at(at)]

    def kept(p, k):
        kind, m = order[p]
        return p_half.at[m, k] if kind == "i" else q_half.at[m, k]

    def bufs(p, inner, outer):
        kind, m = order[p]
        return inner.at[m] if kind == "i" else outer.at[m]

    def step_one(p):
        one[p] = [rs.start((p, k), source(p, at), bufs(p, a_in, a_out).at[k], yp if y_first(p) else xp)
                  for k, at in enumerate(parts(p, False))]
        own_half[p] = []
        for k, at in enumerate(parts(p, True)):
            copy = pltpu.make_async_copy(source(p, at), kept(p, k), own_sem.at[p, k])
            copy.start()
            own_half[p].append(copy)

    def step_two(p):
        for copy in one[p]:
            copy.wait_recv()
        for copy in own_half[p]:
            copy.wait()
        for k in (0, 1):
            ref = kept(p, k)
            ref[...] = (ref[...].astype(F32) + bufs(p, a_in, a_out)[k].astype(F32)).astype(BF16)
        go_bit = (1 - x) if y_first(p) else (1 - y)
        two[p] = rs.start((p, 2), kept(p, go_bit), bufs(p, b_in, b_out), xp if y_first(p) else yp)

    def span(p, ref, lo, hi):
        if order[p][0] == "i":
            return ref.at[:, :, lo * LANES:hi * LANES]
        return ref.at[:, lo * LANES:hi * LANES, :]

    def right_copy(p, s):
        here = kept(p, x if y_first(p) else y)
        return pltpu.make_async_remote_copy(
            src_ref=span(p, here, s + 1, n_z), dst_ref=span(p, bufs(p, z_in, z_out), s + 2, n_z + 1),
            send_sem=rs_send.at[p, 3], recv_sem=rs_recv.at[p, 3], device_id=(f, c, z + 1), device_id_type=MESH)

    def left_copy(p, s):
        here = kept(p, x if y_first(p) else y)
        return pltpu.make_async_remote_copy(
            src_ref=span(p, here, 0, s), dst_ref=span(p, bufs(p, z_in, z_out), 0, s),
            send_sem=rs_send.at[p, 4], recv_sem=rs_recv.at[p, 4], device_id=(f, c, z - 1), device_id_type=MESH)

    def add_into(p, lo, hi, shift):
        here = kept(p, x if y_first(p) else y)
        a, b = span(p, here, lo, hi), span(p, bufs(p, z_in, z_out), lo + shift, hi + shift)
        a[...] = (a[...].astype(F32) + b[...].astype(F32)).astype(BF16)

    def step_z(p, s):
        if s == 0:
            two[p].wait_recv()
            here = kept(p, x if y_first(p) else y)
            here[...] = (here[...].astype(F32) + bufs(p, b_in, b_out)[...].astype(F32)).astype(BF16)

        @pl.when(z == s)
        def _():
            if s > 0:
                landed = span(p, bufs(p, z_in, z_out), s + 1, n_z + 1)
                pltpu.make_async_copy(landed, landed, rs_recv.at[p, 3]).wait()
            if s < last:
                if s > 0:
                    add_into(p, s + 1, n_z, 1)
                right_copy(p, s).start()

        @pl.when(z == last - s)
        def _():
            e = last - s
            if s > 0:
                landed = span(p, bufs(p, z_in, z_out), 0, e + 1)
                pltpu.make_async_copy(landed, landed, rs_recv.at[p, 4]).wait()
            if e > 0:
                if s > 0:
                    add_into(p, 0, e, 0)
                left_copy(p, e).start()

    norm[...] = jnp.zeros_like(norm)

    def add_squares(values):
        square = values * values
        parts = [square[8 * i:8 * i + 8] for i in range(square.shape[0] // 8)]
        while len(parts) > 1:
            parts = [a + b for a, b in zip(parts[::2], parts[1::2])]
        for k in range(square.shape[1] // LANES):
            norm[...] = norm[...] + parts[0][:, k * LANES:(k + 1) * LANES]

    def step_core(p):
        kind, m = order[p]
        here = kept(p, x if y_first(p) else y)
        total, result = (f_in, o_in) if kind == "i" else (f_out, o_out)
        for s in range(n_z):
            @pl.when(z == s)
            def _():
                value = span(p, here, s, s + 1)[...].astype(F32)
                if s > 0:
                    value = value + span(p, bufs(p, z_in, z_out), s + 1, s + 2)[...].astype(F32)
                if s < last:
                    value = value + span(p, bufs(p, z_in, z_out), s, s + 1)[...].astype(F32)
                total[m] = value
        result[m, t] = total[m, t]
        add_squares(total[m, 0])
        add_squares(total[m, 1])
        four[p] = rs.start((p, 5), total.at[m, 1 - t], result.at[m, t], core)

    def in_range(p):
        return 0 <= p < pieces

    ready = [2 * n_ff]
    started = [0]
    step = [0]

    def first_sends(upto):
        while started[0] < min(upto, ready[0], pieces):
            step_one(started[0])
            started[0] += 1

    passes, chores = [], []

    def pump(n=1):
        for _ in range(n):
            k = step[0]
            first_sends(k + LOOK)
            if in_range(k) and k >= started[0]:
                return
            if in_range(k):
                step_two(k)
            for unused in range(PASSES):
                if passes:
                    pass_along(*passes.pop(0))
            for s in range(n_z):
                if in_range(k - 1 - 2 * s):
                    step_z(k - 1 - 2 * s, s)
            if in_range(k - 2 * n_z):
                step_core(k - 2 * n_z)
            if chores:
                chore = chores.pop(0)
                if chore is not None:
                    chore()
            step[0] += 1

    first_sends(2)

    def share_out(j, src, dst):
        for xs in (0, 1):
            own = loops & (x == xs)
            there = dst.at[2 * z + y]
            local = pltpu.make_async_copy(src.at[xs], there, t_recv.at[j, y])

            @pl.when(own)
            def _():
                local.start()
            chain.start(jnp.logical_not(own), pltpu.make_async_remote_copy(
                src_ref=src.at[xs], dst_ref=there, send_sem=t_send.at[j, xs], recv_sem=t_recv.at[j, y],
                device_id=(f_base + x, 2 * t + xs, z), device_id_type=MESH))

    def pass_along(j, dst, s, part):
        lanes = pl.ds(part * (width // PARTS), width // PARTS)
        if s == 0 and part == 0:
            for ys in (0, 1):
                pltpu.make_async_copy(dst.at[2 * z + ys], dst.at[2 * z + ys], t_recv.at[j, ys]).wait()
        for side, (there, back_at) in enumerate(((z + 1, z - s), (z - 1, z + s))):
            valid = (back_at >= 0) & (back_at <= last)
            block = dst.at[pl.ds(2 * lax.clamp(0, back_at, last), 2), :, lanes]
            if s > 0:
                @pl.when(valid)
                def _():
                    pltpu.make_async_copy(block, block, g_recv.at[j, side, s, part]).wait()
            if s < last:
                chain.start(valid & (there >= 0) & (there <= last), pltpu.make_async_remote_copy(
                    src_ref=block, dst_ref=block, send_sem=g_send.at[j, side, s, part],
                    recv_sem=g_recv.at[j, side, s + 1, part],
                    device_id=(f, c, lax.clamp(0, there, last)), device_id_type=MESH))

    def pass_all(j, dst):
        passes.extend((j, dst, s, part) for s in range(n_z) for part in range(PARTS))

    def wide(k):
        return cat([vz[zi, k:k + 1, :] for zi in range(n_z)], 1)

    def narrow(k):
        return cat([vz[zi, k:k + 1, lanes_at(t)] for zi in range(n_z)], 1)

    def tally(j, values):
        if values.shape[0] == 16:
            sums[j] = sums[j] + values[:8] + values[8:]
        else:
            sums[j, 0:1] = sums[j, 0:1] + jnp.sum(values, axis=0, keepdims=True)

    sums[...] = jnp.zeros_like(sums)

    ffn_bias = reorder(wide(11 + n_ff), n_hi)
    for name in ("f", "mid", "cot"):
        loads[name].wait()
    f_copy.wait_recv()

    def mix(rows, at, p):
        out = buf[0, at, :] + f_recv[at, :].astype(F32) + ffn_bias
        tally(3, cotb[p, rows, :].astype(F32) * out)
        mixed[p, rows, :] = (mid[at, :] + mod[3:4, :] * out).astype(BF16)
    step_rows(piece, mix)
    share_out(0, mixed, o_mixed)

    first_sends(LOOK)
    for name in ("d", "attn"):
        loads[name].wait()
    d_copy.wait_recv()

    def second_norm(rows, at, p):
        grad = buf[1, at, :] + d_recv[at, :].astype(F32)
        normed, scale = normalize(mid[at, :])
        tally(4, grad * normed)
        tally(5, grad)
        w = grad * (1.0 + mod[4:5, :])
        pulled = scale * (w - jnp.mean(w, axis=-1, keepdims=True) - normed * jnp.mean(w * normed, axis=-1, keepdims=True))
        total = cotb[p, rows, :].astype(F32) + pulled
        dmid[at, :] = total
        tally(0, total * attn[at, :])
        low = (total * mod[0:1, :]).astype(BF16)
        ga[t, at, :] = low
        tally(6, low.astype(F32))
    step_rows(piece, second_norm)
    ga_copy = misc.start(2, ga.at[t], ga.at[t], core)


    loads["wo"].wait()
    loads["o"].wait()
    ga_copy.wait_recv()
    pump(1)
    for j in (0, 1):
        ga_j = ga[:, :, j * hw:(j + 1) * hw].reshape(full, hw)
        part = dot(ga_j, wo[j], NT)
        if j == 0:
            first_part = part
    go[...] = (first_part + part).astype(BF16)
    for name in ("q", "k", "v", "lse", "ma", "mb", "qr", "kr"):
        loads[name].wait()
    pass_all(0, o_mixed)

    vs[...] = jnp.zeros_like(vs)

    def head_back(raw, grad, gain):
        scale = lax.rsqrt(head_mean(raw * raw) + NORM_EPS)
        normed = raw * scale
        gain_grad = jnp.sum(grad * normed, axis=0, keepdims=True)
        w = grad * gain
        return (scale * (w - normed * head_mean(w * normed))).astype(BF16), gain_grad

    def attend_back(i, carry):
        at = lanes_at(i)
        q2, k2, v2, g2, o2 = q8[:, at], kh[:, at], vv[:, at], go[:, at], oo[:, at]
        mine_a, mine_b = ma[...], mb[...]
        lanes = lane_of((full, LANES))
        low, l64 = lanes < HD, lanes % HD
        product = o2.astype(F32) * g2.astype(F32)
        dqs, dks, dvs = [], [], []
        one_like, zero_like = jnp.ones_like(v2), jnp.zeros_like(v2)
        for h in (0, 1):
            here = low if h == 0 else jnp.logical_not(low)
            l1, l2, l3 = split_three(lse[:, at][:, HD * h:HD * h + 1])
            qa = jnp.where(l64 == 40, -l1, jnp.where(l64 == 41, -l2, jnp.where(l64 == 42, -l3, mine_a)))
            ka = jnp.where((l64 >= 40) & (l64 < 43), one_like, mine_b)
            weight = jnp.exp(dot(jnp.where(here, k2, ka), jnp.where(here, q2, qa), NT))
            d1, d2, d3 = split_three(jnp.sum(jnp.where(here, product, 0.0), axis=1, keepdims=True))
            da = jnp.where(l64 == 0, -d1, jnp.where(l64 == 1, -d2, jnp.where(l64 == 2, -d3, zero_like)))
            va = jnp.where(l64 < 3, one_like, zero_like)
            ds = (weight * dot(jnp.where(here, v2, va), jnp.where(here, g2, da), NT)).astype(BF16)
            dvs.append(dot(weight.astype(BF16), g2, NN))
            dks.append(dot(ds, q2, NN))
            dqs.append(dot(ds, k2, TN))
        dq = jnp.where(low, dqs[0], dqs[1]) * 0.125
        dk = jnp.where(low, dks[0], dks[1])
        gq, q_gain = head_back(qr[:, at], dq, vs[8:9, at])
        gk, k_gain = head_back(kr[:, at], dk, vs[9:10, at])
        gv = jnp.where(low, dvs[0], dvs[1]).astype(BF16)
        q8[:, at] = gq
        kh[:, at] = gk
        vv[:, at] = gv
        vs[0:1, at] = jnp.sum(gq.astype(F32), axis=0, keepdims=True)
        vs[1:2, at] = jnp.sum(gv.astype(F32), axis=0, keepdims=True)
        vs[2:3, at] = q_gain
        vs[3:4, at] = k_gain
        return carry

    vs[8:9, :] = narrow(8)
    vs[9:10, :] = narrow(9)
    pairs = n_z
    for i in range(0, pairs, 2):
        lax.fori_loop(i, i + 2, attend_back, 0)
        pump(1)
    ada_refs, ada_loads = [], []
    for j in range(6):
        rows_at, cols_at = (j // 2) * LANES, (j % 2) * (n_z * LANES // 2)
        ada_refs.append(qr.at[rows_at:rows_at + LANES, cols_at:cols_at + n_z * LANES // 2])
        ada_loads.append(pltpu.make_async_copy(x_weight.at[3 + n_ff + j], ada_refs[j], load_sem.at[len(names) + j]))
        ada_loads[j].start()
    loads["wq"].wait()
    part = dot(q8[...], wq[0].reshape(width, n_z * LANES), NT)
    part = part + dot(kh[...], wq[1].reshape(width, n_z * LANES), NT)
    part = part + dot(vv[...], wq[2].reshape(width, n_z * LANES), NT)
    buf[0] = jnp.where(t == 0, part[:half], part[half:])
    f_recv[...] = jnp.where(t == 0, part[half:], part[:half]).astype(BF16)
    h_copy = misc.start(3, f_recv, d_recv, core)
    for j in (0, 1):
        ga_j = ga[:, :, j * hw:(j + 1) * hw].reshape(full, hw)
        q_full[j] = dot(oo[...], ga_j, TN).astype(BF16)
    ready[0] += 1
    loads["h1"].wait()
    h1_all = h1[...].reshape(full, width)
    for m, ref in ((2, vv), (1, kh), (0, q8)):
        p_full[m] = dot(h1_all, ref[...], TN).astype(BF16).reshape(p_full.shape[1:])
        ready[0] += 1
    loads["tok"].wait()
    pump(1)
    h_copy.wait_recv()

    def first_norm(rows, at, p):
        grad = buf[0, at, :] + d_recv[at, :].astype(F32)
        normed, scale = normalize(tokb[p, rows, :].astype(F32))
        tally(1, grad * normed)
        tally(2, grad)
        w = grad * (1.0 + mod[1:2, :])
        pulled = scale * (w - jnp.mean(w, axis=-1, keepdims=True) - normed * jnp.mean(w * normed, axis=-1, keepdims=True))
        cotb[p, rows, :] = (dmid[at, :] + pulled).astype(BF16)
    step_rows(piece, first_norm)
    share_out(1, cotb, o_grad)
    pass_all(1, o_grad)
    pump(1)

    for j in range(7):
        vd[j:j + 1, :] = jnp.sum(sums[j], axis=0, keepdims=True)
    vd[7:8, :] = gf_sum[0:1, :] * 0.5
    v_copy = misc.start(4, vd, vdr, core)
    vs[4:8, :] = gu_sum[0:4, :]
    cols = width // n_z
    n_ada = 6
    chips = 4 * n_z
    waits = {}

    def exact(a, b, dims):
        return lax.dot_general(a, b, (dims, ((), ())), precision=PRECISE, preferred_element_type=F32)

    def arrive(name):
        for copy in waits.pop(name):
            copy.wait_recv()

    def mods(j):
        return d_mod[...].reshape(chips, 8, cols)[:, j, :]

    def along_line():
        v_copy.wait_recv()
        vd_all = reorder(vd[...] + vdr[...], n_hi, inverse=True)
        for zi in range(n_z):
            vdz[zi] = vd_all[:, zi * cols:(zi + 1) * cols]
        d_mod[x, y, z] = vdz[z]
        zv[z] = vs[0:8, lanes_at(z)]
        waits["line"] = []
        for d, target in enumerate(zs):
            zi = lax.rem(z + 1 + d, n_z)
            waits["line"].append(misc.start(5 + d, vdz.at[zi], d_mod.at[x, y, z], target))
            waits["line"].append(misc.start(4 + n_z + d, vs.at[pl.ds(0, 8), lanes_at(zi)], zv.at[z], target))

    slot = 3 + 2 * n_z

    def over_plane():
        arrive("line")
        total = zv[0]
        for zi in range(1, n_z):
            total = total + zv[zi]
        v_all[x, y] = total
        waits["plane"] = []
        for d, target in enumerate(plane):
            waits["plane"].append(misc.start(slot + d, d_mod.at[x, y], d_mod.at[x, y], target))
            waits["plane"].append(misc.start(slot + 3 + d, v_all.at[x, y], v_all.at[x, y], target))

    def products():
        arrive("plane")
        v_half[t] = (v_all[0, 0] + v_all[0, 1]) + (v_all[1, 0] + v_all[1, 1])
        waits["vec"] = [misc.start(slot + 6, v_half.at[t], v_half.at[t], core)]
        for copy in ada_loads:
            copy.wait()
        total = 0.0
        for j, ref in enumerate(ada_refs):
            total = total + exact(mods(j), ref[...].astype(BF16).astype(F32), NT)
        cond_z[z] = total
        waits["cond line"] = [misc.start(slot + 7 + d, cond_z.at[z], cond_z.at[z], target) for d, target in enumerate(zs)]
        for j in range(n_ada):
            o_ada[j] = exact(act[...], mods(j), TN)
            if n_hi == 1:
                add_squares(o_ada[j])

    def cond_plane():
        arrive("cond line")
        total = cond_z[0]
        for zi in range(1, n_z):
            total = total + cond_z[zi]
        cond_all[t, c] = total
        at = slot + 6 + n_z
        waits["cond plane"] = [misc.start(at + d, cond_all.at[t, c], cond_all.at[t, c], target)
                               for d, target in enumerate(plane)]

    def cond_core():
        arrive("cond plane")
        waits["cond core"] = [misc.start(slot + 9 + n_z, cond_all.at[t], cond_all.at[t], core)]

    chores.extend([along_line, None, over_plane, None, products, None, cond_plane, None, cond_core])

    while step[0] < pieces + 2 * n_z or chores:
        pump(1)
    while passes:
        pass_along(*passes.pop(0))
    arrive("cond core")
    mine = pl.ds(pl.multiple_of(2 * n_z * t, 2 * n_z), 2 * n_z)
    o_cond[...] = cat([cond_all[ti, ck, mine, :] for ti in (0, 1) for ck in range(4)], 1)

    arrive("vec")
    mod_sum = jnp.sum(d_mod[...].reshape(chips, 8, cols), axis=0)
    o_vec[...] = cat([mod_sum[:n_ada], cat([v_half[0], v_half[1]], 1), mod_sum[n_ada:]], 0)
    if n_hi == 1:
        square = o_vec[...] * o_vec[...]
        square = square[:8] + square[8:]
        vec_squares = sum(square[:, k * LANES:(k + 1) * LANES] for k in range(cols // LANES))
        slot = slot + 10 + n_z
        norm_plane[c] = norm[...] + jnp.where((f == 0) & (c == 0), vec_squares, 0.0)
        copies = [misc.start(slot + d, norm_plane.at[c], norm_plane.at[c], target) for d, target in enumerate(plane)]
        for copy in copies:
            copy.wait_recv()
        norm_line[t, z] = (norm_plane[0] + norm_plane[1]) + (norm_plane[2] + norm_plane[3])
        copies = [misc.start(slot + 3 + d, norm_line.at[t, z], norm_line.at[t, z], target)
                  for d, target in enumerate([core] + zs + other_line)]
        for copy in copies:
            copy.wait_recv()
        total = norm_line[0, 0]
        for ti in (0, 1):
            for zi in range(n_z):
                if ti + zi > 0:
                    total = total + norm_line[ti, zi]
        total = jnp.sum(jnp.sum(total, axis=0, keepdims=True), axis=1, keepdims=True)
        o_norm[...] = jnp.broadcast_to(jnp.sqrt(total), o_norm.shape)
    else:
        o_norm[...] = jnp.zeros_like(o_norm)
    for p in range(pieces):
        four[p].wait_recv()
    for p in range(pieces):
        for s in range(n_z):
            @pl.when(z == s)
            def _():
                if s < last:
                    right_copy(p, s).wait_send()
                if s > 0:
                    left_copy(p, s).wait_send()
    chain.finish()
    rs.finish()
    misc.finish()


def backward(operands, n_z, n_ff, n_hi):
    n_in, n_out = 3 + n_ff, 1 + n_ff
    here, width = n_z * LANES, 8 * LANES
    half, full = 2 * PIECE, 4 * PIECE
    hw, cols = width // 2, width // n_z
    S, V, dma = jax.ShapeDtypeStruct, pltpu.VMEM, pltpu.SemaphoreType.DMA
    any_space, vmem = pl.BlockSpec(memory_space=pl.ANY), pl.BlockSpec(memory_space=pltpu.VMEM)
    piece = operands[12].shape[1]
    rows_out = S((2 * n_z, piece, width), BF16)
    pieces = n_in + n_out
    slots = 24 + 5 * n_z
    return pl.pallas_call(
        functools.partial(backward_kernel, n_z, n_ff, n_hi),
        out_shape=(rows_out, rows_out, S((n_in, 2, LANES, LANES), F32), S((n_out, 2, LANES, LANES), F32),
                   S((16, cols), F32), S((6, LANES, cols), F32), S((2 * n_z, width), F32),
                   S((8, LANES), F32)),
        in_specs=[any_space] * (len(operands) - 5) + [vmem] * 5,
        out_specs=tuple([any_space] * 2 + [vmem] * 6),
        scratch_shapes=[
            V((3, 2, 4, LANES, here), BF16), V((2, here, hw), BF16), V((2, half, width), BF16),
            V((full, here), F32), V((full, here), F32), V((full, here), BF16), V((full, here), BF16),
            V((full, here), BF16), V((full, here), BF16), V((full, here), F32), V((full, LANES), BF16),
            V((full, LANES), BF16), V((2, piece, width), BF16), V((2, piece, width), BF16), V((half, width), F32),
            V((half, width), F32), V((2, half, width), F32), V((half, width), BF16), V((half, width), BF16),
            V((half, width), F32), V((2, half, width), BF16), V((full, here), BF16), V((2, piece, width), BF16),
            V((8, 8, width), F32), V((8, width), F32), V((8, width), F32), V((16, here), F32),
            V((n_z, 8, cols), F32), V((n_z, 8, LANES), F32), V((2, 2, 8, LANES), F32),
            V((2, 2, n_z, 8, cols), F32), V((2, 8, LANES), F32), V((8, LANES), F32), V((4, 8, LANES), F32), V((2, n_z, 8, LANES), F32), V((n_z, 4 * n_z, LANES), F32), V((2, 4, 4 * n_z, LANES), F32),
            V((3, 2, 4, LANES, here), BF16), V((2, here, hw), BF16),
            V((n_in, 2, 2, LANES, here), BF16), V((n_out, 2, 2, here, LANES), BF16),
            V((n_in, 2, 2, LANES, here), BF16), V((n_out, 2, 2, here, LANES), BF16),
            V((n_in, 2, LANES, here), BF16), V((n_out, 2, here, LANES), BF16),
            V((n_in, 2, LANES, here + LANES), BF16), V((n_out, 2, here + LANES, LANES), BF16),
            V((n_in, 2, LANES, LANES), F32), V((n_out, 2, LANES, LANES), F32),
            dma((24,)), dma((pieces, 2)), dma((pieces, 6)), dma((pieces, 6)), dma((slots,)), dma((slots,)),
            dma((2, 2)), dma((2, 2)), dma((2, 2, n_z, PARTS)), dma((2, 2, n_z, PARTS)),
        ],
        compiler_params=pltpu.CompilerParams(collective_id=1, has_side_effects=True, vmem_limit_bytes=VMEM_BYTES),
    )(*operands)


def update_kernel(n_z, n_hi, *refs):
    (norm, cond_sum, cond, g_vec, w_vec, m_vec, v_vec, g_in, g_ada, g_out, w_in, m_in, v_in, w_out, m_out, v_out, mixed, grads,
     w_vec_new, m_vec_new, v_vec_new, c_vec_new, o_bias, o_cond, o_norm,
     w_in_new, m_in_new, v_in_new, c_in_new, w_out_new, m_out_new, v_out_new, c_out_new, o_mixed, o_grads,
     gi, ga, go, wi, mi, vi, ci, wo, mo, vo, co, low, wide, low_out, high, load_sem, store_sem) = refs
    n_seq, piece = mixed.shape[:2]
    loads, stores = {}, []

    def load(name, src, dst):
        loads[name] = pltpu.make_async_copy(src, dst, load_sem.at[len(loads)])
        loads[name].start()

    def store(src, dst):
        copy = pltpu.make_async_copy(src, dst, store_sem.at[len(stores)])
        copy.start()
        stores.append(copy)

    load("grads", grads, low.at[1])
    load("mixed", mixed, low.at[0])
    for name, src, dst in (("gi", g_in, gi), ("ga", g_ada, ga), ("wi", w_in, wi), ("mi", m_in, mi), ("vi", v_in, vi),
                           ("go", g_out, go), ("wo", w_out, wo), ("mo", m_out, mo), ("vo", v_out, vo)):
        load(name, src, dst)
    n_all, n_rows, cols = w_in.shape
    n_out = w_out.shape[0]
    factor = (CLIP_NORM / jnp.maximum(norm[0:1, 0:1], CLIP_NORM))
    factor_in = jnp.broadcast_to(factor, (1, cols))
    factor_out = jnp.broadcast_to(factor, (1, w_out.shape[2]))
    o_norm[...] = norm[0:1, 0:1]
    back = reorder(cond_sum[...], n_hi, inverse=True)
    rows = [back[n_z * yy + zi:n_z * yy + zi + 1] for zi in range(n_z) for yy in (0, 1)]
    gate = 1.0 / (1.0 + jnp.exp(-cond[...]))
    o_cond[...] = cat(rows, 0) * (gate * (1.0 + cond[...] * (1.0 - gate)))
    loads["grads"].wait()
    for i in range(n_seq):
        high[0:piece, i, :] = low[1, i].astype(F32)
    store(high.at[pl.ds(0, piece)], o_grads)
    w_vec_new[...], m_vec_new[...], v_vec_new[...], c_vec_new[...] = adam_update(
        w_vec[...], m_vec[...], v_vec[...], g_vec[...], factor_in, RATE_VECTOR, 0.0)
    last = g_vec.shape[0]
    o_bias[...] = g_vec[last - 1:last] * factor_in
    for name in ("gi", "ga", "wi", "mi", "vi"):
        loads[name].wait()
    lead = n_all - ga.shape[0]

    def update(m, grad):
        wi[m], mi[m], vi[m], ci[m] = adam_update(wi[m], mi[m], vi[m], grad, factor_in, RATE_MATRIX, WEIGHT_DECAY)

    def lead_rows(m, carry):
        update(m, cat([gi[m, 0], gi[m, 1]], 1))
        return carry

    def ada_rows(m, carry):
        update(lead + m, ga[m])
        return carry

    for lo, hi, body, shift in ((0, lead, lead_rows, 0), (0, n_all - lead, ada_rows, lead)):
        lax.fori_loop(lo, hi, body, 0)
        at = pl.ds(shift, hi)
        for src, dst in ((wi, w_in_new), (mi, m_in_new), (vi, v_in_new), (ci, c_in_new)):
            store(src.at[at], dst.at[at])
    for name in ("go", "wo", "mo", "vo"):
        loads[name].wait()
    for m in range(n_out):
        grad = cat([go[m, 0], go[m, 1]], 0)
        wo[m], mo[m], vo[m], co[m] = adam_update(wo[m], mo[m], vo[m], grad, factor_out, RATE_MATRIX, WEIGHT_DECAY)
    for src, dst in ((wo, w_out_new), (mo, m_out_new), (vo, v_out_new), (co, c_out_new)):
        store(src, dst)
    loads["mixed"].wait()
    for i in range(n_seq):
        wide[0:piece, i, :] = low[0, i].astype(F32)
    low_out[...] = wide[0:piece].astype(BF16)
    store(low_out, o_mixed)
    for copy in stores:
        copy.wait()


def update(small, large, rows_low, n_z, n_hi):
    S, V, dma = jax.ShapeDtypeStruct, pltpu.VMEM, pltpu.SemaphoreType.DMA
    any_space, vmem = pl.BlockSpec(memory_space=pl.ANY), pl.BlockSpec(memory_space=pltpu.VMEM)
    w_vec = small[4]
    g_in, g_ada, g_out, w_in, w_out = large[0], large[1], large[2], large[3], large[6]
    kinds = [S(a.shape, F32) for a in (w_vec, w_in, w_out)]
    news = [[k] * 3 + [S(k.shape, BF16)] for k in kinds]
    n_seq, piece, width = rows_low[0].shape
    turned = (piece, n_seq, width)
    whole = (PIECE, n_seq, width)
    return pl.pallas_call(
        functools.partial(update_kernel, n_z, n_hi),
        out_shape=tuple(news[0] + [S((1, w_vec.shape[1]), F32), S(small[2].shape, F32), S((1, 1), F32)] + news[1] + news[2] + [S(turned, BF16), S(turned, F32)]),
        in_specs=[vmem] * len(small) + [any_space] * (len(large) + 2),
        out_specs=tuple([vmem] * 7 + [any_space] * 10),
        scratch_shapes=[
            V(g_in.shape, F32), V(g_ada.shape, F32), V(g_out.shape, F32),
            V(w_in.shape, F32), V(w_in.shape, F32), V(w_in.shape, F32), V(w_in.shape, BF16),
            V(w_out.shape, F32), V(w_out.shape, F32), V(w_out.shape, F32), V(w_out.shape, BF16),
            V((2,) + rows_low[0].shape, BF16), V(whole, F32), V(turned, BF16), V(whole, F32), dma((11,)), dma((16,)),
        ],
        compiler_params=pltpu.CompilerParams(vmem_limit_bytes=VMEM_BYTES),
    )(*small, *large, *rows_low)


def condition_kernel(n_z, n_hi, labels, ids, table, act, cond, columns, sem):
    z = lax.axis_index("tp")
    n_seq, piece = ids.shape
    copies = [pltpu.make_async_copy(table.at[pl.ds(labels[i], 1)], cond.at[pl.ds(i, 1)], sem.at[i]) for i in range(n_seq)]
    for copy in copies:
        copy.start()
    low_ids = ids[...].astype(F32).astype(BF16)
    row = lax.broadcasted_iota(jnp.int32, (n_seq, LANES), 0)
    columns[...] = jnp.full(columns.shape, 10.0, BF16)
    for k in (0, 1):
        pick = jnp.where(row == 2 * z + k, 1.0, 0.0).astype(BF16)
        columns[k, 0:piece, :] = dot(low_ids, pick, TN).astype(BF16)
    for copy in copies:
        copy.wait()
    value = cond[...]
    value = (value / (1.0 + jnp.exp(-value))).astype(BF16).astype(F32)
    act[...] = reorder(cat([value[2 * zi + yi:2 * zi + yi + 1] for yi in (0, 1) for zi in range(n_z)], 0), n_hi)


def condition(labels, ids, table, n_z, n_hi):
    S, vmem = jax.ShapeDtypeStruct, pl.BlockSpec(memory_space=pltpu.VMEM)
    rows = S((labels.shape[0], table.shape[1]), F32)
    return pl.pallas_call(
        functools.partial(condition_kernel, n_z, n_hi),
        out_shape=(rows, rows, S((2, PIECE, LANES), BF16)),
        in_specs=[pl.BlockSpec(memory_space=pltpu.SMEM), vmem, pl.BlockSpec(memory_space=pl.ANY)],
        out_specs=(vmem, vmem, vmem),
        scratch_shapes=[pltpu.SemaphoreType.DMA((labels.shape[0],))],
        compiler_params=pltpu.CompilerParams(vmem_limit_bytes=VMEM_BYTES),
    )(labels, ids, table)


def per_device(n_f, n_c, n_z, tokens, cotangent, class_table, labels, scale_ids, in_weight, in_first, in_second,
               out_weight, out_first, out_second, vectors, vec_first, vec_second):
    n_hi = n_f // 2
    f, c, z, t, x, y = place()
    seqs, piece, width = tokens.shape
    cols = in_weight.shape[2]
    n_ff = out_weight.shape[0] - 1
    ada = 3 + n_ff
    half = cols // 2
    pairs = [[2 * i, 2 * i + 1] for i in range(n_hi)]
    his = [[i + 2 * j for j in range(n_hi)] for i in range(2)]

    def into(a):
        if n_hi == 1:
            return a
        shape = a.shape[:-1]
        return jnp.swapaxes(a.reshape(shape + (n_hi, 2 * n_c, -1)), -3, -2).reshape(a.shape)

    def back(a):
        if n_hi == 1:
            return a
        shape = a.shape[:-1]
        return jnp.swapaxes(a.reshape(shape + (2 * n_c, n_hi, -1)), -3, -2).reshape(a.shape)

    in_weight, in_first, in_second = [a.transpose(1, 0, 2) for a in (in_weight, in_first, in_second)]
    in_low, out_low = in_weight, out_weight
    if n_hi > 1:
        in_low = lax.all_gather(in_low.astype(BF16), "fsdp", axis=1, tiled=True, axis_index_groups=his).astype(F32)
        out_low = lax.all_gather(out_low.astype(BF16), "fsdp", axis=2, tiled=True, axis_index_groups=his).astype(F32)
    rows = in_low.shape[1]

    act, conditions, ids = condition(labels, scale_ids, class_table, n_z, n_hi)
    *kept, vec_all, act_rows = forward(
        in_low, out_low, into(tokens).transpose(1, 0, 2), into(cotangent).transpose(1, 0, 2), ids, act, vectors, n_z, n_hi)
    big, small = kept[:-3], kept[-3:]
    mixed, grad_low, g_in, g_out, g_vec, g_ada, cond_sum, norm = backward(
        big + [in_low] + small + [vec_all, act_rows], n_z, n_ff, n_hi)
    if n_hi > 1:
        g_vec = lax.psum(g_vec, "fsdp", axis_index_groups=his)
        g_in = lax.psum_scatter(g_in, "fsdp", scatter_dimension=2, tiled=True, axis_index_groups=his)
        g_ada = lax.psum_scatter(g_ada, "fsdp", scatter_dimension=1, tiled=True, axis_index_groups=his)
        g_out = lax.psum_scatter(g_out, "fsdp", scatter_dimension=3, tiled=True, axis_index_groups=his)
        squares = jnp.sum(g_in * g_in) + jnp.sum(g_ada * g_ada) + jnp.sum(g_out * g_out)
        squares = squares + jnp.where((f == 0) & (c == 0), jnp.sum(g_vec * g_vec), 0.0)
        norm = jnp.broadcast_to(jnp.sqrt(lax.psum(squares, ("fsdp", "ctx", "tp"))), norm.shape)
    *news, mixed, input_grad = update(
        [norm, cond_sum, conditions, g_vec, vectors, vec_first, vec_second],
        [g_in, g_ada, g_out, in_weight, in_first, in_second, out_weight, out_first, out_second], [mixed, grad_low],
        n_z, n_hi)
    bias_grad, condition_grad, norm = news[4:7]
    del news[4:7]
    mixed = mixed.transpose(1, 0, 2)
    vec_new, in_new, out_new = news[:4], [a.transpose(1, 0, 2) for a in news[4:8]], news[8:]
    input_grad = input_grad.transpose(1, 0, 2)
    return (back(mixed), back(input_grad), condition_grad, norm.reshape(()), *in_new, *out_new, *vec_new, bias_grad[0])


def solution(mesh):
    in_matrix = P(("fsdp", "ctx"), None, "tp")
    out_matrix = P(None, "tp", ("fsdp", "ctx"))
    vector = P(None, "tp")
    rows = P("fsdp", "ctx", None)
    return jax.shard_map(
        functools.partial(per_device, mesh.shape["fsdp"], mesh.shape["ctx"], mesh.shape["tp"]),
        mesh=mesh,
        in_specs=(rows, rows, P(), P("fsdp"), P("fsdp", "ctx"), in_matrix, in_matrix, in_matrix,
                  out_matrix, out_matrix, out_matrix, vector, vector, vector),
        out_specs=(rows, rows, P("fsdp", None), P(), in_matrix, in_matrix, in_matrix, in_matrix,
                   out_matrix, out_matrix, out_matrix, out_matrix, vector, vector, vector, vector, P("tp")),
        check_vma=False,
    )
```
